128 devices in a mesh: tower: 2 (over core), dp: 64 (over z, x, y).
Axes of the slice: x: 4, y: 4, z: 4, core: 2. Of those that a mesh axis runs over, the one named last changes fastest.
Arguments:
- image_tokens: bfloat16 [1024, 50, 768], P(('tower', 'dp')), may hold values from -6 to 6
- image_first_gain: float32 [768], replicated, may hold values from 0.5 to 1.5
- image_first_shift: float32 [768], replicated, may hold values from -3 to 3
- image_joint_weight: bfloat16 [768, 2304], replicated, may hold values from -0.21875 to 0.21875
- image_output_weight: bfloat16 [768, 768], replicated, may hold values from -1.25 to 1.25
- image_second_gain: float32 [768], replicated, may hold values from 0.5 to 1.5
- image_second_shift: float32 [768], replicated, may hold values from -3 to 3
- image_widen_weight: bfloat16 [768, 3072], replicated, may hold values from -0.21875 to 0.21875
- image_narrow_weight: bfloat16 [3072, 768], replicated, may hold values from -0.109375 to 0.109375
- image_final_gain: float32 [768], replicated, may hold values from 0.5 to 1.5
- image_final_shift: float32 [768], replicated, may hold values from -3 to 3
- image_projection: bfloat16 [768, 512], replicated, may hold values from -0.21875 to 0.21875
- image_block_out_grad: bfloat16 [1024, 50, 768], P(('tower', 'dp')), may hold values from -0.00018310547 to 0.00018310547
- text_tokens: bfloat16 [1024, 77, 512], P(('tower', 'dp')), may hold values from -6 to 6
- caption_lengths: int32 [1024], P(('tower', 'dp')), may hold values from 5 to 77, as said below
- text_first_gain: float32 [512], replicated, may hold values from 0.5 to 1.5
- text_first_shift: float32 [512], replicated, may hold values from -3 to 3
- text_joint_weight: bfloat16 [512, 1536], replicated, may hold values from -0.25 to 0.25
- text_output_weight: bfloat16 [512, 512], replicated, may hold values from -1 to 1
- text_second_gain: float32 [512], replicated, may hold values from 0.5 to 1.5
- text_second_shift: float32 [512], replicated, may hold values from -3 to 3
- text_widen_weight: bfloat16 [512, 2048], replicated, may hold values from -0.25 to 0.25
- text_narrow_weight: bfloat16 [2048, 512], replicated, may hold values from -0.125 to 0.125
- text_final_gain: float32 [512], replicated, may hold values from 0.5 to 1.5
- text_final_shift: float32 [512], replicated, may hold values from -3 to 3
- text_projection: bfloat16 [512, 512], replicated, may hold values from -0.25 to 0.25
- text_block_out_grad: bfloat16 [1024, 77, 512], P(('tower', 'dp')), may hold values from -0.00024414062 to 0.00024414062
- log_scale: float32 [1], replicated, may hold values from 3.4 to 4.1
Outputs:
- loss: float32 [1], replicated
- image_embedding: bfloat16 [1024, 512], P(('tower', 'dp'))
- text_embedding: bfloat16 [1024, 512], P(('tower', 'dp'))
- image_tokens_grad: float32 [1024, 50, 768], P(('tower', 'dp'))
- image_first_gain_grad: float32 [768], P('dp')
- image_first_shift_grad: float32 [768], P('dp')
- image_joint_weight_grad: float32 [768, 2304], P('dp')
- image_output_weight_grad: float32 [768, 768], P('dp')
- image_second_gain_grad: float32 [768], P('dp')
- image_second_shift_grad: float32 [768], P('dp')
- image_widen_weight_grad: float32 [768, 3072], P('dp')
- image_narrow_weight_grad: float32 [3072, 768], P('dp')
- image_final_gain_grad: float32 [768], P('dp')
- image_final_shift_grad: float32 [768], P('dp')
- image_projection_grad: float32 [768, 512], P('dp')
- text_tokens_grad: float32 [1024, 77, 512], P(('tower', 'dp'))
- text_first_gain_grad: float32 [512], P('dp')
- text_first_shift_grad: float32 [512], P('dp')
- text_joint_weight_grad: float32 [512, 1536], P('dp')
- text_output_weight_grad: float32 [512, 512], P('dp')
- text_second_gain_grad: float32 [512], P('dp')
- text_second_shift_grad: float32 [512], P('dp')
- text_widen_weight_grad: float32 [512, 2048], P('dp')
- text_narrow_weight_grad: float32 [2048, 512], P('dp')
- text_final_gain_grad: float32 [512], P('dp')
- text_final_shift_grad: float32 [512], P('dp')
- text_projection_grad: float32 [512, 512], P('dp')
- log_scale_grad: float32 [1], replicated
The draws below stay inside these ranges and needn't reach their ends.
Inputs may be any that keep to these rules, and one draw needn't show every extreme that they name: `caption_lengths`: each caption's end-of-text token stands at position length minus 1; some caption has 77 tokens and some has 5.
All inputs are finite; a program needn't handle non-finite values.
Results may differ from the reference program's by a relative error of at most 0.024.
Values may be sent and summed in bfloat16 or wider, within the bound.
No kernel may reach another device: no remote copies, remote signals or barrier semaphores. Data moves between devices by JAX's collectives and lax.ppermute only.
A program may use at most 256 MiB of HBM per device.

```python
import jax
import jax.numpy as jnp
from jax import lax

IMG_WIDTH = 768
IMG_HEADS = 12
IMG_FF = 3072
TXT_WIDTH = 512
TXT_HEADS = 8
TXT_FF = 2048
EMBED = 512
IMG_LEN = 50
TXT_LEN = 77
PAIRS = 1024


def draw_caption_lengths(key, part):
    key = jax.random.fold_in(key, 11)
    keys = jax.random.split(key, 3)
    lengths = jax.random.randint(keys[0], (PAIRS,), 5, TXT_LEN + 1)
    longest = jax.random.randint(keys[1], (), 0, PAIRS)
    offset = jax.random.randint(keys[2], (), 1, PAIRS)
    shortest = (longest + offset) % PAIRS
    place = jnp.arange(PAIRS)
    lengths = jnp.where(place == longest, TXT_LEN, lengths)
    lengths = jnp.where(place == shortest, 5, lengths)
    return lengths.astype(jnp.int32)


def levels(own_key, dims, cuts, smallest, high):
    level, own = 1.0, jax.random.fold_in(own_key, 6)
    for axis_at, shards_of in cuts:
        draws = jnp.exp(jax.random.uniform(jax.random.fold_in(own, axis_at), (shards_of,), jnp.float32, smallest / len(cuts), high / len(cuts)))
        level = level * jnp.repeat(draws, dims[axis_at] // shards_of).reshape([-1 if axis == axis_at else 1 for axis in range(len(dims))])
    return level


def scatter_about(rng, shape, scale, bound, pieces=(), kind=jnp.bfloat16):
    drawn = scale * jax.random.normal(rng, shape, jnp.float32)
    if pieces:
        drawn = drawn * levels(rng, shape, pieces, -0.22, 0.18)
    return jnp.clip(drawn, -bound, bound).astype(kind)


def setup_inputs(seed: int = 0) -> dict:
    seeds = jax.random.split(jax.random.key(seed), 29)
    image_tokens = scatter_about(seeds[0], (PAIRS, IMG_LEN, IMG_WIDTH), 1.0, 6.0, ((0, 128),))
    image_first_gain = jnp.clip(1.0 + 0.1 * jax.random.normal(seeds[1], (IMG_WIDTH,), jnp.float32), 0.5, 1.5)
    image_first_shift = scatter_about(seeds[2], (IMG_WIDTH,), 0.5, 3.0, (), jnp.float32)
    image_joint_weight = scatter_about(seeds[3], (IMG_WIDTH, 3 * IMG_WIDTH), IMG_WIDTH ** -0.5, 0.21875)
    image_output_weight = scatter_about(seeds[4], (IMG_WIDTH, IMG_WIDTH), (IMG_WIDTH // 32) ** -0.5, 1.25)
    image_second_gain = jnp.clip(1.0 + 0.1 * jax.random.normal(seeds[5], (IMG_WIDTH,), jnp.float32), 0.5, 1.5)
    image_second_shift = scatter_about(seeds[6], (IMG_WIDTH,), 0.5, 3.0, (), jnp.float32)
    image_widen_weight = scatter_about(seeds[7], (IMG_WIDTH, IMG_FF), IMG_WIDTH ** -0.5, 0.21875)
    image_narrow_weight = scatter_about(seeds[8], (IMG_FF, IMG_WIDTH), IMG_FF ** -0.5, 0.109375)
    image_final_gain = jnp.clip(1.0 + 0.1 * jax.random.normal(seeds[9], (IMG_WIDTH,), jnp.float32), 0.5, 1.5)
    image_final_shift = scatter_about(seeds[10], (IMG_WIDTH,), 0.5, 3.0, (), jnp.float32)
    image_projection = scatter_about(seeds[11], (IMG_WIDTH, EMBED), IMG_WIDTH ** -0.5, 0.21875)
    image_block_out_grad = scatter_about(seeds[12], (PAIRS, IMG_LEN, IMG_WIDTH), (20.0 * PAIRS ** -1 * (EMBED * IMG_WIDTH) ** -0.5), 0.00018310547, ((0, 128),))
    text_tokens = scatter_about(seeds[13], (PAIRS, TXT_LEN, TXT_WIDTH), 1.0, 6.0, ((0, 128),))
    caption_lengths = draw_caption_lengths(jax.random.fold_in(seeds[28], 71), 0)
    text_first_gain = jnp.clip(1.0 + 0.1 * jax.random.normal(seeds[15], (TXT_WIDTH,), jnp.float32), 0.5, 1.5)
    text_first_shift = scatter_about(seeds[16], (TXT_WIDTH,), 0.5, 3.0, (), jnp.float32)
    text_joint_weight = scatter_about(seeds[17], (TXT_WIDTH, 3 * TXT_WIDTH), TXT_WIDTH ** -0.5, 0.25)
    text_output_weight = scatter_about(seeds[18], (TXT_WIDTH, TXT_WIDTH), (TXT_WIDTH // 16) ** -0.5, 1.0)
    text_second_gain = jnp.clip(1.0 + 0.1 * jax.random.normal(seeds[19], (TXT_WIDTH,), jnp.float32), 0.5, 1.5)
    text_second_shift = scatter_about(seeds[20], (TXT_WIDTH,), 0.5, 3.0, (), jnp.float32)
    text_widen_weight = scatter_about(seeds[21], (TXT_WIDTH, TXT_FF), TXT_WIDTH ** -0.5, 0.25)
    text_narrow_weight = scatter_about(seeds[22], (TXT_FF, TXT_WIDTH), TXT_FF ** -0.5, 0.125)
    text_final_gain = jnp.clip(1.0 + 0.1 * jax.random.normal(seeds[23], (TXT_WIDTH,), jnp.float32), 0.5, 1.5)
    text_final_shift = scatter_about(seeds[24], (TXT_WIDTH,), 0.5, 3.0, (), jnp.float32)
    text_projection = scatter_about(seeds[25], (TXT_WIDTH, EMBED), TXT_WIDTH ** -0.5, 0.25)
    text_block_out_grad = scatter_about(seeds[26], (PAIRS, TXT_LEN, TXT_WIDTH), (20.0 * PAIRS ** -1 * (EMBED * TXT_WIDTH) ** -0.5), 0.00024414062, ((0, 128),))
    log_scale = jnp.clip(jax.random.uniform(seeds[27], (1,), jnp.float32, 3.4, 4.1), 3.4, 4.1)
    return dict(image_tokens=image_tokens, image_first_gain=image_first_gain, image_first_shift=image_first_shift, image_joint_weight=image_joint_weight, image_output_weight=image_output_weight, image_second_gain=image_second_gain, image_second_shift=image_second_shift, image_widen_weight=image_widen_weight, image_narrow_weight=image_narrow_weight, image_final_gain=image_final_gain, image_final_shift=image_final_shift, image_projection=image_projection, image_block_out_grad=image_block_out_grad, text_tokens=text_tokens, caption_lengths=caption_lengths, text_first_gain=text_first_gain, text_first_shift=text_first_shift, text_joint_weight=text_joint_weight, text_output_weight=text_output_weight, text_second_gain=text_second_gain, text_second_shift=text_second_shift, text_widen_weight=text_widen_weight, text_narrow_weight=text_narrow_weight, text_final_gain=text_final_gain, text_final_shift=text_final_shift, text_projection=text_projection, text_block_out_grad=text_block_out_grad, log_scale=log_scale)


@jax.custom_vjp
def low(v):
    return lax.optimization_barrier(v.astype(jnp.bfloat16)).astype(jnp.float32)

@jax.custom_vjp
def low_back(v):
    return v

def low_keep(v):
    return (low(v), None)

def low_pass(kept, grad):
    return (grad,)

def back_keep(v):
    return (v, None)

def back_low(kept, grad):
    return (low(grad),)
low.defvjp(low_keep, low_pass)
low_back.defvjp(back_keep, back_low)
exact_precision = lax.Precision.HIGHEST

def layer_norm(values, gain, shift):
    centre = lax.optimization_barrier(jnp.mean(values, axis=-1, keepdims=True))
    offset = values - centre
    spread = lax.optimization_barrier(jnp.mean(offset * offset, axis=-1, keepdims=True))
    return offset * lax.rsqrt(spread + 1e-05) * gain + shift

def project(left, right):
    return jnp.matmul(left, right, precision=exact_precision)

def block(tokens, params, heads, causal):
    first_gain, first_shift, joint_weight, output_weight, second_gain, second_shift, widen_weight, narrow_weight = params
    batch, length, width = tokens.shape
    head_size = width // heads
    factor = head_size ** (-0.5)
    normed_one = low(layer_norm(tokens, first_gain, first_shift))
    joint = low(low_back(project(normed_one, joint_weight)))
    joint = joint.reshape(batch, length, 3, heads, head_size)
    scores = low_back(jnp.einsum('blhd,bmhd->bhlm', joint[:, :, 0], joint[:, :, 1], precision=exact_precision) * factor)
    if causal:
        place = jnp.arange(length)
        scores = jnp.where(place[None, :] <= place[:, None], scores, -1e+30)
    probs = low(jax.nn.softmax(scores, axis=-1))
    context = jnp.einsum('bhlm,bmhd->blhd', probs, joint[:, :, 2], precision=exact_precision)
    context = low(low_back(context.reshape(batch, length, width)))
    mixed = tokens + low_back(project(context, output_weight))
    normed_two = low(layer_norm(mixed, second_gain, second_shift))
    widened = low_back(project(normed_two, widen_weight))
    active = low(widened * jax.nn.sigmoid(1.702 * widened))
    return mixed + low_back(project(active, narrow_weight))

def embed(pooled, gain, shift, projection):
    normed = low(layer_norm(pooled, gain, shift))
    raw = low_back(project(normed, projection))
    return low(raw * lax.rsqrt(lax.optimization_barrier(jnp.sum(raw * raw, axis=-1, keepdims=True)) + 1e-06))

def forward(image_tokens, image_params, text_tokens, text_params, log_scale, ends):
    block_rows = 32
    groups = PAIRS // block_rows

    def image_group(tokens):
        output = block(tokens, image_params[:8], IMG_HEADS, False)
        return (embed(output[:, 0], image_params[8], image_params[9], image_params[10]), output)

    def text_group(inputs):
        tokens, last = inputs
        output = block(tokens, text_params[:8], TXT_HEADS, True)
        chooser = (jnp.arange(TXT_LEN)[None, :] == last[:, None]).astype(output.dtype)
        chosen = lax.optimization_barrier(jnp.sum(chooser[:, :, None] * output, axis=1))
        return (embed(chosen, text_params[8], text_params[9], text_params[10]), output)
    image_embedding, image_out = lax.map(jax.checkpoint(image_group), image_tokens.reshape(groups, block_rows, IMG_LEN, IMG_WIDTH))
    text_embedding, text_out = lax.map(jax.checkpoint(text_group), (text_tokens.reshape(groups, block_rows, TXT_LEN, TXT_WIDTH), ends.reshape(groups, block_rows)))
    image_embedding = image_embedding.reshape(PAIRS, EMBED)
    text_embedding = text_embedding.reshape(PAIRS, EMBED)
    image_out = image_out.reshape(PAIRS, IMG_LEN, IMG_WIDTH)
    text_out = text_out.reshape(PAIRS, TXT_LEN, TXT_WIDTH)
    scale = jnp.exp(log_scale[0])
    sims = scale * project(image_embedding, text_embedding.T)
    row_total = jax.nn.logsumexp(sims, axis=1)
    column_total = jax.nn.logsumexp(sims, axis=0)
    loss = (jnp.sum(row_total) + jnp.sum(column_total) - 2.0 * jnp.sum(jnp.diagonal(sims))) / (2.0 * PAIRS)
    return ((loss, image_out, text_out), (image_embedding, text_embedding))

def reference(image_tokens, image_first_gain, image_first_shift, image_joint_weight, image_output_weight, image_second_gain, image_second_shift, image_widen_weight, image_narrow_weight, image_final_gain, image_final_shift, image_projection, image_block_out_grad, text_tokens, caption_lengths, text_first_gain, text_first_shift, text_joint_weight, text_output_weight, text_second_gain, text_second_shift, text_widen_weight, text_narrow_weight, text_final_gain, text_final_shift, text_projection, text_block_out_grad, log_scale):
    image_params = tuple((weight.astype(jnp.float32) for weight in (image_first_gain, image_first_shift, image_joint_weight, image_output_weight, image_second_gain, image_second_shift, image_widen_weight, image_narrow_weight, image_final_gain, image_final_shift, image_projection)))
    text_params = tuple((weight.astype(jnp.float32) for weight in (text_first_gain, text_first_shift, text_joint_weight, text_output_weight, text_second_gain, text_second_shift, text_widen_weight, text_narrow_weight, text_final_gain, text_final_shift, text_projection)))
    ends = (caption_lengths - 1).astype(jnp.int32)

    def objective(image_input, image_set, text_input, text_set, scale_log):
        return forward(image_input, image_set, text_input, text_set, scale_log, ends)
    primal, pull, embeds = jax.vjp(objective, image_tokens.astype(jnp.float32), image_params, text_tokens.astype(jnp.float32), text_params, log_scale.astype(jnp.float32), has_aux=True)
    loss = primal[0]
    image_grad, image_grads, text_grad, text_grads, scale_grad = pull((jnp.ones_like(loss), image_block_out_grad.astype(jnp.float32), text_block_out_grad.astype(jnp.float32)))
    return (loss.reshape(1), embeds[0].astype(jnp.bfloat16), embeds[1].astype(jnp.bfloat16), image_grad, image_grads[0], image_grads[1], image_grads[2], image_grads[3], image_grads[4], image_grads[5], image_grads[6], image_grads[7], image_grads[8], image_grads[9], image_grads[10], text_grad, text_grads[0], text_grads[1], text_grads[2], text_grads[3], text_grads[4], text_grads[5], text_grads[6], text_grads[7], text_grads[8], text_grads[9], text_grads[10], scale_grad)
```

```python
import functools

import jax
import jax.numpy as jnp
from jax import lax
from jax.experimental import pallas as pl
from jax.experimental.pallas import tpu as pltpu
from jax.sharding import PartitionSpec as P

F32 = jnp.float32
BF16 = jnp.bfloat16
BATCH = 8
EMBED = 512
TILE = 256
DEVS = 64


class Tower:
    def __init__(self, width, heads, hidden, length, padded, rows, causal):
        self.width = width
        self.heads = heads
        self.hidden = hidden
        self.length = length
        self.padded = padded
        self.real = BATCH * length
        self.rows = rows
        self.spread = BATCH * padded
        self.causal = causal


IMAGE = Tower(768, 12, 3072, 50, 64, 400, False)
TEXT = Tower(512, 8, 2048, 77, 80, 640, True)

VMEM_LIMIT = 58 * 1024 * 1024


def mm(left, right):
    return lax.dot_general(left, right, (((1,), (0,)), ((), ())), preferred_element_type=F32)


def mm_nt(left, right):
    return lax.dot_general(left, right, (((1,), (1,)), ((), ())), preferred_element_type=F32)


def mm_tn(left, right):
    return lax.dot_general(left, right, (((0,), (0,)), ((), ())), preferred_element_type=F32)


def normalise(values):
    centre = jnp.mean(values, axis=-1, keepdims=True)
    offset = values - centre
    inverse = lax.rsqrt(jnp.mean(offset * offset, axis=-1, keepdims=True) + 1e-05)
    return offset * inverse, inverse


def norm_back(upstream, gain, normal, inverse):
    scaled = upstream * gain
    inner = (
        scaled
        - jnp.mean(scaled, axis=-1, keepdims=True)
        - normal * jnp.mean(scaled * normal, axis=-1, keepdims=True)
    )
    return inner * inverse


def column_sum(values):
    return jnp.sum(values, axis=0, keepdims=True)


def sigmoid(values):
    return 1.0 / (1.0 + jnp.exp(-values))


def vec(ref):
    return ref[...].reshape(1, -1)


def chunks(count, size=128):
    return [(at, min(size, count - at)) for at in range(0, count, size)]


def loop(count, body):
    def step(i, carry):
        body(i)
        return carry

    lax.fori_loop(0, count, step, 0)


def tile_loop(width, body):
    loop(width // TILE, lambda n: body(n, pl.ds(pl.multiple_of(n * TILE, TILE), TILE)))


def put_tiles(ref, n, rows, values):
    for i in range(TILE // 128):
        ref[n * (TILE // 128) + i, 0:rows, :] = values[:, 128 * i : 128 * i + 128]


def head_masks():
    lane = lax.broadcasted_iota(jnp.int32, (1, 128), 1)
    first = jnp.where(lane < 64, 1.0, 0.0).astype(BF16)
    second = jnp.where(lane < 64, 0.0, 1.0).astype(BF16)
    return first, second


def two_heads(values, masks):
    return jnp.concatenate([values * masks[0], values * masks[1]], axis=0)


def own_head(values, padded):
    lane = lax.broadcasted_iota(jnp.int32, (padded, 128), 1)
    return jnp.where(lane < 64, values[:padded], values[padded:])


def pooled_row(t, ends, b):
    return ends[b] * BATCH + b


def front_kernel(
    t,
    ends,
    tokens,
    first_gain,
    first_shift,
    joint_weight,
    output_weight,
    second_gain,
    second_shift,
    widen_weight,
    narrow_weight,
    final_gain,
    final_shift,
    projection,
    normed_one,
    joint,
    probs,
    context,
    mixed,
    mixed_row,
    wide_row,
    pooled,
    raw_out,
    unit,
    joint_wide,
    context_wide,
):
    width, padded, rows = t.width, t.padded, t.rows
    if t.real < rows:
        normed_one[t.real - 8 : rows, :] = jnp.zeros((rows - t.real + 8, width), BF16)
    for at, size in chunks(t.real):
        normal, _ = normalise(tokens[at : at + size, :].astype(F32))
        normed_one[at : at + size, :] = (normal * vec(first_gain) + vec(first_shift)).astype(BF16)
    if t.spread > rows:
        fill = (3 * width // 128, t.spread - rows, 128)
        joint_wide[:, rows : t.spread, :] = jnp.zeros(fill, F32)

    def joint_step(n, cols):
        put_tiles(joint_wide, n, rows, mm(normed_one[...], joint_weight[:, cols]))

    tile_loop(3 * width, joint_step)

    masks = head_masks()
    key_at = lax.broadcasted_iota(jnp.int32, (padded, 2 * padded), 0)
    query_at = lax.broadcasted_iota(jnp.int32, (padded, 2 * padded), 1)
    query_at = jnp.where(query_at < padded, query_at, query_at - padded)
    valid = key_at <= query_at if t.causal else key_at < t.length
    pairs = range(t.heads // 2)

    def attend(b):
        some = pl.ds(b, padded, stride=BATCH)
        for c in range(3 * width // 128):
            joint[b, :, 128 * c : 128 * c + 128] = joint_wide[c, some, :].astype(BF16)
        scores = []
        for p in pairs:
            at = 128 * p
            queries = joint[b, :, at : at + 128]
            keys = joint[b, :, width + at : width + at + 128]
            scores.append(mm_nt(keys, two_heads(queries, masks)) * 0.125)
        lows = []
        for p in pairs:
            score = jnp.where(valid, scores[p], -1e30)
            raised = jnp.exp(score - jnp.max(score, axis=0, keepdims=True))
            low = (raised * (1.0 / column_sum(raised))).astype(BF16)
            probs[b, p] = low
            lows.append(low)
        for p in pairs:
            at = 2 * width + 128 * p
            both = mm_tn(lows[p], joint[b, :, at : at + 128])
            context_wide[p, some, :] = own_head(both, padded)

    loop(BATCH, attend)
    for p in pairs:
        context[:, 128 * p : 128 * p + 128] = context_wide[p, 0:rows, :].astype(BF16)

    def mix_step(n, cols):
        mixed[:, cols] = mm(context[...], output_weight[:, cols])

    tile_loop(width, mix_step)
    for at, size in chunks(t.real):
        mixed[at : at + size, :] += tokens[at : at + size, :].astype(F32)
    for b in range(BATCH):
        mixed_row[b : b + 1, :] = mixed[pl.ds(pooled_row(t, ends, b), 1), :]

    row = mixed_row[...]
    normal, _ = normalise(row)
    normed = (normal * vec(second_gain) + vec(second_shift)).astype(BF16)
    wide = mm(normed, widen_weight[...])
    wide_row[...] = wide
    active = (wide * sigmoid(1.702 * wide)).astype(BF16)
    last = row + mm(active, narrow_weight[...])
    pooled[...] = last
    normal, _ = normalise(last)
    normed = (normal * vec(final_gain) + vec(final_shift)).astype(BF16)
    raw = mm(normed, projection[...])
    raw_out[...] = raw
    factor = lax.rsqrt(jnp.sum(raw * raw, axis=-1, keepdims=True) + 1e-06)
    unit[...] = (raw * factor).astype(BF16)


def middle_kernel(
    t,
    ends,
    mixed,
    block_grad,
    second_gain,
    second_shift,
    widen_weight,
    narrow_weight,
    normed_two,
    active_out,
    widened_grad,
    mixed_grad,
    grad_row,
    gain_grad,
    shift_grad,
    narrow_in,
    wide_in,
):
    step = pl.program_id(0)

    @pl.when(step == 0)
    def _():
        if t.real < t.rows:
            wide_in[t.real : t.rows, :] = jnp.zeros((t.rows - t.real, t.width), F32)
        for at, size in chunks(t.rows):
            normal, _ = normalise(mixed[at : at + size, :])
            normed_two[at : at + size, :] = (normal * vec(second_gain) + vec(second_shift)).astype(
                BF16
            )
        for at, size in chunks(t.real):
            wide_in[at : at + size, :] = block_grad[at : at + size, :].astype(F32)
        for b in range(BATCH):
            row = pl.ds(pooled_row(t, ends, b), 1)
            grad_row[b : b + 1, :] = wide_in[row, :]
            wide_in[row, :] = jnp.zeros((1, t.width), F32)
        narrow_in[...] = wide_in[...].astype(BF16)
        mixed_grad[...] = jnp.zeros_like(mixed_grad)

    wide = mm(normed_two[...], widen_weight[...])
    sig = sigmoid(1.702 * wide)
    active_out[...] = (wide * sig).astype(BF16)
    slope = sig + 1.702 * wide * sig * (1.0 - sig)
    low = (mm_nt(narrow_in[...], narrow_weight[...]) * slope).astype(BF16)
    widened_grad[...] = low
    mixed_grad[...] += mm_nt(low, widen_weight[...])

    @pl.when(step == pl.num_programs(0) - 1)
    def _():
        gain = shift = 0.0
        for at, size in chunks(t.rows):
            some = slice(at, at + size)
            normal, inverse = normalise(mixed[some, :])
            up = mixed_grad[some, :]
            gain += column_sum(up * normal)
            shift += column_sum(up)
            mixed_grad[some, :] = wide_in[some, :] + norm_back(
                up, vec(second_gain), normal, inverse
            )
        gain_grad[...] = gain
        shift_grad[...] = shift


def split_dot(weights, right):
    high = weights.astype(BF16)
    rest = weights - high.astype(F32)
    middle = rest.astype(BF16)
    low = (rest - middle.astype(F32)).astype(BF16)
    return mm(high, right) + mm(middle, right) + mm(low, right)


def head_back(
    unit_grad,
    raw,
    pooled,
    mixed_row,
    wide_row,
    grad_row,
    final_gain,
    final_shift,
    second_gain,
    second_shift,
    projection,
    widen_weight,
    narrow_weight,
    outs,
):
    (
        final_gain_grad,
        final_shift_grad,
        second_gain_grad,
        second_shift_grad,
        final_out,
        raw_grad_out,
        narrow_in_row,
        wide_grad_row,
        mixed_grad_row,
    ) = outs
    factor = lax.rsqrt(jnp.sum(raw * raw, axis=-1, keepdims=True) + 1e-06)
    raw_grad = factor * unit_grad - raw * (factor * factor * factor) * jnp.sum(
        unit_grad * raw, axis=-1, keepdims=True
    )
    raw_grad = raw_grad.astype(BF16)
    raw_grad_out[...] = raw_grad.astype(F32)
    normal, inverse = normalise(pooled)
    final_out[...] = (normal * final_gain + final_shift).astype(BF16).astype(F32)
    up = mm_nt(raw_grad, projection[...])
    final_gain_grad[...] = column_sum(up * normal)
    final_shift_grad[...] = column_sum(up)
    out_grad = grad_row + norm_back(up, final_gain, normal, inverse)
    narrow_in = out_grad.astype(BF16)
    narrow_in_row[...] = narrow_in.astype(F32)
    sig = sigmoid(1.702 * wide_row)
    slope = sig + 1.702 * wide_row * sig * (1.0 - sig)
    low = (mm_nt(narrow_in, narrow_weight[...]) * slope).astype(BF16)
    wide_grad_row[...] = low.astype(F32)
    up = mm_nt(low, widen_weight[...])
    normal, inverse = normalise(mixed_row)
    second_gain_grad[...] = column_sum(up * normal)
    second_shift_grad[...] = column_sum(up)
    mixed_grad_row[...] = out_grad + norm_back(up, second_gain, normal, inverse)


def pair_kernel(place, log_scale, own, other, image_unit, text_unit, *refs):
    image_in, text_in = refs[:12], refs[12:24]
    loss, scale_grad = refs[24], refs[25]
    image_outs, text_outs = refs[26:35], refs[35:44]
    half = own.shape[0]
    pairs = 2 * half
    scale = jnp.exp(jnp.full((1, 1), log_scale[0], F32))
    blocks = (own, other)

    def totals(left_at, right_at):
        sums, moments = [], []
        for right in blocks:
            column, moment = None, None
            for left in blocks:
                for piece in range(0, half, 256):
                    sims = scale * mm_nt(
                        left[piece : piece + 256, left_at : left_at + EMBED],
                        right[:, right_at : right_at + EMBED],
                    )
                    raised = jnp.exp(sims)
                    add, more = column_sum(raised), column_sum(raised * sims)
                    column = add if column is None else column + add
                    moment = more if moment is None else moment + more
            sums.append(column)
            moments.append(moment)
        return sums, moments

    column_sums, column_moments = totals(0, EMBED)
    row_sums, row_moments = totals(EMBED, 0)
    log_total = jnp.zeros((1, 1), F32)
    weighted = jnp.zeros((1, 1), F32)
    trace = jnp.zeros((1, 1), F32)
    for i in range(2):
        for total, moment in ((column_sums[i], column_moments[i]), (row_sums[i], row_moments[i])):
            log_total += jnp.sum(jnp.log(total), axis=-1, keepdims=True)
            weighted += jnp.sum(moment / total, axis=-1, keepdims=True)
        product = blocks[i][:, :EMBED].astype(F32) * blocks[i][:, EMBED:].astype(F32)
        trace += jnp.sum(column_sum(product), axis=-1, keepdims=True)
    trace = scale * trace
    loss[...] = jnp.broadcast_to((log_total - 2.0 * trace) / (2.0 * pairs), loss.shape)
    scale_grad[...] = jnp.broadcast_to((weighted - 2.0 * trace) / (2.0 * pairs), loss.shape)

    lane = lax.broadcasted_iota(jnp.int32, (BATCH, half), 1)
    sub = lax.broadcasted_iota(jnp.int32, (BATCH, half), 0)
    identity = jnp.where(lane == sub + place[1] * BATCH, 2.0, 0.0)

    def grads(unit, at, other_sums):
        raised = [jnp.exp(scale * mm_nt(unit[...], block[:, at : at + EMBED])) for block in blocks]
        own_sum = sum(jnp.sum(r, axis=-1, keepdims=True) for r in raised)
        result = None
        for i in range(2):
            weight = raised[i] * (1.0 / own_sum + 1.0 / other_sums[i])
            if i == 0:
                weight = weight - identity
            weight = weight / (2.0 * pairs)
            part = split_dot(weight, blocks[i][:, at : at + EMBED])
            result = part if result is None else result + part
        return scale * result

    image_grad = grads(image_unit, EMBED, column_sums)
    text_grad = grads(text_unit, 0, row_sums)
    for unit_grad, ins, outs in (
        (image_grad, image_in, image_outs),
        (text_grad, text_in, text_outs),
    ):
        values = [ref[...] for ref in ins[:5]] + [vec(ref) for ref in ins[5:9]]
        head_back(unit_grad, *values, *ins[9:12], outs)


def back_kernel(
    t,
    ends,
    mixed_grad,
    mixed_grad_row,
    joint,
    probs,
    tokens,
    first_gain,
    output_weight,
    joint_weight,
    grads,
    tokens_grad,
    gain_grad,
    shift_grad,
    grad,
    context_grad,
    joint_grad,
    normed_grad,
):
    width, padded, rows = t.width, t.padded, t.rows
    grad[...] = mixed_grad[...]
    for b in range(BATCH):
        grad[pl.ds(pooled_row(t, ends, b), 1), :] = mixed_grad_row[b : b + 1, :]
    mixed_low = slice(3 * width, 4 * width)
    grads[:, mixed_low] = grad[...].astype(BF16)
    if t.spread > rows:
        fill = (width // 128, t.spread - rows, 128)
        context_grad[:, rows : t.spread, :] = jnp.zeros(fill, F32)

    def context_step(n, cols):
        put_tiles(context_grad, n, rows, mm_nt(grads[:, mixed_low], output_weight[cols, :]))

    tile_loop(width, context_step)
    masks = head_masks()
    pairs = range(t.heads // 2)

    def attend(b):
        some = pl.ds(b, padded, stride=BATCH)
        ups = [two_heads(context_grad[p, some, :].astype(BF16), masks) for p in pairs]
        backs = []
        for p in pairs:
            at = 2 * width + 128 * p
            backs.append(mm_nt(joint[b, :, at : at + 128], ups[p]))
        lows = []
        for p in pairs:
            wide = probs[b, p].astype(F32)
            back = wide * (backs[p] - column_sum(backs[p] * wide))
            lows.append(back.astype(BF16))
        for p in pairs:
            at = 128 * p
            queries = joint[b, :, at : at + 128]
            keys = joint[b, :, width + at : width + at + 128]
            joint_grad[2 * len(pairs) + p, some, :] = mm(probs[b, p], ups[p])
            joint_grad[len(pairs) + p, some, :] = mm(lows[p], two_heads(queries, masks)) * 0.125
            joint_grad[p, some, :] = own_head(mm_tn(lows[p], keys), padded) * 0.125

    loop(BATCH, attend)
    for c in range(3 * width // 128):
        grads[:, 128 * c : 128 * c + 128] = joint_grad[c, 0:rows, :].astype(BF16)

    def normed_step(n, cols):
        normed_grad[:, cols] = mm_nt(grads[:, 0 : 3 * width], joint_weight[cols, :])

    tile_loop(width, normed_step)
    gain = shift = 0.0
    for at, size in chunks(t.real):
        some = slice(at, at + size)
        normal, inverse = normalise(tokens[some, :].astype(F32))
        up = normed_grad[some, :]
        gain += column_sum(up * normal)
        shift += column_sum(up)
        tokens_grad[some, :] = grad[some, :] + norm_back(up, vec(first_gain), normal, inverse)
    gain_grad[...] = gain
    shift_grad[...] = shift


def turn(source, target):
    def step(n):
        cols = pl.ds(pl.multiple_of(n * 128, 128), 128)
        target[cols, :] = source[:, cols].T

    loop(source.shape[1] // 128, step)


def lanes_down(values):
    return jnp.concatenate(
        [values[:, :, at : at + 128] for at in range(0, values.shape[2], 128)], axis=1
    )


def put(out, received, devices, units, values):
    count = values.shape[1] // 16
    values = values.reshape(values.shape[0], count, 16, 128)
    if received is not None:
        values = values + received[devices, units : units + count].astype(F32)
    out[devices, units : units + count] = values.astype(BF16)


def pack_twelve(first, second, received, out, unit=0, each=4):
    cols = first.shape[1]
    count = cols // 128
    sub = lax.broadcasted_iota(jnp.int32, (each, 8, cols), 1) < 4

    def step(e):
        rows = pl.ds(pl.multiple_of(e * (24 * each), 8), 24 * each)
        x = first[rows, :].reshape(each, 24, cols)
        y = second[rows, :].reshape(each, 24, cols)
        left, right = x[:, 8:16], y[:, 8:16]
        even = jnp.where(sub, left, pltpu.roll(right, 4, 1))
        odd = jnp.where(sub, pltpu.roll(left, 4, 1), right)
        parts = []
        for a, b, c in ((x[:, 0:8], y[:, 0:8], even), (x[:, 16:24], y[:, 16:24], odd)):
            parts.append(jnp.concatenate([lanes_down(v) for v in (a, b, c)], axis=1))
        if parts[0].shape[1] % 16:
            fill = jnp.zeros((each, 16 - parts[0].shape[1] % 16, 128), F32)
            parts = [jnp.concatenate([part, fill], axis=1) for part in parts]
        height = parts[0].shape[1]
        values = jnp.stack(parts, axis=1).reshape(2 * each, height, 128)
        devices = pl.ds(pl.multiple_of(e * (2 * each), 2 * each), 2 * each)
        put(out, received, devices, unit, values)

    loop(32 // each, step)


def pack_rows(result, rows, received, out, unit=0, each=8):
    total = result.shape[0] // rows
    cols = result.shape[1]

    def step(e):
        some = pl.ds(pl.multiple_of(e * (rows * each), 8), rows * each)
        values = lanes_down(result[some, :].reshape(each, rows, cols))
        put(out, received, pl.ds(pl.multiple_of(e * each, each), each), unit, values)

    loop(total // each, step)


def take_patched(t, ends, source, new, target):
    real = source.shape[0]
    if real < t.rows:
        target[real - 8 :, :] = jnp.zeros((t.rows - real + 8, target.shape[1]), BF16)
    target[0:real, :] = source[...]
    sub = lax.broadcasted_iota(jnp.int32, (16, 1), 0)

    def patch(b):
        row = pooled_row(t, ends, b)
        base = pl.multiple_of((row // 16) * 16, 16)
        some = pl.ds(base, 16)
        old = target[some, :].astype(F32)
        target[some, :] = jnp.where(sub == row - base, new[pl.ds(b, 1), :], old).astype(BF16)

    loop(BATCH, patch)


def wide_weight_kernel(t, patched, added, buffered, left_count, place, ends, *refs):
    refs = list(refs)
    lefts = [refs.pop(0) for _ in range(left_count)]
    tiles = [refs.pop(0) for _ in range(2 if t is IMAGE else 1)]
    news = [refs.pop(0) for _ in tiles] if patched else [None] * len(tiles)
    received = refs.pop(0) if added else None
    if buffered:
        refs.pop(0)
    out = refs.pop(0)
    turned = [refs.pop(0) for _ in range(left_count)]
    results = [refs.pop(0) for _ in tiles]
    step = pl.program_id(0)

    @pl.when(step == 0)
    def _():
        for left, target in zip(lefts, turned):
            turn(left, target)

    half = place[0] if added else 1 - place[0]
    for i, (tile, new, result) in enumerate(zip(tiles, news, results)):
        if patched:
            ready = refs[i]
            take_patched(t, ends, tile, new, ready)
            tile = ready
        if left_count == 1:
            result[...] = mm(turned[0][...], tile[...])
        else:
            steps = pl.num_programs(0)
            at = half * (len(tiles) * steps) + i * steps + step
            late = at >= 3 * t.width // tile.shape[1]

            @pl.when(late)
            def _():
                result[...] = mm(turned[1][...], tile[...])

            @pl.when(jnp.logical_not(late))
            def _():
                result[...] = mm(turned[0][...], tile[...])

    if t is IMAGE:
        pack_twelve(*results, received, out)
    else:
        pack_rows(results[0], 8, received, out)


def narrow_weight_kernel(t, added, place, ends, active, grad, new, *refs):
    refs = list(refs)
    received = refs.pop(0) if added else None
    refs.pop(0)
    out, turned, result, ready = refs
    step = pl.program_id(0)

    @pl.when(step == 0)
    def _():
        take_patched(t, ends, grad, new, ready)

    turn(active, turned)
    result[...] = mm(turned[...], ready[...])
    pack_rows(result, t.hidden // DEVS, received, out, each=4)


FEED_UNITS = 27
REST_UNITS = 18
FEED_AT = {"text": (0, 4), "image": (9, 18)}
REST_AT = {"text": 0, "image": 9}
MISC_AT = 4


def buffer_call(kernel, name, grid, scalars, ins, units, block, at, scratch, flops, added, received, buffer):
    def where(i, *_):
        if block[0] == DEVS:
            return (0, at // block[1] + i, 0, 0)
        return (i, at // block[1], 0, 0)

    spec = pl.BlockSpec((block[0], block[1], 16, 128), where)
    arrays = [a for a, _ in ins]
    specs = [s for _, s in ins]
    if added:
        arrays.append(received)
        specs.append(spec)
    aliases = {}
    if buffer is not None:
        aliases = {len(scalars) + len(arrays): 0}
        arrays.append(buffer)
        specs.append(pl.BlockSpec(memory_space=pl.ANY))
    return pl.pallas_call(
        kernel,
        name=name,
        out_shape=jax.ShapeDtypeStruct((DEVS, units, 16, 128), BF16),
        grid_spec=pltpu.PrefetchScalarGridSpec(
            num_scalar_prefetch=len(scalars),
            grid=(grid,),
            in_specs=specs,
            out_specs=spec,
            scratch_shapes=[pltpu.VMEM(shape, kind) for shape, kind in scratch],
        ),
        input_output_aliases=aliases,
        compiler_params=pltpu.CompilerParams(vmem_limit_bytes=VMEM_LIMIT),
        cost_estimate=pl.CostEstimate(flops=flops, bytes_accessed=8 << 20, transcendentals=0),
    )(*scalars, *arrays)


def whole(array):
    return array, pl.BlockSpec(array.shape, lambda i, *_: (0,) * array.ndim)


def wide_weights(t, name, place, ends, lefts, grad, new, units, at, received, buffer):
    added = received is not None
    steps = 3 if t is IMAGE else 2
    cols = TILE if t is IMAGE else 512

    def columns(shift):
        def index(i, place, ends):
            half = place[0] if added else 1 - place[0]
            return (0, half * (2 * steps if t is IMAGE else steps) + shift + i)

        return index

    shifts = (0, steps) if t is IMAGE else (0,)
    ins = [whole(left) for left in lefts]
    ins += [(grad, pl.BlockSpec((t.rows, cols), columns(s))) for s in shifts]
    if new is not None:
        ins += [(new, pl.BlockSpec((BATCH, cols), columns(s))) for s in shifts]
    scratch = [((t.width, t.rows), BF16) for _ in lefts]
    scratch += [((t.width, cols), F32) for _ in shifts]
    if new is not None:
        scratch += [((t.rows, cols), BF16) for _ in shifts]
    kernel = functools.partial(
        wide_weight_kernel, t, new is not None, added, buffer is not None, len(lefts)
    )
    block = (DEVS, 3 if t is IMAGE else 2)
    flops = 4 * t.rows * t.width * t.width * 2
    return buffer_call(
        kernel, name, steps, (place, ends), ins, units, block, at, scratch, flops, added, received, buffer
    )


def narrow_weights(t, name, place, ends, active, grad, new, units, at, received, buffer):
    added = received is not None
    cols = t.width // 2

    def column(i, place, ends):
        return (0, place[0] if added else 1 - place[0])

    ins = [
        (active, pl.BlockSpec((t.rows, t.width), lambda i, *_: (0, i))),
        (grad, pl.BlockSpec((t.real, cols), column)),
        (new, pl.BlockSpec((BATCH, cols), column)),
    ]
    scratch = [((t.width, t.rows), BF16), ((t.width, cols), F32), ((t.rows, cols), BF16)]
    block = (16, 9 if t is IMAGE else 4)
    flops = 4 * t.rows * t.width * t.width * 2
    return buffer_call(
        functools.partial(narrow_weight_kernel, t, added),
        name,
        4,
        (place, ends),
        ins,
        units,
        block,
        at,
        scratch,
        flops,
        added,
        received,
        buffer,
    )


def misc_kernel(added, place, *refs):
    refs = list(refs)
    image_final, image_raw, text_final, text_raw = refs[:4]
    refs = refs[4:]
    half = place[0] if added else 1 - place[0]
    received = None
    if added:
        vectors, received, refs = refs[:16], refs[16], refs[17:]
    _, out, first, second, third = refs[:5]

    def columns(ref, at, size):
        return ref[:, pl.ds(pl.multiple_of(half * 256 + at, 128), size)].astype(BF16)

    final = image_final[...].astype(BF16)
    first[...] = mm_tn(final, columns(image_raw, 0, 128))
    second[...] = mm_tn(final, columns(image_raw, 128, 128))
    pack_twelve(first, second, received, out, 2, 8)
    third[...] = mm_tn(text_final[...].astype(BF16), columns(text_raw, 0, 256))
    pack_rows(third, 8, received, out, 0)
    if not added:
        out[:, 1] = jnp.zeros((DEVS, 16, 128), BF16)
        return
    spread = refs[5]
    spread[...] = jnp.zeros_like(spread)
    for tower, refs_of, width in ((0, vectors[:8], 768), (1, vectors[8:], 512)):
        each = width // DEVS
        device = lax.broadcasted_iota(jnp.int32, (DEVS, width), 0)
        column = lax.broadcasted_iota(jnp.int32, (DEVS, width), 1)
        mine = jnp.logical_and(column >= device * each, column < device * each + each)
        source = lax.broadcasted_iota(jnp.int32, (width, 128), 0)
        lane = lax.broadcasted_iota(jnp.int32, (width, 128), 1)
        at = lax.rem(source, each)
        high_at = jnp.where(lane == at, 1.0, 0.0).astype(BF16)
        low_at = jnp.where(lane == at + 64, 1.0, 0.0).astype(BF16)
        rows = [refs_of[0][...], refs_of[1][...], refs_of[2][...] + refs_of[3][...]]
        rows += [refs_of[4][...] + refs_of[5][...], refs_of[6][...], refs_of[7][...]]
        for k, row in enumerate(rows):
            row = jnp.where(mine, row, 0.0)
            high = row.astype(BF16)
            low = (row - high.astype(F32)).astype(BF16)
            spread[:, 6 * tower + k, :] = mm(high, high_at) + mm(low, low_at)
    out[:, 1] = spread[...].astype(BF16)


def misc(place, heads, vectors, received, buffer):
    added = received is not None
    ins = [whole(a) for a in (heads[0][4], heads[0][5], heads[1][4], heads[1][5])]
    if added:
        ins += [whole(v) for v in vectors]
    scratch = [((768, 128), F32), ((768, 128), F32), ((512, 256), F32)]
    if added:
        scratch.append(((DEVS, 16, 128), F32))
    return buffer_call(
        functools.partial(misc_kernel, added),
        "misc",
        1,
        (place,),
        ins,
        REST_UNITS,
        (DEVS, 4),
        MISC_AT,
        scratch,
        1 << 28,
        added,
        received,
        buffer,
    )


def add_kernel(received, total):
    total[...] = jnp.sum(received[...].astype(F32), axis=0)


def sum_blocks(received, block):
    count, units = received.shape[:2]
    return pl.pallas_call(
        add_kernel,
        name="sum_blocks",
        grid=(units // block,),
        out_shape=jax.ShapeDtypeStruct((units, 16, 128), F32),
        in_specs=[pl.BlockSpec((count, block, 16, 128), lambda i: (0, i, 0, 0))],
        out_specs=pl.BlockSpec((block, 16, 128), lambda i: (i, 0, 0)),
        compiler_params=pltpu.CompilerParams(vmem_limit_bytes=VMEM_LIMIT),
    )(received)


def unpack_kernel(place, feed_mine, rest_mine, feed_other, rest_other, *outs):
    (
        image_joint,
        image_output,
        image_widen,
        image_narrow,
        image_projection,
        text_joint,
        text_output,
        text_widen,
        text_narrow,
        text_projection,
    ) = outs[:10]
    odd = place[1] % 2

    def emit(half, feed, rest):
        def into(ref, col, body, tail):
            @pl.when(odd == 0)
            def _():
                ref[0:8, col : col + 128] = body
                ref[8:12, col : col + 128] = tail

            @pl.when(odd == 1)
            def _():
                ref[0:4, col : col + 128] = tail
                ref[4:12, col : col + 128] = body

        def image_wide(source, at, store):
            for tile in range(3):
                block = source[16 * (at + 3 * tile) : 16 * (at + 3 * tile) + 48, :]
                for side in range(2):
                    for g in range(2):
                        body = block[16 * side + 8 * g : 16 * side + 8 * g + 8]
                        tail = block[32 + 8 * g + 4 * side : 36 + 8 * g + 4 * side]
                        store(half * 1536 + side * 768 + tile * 256 + g * 128, body, tail)

        def joint_store(col, body, tail):
            if col < 2304:
                into(image_joint, col, body, tail)
            else:
                into(image_output, col - 2304, body, tail)

        image_wide(feed, FEED_AT["image"][0], functools.partial(into, image_widen))
        image_wide(rest, REST_AT["image"], joint_store)
        at = 16 * FEED_AT["image"][1]
        for g in range(3):
            col = half * 384 + 128 * g
            image_narrow[:, col : col + 128] = feed[at + 48 * g : at + 48 * g + 48, :]
        at = 16 * (MISC_AT + 2)
        for side in range(2):
            col = half * 256 + 128 * side
            tail = rest[at + 16 + 4 * side : at + 20 + 4 * side, :]
            into(image_projection, col, rest[at + 8 * side : at + 8 * side + 8, :], tail)
        for g in range(8):
            col = half * 1024 + 128 * g
            text_widen[:, col : col + 128] = feed[8 * g : 8 * g + 8, :]
            block = rest[8 * g : 8 * g + 8, :]
            if col < 1536:
                text_joint[:, col : col + 128] = block
            else:
                text_output[:, col - 1536 : col - 1408] = block
        for g in range(2):
            col = half * 256 + 128 * g
            text_narrow[:, col : col + 128] = feed[64 + 32 * g : 96 + 32 * g, :]
            at = 16 * MISC_AT + 8 * g
            text_projection[:, col : col + 128] = rest[at : at + 8, :]

    for half in range(2):

        @pl.when(place[0] == half)
        def _():
            emit(half, feed_mine, rest_mine)
            emit(1 - half, feed_other, rest_other)

    at = 16 * (MISC_AT + 1)
    vectors = rest_mine[at : at + 16, :] + rest_other[at : at + 16, :]
    for k in range(12):
        each = 12 if k < 6 else 8
        outs[10 + k][...] = vectors[k : k + 1, 0:each] + vectors[k : k + 1, 64 : 64 + each]


SMEM = pl.BlockSpec(memory_space=pltpu.SMEM)
VMEM = pl.BlockSpec(memory_space=pltpu.VMEM)


def call(body, name, scalars, arrays, outs, scratch=(), flops=1 << 32):
    return pl.pallas_call(
        body,
        name=name,
        out_shape=tuple(jax.ShapeDtypeStruct(shape, kind) for shape, kind in outs),
        in_specs=[SMEM] * len(scalars) + [VMEM] * len(arrays),
        out_specs=tuple(VMEM for _ in outs),
        scratch_shapes=[pltpu.VMEM(shape, kind) for shape, kind in scratch],
        compiler_params=pltpu.CompilerParams(vmem_limit_bytes=VMEM_LIMIT),
        cost_estimate=pl.CostEstimate(flops=flops, bytes_accessed=20 << 20, transcendentals=0),
    )(*scalars, *arrays)


def front(t, name, ends, tokens, params):
    rows, width, hidden = t.rows, t.width, t.hidden
    return call(
        functools.partial(front_kernel, t),
        name + "_front",
        (ends,),
        (tokens, *params),
        (
            ((rows, width), BF16),
            ((BATCH, t.padded, 3 * width), BF16),
            ((BATCH, t.heads // 2, t.padded, 2 * t.padded), BF16),
            ((rows, width), BF16),
            ((rows, width), F32),
            ((BATCH, width), F32),
            ((BATCH, hidden), F32),
            ((BATCH, width), F32),
            ((BATCH, EMBED), F32),
            ((BATCH, EMBED), BF16),
        ),
        (((3 * width // 128, t.spread, 128), F32), ((width // 128, t.spread, 128), F32)),
    )


def middle(t, name, ends, mixed, block_grad, gain, shift, widen, narrow):
    rows, width, hidden = t.rows, t.width, t.hidden
    outs = (
        ((rows, width), BF16),
        ((rows, hidden), BF16),
        ((rows, hidden), BF16),
        ((rows, width), F32),
        ((BATCH, width), F32),
        ((1, width), F32),
        ((1, width), F32),
    )

    def held(shape):
        return pl.BlockSpec(shape, lambda i, *_: (0,) * len(shape))

    tiled = pl.BlockSpec((rows, TILE), lambda i, *_: (0, i))
    out_specs = [held(shape) for shape, _ in outs]
    out_specs[1] = out_specs[2] = tiled
    in_specs = [held(a.shape) for a in (mixed, block_grad, gain, shift)]
    in_specs.append(pl.BlockSpec((width, TILE), lambda i, *_: (0, i)))
    in_specs.append(pl.BlockSpec((TILE, width), lambda i, *_: (i, 0)))
    return pl.pallas_call(
        functools.partial(middle_kernel, t),
        name=name + "_middle",
        out_shape=tuple(jax.ShapeDtypeStruct(shape, kind) for shape, kind in outs),
        grid_spec=pltpu.PrefetchScalarGridSpec(
            num_scalar_prefetch=1,
            grid=(hidden // TILE,),
            in_specs=in_specs,
            out_specs=tuple(out_specs),
            scratch_shapes=[pltpu.VMEM((rows, width), BF16), pltpu.VMEM((rows, width), F32)],
        ),
        compiler_params=pltpu.CompilerParams(vmem_limit_bytes=VMEM_LIMIT),
        cost_estimate=pl.CostEstimate(flops=1 << 33, bytes_accessed=20 << 20, transcendentals=0),
    )(ends, mixed, block_grad, gain, shift, widen, narrow)


def back(t, name, ends, mixed_grad, row, joint, probs, tokens, gain, output, joint_weight):
    rows, width = t.rows, t.width
    return call(
        functools.partial(back_kernel, t),
        name + "_back",
        (ends,),
        (mixed_grad, row, joint, probs, tokens, gain, output, joint_weight),
        (
            ((rows, 4 * width), BF16),
            ((t.real, width), F32),
            ((1, width), F32),
            ((1, width), F32),
        ),
        (
            ((rows, width), F32),
            ((width // 128, t.spread, 128), F32),
            ((3 * width // 128, t.spread, 128), F32),
            ((rows, width), F32),
        ),
        1 << 33,
    )


SWAP = [(0, 1), (1, 0)]


def by_token(tokens):
    return tokens.transpose(1, 0, 2).reshape(-1, tokens.shape[2])


def shards(*args):
    image_tokens, image_weights, image_block_grad = args[0], args[1:12], args[12]
    text_tokens, caption_lengths = args[13], args[14]
    text_weights, text_block_grad, log_scale = args[15:26], args[26], args[27]
    core = lax.axis_index("tower")
    dp = lax.axis_index("dp")
    place = jnp.stack([core, dp]).astype(jnp.int32)
    image_ends = jnp.zeros((BATCH,), jnp.int32)
    text_ends = (caption_lengths - 1).astype(jnp.int32)
    towers = (
        (IMAGE, "image", image_ends, by_token(image_tokens), image_weights, by_token(image_block_grad)),
        (TEXT, "text", text_ends, by_token(text_tokens), text_weights, by_token(text_block_grad)),
    )
    fronts = [front(t, name, ends, tokens, w) for t, name, ends, tokens, w, _ in towers]
    units = [f[9] for f in fronts]
    both = jnp.concatenate(units, axis=1)
    own = lax.all_to_all(
        jnp.broadcast_to(both[None], (DEVS, *both.shape)), "dp", 0, 0, tiled=True
    ).reshape(DEVS * BATCH, 2 * EMBED)
    other = lax.ppermute(own, "tower", SWAP)

    middles = []
    for (t, name, ends, _, w, block_grad), f in zip(towers, fronts):
        middles.append(middle(t, name, ends, f[4], block_grad, w[4], w[5], w[6], w[7]))

    pair_in = []
    pair_out = [((1, 128), F32), ((1, 128), F32)]
    for (t, _, _, _, w, _), f, m in zip(towers, fronts, middles):
        pair_in += [f[8], f[7], f[5], f[6], m[4], w[8], w[9], w[4], w[5], w[10], w[6], w[7]]
        pair_out += [((1, t.width), F32)] * 4 + [
            ((BATCH, t.width), F32),
            ((BATCH, EMBED), F32),
            ((BATCH, t.width), F32),
            ((BATCH, t.hidden), F32),
            ((BATCH, t.width), F32),
        ]
    paired = call(
        pair_kernel, "pairs", (place, log_scale), (own, other, *units, *pair_in), pair_out
    )
    loss, scale_grad = paired[0][0, :1], paired[1][0, :1]
    heads = (paired[2:11], paired[11:20])

    def feed(received):
        buffer = None
        for (t, name, ends, _, _, block_grad), m, h in zip(towers, middles, heads):
            at = FEED_AT[name]
            buffer = wide_weights(
                t, name + "_widen", place, ends, (m[0],), m[2], h[7], FEED_UNITS, at[0], received, buffer
            )
            buffer = narrow_weights(
                t, name + "_narrow", place, ends, m[1], block_grad, h[6], FEED_UNITS, at[1], received, buffer
            )
        return buffer

    feed_received = lax.ppermute(feed(None), "tower", SWAP)
    feed_total = lax.all_to_all(feed(feed_received), "dp", 0, 0, tiled=True)

    backs = []
    for (t, name, ends, tokens, w, _), f, m, h in zip(towers, fronts, middles, heads):
        backs.append(back(t, name, ends, m[3], h[8], f[1], f[2], tokens, w[0], w[3], w[2]))

    vectors = []
    for m, h, k in zip(middles, heads, backs):
        vectors += [k[2], k[3], m[5], h[2], m[6], h[3], h[0], h[1]]

    def rest(received):
        buffer = None
        for (t, name, ends, _, _, _), f, k in zip(towers, fronts, backs):
            buffer = wide_weights(
                t, name + "_joint", place, ends, (f[0], f[3]), k[0], None, REST_UNITS, REST_AT[name], received, buffer
            )
        return misc(place, heads, vectors, received, buffer)

    rest_received = lax.ppermute(rest(None), "tower", SWAP)
    rest_total = lax.all_to_all(rest(rest_received), "dp", 0, 0, tiled=True)
    mine = [
        sum_blocks(feed_total, 9).reshape(-1, 128),
        sum_blocks(rest_total, 9).reshape(-1, 128),
    ]
    theirs = [lax.ppermute(m, "tower", SWAP) for m in mine]
    weight_outs = (
        ((12, 2304), F32),
        ((12, 768), F32),
        ((12, 3072), F32),
        ((48, 768), F32),
        ((12, 512), F32),
        ((8, 1536), F32),
        ((8, 512), F32),
        ((8, 2048), F32),
        ((32, 512), F32),
        ((8, 512), F32),
    )
    vector_outs = (((1, 12), F32),) * 6 + (((1, 8), F32),) * 6
    grads = call(unpack_kernel, "unpack", (place,), (*mine, *theirs), weight_outs + vector_outs)

    def ordered(vectors, weights):
        joint, output, widen, narrow, projection = weights
        v = [x.reshape(-1) for x in vectors]
        return [v[0], v[1], joint, output, v[2], v[3], widen, narrow, v[4], v[5], projection]

    def by_sequence(t, grad):
        return grad.reshape(t.length, BATCH, t.width).transpose(1, 0, 2)

    return (
        loss,
        units[0],
        units[1],
        by_sequence(IMAGE, backs[0][1]),
        *ordered(grads[10:16], grads[:5]),
        by_sequence(TEXT, backs[1][1]),
        *ordered(grads[16:22], grads[5:10]),
        scale_grad,
    )


def solution(mesh):
    spread = P(("tower", "dp"), None, None)
    weights = [P()] * 11
    placed = (spread, *weights, spread, spread, P(("tower", "dp")), *weights, spread, P())
    vector, matrix = P("dp"), P("dp", None)
    grads = [vector, vector, matrix, matrix, vector, vector, matrix, matrix, vector, vector, matrix]
    units = P(("tower", "dp"), None)
    return jax.shard_map(
        shards,
        mesh=mesh,
        in_specs=placed,
        out_specs=(P(), units, units, spread, *grads, spread, *grads, P()),
        check_vma=False,
    )
```

```python
import functools

import jax
import jax.numpy as jnp
from jax import lax
from jax.experimental import pallas as pl
from jax.experimental.pallas import tpu as pltpu
from jax.sharding import PartitionSpec as P

F32 = jnp.float32
BF16 = jnp.bfloat16
BATCH = 8
EMBED = 512
TILE = 256
DEVS = 64


class Tower:
    def __init__(self, width, heads, hidden, length, padded, rows, extra, causal):
        self.width = width
        self.heads = heads
        self.hidden = hidden
        self.length = length
        self.padded = padded
        self.real = BATCH * length
        self.rows = rows
        self.extra = extra
        self.spread = BATCH * padded
        self.lanes = -(-rows // 128) * 128
        self.causal = causal


IMAGE = Tower(768, 12, 3072, 50, 64, 416, 400, False)
TEXT = Tower(512, 8, 2048, 77, 80, 640, 624, True)

VMEM_LIMIT = 58 * 1024 * 1024


def mm(left, right):
    return lax.dot_general(left, right, (((1,), (0,)), ((), ())), preferred_element_type=F32)


def mm_nt(left, right):
    return lax.dot_general(left, right, (((1,), (1,)), ((), ())), preferred_element_type=F32)


def mm_tn(left, right):
    return lax.dot_general(left, right, (((0,), (0,)), ((), ())), preferred_element_type=F32)


def normalise(values):
    centre = jnp.mean(values, axis=-1, keepdims=True)
    offset = values - centre
    inverse = lax.rsqrt(jnp.mean(offset * offset, axis=-1, keepdims=True) + 1e-05)
    return offset * inverse, inverse


def norm_back(upstream, gain, normal, inverse):
    scaled = upstream * gain
    inner = (
        scaled
        - jnp.mean(scaled, axis=-1, keepdims=True)
        - normal * jnp.mean(scaled * normal, axis=-1, keepdims=True)
    )
    return inner * inverse


def column_sum(values):
    return jnp.sum(values, axis=0, keepdims=True)


def sigmoid(values):
    return 0.5 + 0.5 * jnp.tanh(0.5 * values)


def vec(ref):
    return ref[...].reshape(1, -1)


def chunks(count, size=128):
    return [(at, min(size, count - at)) for at in range(0, count, size)]


def loop(count, body):
    def step(i, carry):
        body(i)
        return carry

    lax.fori_loop(0, count, step, 0)


def tile_loop(width, body):
    loop(width // TILE, lambda n: body(n, pl.ds(pl.multiple_of(n * TILE, TILE), TILE)))


def put_tiles(ref, n, rows, values):
    for i in range(TILE // 128):
        ref[n * (TILE // 128) + i, 0:rows, :] = values[:, 128 * i : 128 * i + 128]


class Lazy:
    def __init__(self, queue, source, target, sem):
        self.copy = pltpu.make_async_copy(source, target, sem)
        self.target = target
        self.queue = queue
        self.started = self.waited = False

    def start(self):
        if not self.started:
            self.copy.start()
            self.started = True

    def get(self):
        if not self.waited:
            self.start()
            self.copy.wait()
            self.waited = True
            for item in self.queue:
                if not item.started:
                    item.start()
                    break
        return self.target


class Staged:
    def __init__(self, out, stage, sems, pending):
        self.out = out
        self.ref = stage
        self.sems = sems
        self.pending = pending

    def send(self, source, target):
        copy = pltpu.make_async_copy(source, target, self.sems.at[len(self.pending)])
        copy.start()
        self.pending.append(copy)

    def done(self):
        self.send(self.ref, self.out)

    def units_done(self, devices, units, out_units):
        self.send(self.ref.at[devices, units], self.out.at[devices, out_units])


def head_masks():
    lane = lax.broadcasted_iota(jnp.int32, (1, 128), 1)
    first = jnp.where(lane < 64, 1.0, 0.0).astype(BF16)
    second = jnp.where(lane < 64, 0.0, 1.0).astype(BF16)
    return first, second


def two_heads(values, masks):
    return jnp.concatenate([values * masks[0], values * masks[1]], axis=0)


def own_head(values, padded):
    lane = lax.broadcasted_iota(jnp.int32, (padded, 128), 1)
    return jnp.where(lane < 64, values[:padded], values[padded:])


def pooled_row(t, ends, b):
    return ends[b] * BATCH + b


def front_kernel(
    t,
    ends,
    tokens,
    first_gain,
    first_shift,
    joint_weight,
    output_weight,
    second_gain,
    second_shift,
    widen_weight,
    narrow_weight,
    final_gain,
    final_shift,
    projection,
    block_grad,
    turned,
    joint,
    probs,
    mixed,
    mixed_row,
    wide_row,
    pooled,
    raw_out,
    unit,
    grad_row,
    joint_wide,
    context_wide,
    normed_one,
    context,
):
    width, padded, rows = t.width, t.padded, t.rows
    staged = (turned, joint, probs, mixed)
    turned, joint, probs, mixed = [out.ref for out in staged]
    for at, size in chunks(t.real):
        mixed[at : at + size, :] = block_grad[at : at + size, :].astype(F32)
    for b in range(BATCH):
        grad_row[b : b + 1, :] = mixed[pl.ds(pooled_row(t, ends, b), 1), :]
    pad = t.real - t.real % 16
    normed_one[pad:rows, :] = jnp.zeros((rows - pad, width), BF16)
    for at, size in chunks(t.real):
        normal, _ = normalise(tokens[at : at + size, :].astype(F32))
        normed_one[at : at + size, :] = (normal * vec(first_gain) + vec(first_shift)).astype(BF16)
    if t.spread > rows:
        fill = (3 * width // 128, t.spread - rows, 128)
        joint_wide[:, rows : t.spread, :] = jnp.zeros(fill, F32)

    joint_weight = joint_weight.get()

    def joint_step(n, cols):
        put_tiles(joint_wide, n, rows, mm(normed_one[...], joint_weight[:, cols]))

    tile_loop(3 * width, joint_step)

    masks = head_masks()
    key_at = lax.broadcasted_iota(jnp.int32, (padded, 2 * padded), 0)
    query_at = lax.broadcasted_iota(jnp.int32, (padded, 2 * padded), 1)
    query_at = jnp.where(query_at < padded, query_at, query_at - padded)
    valid = key_at <= query_at if t.causal else key_at < t.length
    pairs = range(t.heads // 2)

    def attend(b):
        some = pl.ds(b, padded, stride=BATCH)
        for c in range(3 * width // 128):
            joint[b, :, 128 * c : 128 * c + 128] = joint_wide[c, some, :].astype(BF16)
        scores = []
        for p in pairs:
            at = 128 * p
            queries = joint[b, :, at : at + 128]
            keys = joint[b, :, width + at : width + at + 128]
            scores.append(mm_nt(keys, two_heads(queries, masks)) * 0.125)
        lows = []
        for p in pairs:
            score = jnp.where(valid, scores[p], -1e30)
            raised = jnp.exp(score - jnp.max(score, axis=0, keepdims=True))
            low = (raised * (1.0 / column_sum(raised))).astype(BF16)
            probs[b, p] = low
            lows.append(low)
        for p in pairs:
            at = 2 * width + 128 * p
            both = mm_tn(lows[p], joint[b, :, at : at + 128])
            context_wide[p, some, :] = own_head(both, padded)

    loop(BATCH, attend)
    staged[1].done()
    staged[2].done()
    for p in pairs:
        context[:, 128 * p : 128 * p + 128] = context_wide[p, 0:rows, :].astype(BF16)
    turn(normed_one, turned.at[0:width])
    turn(context, turned.at[width : 2 * width])
    staged[0].done()
    output_weight = output_weight.get()

    def mix_step(n, cols):
        mixed[:, cols] = mm(context[...], output_weight[:, cols])

    tile_loop(width, mix_step)
    for at, size in chunks(t.real):
        mixed[at : at + size, :] += tokens[at : at + size, :].astype(F32)
    for b in range(BATCH):
        mixed_row[b : b + 1, :] = mixed[pl.ds(pooled_row(t, ends, b), 1), :]
    row = mixed_row[...]
    mixed[t.real : rows, :] = jnp.zeros((rows - t.real, width), F32)
    mixed[t.extra : t.extra + BATCH, :] = row
    staged[3].done()

    normal, _ = normalise(row)
    normed = (normal * vec(second_gain) + vec(second_shift)).astype(BF16)
    wide = mm(normed, widen_weight.get()[...])
    wide_row[...] = wide
    active = (wide * sigmoid(1.702 * wide)).astype(BF16)
    last = row + mm(active, narrow_weight.get()[...])
    pooled[...] = last
    normal, _ = normalise(last)
    normed = (normal * vec(final_gain) + vec(final_shift)).astype(BF16)
    raw = mm(normed, projection.get()[...])
    raw_out[...] = raw
    factor = lax.rsqrt(jnp.sum(raw * raw, axis=-1, keepdims=True) + 1e-06)
    unit[...] = (raw * factor).astype(BF16)


def fronts_kernel(ends, held, lazies, outs, scratch):
    order = [5, 6, 0, 7, 8, 9, 1, 2, 3, 4]
    weights = [lazies[order.index(i)] for i in range(10)]
    for i in (1, 0):
        t = (IMAGE, TEXT)[i]
        tokens, g1, s1, g2, s2, gf, sf, block_grad = held[8 * i : 8 * i + 8]
        joint, output, widen, narrow, projection = weights[5 * i : 5 * i + 5]
        params = (g1, s1, joint, output, g2, s2, widen, narrow, gf, sf, projection, block_grad)
        front_kernel(
            t, ends[i], tokens, *params, *outs[10 * i : 10 * i + 10], *scratch[4 * i : 4 * i + 4]
        )


def middle_kernel(
    t,
    place,
    ends,
    mixed,
    block_grad,
    second_gain,
    second_shift,
    widen_weight,
    narrow_weight,
    normed_turned,
    active_turned,
    wide_own,
    wide_send,
    narrow_own,
    narrow_send,
    mixed_grad,
    gain_grad,
    shift_grad,
    normed_two,
    narrow_in,
    wide_in,
):
    step = pl.program_id(0)
    half_steps = pl.num_programs(0) // 2

    @pl.when(step == 0)
    def _():
        wide_in[t.real : t.rows, :] = jnp.zeros((t.rows - t.real, t.width), F32)
        for at, size in chunks(t.rows):
            normal, _ = normalise(mixed[at : at + size, :])
            normed_two[at : at + size, :] = (normal * vec(second_gain) + vec(second_shift)).astype(
                BF16
            )
        turn(normed_two, normed_turned)
        for at, size in chunks(t.real):
            wide_in[at : at + size, :] = block_grad[at : at + size, :].astype(F32)
        for b in range(BATCH):
            wide_in[pl.ds(pooled_row(t, ends, b), 1), :] = jnp.zeros((1, t.width), F32)
        narrow_in[...] = wide_in[...].astype(BF16)
        cols = t.width // 2
        own = pl.multiple_of(place[0] * cols, 128)
        narrow_own[...] = narrow_in[:, pl.ds(own, cols)]
        narrow_send[...] = narrow_in[:, pl.ds(pl.multiple_of(cols - own, 128), cols)]
        mixed_grad[...] = jnp.zeros_like(mixed_grad)

    wide = mm(normed_two[...], widen_weight[...])
    sig = sigmoid(1.702 * wide)
    active_turned[:, 0 : t.rows] = (wide * sig).astype(BF16).T
    slope = sig + 1.702 * wide * sig * (1.0 - sig)
    low = (mm_nt(narrow_in[...], narrow_weight[...]) * slope).astype(BF16)
    mixed_grad[...] += mm_nt(low, widen_weight[...])

    @pl.when(step < half_steps)
    def _():
        wide_own[...] = low

    @pl.when(step >= half_steps)
    def _():
        wide_send[...] = low

    @pl.when(step == pl.num_programs(0) - 1)
    def _():
        gain = shift = 0.0
        for at, size in chunks(t.rows):
            some = slice(at, at + size)
            normal, inverse = normalise(mixed[some, :])
            up = mixed_grad[some, :]
            gain += column_sum(up * normal)
            shift += column_sum(up)
            mixed_grad[some, :] = wide_in[some, :] + norm_back(
                up, vec(second_gain), normal, inverse
            )
        gain_grad[...] = gain
        shift_grad[...] = shift


def split_dot(weights, right):
    high = weights.astype(BF16)
    rest = weights - high.astype(F32)
    middle = rest.astype(BF16)
    low = (rest - middle.astype(F32)).astype(BF16)
    return mm(high, right) + mm(middle, right) + mm(low, right)


def row_sizes(t):
    return t.hidden // 2, t.width // 2, EMBED // 2


def row_at(t, part):
    before = 0 if t is IMAGE else sum(row_sizes(IMAGE)) + IMAGE.width
    return before + sum(row_sizes(t)[:part])


ROW_TOTAL = sum(row_sizes(IMAGE)) + IMAGE.width + sum(row_sizes(TEXT)) + TEXT.width


def head_back(
    unit_grad,
    raw,
    pooled,
    mixed_row,
    wide_row,
    grad_row,
    final_gain,
    final_shift,
    second_gain,
    second_shift,
    projection,
    widen_weight,
    narrow_weight,
    outs,
):
    (
        final_gain_grad,
        final_shift_grad,
        second_gain_grad,
        second_shift_grad,
        final_out,
        raw_grad_out,
        narrow_in_row,
        wide_grad_row,
        mixed_grad_row,
    ) = outs
    factor = lax.rsqrt(jnp.sum(raw * raw, axis=-1, keepdims=True) + 1e-06)
    raw_grad = factor * unit_grad - raw * (factor * factor * factor) * jnp.sum(
        unit_grad * raw, axis=-1, keepdims=True
    )
    raw_grad = raw_grad.astype(BF16)
    raw_grad_out[...] = raw_grad.astype(F32)
    normal, inverse = normalise(pooled)
    final_out[...] = (normal * final_gain + final_shift).astype(BF16).astype(F32)
    up = mm_nt(raw_grad, projection.get()[...])
    final_gain_grad[...] = column_sum(up * normal)
    final_shift_grad[...] = column_sum(up)
    out_grad = grad_row + norm_back(up, final_gain, normal, inverse)
    narrow_in = out_grad.astype(BF16)
    narrow_in_row[...] = narrow_in.astype(F32)
    sig = sigmoid(1.702 * wide_row)
    slope = sig + 1.702 * wide_row * sig * (1.0 - sig)
    low = (mm_nt(narrow_in, narrow_weight.get()[...]) * slope).astype(BF16)
    wide_grad_row[...] = low.astype(F32)
    up = mm_nt(low, widen_weight.get()[...])
    normal, inverse = normalise(mixed_row)
    second_gain_grad[...] = column_sum(up * normal)
    second_shift_grad[...] = column_sum(up)
    mixed_grad_row[...] = out_grad + norm_back(up, second_gain, normal, inverse)


def pair_kernel(scalars, held, lazies, outs, scratch):
    place, log_scale = scalars
    own, other, image_unit, text_unit = held[:4]
    image_in, text_in = held[4:13], held[13:22]
    loss, scale_grad = outs[:2]
    image_outs, text_outs, row_send = outs[2:11], outs[11:20], outs[20]
    half = own.shape[0]
    pairs = 2 * half
    scale = jnp.exp(jnp.full((1, 1), log_scale[0], F32))
    blocks = (own, other)

    def totals(left_at, right_at):
        sums, moments = [], []
        for right in blocks:
            column, moment = None, None
            for left in blocks:
                for piece in range(0, half, 256):
                    sims = scale * mm_nt(
                        left[piece : piece + 256, left_at : left_at + EMBED],
                        right[:, right_at : right_at + EMBED],
                    )
                    raised = jnp.exp(sims)
                    add, more = column_sum(raised), column_sum(raised * sims)
                    column = add if column is None else column + add
                    moment = more if moment is None else moment + more
            sums.append(column)
            moments.append(moment)
        return sums, moments

    column_sums, column_moments = totals(0, EMBED)
    row_sums, row_moments = totals(EMBED, 0)
    log_total = jnp.zeros((1, 1), F32)
    weighted = jnp.zeros((1, 1), F32)
    trace = jnp.zeros((1, 1), F32)
    for i in range(2):
        for total, moment in ((column_sums[i], column_moments[i]), (row_sums[i], row_moments[i])):
            log_total += jnp.sum(jnp.log(total), axis=-1, keepdims=True)
            weighted += jnp.sum(moment / total, axis=-1, keepdims=True)
        product = blocks[i][:, :EMBED].astype(F32) * blocks[i][:, EMBED:].astype(F32)
        trace += jnp.sum(column_sum(product), axis=-1, keepdims=True)
    trace = scale * trace
    loss[...] = jnp.broadcast_to((log_total - 2.0 * trace) / (2.0 * pairs), loss.shape)
    scale_grad[...] = jnp.broadcast_to((weighted - 2.0 * trace) / (2.0 * pairs), loss.shape)

    lane = lax.broadcasted_iota(jnp.int32, (BATCH, half), 1)
    sub = lax.broadcasted_iota(jnp.int32, (BATCH, half), 0)
    identity = jnp.where(lane == sub + place[1] * BATCH, 2.0, 0.0)

    def grads(unit, at, other_sums):
        raised = [jnp.exp(scale * mm_nt(unit[...], block[:, at : at + EMBED])) for block in blocks]
        own_sum = sum(jnp.sum(r, axis=-1, keepdims=True) for r in raised)
        result = None
        for i in range(2):
            weight = raised[i] * (1.0 / own_sum + 1.0 / other_sums[i])
            if i == 0:
                weight = weight - identity
            weight = weight / (2.0 * pairs)
            part = split_dot(weight, blocks[i][:, at : at + EMBED])
            result = part if result is None else result + part
        return scale * result

    image_grad = grads(image_unit, EMBED, column_sums)
    text_grad = grads(text_unit, 0, row_sums)
    for unit_grad, ins, weights, results in (
        (text_grad, text_in, lazies[0:3], text_outs),
        (image_grad, image_in, lazies[3:6], image_outs),
    ):
        values = [ref[...] for ref in ins[:5]] + [vec(ref) for ref in ins[5:9]]
        projection, narrow, widen = weights
        head_back(unit_grad, *values, projection, widen, narrow, results)
    at = 0
    for t, results in ((IMAGE, image_outs), (TEXT, text_outs)):
        for ref, size in zip((results[7], results[6], results[5]), row_sizes(t)):
            start = pl.multiple_of((1 - place[0]) * size, 128)
            row_send[:, at : at + size] = ref[:, pl.ds(start, size)]
            at += size
        row_send[:, at : at + t.width] = results[4][...]
        at += t.width


def back_kernel(t, scalars, held, lazies, outs, scratch):
    place, ends = scalars
    tokens, first_gain, mixed_grad_row = held
    output_weight, mixed_grad, joint, probs, joint_weight = lazies
    own, send, tokens_out, gain_grad, shift_grad = outs
    context_grad, joint_grad, normed_grad, grads = scratch
    width, padded, rows = t.width, t.padded, t.rows
    tokens_grad = tokens_out.ref
    grad = mixed_grad.get()
    for b in range(BATCH):
        grad[pl.ds(pooled_row(t, ends, b), 1), :] = mixed_grad_row[b : b + 1, :]
    mixed_low = slice(3 * width, 4 * width)
    grads[:, mixed_low] = grad[...].astype(BF16)
    if t.spread > rows:
        fill = (width // 128, t.spread - rows, 128)
        context_grad[:, rows : t.spread, :] = jnp.zeros(fill, F32)
    output_weight = output_weight.get()

    def context_step(n, cols):
        put_tiles(context_grad, n, rows, mm_nt(grads[:, mixed_low], output_weight[cols, :]))

    tile_loop(width, context_step)
    masks = head_masks()
    pairs = range(t.heads // 2)
    joint, probs = joint.get(), probs.get()

    def attend(b):
        some = pl.ds(b, padded, stride=BATCH)
        ups = [two_heads(context_grad[p, some, :].astype(BF16), masks) for p in pairs]
        backs = []
        for p in pairs:
            at = 2 * width + 128 * p
            backs.append(mm_nt(joint[b, :, at : at + 128], ups[p]))
        lows = []
        for p in pairs:
            wide = probs[b, p].astype(F32)
            back = wide * (backs[p] - column_sum(backs[p] * wide))
            lows.append(back.astype(BF16))
        for p in pairs:
            at = 128 * p
            queries = joint[b, :, at : at + 128]
            keys = joint[b, :, width + at : width + at + 128]
            joint_grad[2 * len(pairs) + p, some, :] = mm(probs[b, p], ups[p])
            joint_grad[len(pairs) + p, some, :] = mm(lows[p], two_heads(queries, masks)) * 0.125
            joint_grad[p, some, :] = own_head(mm_tn(lows[p], keys), padded) * 0.125

    loop(BATCH, attend)
    for c in range(3 * width // 128):
        grads[:, 128 * c : 128 * c + 128] = joint_grad[c, 0:rows, :].astype(BF16)
    start = pl.multiple_of(place[0] * (2 * width), 128)
    own.send(grads.at[:, pl.ds(start, 2 * width)], own.out)
    start = pl.multiple_of(2 * width - start, 128)
    send.send(grads.at[:, pl.ds(start, 2 * width)], send.out)
    joint_weight = joint_weight.get()

    def normed_step(n, cols):
        normed_grad[:, cols] = mm_nt(grads[:, 0 : 3 * width], joint_weight[cols, :])

    tile_loop(width, normed_step)
    gain = shift = 0.0
    for at, size in chunks(t.real):
        some = slice(at, at + size)
        normal, inverse = normalise(tokens[some, :].astype(F32))
        up = normed_grad[some, :]
        gain += column_sum(up * normal)
        shift += column_sum(up)
        tokens_grad[some, :] = grad[some, :] + norm_back(up, vec(first_gain), normal, inverse)
    gain_grad[...] = gain
    shift_grad[...] = shift
    tokens_out.done()

def turn(source, target):
    def step(n):
        cols = pl.ds(pl.multiple_of(n * 128, 128), 128)
        target[cols, 0 : source.shape[0]] = source[:, cols].T

    loop(source.shape[1] // 128, step)


def lanes_down(values):
    return jnp.concatenate(
        [values[:, :, at : at + 128] for at in range(0, values.shape[2], 128)], axis=1
    )


def put(out, device, unit, values):
    count = values.shape[1] // 16
    size = values.shape[0]
    values = values.reshape(size, count, 16, 128).astype(BF16)
    out[pl.ds(device, size), unit : unit + count] = values


def pack_twelve(first, second, out, unit=0, each=4):
    cols = first.shape[1]
    count = cols // 128
    sub = lax.broadcasted_iota(jnp.int32, (each, 8, cols), 1) < 4

    def step(e):
        rows = pl.ds(pl.multiple_of(e * (24 * each), 8), 24 * each)
        x = first[rows, :].reshape(each, 24, cols)
        y = second[rows, :].reshape(each, 24, cols)
        left, right = x[:, 8:16], y[:, 8:16]
        even = jnp.where(sub, left, pltpu.roll(right, 4, 1))
        odd = jnp.where(sub, pltpu.roll(left, 4, 1), right)
        parts = []
        for a, b, c in ((x[:, 0:8], y[:, 0:8], even), (x[:, 16:24], y[:, 16:24], odd)):
            parts.append(jnp.concatenate([lanes_down(v) for v in (a, b, c)], axis=1))
        if parts[0].shape[1] % 16:
            fill = jnp.zeros((each, 16 - parts[0].shape[1] % 16, 128), F32)
            parts = [jnp.concatenate([part, fill], axis=1) for part in parts]
        height = parts[0].shape[1]
        values = jnp.stack(parts, axis=1).reshape(2 * each, height, 128)
        put(out, e * (2 * each), unit, values)

    loop(32 // each, step)


def pack_rows(result, rows, out, unit=0, each=8, device=0):
    total = result.shape[0] // rows
    cols = result.shape[1]

    def step(e):
        some = pl.ds(pl.multiple_of(e * (rows * each), 8), rows * each)
        values = lanes_down(result[some, :].reshape(each, rows, cols))
        put(out, device + e * each, unit, values)

    loop(total // each, step)


def put_extra(t, ref, rows):
    rows = jnp.concatenate([rows, jnp.zeros_like(rows)], axis=0)
    ref[t.extra : t.extra + 16, :] = rows.astype(BF16)


def wide_grads(t, half, product, send, at, first, second):
    if t is IMAGE:
        for i in range(3):
            first[...] = product(256 * i, 256)
            second[...] = product(768 + 256 * i, 256)
            pack_twelve(first, second, send.ref, 3 * i)
            units = slice(3 * i, 3 * i + 3)
            send.units_done(slice(None), units, slice(at + 3 * i, at + 3 * i + 3))
    else:
        for i in range(2):
            first[...] = product(512 * i, 512)
            pack_rows(first, 8, send.ref, 2 * i)
            units = slice(2 * i, 2 * i + 2)
            send.units_done(slice(None), units, slice(at + 2 * i, at + 2 * i + 2))


def feed_kernel(t, at, scalars, held, lazies, outs, scratch):
    (place,) = scalars
    rows = lazies[0:4]
    normed, wides, narrows = lazies[4:6], lazies[6:8], lazies[8:10]
    actives = lazies[10:18]
    (out,) = outs
    first, second, narrow_result = scratch
    wide_rows, narrow_rows = rows[0:2], rows[2:4]
    for row, ref in zip(wide_rows, wides):
        put_extra(t, ref.get(), row.get()[...])
    lefts = [ref.get() for ref in normed]
    wides = [ref.get() for ref in wides]

    def product(tile, size):
        return sum(mm(a[:, 0 : t.rows], b[:, tile : tile + size]) for a, b in zip(lefts, wides))

    wide_grads(t, place[0], product, out, at, first, second)
    for row, ref in zip(narrow_rows, narrows):
        put_extra(t, ref.get(), row.get()[...])
    narrows = [ref.get() for ref in narrows]
    wide_units, units = (9, 9) if t is IMAGE else (4, 4)
    some = slice(wide_units, wide_units + units)
    for j in range(4):
        pair = [actives[2 * j].get(), actives[2 * j + 1].get()]
        narrow_result[...] = sum(mm(a[:, 0 : t.rows], b[...]) for a, b in zip(pair, narrows))
        pack_rows(narrow_result, t.hidden // DEVS, out.ref, wide_units, 4, 16 * j)
        out.units_done(
            slice(16 * j, 16 * j + 16), some, slice(at + wide_units, at + wide_units + units)
        )


def rest_kernel(scalars, held, lazies, outs, scratch):
    (place,) = scalars
    (out,) = outs
    first, second, third = scratch[:3]
    misc_scratch, spread = scratch[3:6], scratch[6]
    half = place[0]
    misc, text_stage, image_stage = [Staged(out.out, ref, out.sems, out.pending) for ref in scratch[7:10]]
    misc_grads(half, held[:5], held[5:], misc, misc_scratch, spread)
    for t, ins, stage, results in (
        (TEXT, lazies[0:4], text_stage, (third, None)),
        (IMAGE, lazies[4:8], image_stage, (first, second)),
    ):
        width = t.width
        lefts, rights = [ref.get() for ref in ins[0::2]], [ref.get() for ref in ins[1::2]]

        def product(tile, size):
            late = jnp.where(half * (2 * width) + tile >= 3 * width, width, 0)
            rows = pl.ds(pl.multiple_of(late, 128), width)
            return sum(
                mm(a[rows, 0 : t.rows], b[:, tile : tile + size]) for a, b in zip(lefts, rights)
            )

        wide_grads(t, half, product, stage, REST_AT["image" if t is IMAGE else "text"], *results)


IMAGE_FEED_UNITS = 18
LATE_UNITS = 25
TEXT_FEED_AT = 0
REST_AT = {"text": 8, "image": 16}
MISC_AT = 12


def misc_grads(half, factors, vectors, out, scratch, spread):
    image_final, image_raw, text_final, text_raw, received = factors
    first, second, third = scratch

    def both(mine, at, size, start=0):
        mine = mine[:, pl.ds(start, size)]
        return jnp.concatenate([mine, received[:, at : at + size]], axis=0).astype(BF16)

    def raw_columns(t, ref, at, size):
        start = pl.multiple_of(half * 256 + at, 128)
        return both(ref, row_at(t, 2) + at, size, start)

    final = both(image_final, row_at(IMAGE, 3), IMAGE.width)
    first[...] = mm_tn(final, raw_columns(IMAGE, image_raw, 0, 128))
    second[...] = mm_tn(final, raw_columns(IMAGE, image_raw, 128, 128))
    final = both(text_final, row_at(TEXT, 3), TEXT.width)
    third[...] = mm_tn(final, raw_columns(TEXT, text_raw, 0, 256))
    pack_twelve(first, second, out.ref, 2, 8)
    pack_rows(third, 8, out.ref, 0)
    spread[...] = jnp.zeros_like(spread)
    for tower, refs_of, width in ((0, vectors[:8], 768), (1, vectors[8:], 512)):
        each = width // DEVS
        device = lax.broadcasted_iota(jnp.int32, (DEVS, width), 0)
        column = lax.broadcasted_iota(jnp.int32, (DEVS, width), 1)
        mine = jnp.logical_and(column >= device * each, column < device * each + each)
        source = lax.broadcasted_iota(jnp.int32, (width, 128), 0)
        lane = lax.broadcasted_iota(jnp.int32, (width, 128), 1)
        at = lax.rem(source, each)
        high_at = jnp.where(lane == at, 1.0, 0.0).astype(BF16)
        low_at = jnp.where(lane == at + 64, 1.0, 0.0).astype(BF16)
        rows = [refs_of[0][...], refs_of[1][...], refs_of[2][...] + refs_of[3][...]]
        rows += [refs_of[4][...] + refs_of[5][...], refs_of[6][...], refs_of[7][...]]
        for k, row in enumerate(rows):
            row = jnp.where(mine, row, 0.0)
            high = row.astype(BF16)
            low = (row - high.astype(F32)).astype(BF16)
            spread[:, 6 * tower + k, :] = mm(high, high_at) + mm(low, low_at)
    out.ref[:, 1] = spread[...].astype(BF16)
    out.units_done(slice(None), slice(0, 4), slice(MISC_AT, MISC_AT + 4))


def add_kernel(received, total):
    total[...] = jnp.sum(received[...].astype(F32), axis=0)


def sum_blocks(received, block):
    count, units = received.shape[:2]
    return pl.pallas_call(
        add_kernel,
        name="sum_blocks",
        grid=(units // block,),
        out_shape=jax.ShapeDtypeStruct((units, 16, 128), F32),
        in_specs=[pl.BlockSpec((count, block, 16, 128), lambda i: (0, i, 0, 0))],
        out_specs=pl.BlockSpec((block, 16, 128), lambda i: (i, 0, 0)),
        compiler_params=pltpu.CompilerParams(vmem_limit_bytes=VMEM_LIMIT),
    )(received)


def unpack_kernel(place, feed_mine, late_mine, feed_other, late_other, *outs):
    (
        image_joint,
        image_output,
        image_widen,
        image_narrow,
        image_projection,
        text_joint,
        text_output,
        text_widen,
        text_narrow,
        text_projection,
    ) = outs[:10]
    odd = place[1] % 2

    def emit(half, feed, late):
        def into(ref, col, body, tail):
            @pl.when(odd == 0)
            def _():
                ref[0:8, col : col + 128] = body
                ref[8:12, col : col + 128] = tail

            @pl.when(odd == 1)
            def _():
                ref[0:4, col : col + 128] = tail
                ref[4:12, col : col + 128] = body

        def image_wide(source, at, store):
            for tile in range(3):
                block = source[16 * (at + 3 * tile) : 16 * (at + 3 * tile) + 48, :]
                for side in range(2):
                    for g in range(2):
                        body = block[16 * side + 8 * g : 16 * side + 8 * g + 8]
                        tail = block[32 + 8 * g + 4 * side : 36 + 8 * g + 4 * side]
                        store(half * 1536 + side * 768 + tile * 256 + g * 128, body, tail)

        def joint_store(col, body, tail):
            if col < 2304:
                into(image_joint, col, body, tail)
            else:
                into(image_output, col - 2304, body, tail)

        image_wide(feed, 0, functools.partial(into, image_widen))
        image_wide(late, REST_AT["image"], joint_store)
        at = 16 * 9
        for g in range(3):
            col = half * 384 + 128 * g
            image_narrow[:, col : col + 128] = feed[at + 48 * g : at + 48 * g + 48, :]
        at = 16 * (MISC_AT + 2)
        for side in range(2):
            col = half * 256 + 128 * side
            tail = late[at + 16 + 4 * side : at + 20 + 4 * side, :]
            into(image_projection, col, late[at + 8 * side : at + 8 * side + 8, :], tail)
        for g in range(8):
            col = half * 1024 + 128 * g
            at = 16 * TEXT_FEED_AT + 8 * g
            text_widen[:, col : col + 128] = late[at : at + 8, :]
            at = 16 * REST_AT["text"] + 8 * g
            block = late[at : at + 8, :]
            if col < 1536:
                text_joint[:, col : col + 128] = block
            else:
                text_output[:, col - 1536 : col - 1408] = block
        for g in range(2):
            col = half * 256 + 128 * g
            at = 16 * (TEXT_FEED_AT + 4) + 32 * g
            text_narrow[:, col : col + 128] = late[at : at + 32, :]
            at = 16 * MISC_AT + 8 * g
            text_projection[:, col : col + 128] = late[at : at + 8, :]

    for half in range(2):

        @pl.when(place[0] == half)
        def _():
            emit(half, feed_mine, late_mine)
            emit(1 - half, feed_other, late_other)

    at = 16 * (MISC_AT + 1)
    vectors = late_mine[at : at + 16, :] + late_other[at : at + 16, :]
    for k in range(12):
        each = 12 if k < 6 else 8
        outs[10 + k][...] = vectors[k : k + 1, 0:each] + vectors[k : k + 1, 64 : 64 + each]


SMEM = pl.BlockSpec(memory_space=pltpu.SMEM)
VMEM = pl.BlockSpec(memory_space=pltpu.VMEM)


def call(body, name, scalars, arrays, outs, scratch=(), flops=1 << 32):
    return pl.pallas_call(
        body,
        name=name,
        out_shape=tuple(jax.ShapeDtypeStruct(shape, kind) for shape, kind in outs),
        in_specs=[SMEM] * len(scalars) + [VMEM] * len(arrays),
        out_specs=tuple(VMEM for _ in outs),
        scratch_shapes=[pltpu.VMEM(shape, kind) for shape, kind in scratch],
        compiler_params=pltpu.CompilerParams(vmem_limit_bytes=VMEM_LIMIT),
        cost_estimate=pl.CostEstimate(flops=flops, bytes_accessed=20 << 20, transcendentals=0),
    )(*scalars, *arrays)


BIG = 1 << 18


def lazy_call(body, name, scalars, held, lazies, outs, scratch=(), flops=1 << 33, buffer=None, after=(), ahead=3):
    many = 24

    def kernel(*refs):
        refs = list(refs)

        def take(count):
            got = refs[:count]
            del refs[:count]
            return got

        scalar_refs, held_refs = take(len(scalars)), take(len(held))
        sources = take(len(lazies))
        take(len(after) + (buffer is not None))
        out_refs = take(len(outs))
        targets = take(len(lazies))
        stages = take(sum(1 for out in outs if out[2]))
        scratch_refs = take(len(scratch))
        in_sems, out_sems = refs
        lazy = []
        for i, (source, target, (_, index, _)) in enumerate(zip(sources, targets, lazies)):
            if index is not None:
                source = source.at[index(*scalar_refs)]
            lazy.append(Lazy(lazy, source, target, in_sems.at[i]))
        for item in lazy[:ahead]:
            item.start()
        pending = []
        results = []
        for out, ref in zip(outs, out_refs):
            if out[2] is None:
                results.append(ref)
            else:
                results.append(Staged(ref, stages.pop(0) if out[2] else None, out_sems, pending))
        body(scalar_refs, held_refs, lazy, results, scratch_refs)
        for item in lazy:
            if item.started:
                item.get()
        for copy in pending:
            copy.wait()

    any_spec = pl.BlockSpec(memory_space=pl.ANY)
    scratch_shapes = [pltpu.VMEM(shape, array.dtype) for array, _, shape in lazies]
    scratch_shapes += [pltpu.VMEM(stage, kind) for _, kind, stage in outs if stage]
    scratch_shapes += [pltpu.VMEM(shape, kind) for shape, kind in scratch]
    scratch_shapes += [pltpu.SemaphoreType.DMA((max(1, len(lazies)),)), pltpu.SemaphoreType.DMA((many,))]
    arrays = [*held, *[array for array, _, _ in lazies], *after]
    specs = [SMEM] * len(scalars) + [VMEM] * len(held) + [any_spec] * (len(lazies) + len(after))
    aliases = {}
    if buffer is not None:
        aliases = {len(scalars) + len(arrays): 0}
        arrays.append(buffer)
        specs.append(any_spec)
    return pl.pallas_call(
        kernel,
        name=name,
        out_shape=tuple(jax.ShapeDtypeStruct(shape, kind) for shape, kind, _ in outs),
        in_specs=specs,
        out_specs=tuple(VMEM if stage is None else any_spec for _, _, stage in outs),
        scratch_shapes=scratch_shapes,
        input_output_aliases=aliases,
        compiler_params=pltpu.CompilerParams(vmem_limit_bytes=VMEM_LIMIT),
        cost_estimate=pl.CostEstimate(flops=flops, bytes_accessed=20 << 20, transcendentals=0),
    )(*scalars, *arrays)


def all_of(array):
    return array, None, array.shape


def staged(shape, kind):
    return shape, kind, shape


def plain(shape, kind):
    return shape, kind, None


def fronts_call(ends, tokens, block_grads, weights):
    held, lazies, outs, scratch = [], [], [], []
    for t, token, grad, w in zip((IMAGE, TEXT), tokens, block_grads, weights):
        rows, width, hidden = t.rows, t.width, t.hidden
        held += [token, w[0], w[1], w[4], w[5], w[8], w[9], grad]
        lazies += [all_of(w[i]) for i in (2, 3, 6, 7, 10)]
        outs += [
            staged((2 * width, t.lanes), BF16),
            staged((BATCH, t.padded, 3 * width), BF16),
            staged((BATCH, t.heads // 2, t.padded, 2 * t.padded), BF16),
            staged((rows, width), F32),
            plain((BATCH, width), F32),
            plain((BATCH, hidden), F32),
            plain((BATCH, width), F32),
            plain((BATCH, EMBED), F32),
            plain((BATCH, EMBED), BF16),
            plain((BATCH, width), F32),
        ]
        scratch += [
            ((3 * width // 128, t.spread, 128), F32),
            ((width // 128, t.spread, 128), F32),
            ((rows, width), BF16),
            ((rows, width), BF16),
        ]
    lazies = [lazies[i] for i in (5, 6, 0, 7, 8, 9, 1, 2, 3, 4)]
    results = lazy_call(fronts_kernel, "fronts", ends, held, lazies, outs, scratch)
    return results[:10], results[10:]


def middle(t, name, place, ends, mixed, block_grad, gain, shift, widen, narrow, after):
    rows, width, hidden = t.rows, t.width, t.hidden
    steps = hidden // TILE
    outs = (
        ((width, t.lanes), BF16),
        ((hidden, t.lanes), BF16),
        ((rows, hidden // 2), BF16),
        ((rows, hidden // 2), BF16),
        ((rows, width // 2), BF16),
        ((rows, width // 2), BF16),
        ((rows, width), F32),
        ((1, width), F32),
        ((1, width), F32),
    )

    def held(shape):
        return pl.BlockSpec(shape, lambda i, *_: (0,) * len(shape))

    def tile(i, place):
        return lax.rem(i + place[0] * (steps // 2), steps)

    out_specs = [held(shape) for shape, _ in outs]
    out_specs[1] = pl.BlockSpec((TILE, t.lanes), lambda i, place, ends: (tile(i, place), 0))
    out_specs[2] = pl.BlockSpec((rows, TILE), lambda i, *_: (0, jnp.minimum(i, steps // 2 - 1)))
    out_specs[3] = pl.BlockSpec((rows, TILE), lambda i, *_: (0, jnp.maximum(i - steps // 2, 0)))
    in_specs = [held(a.shape) for a in (mixed, block_grad, gain, shift)]
    in_specs.append(pl.BlockSpec((width, TILE), lambda i, place, ends: (0, tile(i, place))))
    in_specs.append(pl.BlockSpec((TILE, width), lambda i, place, ends: (tile(i, place), 0)))
    in_specs += [pl.BlockSpec(memory_space=pl.ANY)] * len(after)

    def kernel(*refs):
        middle_kernel(t, *refs[:8], *refs[8 + len(after) :])

    return pl.pallas_call(
        kernel,
        name=name + "_middle",
        out_shape=tuple(jax.ShapeDtypeStruct(shape, kind) for shape, kind in outs),
        grid_spec=pltpu.PrefetchScalarGridSpec(
            num_scalar_prefetch=2,
            grid=(steps,),
            in_specs=in_specs,
            out_specs=tuple(out_specs),
            scratch_shapes=[
                pltpu.VMEM((rows, width), BF16),
                pltpu.VMEM((rows, width), BF16),
                pltpu.VMEM((rows, width), F32),
            ],
        ),
        compiler_params=pltpu.CompilerParams(vmem_limit_bytes=VMEM_LIMIT),
        cost_estimate=pl.CostEstimate(flops=1 << 35, bytes_accessed=20 << 20, transcendentals=0),
    )(place, ends, mixed, block_grad, gain, shift, widen, narrow, *after)


def back(t, name, place, ends, row, tokens, gain, output, mixed_grad, joint, probs, joint_weight, after):
    rows, width = t.rows, t.width
    lazies = [all_of(a) for a in (output, mixed_grad, joint, probs, joint_weight)]
    outs = [
        ((rows, 2 * width), BF16, ()),
        ((rows, 2 * width), BF16, ()),
        staged((t.real, width), F32),
        plain((1, width), F32),
        plain((1, width), F32),
    ]
    scratch = [
        ((width // 128, t.spread, 128), F32),
        ((3 * width // 128, t.spread, 128), F32),
        ((rows, width), F32),
        ((rows, 4 * width), BF16),
    ]
    return lazy_call(
        functools.partial(back_kernel, t),
        name + "_back",
        (place, ends),
        (tokens, gain, row),
        lazies,
        outs,
        scratch,
        after=after,
    )


def feed(t, name, place, rows_own, rows_other, own, other, buffer, after):
    rows, width, hidden = t.rows, t.width, t.hidden
    wide_units, units = (9, 9) if t is IMAGE else (4, 4)
    lazies = []
    for part, size in enumerate((hidden // 2, width // 2)):
        def mine(place, size=size):
            return slice(None), pl.ds(pl.multiple_of(place[0] * size, 128), size)

        def theirs(place, part=part, size=size):
            return slice(None), slice(row_at(t, part), row_at(t, part) + size)

        lazies.append((rows_own[part], mine, (BATCH, size)))
        lazies.append((rows_other, theirs, (BATCH, size)))
    lazies += [all_of(own[0]), all_of(other[0]), all_of(own[2]), all_of(other[2])]
    lazies += [all_of(own[3]), all_of(other[3])]
    for j in range(4):
        some = slice(width * j, width * j + width)
        for side in (own, other):
            lazies.append((side[1], lambda *_, some=some: (some, slice(None)), (width, t.lanes)))
    total = LATE_UNITS if buffer else wide_units + units
    outs = [((DEVS, total, 16, 128), BF16, (DEVS, wide_units + units, 16, 128))]
    cols = 256 if t is IMAGE else 512
    scratch = [
        ((width, cols), F32),
        ((width, cols) if t is IMAGE else (8, 128), F32),
        ((width, width // 2), F32),
    ]
    (out,) = lazy_call(
        functools.partial(feed_kernel, t, TEXT_FEED_AT if buffer else 0),
        name + "_feed",
        (place,),
        (),
        lazies,
        outs,
        scratch,
        after=after,
        ahead=10,
    )
    return out


def rest(place, factors, vectors, sides, buffer):
    lazies = []
    for own, other in (sides[1], sides[0]):
        lazies += [all_of(a) for a in (*own, *other)]
    outs = [((DEVS, LATE_UNITS, 16, 128), BF16, ())]
    scratch = [
        ((768, 256), F32),
        ((768, 256), F32),
        ((512, 512), F32),
        ((768, 128), F32),
        ((768, 128), F32),
        ((512, 256), F32),
        ((DEVS, 16, 128), F32),
        ((DEVS, 4, 16, 128), BF16),
        ((DEVS, 4, 16, 128), BF16),
        ((DEVS, 9, 16, 128), BF16),
    ]
    (out,) = lazy_call(
        rest_kernel, "rest", (place,), [*factors, *vectors], lazies, outs, scratch, buffer=buffer, ahead=4
    )
    return out


def behind(array, after):
    def kernel(*refs):
        pass

    any_spec = pl.BlockSpec(memory_space=pl.ANY)
    return pl.pallas_call(
        kernel,
        name="behind",
        out_shape=jax.ShapeDtypeStruct(array.shape, array.dtype),
        in_specs=[any_spec] * (1 + len(after)),
        out_specs=any_spec,
        input_output_aliases={0: 0},
    )(array, *after)


SWAP = [(0, 1), (1, 0)]


def by_token(tokens):
    return tokens.transpose(1, 0, 2).reshape(-1, tokens.shape[2])


def shards(*args):
    image_tokens, image_weights, image_block_grad = args[0], args[1:12], args[12]
    text_tokens, caption_lengths = args[13], args[14]
    text_weights, text_block_grad, log_scale = args[15:26], args[26], args[27]
    core = lax.axis_index("tower")
    dp = lax.axis_index("dp")
    place = jnp.stack([core, dp]).astype(jnp.int32)
    image_ends = jnp.zeros((BATCH,), jnp.int32)
    text_ends = (caption_lengths - 1).astype(jnp.int32)
    tokens = (by_token(image_tokens), by_token(text_tokens))
    block_grads = (by_token(image_block_grad), by_token(text_block_grad))
    weights = (image_weights, text_weights)
    ends = (image_ends, text_ends)
    kinds = ((0, IMAGE, "image"), (1, TEXT, "text"))
    fronts = fronts_call(ends, tokens, block_grads, weights)
    units = [f[8] for f in fronts]
    both = jnp.concatenate(units, axis=1)
    own = lax.all_to_all(
        jnp.broadcast_to(both[None], (DEVS, *both.shape)), "dp", 0, 0, tiled=True
    ).reshape(DEVS * BATCH, 2 * EMBED)

    def swap(*arrays):
        return [lax.ppermute(array, "tower", SWAP) for array in arrays]

    def middle_of(i, after):
        _, t, name = kinds[i]
        w = weights[i]
        return middle(
            t, name, place, ends[i], fronts[i][3], block_grads[i], w[4], w[5], w[6], w[7], after
        )

    image_middle = middle_of(0, ())
    (other,) = swap(own)

    pair_held = [own, other, *units]
    pair_lazies = []
    pair_out = [plain((1, 128), F32), plain((1, 128), F32)]
    for i, t, _ in kinds:
        f, w = fronts[i], weights[i]
        pair_held += [f[7], f[6], f[4], f[5], f[9], w[8], w[9], w[4], w[5]]
        pair_out += [plain((1, t.width), F32)] * 4 + [
            plain((BATCH, t.width), F32),
            plain((BATCH, EMBED), F32),
            plain((BATCH, t.width), F32),
            plain((BATCH, t.hidden), F32),
            plain((BATCH, t.width), F32),
        ]
    pair_out.append(plain((BATCH, ROW_TOTAL), F32))
    for i in (1, 0):
        w = weights[i]
        pair_lazies += [all_of(w[10]), all_of(w[7]), all_of(w[6])]
    paired = lazy_call(
        pair_kernel,
        "pairs",
        (place, log_scale),
        pair_held,
        pair_lazies,
        pair_out,
        after=(image_middle[0],),
        ahead=6,
    )
    loss, scale_grad = paired[0][0, :1], paired[1][0, :1]
    heads = (paired[2:11], paired[11:20])
    (rows_other,) = swap(paired[20])

    def feed_of(i, m, buffer, after):
        _, t, name = kinds[i]
        h = heads[i]
        sent = swap(m[0], m[1], m[3], m[5])
        mine = (m[0], m[1], m[2], m[4])
        return feed(t, name, place, (h[7], h[6]), rows_other, mine, sent, buffer, after)

    image_feed = feed_of(0, image_middle, False, ())
    feed_total = lax.all_to_all(image_feed, "dp", 0, 0, tiled=True)
    text_middle = middle_of(1, (image_feed,))
    middles = (image_middle, text_middle)

    backs = []
    for i, t, name in kinds:
        f, m, h, w = fronts[i], middles[i], heads[i], weights[i]
        last = backs[-1][0] if backs else text_middle[0]
        backs.append(
            back(t, name, place, ends[i], h[8], tokens[i], w[0], w[3], m[6], f[1], f[2], w[2], (last,))
        )
    late = feed_of(1, text_middle, True, (backs[1][0],))
    sides = []
    for f, k in zip(fronts, backs):
        sides.append(((f[0], k[0]), swap(f[0], k[1])))
    vectors = []
    for m, h, k in zip(middles, heads, backs):
        vectors += [k[3], k[4], m[7], h[2], m[8], h[3], h[0], h[1]]
    factors = [heads[0][4], heads[0][5], heads[1][4], heads[1][5], rows_other]
    late = behind(rest(place, factors, vectors, sides, late), (feed_total,))
    late_total = lax.all_to_all(late, "dp", 0, 0, tiled=True)
    mine = [
        sum_blocks(feed_total, 9).reshape(-1, 128),
        sum_blocks(late_total, 5).reshape(-1, 128),
    ]
    theirs = [lax.ppermute(m, "tower", SWAP) for m in mine]
    weight_outs = (
        ((12, 2304), F32),
        ((12, 768), F32),
        ((12, 3072), F32),
        ((48, 768), F32),
        ((12, 512), F32),
        ((8, 1536), F32),
        ((8, 512), F32),
        ((8, 2048), F32),
        ((32, 512), F32),
        ((8, 512), F32),
    )
    vector_outs = (((1, 12), F32),) * 6 + (((1, 8), F32),) * 6
    grads = call(unpack_kernel, "unpack", (place,), (*mine, *theirs), weight_outs + vector_outs)

    def ordered(vectors, weights):
        joint, output, widen, narrow, projection = weights
        v = [x.reshape(-1) for x in vectors]
        return [v[0], v[1], joint, output, v[2], v[3], widen, narrow, v[4], v[5], projection]

    def by_sequence(t, grad):
        return grad.reshape(t.length, BATCH, t.width).transpose(1, 0, 2)

    return (
        loss,
        units[0],
        units[1],
        by_sequence(IMAGE, backs[0][2]),
        *ordered(grads[10:16], grads[:5]),
        by_sequence(TEXT, backs[1][2]),
        *ordered(grads[16:22], grads[5:10]),
        scale_grad,
    )


def solution(mesh):
    spread = P(("tower", "dp"), None, None)
    weights = [P()] * 11
    placed = (spread, *weights, spread, spread, P(("tower", "dp")), *weights, spread, P())
    vector, matrix = P("dp"), P("dp", None)
    grads = [vector, vector, matrix, matrix, vector, vector, matrix, matrix, vector, vector, matrix]
    units = P(("tower", "dp"), None)
    return jax.shard_map(
        shards,
        mesh=mesh,
        in_specs=placed,
        out_specs=(P(), units, units, spread, *grads, spread, *grads, P()),
        check_vma=False,
    )
```

```python
import functools

import jax
import jax.numpy as jnp
from jax import lax
from jax.experimental import pallas as pl
from jax.experimental.pallas import tpu as pltpu
from jax.sharding import PartitionSpec as P

F32 = jnp.float32
BF16 = jnp.bfloat16
BATCH = 8
EMBED = 512
TILE = 256
DEVS = 64


class Tower:
    def __init__(self, width, heads, hidden, length, padded, rows, extra, causal):
        self.width = width
        self.heads = heads
        self.hidden = hidden
        self.length = length
        self.padded = padded
        self.real = BATCH * length
        self.rows = rows
        self.extra = extra
        self.spread = BATCH * padded
        self.lanes = -(-rows // 128) * 128
        self.causal = causal
        self.step = 768 if width == 768 else 512


IMAGE = Tower(768, 12, 3072, 50, 64, 416, 400, False)
TEXT = Tower(512, 8, 2048, 77, 80, 640, 624, True)

VMEM_LIMIT = 64 * 1024 * 1024


def mm(left, right):
    return lax.dot_general(left, right, (((1,), (0,)), ((), ())), preferred_element_type=F32)


def mm_nt(left, right):
    return lax.dot_general(left, right, (((1,), (1,)), ((), ())), preferred_element_type=F32)


def mm_tn(left, right):
    return lax.dot_general(left, right, (((0,), (0,)), ((), ())), preferred_element_type=F32)


def normalise(values):
    centre = jnp.mean(values, axis=-1, keepdims=True)
    offset = values - centre
    inverse = lax.rsqrt(jnp.mean(offset * offset, axis=-1, keepdims=True) + 1e-05)
    return offset * inverse, inverse


def norm_back(upstream, gain, normal, inverse):
    scaled = upstream * gain
    inner = (
        scaled
        - jnp.mean(scaled, axis=-1, keepdims=True)
        - normal * jnp.mean(scaled * normal, axis=-1, keepdims=True)
    )
    return inner * inverse


def column_sum(values):
    return jnp.sum(values, axis=0, keepdims=True)


def sigmoid(values):
    return 0.5 + 0.5 * jnp.tanh(0.5 * values)


def vec(ref):
    return ref[...].reshape(1, -1)


def chunks(count, size=128):
    return [(at, min(size, count - at)) for at in range(0, count, size)]


UNROLL_TILE, UNROLL_HEADS, UNROLL_PACK, UNROLL_TURN = 9, 4, 4, 3


def loop(count, body, unroll=1):
    def step(i, carry):
        body(i)
        return carry

    lax.fori_loop(0, count, step, 0, unroll=min(unroll, count))


def tile_loop(width, body):
    loop(width // TILE, lambda n: body(n, pl.ds(pl.multiple_of(n * TILE, TILE), TILE)), UNROLL_TILE)


def put_tiles(ref, n, rows, values):
    for i in range(TILE // 128):
        ref[n * (TILE // 128) + i, 0:rows, :] = values[:, 128 * i : 128 * i + 128]


class Lazy:
    def __init__(self, queue, source, target, sem):
        self.copy = pltpu.make_async_copy(source, target, sem)
        self.target = target
        self.queue = queue
        self.started = self.waited = False

    def start(self):
        if not self.started:
            self.copy.start()
            self.started = True

    def get(self):
        if not self.waited:
            self.start()
            self.copy.wait()
            self.waited = True
            for item in self.queue:
                if not item.started:
                    item.start()
                    break
        return self.target


class Staged:
    def __init__(self, out, stage, sems, pending):
        self.out = out
        self.ref = stage
        self.sems = sems
        self.pending = pending

    def send(self, source, target):
        copy = pltpu.make_async_copy(source, target, self.sems.at[len(self.pending)])
        copy.start()
        self.pending.append(copy)

    def done(self):
        self.send(self.ref, self.out)

    def units_done(self, devices, units, out_units):
        self.send(self.ref.at[devices, units], self.out.at[devices, out_units])


def head_masks():
    lane = lax.broadcasted_iota(jnp.int32, (1, 128), 1)
    first = jnp.where(lane < 64, 1.0, 0.0).astype(BF16)
    second = jnp.where(lane < 64, 0.0, 1.0).astype(BF16)
    return first, second


def two_heads(values, masks):
    return jnp.concatenate([values * masks[0], values * masks[1]], axis=0)


def own_head(values, padded):
    lane = lax.broadcasted_iota(jnp.int32, (padded, 128), 1)
    return jnp.where(lane < 64, values[:padded], values[padded:])


def pooled_row(t, lengths, b):
    return b if t is IMAGE else (lengths[b] - 1) * BATCH + b


def front_kernel(
    t,
    lengths,
    tokens,
    first_gain,
    first_shift,
    joint_weight,
    output_weight,
    second_gain,
    second_shift,
    widen_weight,
    narrow_weight,
    final_gain,
    final_shift,
    projection,
    block_grad,
    turned,
    joint,
    probs,
    mixed,
    mixed_row,
    wide_row,
    pooled,
    raw_out,
    unit,
    grad_row,
    joint_wide,
    context_wide,
    normed_one,
    context,
):
    width, padded, rows = t.width, t.padded, t.rows
    staged = (turned, joint, probs, mixed)
    turned, joint, probs, mixed = [out.ref for out in staged]
    for at, size in chunks(t.real):
        mixed[at : at + size, :] = block_grad[at : at + size, :].astype(F32)
    for b in range(BATCH):
        grad_row[b : b + 1, :] = mixed[pl.ds(pooled_row(t, lengths, b), 1), :]
    pad = t.real - t.real % 16
    normed_one[pad:rows, :] = jnp.zeros((rows - pad, width), BF16)
    for at, size in chunks(t.real):
        normal, _ = normalise(tokens[at : at + size, :].astype(F32))
        normed_one[at : at + size, :] = (normal * vec(first_gain) + vec(first_shift)).astype(BF16)
    if t.spread > rows:
        fill = (3 * width // 128, t.spread - rows, 128)
        joint_wide[:, rows : t.spread, :] = jnp.zeros(fill, F32)

    joint_weight = joint_weight.get()

    def joint_step(n, cols):
        put_tiles(joint_wide, n, rows, mm(normed_one[...], joint_weight[:, cols]))

    tile_loop(3 * width, joint_step)

    masks = head_masks()
    key_at = lax.broadcasted_iota(jnp.int32, (padded, 2 * padded), 0)
    query_at = lax.broadcasted_iota(jnp.int32, (padded, 2 * padded), 1)
    query_at = jnp.where(query_at < padded, query_at, query_at - padded)
    valid = key_at <= query_at if t.causal else key_at < t.length
    pairs = range(t.heads // 2)

    def attend(b):
        some = pl.ds(b, padded, stride=BATCH)
        for c in range(3 * width // 128):
            joint[b, :, 128 * c : 128 * c + 128] = joint_wide[c, some, :].astype(BF16)
        scores = []
        for p in pairs:
            at = 128 * p
            queries = joint[b, :, at : at + 128]
            keys = joint[b, :, width + at : width + at + 128]
            scores.append(mm_nt(keys, two_heads(queries, masks)) * 0.125)
        lows = []
        for p in pairs:
            score = jnp.where(valid, scores[p], -1e30)
            raised = jnp.exp(score - jnp.max(score, axis=0, keepdims=True))
            low = (raised * (1.0 / column_sum(raised))).astype(BF16)
            probs[b, p] = low
            lows.append(low)
        for p in pairs:
            at = 2 * width + 128 * p
            both = mm_tn(lows[p], joint[b, :, at : at + 128])
            context_wide[p, some, :] = own_head(both, padded)

    loop(BATCH, attend, UNROLL_HEADS)
    staged[1].done()
    staged[2].done()
    for p in pairs:
        context[:, 128 * p : 128 * p + 128] = context_wide[p, 0:rows, :].astype(BF16)
    turn(normed_one, turned.at[0:width])
    turn(context, turned.at[width : 2 * width])
    staged[0].done()
    output_weight = output_weight.get()

    def mix_step(n, cols):
        mixed[:, cols] = mm(context[...], output_weight[:, cols])

    tile_loop(width, mix_step)
    for at, size in chunks(t.real):
        mixed[at : at + size, :] += tokens[at : at + size, :].astype(F32)
    for b in range(BATCH):
        mixed_row[b : b + 1, :] = mixed[pl.ds(pooled_row(t, lengths, b), 1), :]
    row = mixed_row[...]
    mixed[t.real : rows, :] = jnp.zeros((rows - t.real, width), F32)
    mixed[t.extra : t.extra + BATCH, :] = row
    staged[3].done()

    normal, _ = normalise(row)
    normed = (normal * vec(second_gain) + vec(second_shift)).astype(BF16)
    wide = mm(normed, widen_weight.get()[...])
    wide_row[...] = wide
    active = (wide * sigmoid(1.702 * wide)).astype(BF16)
    last = row + mm(active, narrow_weight.get()[...])
    pooled[...] = last
    normal, _ = normalise(last)
    normed = (normal * vec(final_gain) + vec(final_shift)).astype(BF16)
    raw = mm(normed, projection.get()[...])
    raw_out[...] = raw
    factor = lax.rsqrt(jnp.sum(raw * raw, axis=-1, keepdims=True) + 1e-06)
    unit[...] = (raw * factor).astype(BF16)


def fronts_kernel(scalars, held, lazies, outs, scratch):
    order = [5, 6, 0, 7, 8, 9, 1, 2, 3, 4]
    weights = [lazies[order.index(i)] for i in range(10)]
    for i in (1, 0):
        t = (IMAGE, TEXT)[i]
        tokens, g1, s1, g2, s2, gf, sf, block_grad = held[8 * i : 8 * i + 8]
        joint, output, widen, narrow, projection = weights[5 * i : 5 * i + 5]
        params = (g1, s1, joint, output, g2, s2, widen, narrow, gf, sf, projection, block_grad)
        front_kernel(
            t, scalars[0], tokens, *params, *outs[10 * i : 10 * i + 10], *scratch[4 * i : 4 * i + 4]
        )
    for i in range(2):
        unit = outs[10 * i + 8][...]
        outs[20][:, :, EMBED * i : EMBED * i + EMBED] = jnp.broadcast_to(unit[None], (DEVS, *unit.shape))


def middle_kernel(
    t,
    place,
    lengths,
    mixed,
    block_grad,
    second_gain,
    second_shift,
    widen_weight,
    narrow_weight,
    normed_turned,
    active_turned,
    wide_own,
    wide_send,
    narrow_own,
    narrow_send,
    mixed_grad,
    gain_grad,
    shift_grad,
    normed_two,
    narrow_in,
    wide_in,
):
    step = pl.program_id(0)
    half_steps = pl.num_programs(0) // 2

    @pl.when(step == 0)
    def _():
        wide_in[t.real : t.rows, :] = jnp.zeros((t.rows - t.real, t.width), F32)
        for at, size in chunks(t.rows):
            normal, _ = normalise(mixed[at : at + size, :])
            normed_two[at : at + size, :] = (normal * vec(second_gain) + vec(second_shift)).astype(
                BF16
            )
        turn(normed_two, normed_turned)
        for at, size in chunks(t.real):
            wide_in[at : at + size, :] = block_grad[at : at + size, :].astype(F32)
        for b in range(BATCH):
            wide_in[pl.ds(pooled_row(t, lengths, b), 1), :] = jnp.zeros((1, t.width), F32)
        narrow_in[...] = wide_in[...].astype(BF16)
        cols = t.width // 2
        own = pl.multiple_of(place[0] * cols, 128)
        narrow_own[...] = narrow_in[:, pl.ds(own, cols)]
        narrow_send[...] = narrow_in[:, pl.ds(pl.multiple_of(cols - own, 128), cols)]
        mixed_grad[...] = jnp.zeros_like(mixed_grad)

    lows = []
    for at, size in chunks(t.step, TILE):
        some = slice(at, at + size)
        wide = mm(normed_two[...], widen_weight[:, some])
        back = mm_nt(narrow_in[...], narrow_weight[some, :])
        sig = sigmoid(1.702 * wide)
        active = wide * sig
        active_turned[some, 0 : t.rows] = active.astype(BF16).T
        slope = sig + 1.702 * active * (1.0 - sig)
        lows.append((back * slope).astype(BF16))
    low = jnp.concatenate(lows, axis=1)
    mixed_grad[...] += mm_nt(low, widen_weight[...])

    @pl.when(step < half_steps)
    def _():
        wide_own[...] = low

    @pl.when(step >= half_steps)
    def _():
        wide_send[...] = low

    @pl.when(step == pl.num_programs(0) - 1)
    def _():
        gain = shift = 0.0
        for at, size in chunks(t.rows):
            some = slice(at, at + size)
            normal, inverse = normalise(mixed[some, :])
            up = mixed_grad[some, :]
            gain += column_sum(up * normal)
            shift += column_sum(up)
            mixed_grad[some, :] = wide_in[some, :] + norm_back(
                up, vec(second_gain), normal, inverse
            )
        gain_grad[...] = gain
        shift_grad[...] = shift


def split_dot(weights, right):
    high = weights.astype(BF16)
    rest = weights - high.astype(F32)
    middle = rest.astype(BF16)
    low = (rest - middle.astype(F32)).astype(BF16)
    return mm(high, right) + mm(middle, right) + mm(low, right)


def row_sizes(t):
    return t.hidden // 2, t.width // 2, EMBED // 2


def row_at(t, part):
    before = 0 if t is IMAGE else sum(row_sizes(IMAGE)) + IMAGE.width
    return before + sum(row_sizes(t)[:part])


ROW_TOTAL = sum(row_sizes(IMAGE)) + IMAGE.width + sum(row_sizes(TEXT)) + TEXT.width


def head_back(
    unit_grad,
    raw,
    pooled,
    mixed_row,
    wide_row,
    grad_row,
    final_gain,
    final_shift,
    second_gain,
    second_shift,
    projection,
    widen_weight,
    narrow_weight,
    outs,
):
    (
        final_gain_grad,
        final_shift_grad,
        second_gain_grad,
        second_shift_grad,
        final_out,
        raw_grad_out,
        narrow_in_row,
        wide_grad_row,
        mixed_grad_row,
    ) = outs
    factor = lax.rsqrt(jnp.sum(raw * raw, axis=-1, keepdims=True) + 1e-06)
    raw_grad = factor * unit_grad - raw * (factor * factor * factor) * jnp.sum(
        unit_grad * raw, axis=-1, keepdims=True
    )
    raw_grad = raw_grad.astype(BF16)
    raw_grad_out[...] = raw_grad.astype(F32)
    normal, inverse = normalise(pooled)
    final_out[...] = (normal * final_gain + final_shift).astype(BF16).astype(F32)
    up = mm_nt(raw_grad, projection.get()[...])
    final_gain_grad[...] = column_sum(up * normal)
    final_shift_grad[...] = column_sum(up)
    out_grad = grad_row + norm_back(up, final_gain, normal, inverse)
    narrow_in = out_grad.astype(BF16)
    narrow_in_row[...] = narrow_in.astype(F32)
    sig = sigmoid(1.702 * wide_row)
    slope = sig + 1.702 * wide_row * sig * (1.0 - sig)
    low = (mm_nt(narrow_in, narrow_weight.get()[...]) * slope).astype(BF16)
    wide_grad_row[...] = low.astype(F32)
    up = mm_nt(low, widen_weight.get()[...])
    normal, inverse = normalise(mixed_row)
    second_gain_grad[...] = column_sum(up * normal)
    second_shift_grad[...] = column_sum(up)
    mixed_grad_row[...] = out_grad + norm_back(up, second_gain, normal, inverse)


def pair_kernel(scalars, held, lazies, outs, scratch):
    place, log_scale = scalars
    own, other, image_unit, text_unit = held[:4]
    image_in, text_in = held[4:13], held[13:22]
    loss, scale_grad = outs[:2]
    image_outs, text_outs, row_send = outs[2:11], outs[11:20], outs[20]
    half = own.shape[0]
    pairs = 2 * half
    scale = jnp.exp(jnp.full((1, 1), log_scale[0], F32))
    blocks = (own, other)

    def totals(left_at, right_at):
        sums, moments = [], []
        for right in blocks:
            column, moment = None, None
            for left in blocks:
                for piece in range(0, half, 256):
                    sims = scale * mm_nt(
                        left[piece : piece + 256, left_at : left_at + EMBED],
                        right[:, right_at : right_at + EMBED],
                    )
                    raised = jnp.exp(sims)
                    add, more = column_sum(raised), column_sum(raised * sims)
                    column = add if column is None else column + add
                    moment = more if moment is None else moment + more
            sums.append(column)
            moments.append(moment)
        return sums, moments

    column_sums, column_moments = totals(0, EMBED)
    row_sums, row_moments = totals(EMBED, 0)
    log_total = jnp.zeros((1, 1), F32)
    weighted = jnp.zeros((1, 1), F32)
    trace = jnp.zeros((1, 1), F32)
    for i in range(2):
        for total, moment in ((column_sums[i], column_moments[i]), (row_sums[i], row_moments[i])):
            log_total += jnp.sum(jnp.log(total), axis=-1, keepdims=True)
            weighted += jnp.sum(moment / total, axis=-1, keepdims=True)
        product = blocks[i][:, :EMBED].astype(F32) * blocks[i][:, EMBED:].astype(F32)
        trace += jnp.sum(column_sum(product), axis=-1, keepdims=True)
    trace = scale * trace
    loss[...] = jnp.broadcast_to((log_total - 2.0 * trace) / (2.0 * pairs), loss.shape)
    scale_grad[...] = jnp.broadcast_to((weighted - 2.0 * trace) / (2.0 * pairs), loss.shape)

    lane = lax.broadcasted_iota(jnp.int32, (BATCH, half), 1)
    sub = lax.broadcasted_iota(jnp.int32, (BATCH, half), 0)
    identity = jnp.where(lane == sub + place[1] * BATCH, 2.0, 0.0)

    def grads(unit, at, other_sums):
        raised = [jnp.exp(scale * mm_nt(unit[...], block[:, at : at + EMBED])) for block in blocks]
        own_sum = sum(jnp.sum(r, axis=-1, keepdims=True) for r in raised)
        result = None
        for i in range(2):
            weight = raised[i] * (1.0 / own_sum + 1.0 / other_sums[i])
            if i == 0:
                weight = weight - identity
            weight = weight / (2.0 * pairs)
            part = split_dot(weight, blocks[i][:, at : at + EMBED])
            result = part if result is None else result + part
        return scale * result

    image_grad = grads(image_unit, EMBED, column_sums)
    text_grad = grads(text_unit, 0, row_sums)
    for unit_grad, ins, weights, results in (
        (text_grad, text_in, lazies[0:3], text_outs),
        (image_grad, image_in, lazies[3:6], image_outs),
    ):
        values = [ref[...] for ref in ins[:5]] + [vec(ref) for ref in ins[5:9]]
        projection, narrow, widen = weights
        head_back(unit_grad, *values, projection, widen, narrow, results)
    at = 0
    for t, results in ((IMAGE, image_outs), (TEXT, text_outs)):
        for ref, size in zip((results[7], results[6], results[5]), row_sizes(t)):
            start = pl.multiple_of((1 - place[0]) * size, 128)
            row_send[:, at : at + size] = ref[:, pl.ds(start, size)]
            at += size
        row_send[:, at : at + t.width] = results[4][...]
        at += t.width


def back_kernel(t, scalars, held, lazies, outs, scratch):
    place, lengths = scalars
    tokens, first_gain, mixed_grad_row = held
    output_weight, mixed_grad, joint, probs, joint_weight = lazies
    own, send, tokens_out, gain_grad, shift_grad = outs
    context_grad, joint_grad, normed_grad, grads = scratch
    width, padded, rows = t.width, t.padded, t.rows
    tokens_grad = tokens_out.ref
    grad = mixed_grad.get()
    for b in range(BATCH):
        grad[pl.ds(pooled_row(t, lengths, b), 1), :] = mixed_grad_row[b : b + 1, :]
    mixed_low = slice(3 * width, 4 * width)
    grads[:, mixed_low] = grad[...].astype(BF16)
    if t.spread > rows:
        fill = (width // 128, t.spread - rows, 128)
        context_grad[:, rows : t.spread, :] = jnp.zeros(fill, F32)
    output_weight = output_weight.get()

    def context_step(n, cols):
        put_tiles(context_grad, n, rows, mm_nt(grads[:, mixed_low], output_weight[cols, :]))

    tile_loop(width, context_step)
    masks = head_masks()
    pairs = range(t.heads // 2)
    joint, probs = joint.get(), probs.get()

    def attend(b):
        some = pl.ds(b, padded, stride=BATCH)
        ups = [two_heads(context_grad[p, some, :].astype(BF16), masks) for p in pairs]
        backs = []
        for p in pairs:
            at = 2 * width + 128 * p
            backs.append(mm_nt(joint[b, :, at : at + 128], ups[p]))
        lows = []
        for p in pairs:
            wide = probs[b, p].astype(F32)
            back = wide * (backs[p] - column_sum(backs[p] * wide))
            lows.append(back.astype(BF16))
        for p in pairs:
            at = 128 * p
            queries = joint[b, :, at : at + 128]
            keys = joint[b, :, width + at : width + at + 128]
            joint_grad[2 * len(pairs) + p, some, :] = mm(probs[b, p], ups[p])
            joint_grad[len(pairs) + p, some, :] = mm(lows[p], two_heads(queries, masks)) * 0.125
            joint_grad[p, some, :] = own_head(mm_tn(lows[p], keys), padded) * 0.125

    loop(BATCH, attend, UNROLL_HEADS)
    for c in range(3 * width // 128):
        grads[:, 128 * c : 128 * c + 128] = joint_grad[c, 0:rows, :].astype(BF16)
    start = pl.multiple_of(place[0] * (2 * width), 128)
    own.send(grads.at[:, pl.ds(start, 2 * width)], own.out)
    start = pl.multiple_of(2 * width - start, 128)
    send.send(grads.at[:, pl.ds(start, 2 * width)], send.out)
    joint_weight = joint_weight.get()

    def normed_step(n, cols):
        normed_grad[:, cols] = mm_nt(grads[:, 0 : 3 * width], joint_weight[cols, :])

    tile_loop(width, normed_step)
    gain = shift = 0.0
    for at, size in chunks(t.real):
        some = slice(at, at + size)
        normal, inverse = normalise(tokens[some, :].astype(F32))
        up = normed_grad[some, :]
        gain += column_sum(up * normal)
        shift += column_sum(up)
        tokens_grad[some, :] = grad[some, :] + norm_back(up, vec(first_gain), normal, inverse)
    gain_grad[...] = gain
    shift_grad[...] = shift
    tokens_out.done()

def turn(source, target):
    def step(n):
        cols = pl.ds(pl.multiple_of(n * 128, 128), 128)
        target[cols, 0 : source.shape[0]] = source[:, cols].T

    loop(source.shape[1] // 128, step, UNROLL_TURN)


def lanes_down(values):
    return jnp.concatenate(
        [values[:, :, at : at + 128] for at in range(0, values.shape[2], 128)], axis=1
    )


def put(out, device, unit, values):
    count = values.shape[1] // 16
    size = values.shape[0]
    values = values.reshape(size, count, 16, 128).astype(BF16)
    out[pl.ds(device, size), unit : unit + count] = values


def pack_twelve(first, second, out, unit=0, each=4):
    cols = first.shape[1]
    count = cols // 128
    sub = lax.broadcasted_iota(jnp.int32, (each, 8, cols), 1) < 4

    def step(e):
        rows = pl.ds(pl.multiple_of(e * (24 * each), 8), 24 * each)
        x = first[rows, :].reshape(each, 24, cols)
        y = second[rows, :].reshape(each, 24, cols)
        left, right = x[:, 8:16], y[:, 8:16]
        even = jnp.where(sub, left, pltpu.roll(right, 4, 1))
        odd = jnp.where(sub, pltpu.roll(left, 4, 1), right)
        parts = []
        for a, b, c in ((x[:, 0:8], y[:, 0:8], even), (x[:, 16:24], y[:, 16:24], odd)):
            parts.append(jnp.concatenate([lanes_down(v) for v in (a, b, c)], axis=1))
        if parts[0].shape[1] % 16:
            fill = jnp.zeros((each, 16 - parts[0].shape[1] % 16, 128), F32)
            parts = [jnp.concatenate([part, fill], axis=1) for part in parts]
        height = parts[0].shape[1]
        values = jnp.stack(parts, axis=1).reshape(2 * each, height, 128)
        put(out, e * (2 * each), unit, values)

    loop(32 // each, step, UNROLL_PACK)


def pack_rows(result, rows, out, unit=0, each=8, device=0):
    total = result.shape[0] // rows
    cols = result.shape[1]

    def step(e):
        some = pl.ds(pl.multiple_of(e * (rows * each), 8), rows * each)
        values = lanes_down(result[some, :].reshape(each, rows, cols))
        put(out, device + e * each, unit, values)

    loop(total // each, step, UNROLL_PACK)


def put_extra(t, ref, rows):
    rows = jnp.concatenate([rows, jnp.zeros_like(rows)], axis=0)
    ref[t.extra : t.extra + 16, :] = rows.astype(BF16)


def wide_grads(t, half, product, send, at, first, second):
    if t is IMAGE:
        for i in range(3):
            first[...] = product(256 * i, 256)
            second[...] = product(768 + 256 * i, 256)
            pack_twelve(first, second, send.ref, 3 * i)
            units = slice(3 * i, 3 * i + 3)
            send.units_done(slice(None), units, slice(at + 3 * i, at + 3 * i + 3))
    else:
        for i in range(2):
            first[...] = product(512 * i, 512)
            pack_rows(first, 8, send.ref, 2 * i)
            units = slice(2 * i, 2 * i + 2)
            send.units_done(slice(None), units, slice(at + 2 * i, at + 2 * i + 2))


def feed_kernel(t, at, scalars, held, lazies, outs, scratch):
    (place,) = scalars
    rows = lazies[0:4]
    normed, wides, narrows = lazies[4:6], lazies[6:8], lazies[8:10]
    actives = lazies[10:18]
    (out,) = outs
    first, second, narrow_result = scratch
    wide_rows, narrow_rows = rows[0:2], rows[2:4]
    for row, ref in zip(wide_rows, wides):
        put_extra(t, ref.get(), row.get()[...])
    lefts = [ref.get() for ref in normed]
    wides = [ref.get() for ref in wides]

    def product(tile, size):
        return sum(mm(a[:, 0 : t.rows], b[:, tile : tile + size]) for a, b in zip(lefts, wides))

    wide_grads(t, place[0], product, out, at, first, second)
    for row, ref in zip(narrow_rows, narrows):
        put_extra(t, ref.get(), row.get()[...])
    narrows = [ref.get() for ref in narrows]
    wide_units, units = (9, 9) if t is IMAGE else (4, 4)
    some = slice(wide_units, wide_units + units)
    for j in range(4):
        pair = [actives[2 * j].get(), actives[2 * j + 1].get()]
        narrow_result[...] = sum(mm(a[:, 0 : t.rows], b[...]) for a, b in zip(pair, narrows))
        pack_rows(narrow_result, t.hidden // DEVS, out.ref, wide_units, 4, 16 * j)
        out.units_done(
            slice(16 * j, 16 * j + 16), some, slice(at + wide_units, at + wide_units + units)
        )


def rest_kernel(scalars, held, lazies, outs, scratch):
    (place,) = scalars
    (out,) = outs
    first, second, third = scratch[:3]
    misc_scratch, spread = scratch[3:6], scratch[6]
    half = place[0]
    misc, text_stage, image_stage = [Staged(out.out, ref, out.sems, out.pending) for ref in scratch[7:10]]
    misc_grads(half, held[:5], held[5:], misc, misc_scratch, spread)
    for t, ins, stage, results in (
        (TEXT, lazies[0:4], text_stage, (third, None)),
        (IMAGE, lazies[4:8], image_stage, (first, second)),
    ):
        width = t.width
        lefts, rights = [ref.get() for ref in ins[0::2]], [ref.get() for ref in ins[1::2]]

        def product(tile, size):
            late = jnp.where(half * (2 * width) + tile >= 3 * width, width, 0)
            rows = pl.ds(pl.multiple_of(late, 128), width)
            return sum(
                mm(a[rows, 0 : t.rows], b[:, tile : tile + size]) for a, b in zip(lefts, rights)
            )

        wide_grads(t, half, product, stage, REST_AT["image" if t is IMAGE else "text"], *results)


IMAGE_FEED_UNITS = 18
LATE_UNITS = 25
TEXT_FEED_AT = 0
REST_AT = {"text": 8, "image": 16}
MISC_AT = 12


def misc_grads(half, factors, vectors, out, scratch, spread):
    image_final, image_raw, text_final, text_raw, received = factors
    first, second, third = scratch

    def both(mine, at, size, start=0):
        mine = mine[:, pl.ds(start, size)]
        return jnp.concatenate([mine, received[:, at : at + size]], axis=0).astype(BF16)

    def raw_columns(t, ref, at, size):
        start = pl.multiple_of(half * 256 + at, 128)
        return both(ref, row_at(t, 2) + at, size, start)

    final = both(image_final, row_at(IMAGE, 3), IMAGE.width)
    first[...] = mm_tn(final, raw_columns(IMAGE, image_raw, 0, 128))
    second[...] = mm_tn(final, raw_columns(IMAGE, image_raw, 128, 128))
    final = both(text_final, row_at(TEXT, 3), TEXT.width)
    third[...] = mm_tn(final, raw_columns(TEXT, text_raw, 0, 256))
    pack_twelve(first, second, out.ref, 2, 8)
    pack_rows(third, 8, out.ref, 0)
    spread[...] = jnp.zeros_like(spread)
    for tower, refs_of, width in ((0, vectors[:8], 768), (1, vectors[8:], 512)):
        each = width // DEVS
        device = lax.broadcasted_iota(jnp.int32, (DEVS, width), 0)
        column = lax.broadcasted_iota(jnp.int32, (DEVS, width), 1)
        mine = jnp.logical_and(column >= device * each, column < device * each + each)
        source = lax.broadcasted_iota(jnp.int32, (width, 128), 0)
        lane = lax.broadcasted_iota(jnp.int32, (width, 128), 1)
        at = lax.rem(source, each)
        high_at = jnp.where(lane == at, 1.0, 0.0).astype(BF16)
        low_at = jnp.where(lane == at + 64, 1.0, 0.0).astype(BF16)
        rows = [refs_of[0][...], refs_of[1][...], refs_of[2][...] + refs_of[3][...]]
        rows += [refs_of[4][...] + refs_of[5][...], refs_of[6][...], refs_of[7][...]]
        for k, row in enumerate(rows):
            row = jnp.where(mine, row, 0.0)
            high = row.astype(BF16)
            low = (row - high.astype(F32)).astype(BF16)
            spread[:, 6 * tower + k, :] = mm(high, high_at) + mm(low, low_at)
    out.ref[:, 1] = spread[...].astype(BF16)
    out.units_done(slice(None), slice(0, 4), slice(MISC_AT, MISC_AT + 4))


def unpack_kernel(place, feed_mine, late_mine, feed_other, late_other, *outs):
    (
        image_joint,
        image_output,
        image_widen,
        image_narrow,
        image_projection,
        text_joint,
        text_output,
        text_widen,
        text_narrow,
        text_projection,
    ) = outs[:10]
    odd = place[1] % 2

    def emit(half, feed, late):
        def into(ref, col, body, tail):
            @pl.when(odd == 0)
            def _():
                ref[0:8, col : col + 128] = body
                ref[8:12, col : col + 128] = tail

            @pl.when(odd == 1)
            def _():
                ref[0:4, col : col + 128] = tail
                ref[4:12, col : col + 128] = body

        def image_wide(source, at, store):
            for tile in range(3):
                block = source[16 * (at + 3 * tile) : 16 * (at + 3 * tile) + 48, :]
                for side in range(2):
                    for g in range(2):
                        body = block[16 * side + 8 * g : 16 * side + 8 * g + 8]
                        tail = block[32 + 8 * g + 4 * side : 36 + 8 * g + 4 * side]
                        store(half * 1536 + side * 768 + tile * 256 + g * 128, body, tail)

        def joint_store(col, body, tail):
            if col < 2304:
                into(image_joint, col, body, tail)
            else:
                into(image_output, col - 2304, body, tail)

        image_wide(feed, 0, functools.partial(into, image_widen))
        image_wide(late, REST_AT["image"], joint_store)
        at = 16 * 9
        for g in range(3):
            col = half * 384 + 128 * g
            image_narrow[:, col : col + 128] = feed[at + 48 * g : at + 48 * g + 48, :]
        at = 16 * (MISC_AT + 2)
        for side in range(2):
            col = half * 256 + 128 * side
            tail = late[at + 16 + 4 * side : at + 20 + 4 * side, :]
            into(image_projection, col, late[at + 8 * side : at + 8 * side + 8, :], tail)
        for g in range(8):
            col = half * 1024 + 128 * g
            at = 16 * TEXT_FEED_AT + 8 * g
            text_widen[:, col : col + 128] = late[at : at + 8, :]
            at = 16 * REST_AT["text"] + 8 * g
            block = late[at : at + 8, :]
            if col < 1536:
                text_joint[:, col : col + 128] = block
            else:
                text_output[:, col - 1536 : col - 1408] = block
        for g in range(2):
            col = half * 256 + 128 * g
            at = 16 * (TEXT_FEED_AT + 4) + 32 * g
            text_narrow[:, col : col + 128] = late[at : at + 32, :]
            at = 16 * MISC_AT + 8 * g
            text_projection[:, col : col + 128] = late[at : at + 8, :]

    for half in range(2):

        @pl.when(place[0] == half)
        def _():
            emit(half, feed_mine, late_mine)
            emit(1 - half, feed_other, late_other)

    at = 16 * (MISC_AT + 1)
    vectors = late_mine[at : at + 16, :] + late_other[at : at + 16, :]
    for k in range(12):
        each = 12 if k < 6 else 8
        outs[10 + k][...] = vectors[k : k + 1, 0:each] + vectors[k : k + 1, 64 : 64 + each]


SMEM = pl.BlockSpec(memory_space=pltpu.SMEM)
VMEM = pl.BlockSpec(memory_space=pltpu.VMEM)


def call(body, name, scalars, arrays, outs, scratch=(), flops=1 << 32):
    return pl.pallas_call(
        body,
        name=name,
        out_shape=tuple(jax.ShapeDtypeStruct(shape, kind) for shape, kind in outs),
        in_specs=[SMEM] * len(scalars) + [VMEM] * len(arrays),
        out_specs=tuple(VMEM for _ in outs),
        scratch_shapes=[pltpu.VMEM(shape, kind) for shape, kind in scratch],
        compiler_params=pltpu.CompilerParams(vmem_limit_bytes=VMEM_LIMIT),
        cost_estimate=pl.CostEstimate(flops=flops, bytes_accessed=20 << 20, transcendentals=0),
    )(*scalars, *arrays)


BIG = 1 << 18


def lazy_call(body, name, scalars, held, lazies, outs, scratch=(), flops=1 << 33, buffer=None, after=(), ahead=3):
    many = 24

    def kernel(*refs):
        refs = list(refs)

        def take(count):
            got = refs[:count]
            del refs[:count]
            return got

        scalar_refs, held_refs = take(len(scalars)), take(len(held))
        sources = take(len(lazies))
        take(len(after) + (buffer is not None))
        out_refs = take(len(outs))
        targets = take(len(lazies))
        stages = take(sum(1 for out in outs if out[2]))
        scratch_refs = take(len(scratch))
        in_sems, out_sems = refs
        lazy = []
        for i, (source, target, (_, index, _)) in enumerate(zip(sources, targets, lazies)):
            if index is not None:
                source = source.at[index(*scalar_refs)]
            lazy.append(Lazy(lazy, source, target, in_sems.at[i]))
        for item in lazy[:ahead]:
            item.start()
        pending = []
        results = []
        for out, ref in zip(outs, out_refs):
            if out[2] is None:
                results.append(ref)
            else:
                results.append(Staged(ref, stages.pop(0) if out[2] else None, out_sems, pending))
        body(scalar_refs, held_refs, lazy, results, scratch_refs)
        for item in lazy:
            if item.started:
                item.get()
        for copy in pending:
            copy.wait()

    any_spec = pl.BlockSpec(memory_space=pl.ANY)
    scratch_shapes = [pltpu.VMEM(shape, array.dtype) for array, _, shape in lazies]
    scratch_shapes += [pltpu.VMEM(stage, kind) for _, kind, stage in outs if stage]
    scratch_shapes += [pltpu.VMEM(shape, kind) for shape, kind in scratch]
    scratch_shapes += [pltpu.SemaphoreType.DMA((max(1, len(lazies)),)), pltpu.SemaphoreType.DMA((many,))]
    arrays = [*held, *[array for array, _, _ in lazies], *after]
    specs = [SMEM] * len(scalars) + [VMEM] * len(held) + [any_spec] * (len(lazies) + len(after))
    aliases = {}
    if buffer is not None:
        aliases = {len(scalars) + len(arrays): 0}
        arrays.append(buffer)
        specs.append(any_spec)
    return pl.pallas_call(
        kernel,
        name=name,
        out_shape=tuple(jax.ShapeDtypeStruct(shape, kind) for shape, kind, _ in outs),
        in_specs=specs,
        out_specs=tuple(VMEM if stage is None else any_spec for _, _, stage in outs),
        scratch_shapes=scratch_shapes,
        input_output_aliases=aliases,
        compiler_params=pltpu.CompilerParams(vmem_limit_bytes=VMEM_LIMIT),
        cost_estimate=pl.CostEstimate(flops=flops, bytes_accessed=20 << 20, transcendentals=0),
    )(*scalars, *arrays)


def all_of(array):
    return array, None, array.shape


def staged(shape, kind):
    return shape, kind, shape


def plain(shape, kind):
    return shape, kind, None


def fronts_call(lengths, tokens, block_grads, weights):
    held, lazies, outs, scratch = [], [], [], []
    for t, token, grad, w in zip((IMAGE, TEXT), tokens, block_grads, weights):
        rows, width, hidden = t.rows, t.width, t.hidden
        held += [token, w[0], w[1], w[4], w[5], w[8], w[9], grad]
        lazies += [all_of(w[i]) for i in (2, 3, 6, 7, 10)]
        outs += [
            staged((2 * width, t.lanes), BF16),
            staged((BATCH, t.padded, 3 * width), BF16),
            staged((BATCH, t.heads // 2, t.padded, 2 * t.padded), BF16),
            staged((rows, width), F32),
            plain((BATCH, width), F32),
            plain((BATCH, hidden), F32),
            plain((BATCH, width), F32),
            plain((BATCH, EMBED), F32),
            plain((BATCH, EMBED), BF16),
            plain((BATCH, width), F32),
        ]
        scratch += [
            ((3 * width // 128, t.spread, 128), F32),
            ((width // 128, t.spread, 128), F32),
            ((rows, width), BF16),
            ((rows, width), BF16),
        ]
    lazies = [lazies[i] for i in (5, 6, 0, 7, 8, 9, 1, 2, 3, 4)]
    outs.append(plain((DEVS, BATCH, 2 * EMBED), BF16))
    results = lazy_call(fronts_kernel, "fronts", (lengths,), held, lazies, outs, scratch, ahead=6)
    return results[:10], results[10:20], results[20]


def middle(t, name, place, lengths, mixed, block_grad, gain, shift, widen, narrow, after):
    rows, width, hidden = t.rows, t.width, t.hidden
    steps = hidden // t.step
    outs = (
        ((width, t.lanes), BF16),
        ((hidden, t.lanes), BF16),
        ((rows, hidden // 2), BF16),
        ((rows, hidden // 2), BF16),
        ((rows, width // 2), BF16),
        ((rows, width // 2), BF16),
        ((rows, width), F32),
        ((1, width), F32),
        ((1, width), F32),
    )

    def held(shape):
        return pl.BlockSpec(shape, lambda i, *_: (0,) * len(shape))

    def tile(i, place):
        return lax.rem(i + place[0] * (steps // 2), steps)

    out_specs = [held(shape) for shape, _ in outs]
    out_specs[1] = pl.BlockSpec((t.step, t.lanes), lambda i, place, lengths: (tile(i, place), 0))
    out_specs[2] = pl.BlockSpec((rows, t.step), lambda i, *_: (0, jnp.minimum(i, steps // 2 - 1)))
    out_specs[3] = pl.BlockSpec((rows, t.step), lambda i, *_: (0, jnp.maximum(i - steps // 2, 0)))
    in_specs = [held(a.shape) for a in (mixed, block_grad, gain, shift)]
    in_specs.append(pl.BlockSpec((width, t.step), lambda i, place, lengths: (0, tile(i, place))))
    in_specs.append(pl.BlockSpec((t.step, width), lambda i, place, lengths: (tile(i, place), 0)))
    in_specs += [pl.BlockSpec(memory_space=pl.ANY)] * len(after)

    def kernel(*refs):
        middle_kernel(t, *refs[:8], *refs[8 + len(after) :])

    return pl.pallas_call(
        kernel,
        name=name + "_middle",
        out_shape=tuple(jax.ShapeDtypeStruct(shape, kind) for shape, kind in outs),
        grid_spec=pltpu.PrefetchScalarGridSpec(
            num_scalar_prefetch=2,
            grid=(steps,),
            in_specs=in_specs,
            out_specs=tuple(out_specs),
            scratch_shapes=[
                pltpu.VMEM((rows, width), BF16),
                pltpu.VMEM((rows, width), BF16),
                pltpu.VMEM((rows, width), F32),
            ],
        ),
        compiler_params=pltpu.CompilerParams(vmem_limit_bytes=VMEM_LIMIT),
        cost_estimate=pl.CostEstimate(flops=1 << 35, bytes_accessed=20 << 20, transcendentals=0),
    )(place, lengths, mixed, block_grad, gain, shift, widen, narrow, *after)


def back(t, name, place, lengths, row, tokens, gain, output, mixed_grad, joint, probs, joint_weight, after):
    rows, width = t.rows, t.width
    lazies = [all_of(a) for a in (output, mixed_grad, joint, probs, joint_weight)]
    outs = [
        ((rows, 2 * width), BF16, ()),
        ((rows, 2 * width), BF16, ()),
        staged((t.real, width), F32),
        plain((1, width), F32),
        plain((1, width), F32),
    ]
    scratch = [
        ((width // 128, t.spread, 128), F32),
        ((3 * width // 128, t.spread, 128), F32),
        ((rows, width), F32),
        ((rows, 4 * width), BF16),
    ]
    return lazy_call(
        functools.partial(back_kernel, t),
        name + "_back",
        (place, lengths),
        (tokens, gain, row),
        lazies,
        outs,
        scratch,
        after=after,
    )


def feed(t, name, place, rows_own, rows_other, own, other, buffer, after):
    rows, width, hidden = t.rows, t.width, t.hidden
    wide_units, units = (9, 9) if t is IMAGE else (4, 4)
    lazies = []
    for part, size in enumerate((hidden // 2, width // 2)):
        def mine(place, size=size):
            return slice(None), pl.ds(pl.multiple_of(place[0] * size, 128), size)

        def theirs(place, part=part, size=size):
            return slice(None), slice(row_at(t, part), row_at(t, part) + size)

        lazies.append((rows_own[part], mine, (BATCH, size)))
        lazies.append((rows_other, theirs, (BATCH, size)))
    lazies += [all_of(own[0]), all_of(other[0]), all_of(own[2]), all_of(other[2])]
    lazies += [all_of(own[3]), all_of(other[3])]
    for j in range(4):
        some = slice(width * j, width * j + width)
        for side in (own, other):
            lazies.append((side[1], lambda *_, some=some: (some, slice(None)), (width, t.lanes)))
    total = LATE_UNITS if buffer else wide_units + units
    outs = [((DEVS, total, 16, 128), BF16, (DEVS, wide_units + units, 16, 128))]
    cols = 256 if t is IMAGE else 512
    scratch = [
        ((width, cols), F32),
        ((width, cols) if t is IMAGE else (8, 128), F32),
        ((width, width // 2), F32),
    ]
    (out,) = lazy_call(
        functools.partial(feed_kernel, t, TEXT_FEED_AT if buffer else 0),
        name + "_feed",
        (place,),
        (),
        lazies,
        outs,
        scratch,
        after=after,
        ahead=10,
    )
    return out


def rest(place, factors, vectors, sides, buffer):
    lazies = []
    for own, other in (sides[1], sides[0]):
        lazies += [all_of(a) for a in (*own, *other)]
    outs = [((DEVS, LATE_UNITS, 16, 128), BF16, ())]
    scratch = [
        ((768, 256), F32),
        ((768, 256), F32),
        ((512, 512), F32),
        ((768, 128), F32),
        ((768, 128), F32),
        ((512, 256), F32),
        ((DEVS, 16, 128), F32),
        ((DEVS, 4, 16, 128), BF16),
        ((DEVS, 4, 16, 128), BF16),
        ((DEVS, 9, 16, 128), BF16),
    ]
    (out,) = lazy_call(
        rest_kernel, "rest", (place,), [*factors, *vectors], lazies, outs, scratch, buffer=buffer, ahead=4
    )
    return out


def sum_blocks(received, step):
    devices, units = received.shape[:2]

    def body(scalars, held, lazies, outs, scratch):
        for i, block in enumerate(lazies):
            total = jnp.sum(block.get()[...].astype(F32), axis=0)
            outs[0][16 * step * i : 16 * step * (i + 1), :] = total.reshape(16 * step, 128)

    lazies = []
    for at in range(0, units, step):
        some = slice(at, at + step)
        lazies.append((received, lambda *_, some=some: (slice(None), some), (devices, step, 16, 128)))
    outs = [plain((16 * units, 128), F32)]
    return lazy_call(body, "sum_blocks", (), (), lazies, outs, flops=1 << 34, ahead=len(lazies))[0]


def behind(arrays, after):
    def kernel(*refs):
        pass

    any_spec = pl.BlockSpec(memory_space=pl.ANY)
    return pl.pallas_call(
        kernel,
        name="behind",
        out_shape=[jax.ShapeDtypeStruct(array.shape, array.dtype) for array in arrays],
        in_specs=[any_spec] * (len(arrays) + len(after)),
        out_specs=[any_spec] * len(arrays),
        input_output_aliases={i: i for i in range(len(arrays))},
    )(*arrays, *after)


SWAP = [(0, 1), (1, 0)]


def by_token(tokens):
    return tokens.transpose(1, 0, 2).reshape(-1, tokens.shape[2])


def shards(*args):
    image_tokens, image_weights, image_block_grad = args[0], args[1:12], args[12]
    text_tokens, caption_lengths = args[13], args[14]
    text_weights, text_block_grad, log_scale = args[15:26], args[26], args[27]
    core = lax.axis_index("tower")
    dp = lax.axis_index("dp")
    place = jnp.stack([core, dp]).astype(jnp.int32)
    tokens = (by_token(image_tokens), by_token(text_tokens))
    block_grads = (by_token(image_block_grad), by_token(text_block_grad))
    weights = (image_weights, text_weights)
    kinds = ((0, IMAGE, "image"), (1, TEXT, "text"))
    *fronts, copies = fronts_call(caption_lengths, tokens, block_grads, weights)
    units = [f[8] for f in fronts]
    own = lax.all_to_all(copies, "dp", 0, 0, tiled=True).reshape(DEVS * BATCH, 2 * EMBED)

    def swap(*arrays):
        return [lax.ppermute(array, "tower", SWAP) for array in arrays]

    def middle_of(i, after):
        _, t, name = kinds[i]
        w = weights[i]
        return middle(
            t, name, place, caption_lengths, fronts[i][3], block_grads[i], w[4], w[5], w[6], w[7], after
        )

    image_middle = list(middle_of(0, ()))
    (own,) = behind([own], (image_middle[0],))
    (other,) = swap(own)
    sent = (0, 1, 3, 5)
    for k, array in zip(sent, behind([image_middle[k] for k in sent], (other,))):
        image_middle[k] = array

    pair_held = [own, other, *units]
    pair_lazies = []
    pair_out = [plain((1, 128), F32), plain((1, 128), F32)]
    for i, t, _ in kinds:
        f, w = fronts[i], weights[i]
        pair_held += [f[7], f[6], f[4], f[5], f[9], w[8], w[9], w[4], w[5]]
        pair_out += [plain((1, t.width), F32)] * 4 + [
            plain((BATCH, t.width), F32),
            plain((BATCH, EMBED), F32),
            plain((BATCH, t.width), F32),
            plain((BATCH, t.hidden), F32),
            plain((BATCH, t.width), F32),
        ]
    pair_out.append(plain((BATCH, ROW_TOTAL), F32))
    for i in (1, 0):
        w = weights[i]
        pair_lazies += [all_of(w[10]), all_of(w[7]), all_of(w[6])]
    paired = lazy_call(
        pair_kernel,
        "pairs",
        (place, log_scale),
        pair_held,
        pair_lazies,
        pair_out,
        after=(image_middle[0],),
        ahead=6,
    )
    loss, scale_grad = paired[0][0, :1], paired[1][0, :1]
    heads = (paired[2:11], paired[11:20])
    (rows_other,) = swap(paired[20])

    def feed_of(i, m, buffer, after):
        _, t, name = kinds[i]
        h = heads[i]
        sent = swap(m[0], m[1], m[3], m[5])
        mine = (m[0], m[1], m[2], m[4])
        return feed(t, name, place, (h[7], h[6]), rows_other, mine, sent, buffer, after)

    image_feed = feed_of(0, image_middle, False, ())
    feed_total = lax.all_to_all(image_feed, "dp", 0, 0, tiled=True)
    text_middle = middle_of(1, (image_feed,))
    middles = (image_middle, text_middle)

    backs = []
    for i, t, name in kinds:
        f, m, h, w = fronts[i], middles[i], heads[i], weights[i]
        last = backs[-1][0] if backs else text_middle[0]
        backs.append(
            back(t, name, place, caption_lengths, h[8], tokens[i], w[0], w[3], m[6], f[1], f[2], w[2], (last,))
        )
    late = feed_of(1, text_middle, True, (backs[1][0],))
    sides = []
    for f, k in zip(fronts, backs):
        sides.append(((f[0], k[0]), swap(f[0], k[1])))
    vectors = []
    for m, h, k in zip(middles, heads, backs):
        vectors += [k[3], k[4], m[7], h[2], m[8], h[3], h[0], h[1]]
    factors = [heads[0][4], heads[0][5], heads[1][4], heads[1][5], rows_other]
    (late,) = behind([rest(place, factors, vectors, sides, late)], (feed_total,))
    late_total = lax.all_to_all(late, "dp", 0, 0, tiled=True)
    feed_mine = sum_blocks(feed_total, 3)
    (feed_theirs,) = swap(feed_mine)
    (late_total,) = behind([late_total], (feed_theirs,))
    late_mine = sum_blocks(late_total, 5)
    (late_theirs,) = swap(late_mine)
    mine, theirs = (feed_mine, late_mine), (feed_theirs, late_theirs)
    weight_outs = (
        ((12, 2304), F32),
        ((12, 768), F32),
        ((12, 3072), F32),
        ((48, 768), F32),
        ((12, 512), F32),
        ((8, 1536), F32),
        ((8, 512), F32),
        ((8, 2048), F32),
        ((32, 512), F32),
        ((8, 512), F32),
    )
    vector_outs = (((1, 12), F32),) * 6 + (((1, 8), F32),) * 6
    grads = call(unpack_kernel, "unpack", (place,), (*mine, *theirs), weight_outs + vector_outs)

    def ordered(vectors, weights):
        joint, output, widen, narrow, projection = weights
        v = [x.reshape(-1) for x in vectors]
        return [v[0], v[1], joint, output, v[2], v[3], widen, narrow, v[4], v[5], projection]

    def by_sequence(t, grad):
        return grad.reshape(t.length, BATCH, t.width).transpose(1, 0, 2)

    return (
        loss,
        units[0],
        units[1],
        by_sequence(IMAGE, backs[0][2]),
        *ordered(grads[10:16], grads[:5]),
        by_sequence(TEXT, backs[1][2]),
        *ordered(grads[16:22], grads[5:10]),
        scale_grad,
    )


def solution(mesh):
    spread = P(("tower", "dp"), None, None)
    weights = [P()] * 11
    placed = (spread, *weights, spread, spread, P(("tower", "dp")), *weights, spread, P())
    vector, matrix = P("dp"), P("dp", None)
    grads = [vector, vector, matrix, matrix, vector, vector, matrix, matrix, vector, vector, matrix]
    units = P(("tower", "dp"), None)
    return jax.shard_map(
        shards,
        mesh=mesh,
        in_specs=placed,
        out_specs=(P(), units, units, spread, *grads, spread, *grads, P()),
        check_vma=False,
    )
```

```python
import functools

import jax
import jax.numpy as jnp
from jax import lax
from jax.experimental import pallas as pl
from jax.experimental.pallas import tpu as pltpu
from jax.sharding import PartitionSpec as P

F32 = jnp.float32
BF16 = jnp.bfloat16
BATCH = 8
EMBED = 512
TILE = 256
DEVS = 64


class Tower:
    def __init__(self, width, heads, hidden, length, padded, rows, extra, causal):
        self.width = width
        self.heads = heads
        self.hidden = hidden
        self.length = length
        self.padded = padded
        self.real = BATCH * length
        self.rows = rows
        self.extra = extra
        self.spread = BATCH * padded
        self.lanes = -(-rows // 128) * 128
        self.causal = causal
        self.step = 768 if width == 768 else 512


IMAGE = Tower(768, 12, 3072, 50, 64, 416, 400, False)
TEXT = Tower(512, 8, 2048, 77, 80, 640, 624, True)

VMEM_LIMIT = 64 * 1024 * 1024


def mm(left, right):
    return lax.dot_general(left, right, (((1,), (0,)), ((), ())), preferred_element_type=F32)


def mm_nt(left, right):
    return lax.dot_general(left, right, (((1,), (1,)), ((), ())), preferred_element_type=F32)


def mm_tn(left, right):
    return lax.dot_general(left, right, (((0,), (0,)), ((), ())), preferred_element_type=F32)


def normalise(values):
    centre = jnp.mean(values, axis=-1, keepdims=True)
    offset = values - centre
    inverse = lax.rsqrt(jnp.mean(offset * offset, axis=-1, keepdims=True) + 1e-05)
    return offset * inverse, inverse


def norm_back(upstream, gain, normal, inverse):
    scaled = upstream * gain
    inner = (
        scaled
        - jnp.mean(scaled, axis=-1, keepdims=True)
        - normal * jnp.mean(scaled * normal, axis=-1, keepdims=True)
    )
    return inner * inverse


def column_sum(values):
    return jnp.sum(values, axis=0, keepdims=True)


def sigmoid(values):
    return 0.5 + 0.5 * jnp.tanh(0.5 * values)


def vec(ref):
    return ref[...].reshape(1, -1)


def chunks(count, size=128):
    return [(at, min(size, count - at)) for at in range(0, count, size)]


UNROLL_TILE, UNROLL_HEADS, UNROLL_PACK, UNROLL_TURN = 9, 4, 4, 3


def loop(count, body, unroll=1):
    def step(i, carry):
        body(i)
        return carry

    lax.fori_loop(0, count, step, 0, unroll=min(unroll, count))


def tile_loop(width, body):
    loop(width // TILE, lambda n: body(n, pl.ds(pl.multiple_of(n * TILE, TILE), TILE)), UNROLL_TILE)


def put_tiles(ref, n, rows, values):
    for i in range(TILE // 128):
        ref[n * (TILE // 128) + i, 0:rows, :] = values[:, 128 * i : 128 * i + 128]


class Lazy:
    def __init__(self, queue, source, target, sem):
        self.copy = pltpu.make_async_copy(source, target, sem)
        self.target = target
        self.queue = queue
        self.started = self.waited = False

    def start(self):
        if not self.started:
            self.copy.start()
            self.started = True

    def get(self):
        if not self.waited:
            self.start()
            self.copy.wait()
            self.waited = True
            for item in self.queue:
                if not item.started:
                    item.start()
                    break
        return self.target


class Staged:
    def __init__(self, out, stage, sems, pending):
        self.out = out
        self.ref = stage
        self.sems = sems
        self.pending = pending

    def send(self, source, target):
        copy = pltpu.make_async_copy(source, target, self.sems.at[len(self.pending)])
        copy.start()
        self.pending.append(copy)

    def done(self):
        self.send(self.ref, self.out)

    def units_done(self, devices, units, out_units):
        self.send(self.ref.at[devices, units], self.out.at[devices, out_units])


def head_masks():
    lane = lax.broadcasted_iota(jnp.int32, (1, 128), 1)
    first = jnp.where(lane < 64, 1.0, 0.0).astype(BF16)
    second = jnp.where(lane < 64, 0.0, 1.0).astype(BF16)
    return first, second


def two_heads(values, masks):
    return jnp.concatenate([values * masks[0], values * masks[1]], axis=0)


def own_head(values, padded):
    lane = lax.broadcasted_iota(jnp.int32, (padded, 128), 1)
    return jnp.where(lane < 64, values[:padded], values[padded:])


def pooled_row(t, lengths, b):
    return b if t is IMAGE else (lengths[b] - 1) * BATCH + b


def row_parts(t):
    return {
        "raw": EMBED,
        "unit": EMBED,
        "pooled": t.width,
        "mixed": t.width,
        "grad": t.width,
        "wide": t.hidden,
    }


def row_part(t, name):
    at = 0 if t is IMAGE else sum(row_parts(IMAGE).values())
    for part, size in row_parts(t).items():
        if part == name:
            return slice(at, at + size)
        at += size


ROW_TOTAL = sum(row_parts(IMAGE).values()) + sum(row_parts(TEXT).values())


def front_kernel(
    t,
    lengths,
    tokens,
    first_gain,
    first_shift,
    joint_weight,
    output_weight,
    second_gain,
    second_shift,
    widen_weight,
    narrow_weight,
    final_gain,
    final_shift,
    projection,
    block_grad,
    turned,
    joint,
    probs,
    mixed,
    unit,
    kept,
    joint_wide,
    context_wide,
    normed_one,
    context,
):
    width, padded, rows = t.width, t.padded, t.rows
    staged = (turned, joint, probs, mixed)
    turned, joint, probs, mixed = [out.ref for out in staged]
    mixed_row, grad_row = [kept.at[:, row_part(t, name)] for name in ("mixed", "grad")]
    for at, size in chunks(t.real):
        mixed[at : at + size, :] = block_grad[at : at + size, :].astype(F32)
    for b in range(BATCH):
        grad_row[b : b + 1, :] = mixed[pl.ds(pooled_row(t, lengths, b), 1), :]
    pad = t.real - t.real % 16
    normed_one[pad:rows, :] = jnp.zeros((rows - pad, width), BF16)
    for at, size in chunks(t.real):
        normal, _ = normalise(tokens[at : at + size, :].astype(F32))
        normed_one[at : at + size, :] = (normal * vec(first_gain) + vec(first_shift)).astype(BF16)
    if t.spread > rows:
        fill = (3 * width // 128, t.spread - rows, 128)
        joint_wide[:, rows : t.spread, :] = jnp.zeros(fill, F32)

    joint_weight = joint_weight.get()

    def joint_step(n, cols):
        put_tiles(joint_wide, n, rows, mm(normed_one[...], joint_weight[:, cols]))

    tile_loop(3 * width, joint_step)

    masks = head_masks()
    key_at = lax.broadcasted_iota(jnp.int32, (padded, 2 * padded), 0)
    query_at = lax.broadcasted_iota(jnp.int32, (padded, 2 * padded), 1)
    query_at = jnp.where(query_at < padded, query_at, query_at - padded)
    valid = key_at <= query_at if t.causal else key_at < t.length
    pairs = range(t.heads // 2)

    def attend(b):
        some = pl.ds(b, padded, stride=BATCH)
        for c in range(3 * width // 128):
            joint[b, :, 128 * c : 128 * c + 128] = joint_wide[c, some, :].astype(BF16)
        scores = []
        for p in pairs:
            at = 128 * p
            queries = joint[b, :, at : at + 128]
            keys = joint[b, :, width + at : width + at + 128]
            scores.append(mm_nt(keys, two_heads(queries, masks)) * 0.125)
        lows = []
        for p in pairs:
            score = jnp.where(valid, scores[p], -1e30)
            raised = jnp.exp(score - jnp.max(score, axis=0, keepdims=True))
            low = (raised * (1.0 / column_sum(raised))).astype(BF16)
            probs[b, p] = low
            lows.append(low)
        for p in pairs:
            at = 2 * width + 128 * p
            both = mm_tn(lows[p], joint[b, :, at : at + 128])
            context_wide[p, some, :] = own_head(both, padded)

    loop(BATCH, attend, UNROLL_HEADS)
    staged[1].done()
    staged[2].done()
    for p in pairs:
        context[:, 128 * p : 128 * p + 128] = context_wide[p, 0:rows, :].astype(BF16)
    turn(normed_one, turned.at[0:width])
    turn(context, turned.at[width : 2 * width])
    staged[0].done()
    output_weight = output_weight.get()

    def mix_step(n, cols):
        mixed[:, cols] = mm(context[...], output_weight[:, cols])

    tile_loop(width, mix_step)
    for at, size in chunks(t.real):
        mixed[at : at + size, :] += tokens[at : at + size, :].astype(F32)
    for b in range(BATCH):
        mixed_row[b : b + 1, :] = mixed[pl.ds(pooled_row(t, lengths, b), 1), :]
    row = mixed_row[...]
    mixed[t.real : rows, :] = jnp.zeros((rows - t.real, width), F32)
    mixed[t.extra : t.extra + BATCH, :] = row
    staged[3].done()

    normal, _ = normalise(row)
    normed = (normal * vec(second_gain) + vec(second_shift)).astype(BF16)
    wide = mm(normed, widen_weight.get()[...])
    kept[:, row_part(t, "wide")] = wide
    active = (wide * sigmoid(1.702 * wide)).astype(BF16)
    last = row + mm(active, narrow_weight.get()[...])
    kept[:, row_part(t, "pooled")] = last
    normal, _ = normalise(last)
    normed = (normal * vec(final_gain) + vec(final_shift)).astype(BF16)
    raw = mm(normed, projection.get()[...])
    kept[:, row_part(t, "raw")] = raw
    factor = lax.rsqrt(jnp.sum(raw * raw, axis=-1, keepdims=True) + 1e-06)
    unit[...] = (raw * factor).astype(BF16)
    kept[:, row_part(t, "unit")] = unit[...].astype(F32)


def fronts_kernel(scalars, held, lazies, outs, scratch):
    order = [5, 6, 0, 7, 8, 9, 1, 2, 3, 4]
    weights = [lazies[order.index(i)] for i in range(10)]
    for i in (1, 0):
        t = (IMAGE, TEXT)[i]
        tokens, g1, s1, g2, s2, gf, sf, block_grad = held[8 * i : 8 * i + 8]
        joint, output, widen, narrow, projection = weights[5 * i : 5 * i + 5]
        params = (g1, s1, joint, output, g2, s2, widen, narrow, gf, sf, projection, block_grad)
        front_kernel(
            t, scalars[0], tokens, *params, *outs[5 * i : 5 * i + 5], outs[10], *scratch[4 * i : 4 * i + 4]
        )
    for i in range(2):
        unit = outs[5 * i + 4][...]
        outs[11][:, :, EMBED * i : EMBED * i + EMBED] = jnp.broadcast_to(unit[None], (DEVS, *unit.shape))


def middle_kernel(
    t,
    place,
    lengths,
    mixed,
    block_grad,
    second_gain,
    second_shift,
    widen_weight,
    narrow_weight,
    normed_turned,
    active_turned,
    wide_own,
    wide_send,
    narrow_own,
    narrow_send,
    mixed_grad,
    gain_grad,
    shift_grad,
    normed_two,
    narrow_in,
    wide_in,
):
    step = pl.program_id(0)
    half_steps = pl.num_programs(0) // 2

    @pl.when(step == 0)
    def _():
        wide_in[t.real : t.rows, :] = jnp.zeros((t.rows - t.real, t.width), F32)
        for at, size in chunks(t.rows):
            normal, _ = normalise(mixed[at : at + size, :])
            normed_two[at : at + size, :] = (normal * vec(second_gain) + vec(second_shift)).astype(
                BF16
            )
        turn(normed_two, normed_turned)
        for at, size in chunks(t.real):
            wide_in[at : at + size, :] = block_grad[at : at + size, :].astype(F32)
        for b in range(BATCH):
            wide_in[pl.ds(pooled_row(t, lengths, b), 1), :] = jnp.zeros((1, t.width), F32)
        narrow_in[...] = wide_in[...].astype(BF16)
        cols = t.width // 2
        own = pl.multiple_of(place[0] * cols, 128)
        narrow_own[...] = narrow_in[:, pl.ds(own, cols)]
        narrow_send[...] = narrow_in[:, pl.ds(pl.multiple_of(cols - own, 128), cols)]
        mixed_grad[...] = jnp.zeros_like(mixed_grad)

    lows = []
    for at, size in chunks(t.step, TILE):
        some = slice(at, at + size)
        wide = mm(normed_two[...], widen_weight[:, some])
        back = mm_nt(narrow_in[...], narrow_weight[some, :])
        sig = sigmoid(1.702 * wide)
        active = wide * sig
        active_turned[some, 0 : t.rows] = active.astype(BF16).T
        slope = sig + 1.702 * active * (1.0 - sig)
        lows.append((back * slope).astype(BF16))
    low = jnp.concatenate(lows, axis=1)
    mixed_grad[...] += mm_nt(low, widen_weight[...])

    @pl.when(step < half_steps)
    def _():
        wide_own[...] = low

    @pl.when(step >= half_steps)
    def _():
        wide_send[...] = low

    @pl.when(step == pl.num_programs(0) - 1)
    def _():
        gain = shift = 0.0
        for at, size in chunks(t.rows):
            some = slice(at, at + size)
            normal, inverse = normalise(mixed[some, :])
            up = mixed_grad[some, :]
            gain += column_sum(up * normal)
            shift += column_sum(up)
            mixed_grad[some, :] = wide_in[some, :] + norm_back(
                up, vec(second_gain), normal, inverse
            )
        gain_grad[...] = gain
        shift_grad[...] = shift


def split_dot(weights, right):
    high = weights.astype(BF16)
    rest = weights - high.astype(F32)
    middle = rest.astype(BF16)
    low = (rest - middle.astype(F32)).astype(BF16)
    return mm(high, right) + mm(middle, right) + mm(low, right)


def head_back(
    unit_grad,
    raw,
    pooled,
    mixed_row,
    wide_row,
    grad_row,
    final_gain,
    final_shift,
    second_gain,
    second_shift,
    projection,
    widen_weight,
    narrow_weight,
    outs,
):
    (
        final_gain_grad,
        final_shift_grad,
        second_gain_grad,
        second_shift_grad,
        factors,
        mixed_grad_row,
        narrow_in_row,
        wide_grad_row,
    ) = outs
    own = slice(0, BATCH)
    width = pooled.shape[1]
    factor = lax.rsqrt(jnp.sum(raw * raw, axis=-1, keepdims=True) + 1e-06)
    raw_grad = factor * unit_grad - raw * (factor * factor * factor) * jnp.sum(
        unit_grad * raw, axis=-1, keepdims=True
    )
    raw_grad = raw_grad.astype(BF16)
    factors[:, width:] = raw_grad.astype(F32)
    normal, inverse = normalise(pooled)
    factors[:, 0:width] = (normal * final_gain + final_shift).astype(BF16).astype(F32)
    up = mm_nt(raw_grad, projection.get()[...])
    final_gain_grad[...] = column_sum((up * normal)[own])
    final_shift_grad[...] = column_sum(up[own])
    out_grad = grad_row + norm_back(up, final_gain, normal, inverse)
    narrow_in = out_grad.astype(BF16)
    narrow_in_row[...] = narrow_in.astype(F32)
    sig = sigmoid(1.702 * wide_row)
    slope = sig + 1.702 * wide_row * sig * (1.0 - sig)
    low = (mm_nt(narrow_in, narrow_weight.get()[...]) * slope).astype(BF16)
    wide_grad_row[...] = low.astype(F32)
    up = mm_nt(low, widen_weight.get()[...])
    normal, inverse = normalise(mixed_row)
    second_gain_grad[...] = column_sum((up * normal)[own])
    second_shift_grad[...] = column_sum(up[own])
    mixed_grad_row[...] = (out_grad + norm_back(up, second_gain, normal, inverse))[own]


def pair_kernel(scalars, held, lazies, outs, scratch):
    place, log_scale = scalars
    own, other, kept_own, kept_other = held[:4]
    image_vectors, text_vectors = held[4:8], held[8:12]
    loss, scale_grad = outs[:2]
    image_outs, text_outs = outs[2:10], outs[10:18]

    def rows(t, name):
        some = row_part(t, name)
        return jnp.concatenate([kept_own[:, some], kept_other[:, some]], axis=0)

    half = own.shape[0]
    pairs = 2 * half
    scale = jnp.exp(jnp.full((1, 1), log_scale[0], F32))
    blocks = (own, other)

    def totals(left_at, right_at):
        sums, moments = [], []
        for right in blocks:
            column, moment = None, None
            for left in blocks:
                for piece in range(0, half, 256):
                    sims = scale * mm_nt(
                        left[piece : piece + 256, left_at : left_at + EMBED],
                        right[:, right_at : right_at + EMBED],
                    )
                    raised = jnp.exp(sims)
                    add, more = column_sum(raised), column_sum(raised * sims)
                    column = add if column is None else column + add
                    moment = more if moment is None else moment + more
            sums.append(column)
            moments.append(moment)
        return sums, moments

    column_sums, column_moments = totals(0, EMBED)
    row_sums, row_moments = totals(EMBED, 0)
    log_total = jnp.zeros((1, 1), F32)
    weighted = jnp.zeros((1, 1), F32)
    trace = jnp.zeros((1, 1), F32)
    for i in range(2):
        for total, moment in ((column_sums[i], column_moments[i]), (row_sums[i], row_moments[i])):
            log_total += jnp.sum(jnp.log(total), axis=-1, keepdims=True)
            weighted += jnp.sum(moment / total, axis=-1, keepdims=True)
        product = blocks[i][:, :EMBED].astype(F32) * blocks[i][:, EMBED:].astype(F32)
        trace += jnp.sum(column_sum(product), axis=-1, keepdims=True)
    trace = scale * trace
    loss[...] = jnp.broadcast_to((log_total - 2.0 * trace) / (2.0 * pairs), loss.shape)
    scale_grad[...] = jnp.broadcast_to((weighted - 2.0 * trace) / (2.0 * pairs), loss.shape)

    lane = lax.broadcasted_iota(jnp.int32, (2 * BATCH, half), 1)
    sub = lax.broadcasted_iota(jnp.int32, (2 * BATCH, half), 0)
    diagonal = place[1] * BATCH
    identity = [
        jnp.where(jnp.logical_and(lane == sub + diagonal, sub < BATCH), 2.0, 0.0),
        jnp.where(jnp.logical_and(lane == sub - BATCH + diagonal, sub >= BATCH), 2.0, 0.0),
    ]

    def grads(t, at, other_sums):
        unit = rows(t, "unit").astype(BF16)
        raised = [jnp.exp(scale * mm_nt(unit, block[:, at : at + EMBED])) for block in blocks]
        own_sum = sum(jnp.sum(r, axis=-1, keepdims=True) for r in raised)
        result = None
        for i in range(2):
            weight = raised[i] * (1.0 / own_sum + 1.0 / other_sums[i]) - identity[i]
            weight = weight / (2.0 * pairs)
            part = split_dot(weight, blocks[i][:, at : at + EMBED])
            result = part if result is None else result + part
        return scale * result

    image_grad = grads(IMAGE, EMBED, column_sums)
    text_grad = grads(TEXT, 0, row_sums)
    for t, unit_grad, vectors, weights, results in (
        (TEXT, text_grad, text_vectors, lazies[0:3], text_outs),
        (IMAGE, image_grad, image_vectors, lazies[3:6], image_outs),
    ):
        values = [rows(t, name) for name in ("raw", "pooled", "mixed", "wide", "grad")]
        values += [vec(ref) for ref in vectors]
        projection, narrow, widen = weights
        head_back(unit_grad, *values, projection, widen, narrow, results)

def back_kernel(t, scalars, held, lazies, outs, scratch):
    place, lengths = scalars
    tokens, first_gain, mixed_grad_row = held
    output_weight, mixed_grad, joint, probs, joint_weight = lazies
    own, send, tokens_out, gain_grad, shift_grad = outs
    context_grad, joint_grad, normed_grad, grads = scratch
    width, padded, rows = t.width, t.padded, t.rows
    tokens_grad = tokens_out.ref
    grad = mixed_grad.get()
    for b in range(BATCH):
        grad[pl.ds(pooled_row(t, lengths, b), 1), :] = mixed_grad_row[b : b + 1, :]
    mixed_low = slice(3 * width, 4 * width)
    grads[:, mixed_low] = grad[...].astype(BF16)
    if t.spread > rows:
        fill = (width // 128, t.spread - rows, 128)
        context_grad[:, rows : t.spread, :] = jnp.zeros(fill, F32)
    output_weight = output_weight.get()

    def context_step(n, cols):
        put_tiles(context_grad, n, rows, mm_nt(grads[:, mixed_low], output_weight[cols, :]))

    tile_loop(width, context_step)
    masks = head_masks()
    pairs = range(t.heads // 2)
    joint, probs = joint.get(), probs.get()

    def attend(b):
        some = pl.ds(b, padded, stride=BATCH)
        ups = [two_heads(context_grad[p, some, :].astype(BF16), masks) for p in pairs]
        backs = []
        for p in pairs:
            at = 2 * width + 128 * p
            backs.append(mm_nt(joint[b, :, at : at + 128], ups[p]))
        lows = []
        for p in pairs:
            wide = probs[b, p].astype(F32)
            back = wide * (backs[p] - column_sum(backs[p] * wide))
            lows.append(back.astype(BF16))
        for p in pairs:
            at = 128 * p
            queries = joint[b, :, at : at + 128]
            keys = joint[b, :, width + at : width + at + 128]
            joint_grad[2 * len(pairs) + p, some, :] = mm(probs[b, p], ups[p])
            joint_grad[len(pairs) + p, some, :] = mm(lows[p], two_heads(queries, masks)) * 0.125
            joint_grad[p, some, :] = own_head(mm_tn(lows[p], keys), padded) * 0.125

    loop(BATCH, attend, UNROLL_HEADS)
    for c in range(3 * width // 128):
        grads[:, 128 * c : 128 * c + 128] = joint_grad[c, 0:rows, :].astype(BF16)
    start = pl.multiple_of(place[0] * (2 * width), 128)
    own.send(grads.at[:, pl.ds(start, 2 * width)], own.out)
    start = pl.multiple_of(2 * width - start, 128)
    send.send(grads.at[:, pl.ds(start, 2 * width)], send.out)
    joint_weight = joint_weight.get()

    def normed_step(n, cols):
        normed_grad[:, cols] = mm_nt(grads[:, 0 : 3 * width], joint_weight[cols, :])

    tile_loop(width, normed_step)
    gain = shift = 0.0
    for at, size in chunks(t.real):
        some = slice(at, at + size)
        normal, inverse = normalise(tokens[some, :].astype(F32))
        up = normed_grad[some, :]
        gain += column_sum(up * normal)
        shift += column_sum(up)
        tokens_grad[some, :] = grad[some, :] + norm_back(up, vec(first_gain), normal, inverse)
    gain_grad[...] = gain
    shift_grad[...] = shift
    tokens_out.done()

def turn(source, target):
    def step(n):
        cols = pl.ds(pl.multiple_of(n * 128, 128), 128)
        target[cols, 0 : source.shape[0]] = source[:, cols].T

    loop(source.shape[1] // 128, step, UNROLL_TURN)


def lanes_down(values):
    return jnp.concatenate(
        [values[:, :, at : at + 128] for at in range(0, values.shape[2], 128)], axis=1
    )


def put(out, device, unit, values):
    count = values.shape[1] // 16
    size = values.shape[0]
    values = values.reshape(size, count, 16, 128).astype(BF16)
    out[pl.ds(device, size), unit : unit + count] = values


def pack_twelve(first, second, out, unit=0, each=4):
    cols = first.shape[1]
    count = cols // 128
    sub = lax.broadcasted_iota(jnp.int32, (each, 8, cols), 1) < 4

    def step(e):
        rows = pl.ds(pl.multiple_of(e * (24 * each), 8), 24 * each)
        x = first[rows, :].reshape(each, 24, cols)
        y = second[rows, :].reshape(each, 24, cols)
        left, right = x[:, 8:16], y[:, 8:16]
        even = jnp.where(sub, left, pltpu.roll(right, 4, 1))
        odd = jnp.where(sub, pltpu.roll(left, 4, 1), right)
        parts = []
        for a, b, c in ((x[:, 0:8], y[:, 0:8], even), (x[:, 16:24], y[:, 16:24], odd)):
            parts.append(jnp.concatenate([lanes_down(v) for v in (a, b, c)], axis=1))
        if parts[0].shape[1] % 16:
            fill = jnp.zeros((each, 16 - parts[0].shape[1] % 16, 128), F32)
            parts = [jnp.concatenate([part, fill], axis=1) for part in parts]
        height = parts[0].shape[1]
        values = jnp.stack(parts, axis=1).reshape(2 * each, height, 128)
        put(out, e * (2 * each), unit, values)

    loop(32 // each, step, UNROLL_PACK)


def pack_rows(result, rows, out, unit=0, each=8, device=0):
    total = result.shape[0] // rows
    cols = result.shape[1]

    def step(e):
        some = pl.ds(pl.multiple_of(e * (rows * each), 8), rows * each)
        values = lanes_down(result[some, :].reshape(each, rows, cols))
        put(out, device + e * each, unit, values)

    loop(total // each, step, UNROLL_PACK)


def put_extra(t, ref, rows):
    rows = jnp.concatenate([rows, jnp.zeros_like(rows)], axis=0)
    ref[t.extra : t.extra + 16, :] = rows.astype(BF16)


def wide_grads(t, half, product, send, at, first, second):
    if t is IMAGE:
        for i in range(3):
            first[...] = product(256 * i, 256)
            second[...] = product(768 + 256 * i, 256)
            pack_twelve(first, second, send.ref, 3 * i)
            units = slice(3 * i, 3 * i + 3)
            send.units_done(slice(None), units, slice(at + 3 * i, at + 3 * i + 3))
    else:
        for i in range(2):
            first[...] = product(512 * i, 512)
            pack_rows(first, 8, send.ref, 2 * i)
            units = slice(2 * i, 2 * i + 2)
            send.units_done(slice(None), units, slice(at + 2 * i, at + 2 * i + 2))


def feed_kernel(t, at, scalars, held, lazies, outs, scratch):
    (place,) = scalars
    wide_rows, narrow_rows = held
    normed, wides, narrows = lazies[0:2], lazies[2:4], lazies[4:6]
    actives = lazies[6:14]
    (out,) = outs
    first, second, narrow_result = scratch

    def patch(refs, rows):
        size = rows.shape[1] // 2
        some = pl.ds(pl.multiple_of(place[0] * size, 128), size)
        for side, ref in enumerate(refs):
            put_extra(t, ref.get(), rows[BATCH * side : BATCH * side + BATCH, some])

    patch(wides, wide_rows)
    lefts = [ref.get() for ref in normed]
    wides = [ref.get() for ref in wides]

    def product(tile, size):
        return sum(mm(a[:, 0 : t.rows], b[:, tile : tile + size]) for a, b in zip(lefts, wides))

    wide_grads(t, place[0], product, out, at, first, second)
    patch(narrows, narrow_rows)
    narrows = [ref.get() for ref in narrows]
    wide_units, units = (9, 9) if t is IMAGE else (4, 4)
    some = slice(wide_units, wide_units + units)
    for j in range(4):
        pair = [actives[2 * j].get(), actives[2 * j + 1].get()]
        narrow_result[...] = sum(mm(a[:, 0 : t.rows], b[...]) for a, b in zip(pair, narrows))
        pack_rows(narrow_result, t.hidden // DEVS, out.ref, wide_units, 4, 16 * j)
        out.units_done(
            slice(16 * j, 16 * j + 16), some, slice(at + wide_units, at + wide_units + units)
        )


def rest_kernel(scalars, held, lazies, outs, scratch):
    (place,) = scalars
    (out,) = outs
    first, second, third = scratch[:3]
    misc_scratch, spread = scratch[3:6], scratch[6]
    half = place[0]
    misc, text_stage, image_stage = [Staged(out.out, ref, out.sems, out.pending) for ref in scratch[7:10]]
    misc_grads(half, held[:2], held[2:], misc, misc_scratch, spread)
    for t, ins, stage, results in (
        (TEXT, lazies[0:4], text_stage, (third, None)),
        (IMAGE, lazies[4:8], image_stage, (first, second)),
    ):
        width = t.width
        lefts, rights = [ref.get() for ref in ins[0::2]], [ref.get() for ref in ins[1::2]]

        def product(tile, size):
            late = jnp.where(half * (2 * width) + tile >= 3 * width, width, 0)
            rows = pl.ds(pl.multiple_of(late, 128), width)
            return sum(
                mm(a[rows, 0 : t.rows], b[:, tile : tile + size]) for a, b in zip(lefts, rights)
            )

        wide_grads(t, half, product, stage, REST_AT["image" if t is IMAGE else "text"], *results)


IMAGE_FEED_UNITS = 18
LATE_UNITS = 24
TEXT_FEED_AT = 0
REST_AT = {"text": 8, "image": 15}
MISC_AT = 12


def misc_grads(half, factors, vectors, out, scratch, spread):
    image_factors, text_factors = factors
    first, second, third = scratch

    def product(t, ref, at, size):
        final = ref[:, 0 : t.width].astype(BF16)
        start = pl.multiple_of(t.width + half * 256 + at, 128)
        return mm_tn(final, ref[:, pl.ds(start, size)].astype(BF16))

    first[...] = product(IMAGE, image_factors, 0, 128)
    second[...] = product(IMAGE, image_factors, 128, 128)
    third[...] = product(TEXT, text_factors, 0, 256)
    pack_twelve(first, second, out.ref, 1, 8)
    pack_rows(third, 8, out.ref, 0)
    spread[...] = jnp.zeros_like(spread)
    for side, refs_of, width in ((0, vectors[:8], 768), (64, vectors[8:], 512)):
        each = width // DEVS
        device = lax.broadcasted_iota(jnp.int32, (DEVS, width), 0)
        column = lax.broadcasted_iota(jnp.int32, (DEVS, width), 1)
        mine = jnp.logical_and(column >= device * each, column < device * each + each)
        source = lax.broadcasted_iota(jnp.int32, (width, 128), 0)
        lane = lax.broadcasted_iota(jnp.int32, (width, 128), 1)
        at = lax.rem(source, each)
        high_at = jnp.where(lane == at + side, 1.0, 0.0).astype(BF16)
        low_at = jnp.where(lane == at + side + 32, 1.0, 0.0).astype(BF16)
        rows = [refs_of[0][...], refs_of[1][...], refs_of[2][...] + refs_of[3][...]]
        rows += [refs_of[4][...] + refs_of[5][...], refs_of[6][...], refs_of[7][...]]
        for k, row in enumerate(rows):
            row = jnp.where(mine, row, 0.0)
            high = row.astype(BF16)
            low = (row - high.astype(F32)).astype(BF16)
            spread[:, 8 + k, :] += mm(high, high_at) + mm(low, low_at)
    out.ref[:, 2] = (out.ref[:, 2].astype(F32) + spread[...]).astype(BF16)
    out.units_done(slice(None), slice(0, 3), slice(MISC_AT, MISC_AT + 3))


def unpack_kernel(place, feed_mine, late_mine, feed_other, late_other, *outs):
    (
        image_joint,
        image_output,
        image_widen,
        image_narrow,
        image_projection,
        text_joint,
        text_output,
        text_widen,
        text_narrow,
        text_projection,
    ) = outs[:10]
    odd = place[1] % 2

    def emit(half, feed, late):
        def into(ref, col, body, tail):
            @pl.when(odd == 0)
            def _():
                ref[0:8, col : col + 128] = body
                ref[8:12, col : col + 128] = tail

            @pl.when(odd == 1)
            def _():
                ref[0:4, col : col + 128] = tail
                ref[4:12, col : col + 128] = body

        def image_wide(source, at, store):
            for tile in range(3):
                block = source[16 * (at + 3 * tile) : 16 * (at + 3 * tile) + 48, :]
                for side in range(2):
                    for g in range(2):
                        body = block[16 * side + 8 * g : 16 * side + 8 * g + 8]
                        tail = block[32 + 8 * g + 4 * side : 36 + 8 * g + 4 * side]
                        store(half * 1536 + side * 768 + tile * 256 + g * 128, body, tail)

        def joint_store(col, body, tail):
            if col < 2304:
                into(image_joint, col, body, tail)
            else:
                into(image_output, col - 2304, body, tail)

        image_wide(feed, 0, functools.partial(into, image_widen))
        image_wide(late, REST_AT["image"], joint_store)
        at = 16 * 9
        for g in range(3):
            col = half * 384 + 128 * g
            image_narrow[:, col : col + 128] = feed[at + 48 * g : at + 48 * g + 48, :]
        at = 16 * (MISC_AT + 1)
        for side in range(2):
            col = half * 256 + 128 * side
            tail = late[at + 16 + 4 * side : at + 20 + 4 * side, :]
            into(image_projection, col, late[at + 8 * side : at + 8 * side + 8, :], tail)
        for g in range(8):
            col = half * 1024 + 128 * g
            at = 16 * TEXT_FEED_AT + 8 * g
            text_widen[:, col : col + 128] = late[at : at + 8, :]
            at = 16 * REST_AT["text"] + 8 * g
            block = late[at : at + 8, :]
            if col < 1536:
                text_joint[:, col : col + 128] = block
            else:
                text_output[:, col - 1536 : col - 1408] = block
        for g in range(2):
            col = half * 256 + 128 * g
            at = 16 * (TEXT_FEED_AT + 4) + 32 * g
            text_narrow[:, col : col + 128] = late[at : at + 32, :]
            at = 16 * MISC_AT + 8 * g
            text_projection[:, col : col + 128] = late[at : at + 8, :]

    for half in range(2):

        @pl.when(place[0] == half)
        def _():
            emit(half, feed_mine, late_mine)
            emit(1 - half, feed_other, late_other)

    at = 16 * (MISC_AT + 2) + 8
    vectors = late_mine[at : at + 8, :] + late_other[at : at + 8, :]
    for k in range(12):
        each, side = (12, 0) if k < 6 else (8, 64)
        row = vectors[k % 6 : k % 6 + 1, :]
        outs[10 + k][...] = row[:, side : side + each] + row[:, side + 32 : side + 32 + each]


SMEM = pl.BlockSpec(memory_space=pltpu.SMEM)
VMEM = pl.BlockSpec(memory_space=pltpu.VMEM)


def call(body, name, scalars, arrays, outs, scratch=(), flops=1 << 32):
    return pl.pallas_call(
        body,
        name=name,
        out_shape=tuple(jax.ShapeDtypeStruct(shape, kind) for shape, kind in outs),
        in_specs=[SMEM] * len(scalars) + [VMEM] * len(arrays),
        out_specs=tuple(VMEM for _ in outs),
        scratch_shapes=[pltpu.VMEM(shape, kind) for shape, kind in scratch],
        compiler_params=pltpu.CompilerParams(vmem_limit_bytes=VMEM_LIMIT),
        cost_estimate=pl.CostEstimate(flops=flops, bytes_accessed=20 << 20, transcendentals=0),
    )(*scalars, *arrays)


BIG = 1 << 18


def lazy_call(body, name, scalars, held, lazies, outs, scratch=(), flops=1 << 33, buffer=None, after=(), ahead=3):
    many = 24

    def kernel(*refs):
        refs = list(refs)

        def take(count):
            got = refs[:count]
            del refs[:count]
            return got

        scalar_refs, held_refs = take(len(scalars)), take(len(held))
        sources = take(len(lazies))
        take(len(after) + (buffer is not None))
        out_refs = take(len(outs))
        targets = take(len(lazies))
        stages = take(sum(1 for out in outs if out[2]))
        scratch_refs = take(len(scratch))
        in_sems, out_sems = refs
        lazy = []
        for i, (source, target, (_, index, _)) in enumerate(zip(sources, targets, lazies)):
            if index is not None:
                source = source.at[index(*scalar_refs)]
            lazy.append(Lazy(lazy, source, target, in_sems.at[i]))
        for item in lazy[:ahead]:
            item.start()
        pending = []
        results = []
        for out, ref in zip(outs, out_refs):
            if out[2] is None:
                results.append(ref)
            else:
                results.append(Staged(ref, stages.pop(0) if out[2] else None, out_sems, pending))
        body(scalar_refs, held_refs, lazy, results, scratch_refs)
        for item in lazy:
            if item.started:
                item.get()
        for copy in pending:
            copy.wait()

    any_spec = pl.BlockSpec(memory_space=pl.ANY)
    scratch_shapes = [pltpu.VMEM(shape, array.dtype) for array, _, shape in lazies]
    scratch_shapes += [pltpu.VMEM(stage, kind) for _, kind, stage in outs if stage]
    scratch_shapes += [pltpu.VMEM(shape, kind) for shape, kind in scratch]
    scratch_shapes += [pltpu.SemaphoreType.DMA((max(1, len(lazies)),)), pltpu.SemaphoreType.DMA((many,))]
    arrays = [*held, *[array for array, _, _ in lazies], *after]
    specs = [SMEM] * len(scalars) + [VMEM] * len(held) + [any_spec] * (len(lazies) + len(after))
    aliases = {}
    if buffer is not None:
        aliases = {len(scalars) + len(arrays): 0}
        arrays.append(buffer)
        specs.append(any_spec)
    return pl.pallas_call(
        kernel,
        name=name,
        out_shape=tuple(jax.ShapeDtypeStruct(shape, kind) for shape, kind, _ in outs),
        in_specs=specs,
        out_specs=tuple(VMEM if stage is None else any_spec for _, _, stage in outs),
        scratch_shapes=scratch_shapes,
        input_output_aliases=aliases,
        compiler_params=pltpu.CompilerParams(vmem_limit_bytes=VMEM_LIMIT),
        cost_estimate=pl.CostEstimate(flops=flops, bytes_accessed=20 << 20, transcendentals=0),
    )(*scalars, *arrays)


def all_of(array):
    return array, None, array.shape


def staged(shape, kind):
    return shape, kind, shape


def plain(shape, kind):
    return shape, kind, None


def fronts_call(lengths, tokens, block_grads, weights):
    held, lazies, outs, scratch = [], [], [], []
    for t, token, grad, w in zip((IMAGE, TEXT), tokens, block_grads, weights):
        rows, width, hidden = t.rows, t.width, t.hidden
        held += [token, w[0], w[1], w[4], w[5], w[8], w[9], grad]
        lazies += [all_of(w[i]) for i in (2, 3, 6, 7, 10)]
        outs += [
            staged((2 * width, t.lanes), BF16),
            staged((BATCH, t.padded, 3 * width), BF16),
            staged((BATCH, t.heads // 2, t.padded, 2 * t.padded), BF16),
            staged((rows, width), F32),
            plain((BATCH, EMBED), BF16),
        ]
        scratch += [
            ((3 * width // 128, t.spread, 128), F32),
            ((width // 128, t.spread, 128), F32),
            ((rows, width), BF16),
            ((rows, width), BF16),
        ]
    lazies = [lazies[i] for i in (5, 6, 0, 7, 8, 9, 1, 2, 3, 4)]
    outs.append(plain((BATCH, ROW_TOTAL), F32))
    outs.append(plain((DEVS, BATCH, 2 * EMBED), BF16))
    results = lazy_call(fronts_kernel, "fronts", (lengths,), held, lazies, outs, scratch, ahead=6)
    return results[:5], results[5:10], results[10], results[11]


def middle(t, name, place, lengths, mixed, block_grad, gain, shift, widen, narrow, after):
    rows, width, hidden = t.rows, t.width, t.hidden
    steps = hidden // t.step
    outs = (
        ((width, t.lanes), BF16),
        ((hidden, t.lanes), BF16),
        ((rows, hidden // 2), BF16),
        ((rows, hidden // 2), BF16),
        ((rows, width // 2), BF16),
        ((rows, width // 2), BF16),
        ((rows, width), F32),
        ((1, width), F32),
        ((1, width), F32),
    )

    def held(shape):
        return pl.BlockSpec(shape, lambda i, *_: (0,) * len(shape))

    def tile(i, place):
        return lax.rem(i + place[0] * (steps // 2), steps)

    out_specs = [held(shape) for shape, _ in outs]
    out_specs[1] = pl.BlockSpec((t.step, t.lanes), lambda i, place, lengths: (tile(i, place), 0))
    out_specs[2] = pl.BlockSpec((rows, t.step), lambda i, *_: (0, jnp.minimum(i, steps // 2 - 1)))
    out_specs[3] = pl.BlockSpec((rows, t.step), lambda i, *_: (0, jnp.maximum(i - steps // 2, 0)))
    in_specs = [held(a.shape) for a in (mixed, block_grad, gain, shift)]
    in_specs.append(pl.BlockSpec((width, t.step), lambda i, place, lengths: (0, tile(i, place))))
    in_specs.append(pl.BlockSpec((t.step, width), lambda i, place, lengths: (tile(i, place), 0)))
    in_specs += [pl.BlockSpec(memory_space=pl.ANY)] * len(after)

    def kernel(*refs):
        middle_kernel(t, *refs[:8], *refs[8 + len(after) :])

    return pl.pallas_call(
        kernel,
        name=name + "_middle",
        out_shape=tuple(jax.ShapeDtypeStruct(shape, kind) for shape, kind in outs),
        grid_spec=pltpu.PrefetchScalarGridSpec(
            num_scalar_prefetch=2,
            grid=(steps,),
            in_specs=in_specs,
            out_specs=tuple(out_specs),
            scratch_shapes=[
                pltpu.VMEM((rows, width), BF16),
                pltpu.VMEM((rows, width), BF16),
                pltpu.VMEM((rows, width), F32),
            ],
        ),
        compiler_params=pltpu.CompilerParams(vmem_limit_bytes=VMEM_LIMIT),
        cost_estimate=pl.CostEstimate(flops=1 << 35, bytes_accessed=20 << 20, transcendentals=0),
    )(place, lengths, mixed, block_grad, gain, shift, widen, narrow, *after)


def back(t, name, place, lengths, row, tokens, gain, output, mixed_grad, joint, probs, joint_weight, after):
    rows, width = t.rows, t.width
    lazies = [all_of(a) for a in (output, mixed_grad, joint, probs, joint_weight)]
    outs = [
        ((rows, 2 * width), BF16, ()),
        ((rows, 2 * width), BF16, ()),
        staged((t.real, width), F32),
        plain((1, width), F32),
        plain((1, width), F32),
    ]
    scratch = [
        ((width // 128, t.spread, 128), F32),
        ((3 * width // 128, t.spread, 128), F32),
        ((rows, width), F32),
        ((rows, 4 * width), BF16),
    ]
    return lazy_call(
        functools.partial(back_kernel, t),
        name + "_back",
        (place, lengths),
        (tokens, gain, row),
        lazies,
        outs,
        scratch,
        after=after,
    )


def feed(t, place, head, middle, other, buffer, after):
    rows, width = t.rows, t.width
    name = "image" if t is IMAGE else "text"
    own = (middle[0], middle[1], middle[2], middle[4])
    lazies = [all_of(own[0]), all_of(other[0]), all_of(own[2]), all_of(other[2])]
    lazies += [all_of(own[3]), all_of(other[3])]
    for j in range(4):
        some = slice(width * j, width * j + width)
        for side in (own, other):
            lazies.append((side[1], lambda *_, some=some: (some, slice(None)), (width, t.lanes)))
    cols = 256 if t is IMAGE else 512
    scratch = [
        ((width, cols), F32),
        ((width, cols) if t is IMAGE else (8, 128), F32),
        ((width, width // 2), F32),
    ]
    units = IMAGE_FEED_UNITS if t is IMAGE else 8
    total = LATE_UNITS if buffer else units
    (out,) = lazy_call(
        functools.partial(feed_kernel, t, TEXT_FEED_AT if buffer else 0),
        name + "_feed",
        (place,),
        (head[7], head[6]),
        lazies,
        [((DEVS, total, 16, 128), BF16, (DEVS, units, 16, 128))],
        scratch,
        after=after,
        ahead=10,
    )
    return out


def rest(place, factors, vectors, sides, buffer):
    lazies = []
    for own, other in (sides[1], sides[0]):
        lazies += [all_of(a) for a in (*own, *other)]
    outs = [((DEVS, LATE_UNITS, 16, 128), BF16, ())]
    scratch = [
        ((768, 256), F32),
        ((768, 256), F32),
        ((512, 512), F32),
        ((768, 128), F32),
        ((768, 128), F32),
        ((512, 256), F32),
        ((DEVS, 16, 128), F32),
        ((DEVS, 3, 16, 128), BF16),
        ((DEVS, 4, 16, 128), BF16),
        ((DEVS, 9, 16, 128), BF16),
    ]
    (out,) = lazy_call(
        rest_kernel, "rest", (place,), [*factors, *vectors], lazies, outs, scratch, buffer=buffer, ahead=4
    )
    return out


def sum_blocks(received, step):
    devices, units = received.shape[:2]

    def body(scalars, held, lazies, outs, scratch):
        for i, block in enumerate(lazies):
            total = jnp.sum(block.get()[...].astype(F32), axis=0)
            outs[0][16 * step * i : 16 * step * (i + 1), :] = total.reshape(16 * step, 128)

    lazies = []
    for at in range(0, units, step):
        some = slice(at, at + step)
        lazies.append((received, lambda *_, some=some: (slice(None), some), (devices, step, 16, 128)))
    outs = [plain((16 * units, 128), F32)]
    return lazy_call(body, "sum_blocks", (), (), lazies, outs, flops=1 << 34, ahead=len(lazies))[0]


def behind(arrays, after):
    def kernel(*refs):
        pass

    any_spec = pl.BlockSpec(memory_space=pl.ANY)
    return pl.pallas_call(
        kernel,
        name="behind",
        out_shape=[jax.ShapeDtypeStruct(array.shape, array.dtype) for array in arrays],
        in_specs=[any_spec] * (len(arrays) + len(after)),
        out_specs=[any_spec] * len(arrays),
        input_output_aliases={i: i for i in range(len(arrays))},
    )(*arrays, *after)


SWAP = [(0, 1), (1, 0)]


def by_token(tokens):
    return tokens.transpose(1, 0, 2).reshape(-1, tokens.shape[2])


def shards(*args):
    image_tokens, image_weights, image_block_grad = args[0], args[1:12], args[12]
    text_tokens, caption_lengths = args[13], args[14]
    text_weights, text_block_grad, log_scale = args[15:26], args[26], args[27]
    core = lax.axis_index("tower")
    dp = lax.axis_index("dp")
    place = jnp.stack([core, dp]).astype(jnp.int32)
    tokens = (by_token(image_tokens), by_token(text_tokens))
    block_grads = (by_token(image_block_grad), by_token(text_block_grad))
    weights = (image_weights, text_weights)
    kinds = ((0, IMAGE, "image"), (1, TEXT, "text"))
    *fronts, kept, copies = fronts_call(caption_lengths, tokens, block_grads, weights)
    units = [f[4] for f in fronts]
    own = lax.all_to_all(copies, "dp", 0, 0, tiled=True).reshape(DEVS * BATCH, 2 * EMBED)

    def swap(*arrays):
        return [lax.ppermute(array, "tower", SWAP) for array in arrays]

    def middle_of(i, after):
        _, t, name = kinds[i]
        w = weights[i]
        return middle(
            t, name, place, caption_lengths, fronts[i][3], block_grads[i], w[4], w[5], w[6], w[7], after
        )

    (kept_other,) = swap(kept)
    image_middle = list(middle_of(0, ()))
    (own,) = behind([own], (image_middle[0], kept_other))
    (other,) = swap(own)
    sent = (0, 1, 3, 5)
    for k, array in zip(sent, behind([image_middle[k] for k in sent], (other,))):
        image_middle[k] = array
    image_sent = swap(*[image_middle[k] for k in sent])

    pair_held = [own, other, kept, kept_other]
    for w in weights:
        pair_held += [w[8], w[9], w[4], w[5]]
    pair_lazies = []
    for i in (1, 0):
        w = weights[i]
        pair_lazies += [all_of(w[10]), all_of(w[7]), all_of(w[6])]
    pair_out = [plain((1, 128), F32), plain((1, 128), F32)]
    for t in (IMAGE, TEXT):
        pair_out += [plain((1, t.width), F32)] * 4
        pair_out += [plain((2 * BATCH, t.width + EMBED), F32), plain((BATCH, t.width), F32)]
        pair_out += [plain((2 * BATCH, t.width), F32), plain((2 * BATCH, t.hidden), F32)]
    paired = lazy_call(
        pair_kernel, "pairs", (place, log_scale), pair_held, pair_lazies, pair_out, ahead=6
    )
    loss, scale_grad = paired[0][0, :1], paired[1][0, :1]
    heads = (paired[2:10], paired[10:18])
    image_feed = feed(IMAGE, place, heads[0], image_middle, image_sent, False, ())
    feed_total = lax.all_to_all(image_feed, "dp", 0, 0, tiled=True)
    text_middle = middle_of(1, (image_feed,))
    middles = (image_middle, text_middle)

    backs = []
    for i, t, name in kinds:
        f, m, h, w = fronts[i], middles[i], heads[i], weights[i]
        last = backs[-1][0] if backs else text_middle[0]
        backs.append(
            back(t, name, place, caption_lengths, h[5], tokens[i], w[0], w[3], m[6], f[1], f[2], w[2], (last,))
        )
    text_sent = swap(*[text_middle[k] for k in sent])
    late = feed(TEXT, place, heads[1], text_middle, text_sent, True, (backs[1][0],))
    sides = []
    for f, k in zip(fronts, backs):
        sides.append(((f[0], k[0]), swap(f[0], k[1])))
    vectors = []
    for m, h, k in zip(middles, heads, backs):
        vectors += [k[3], k[4], m[7], h[2], m[8], h[3], h[0], h[1]]
    factors = [heads[0][4], heads[1][4]]
    (late,) = behind([rest(place, factors, vectors, sides, late)], (feed_total,))
    late_total = lax.all_to_all(late, "dp", 0, 0, tiled=True)
    feed_mine = sum_blocks(feed_total, 3)
    (feed_theirs,) = swap(feed_mine)
    (late_total,) = behind([late_total], (feed_theirs,))
    late_mine = sum_blocks(late_total, 4)
    (late_theirs,) = swap(late_mine)
    mine, theirs = (feed_mine, late_mine), (feed_theirs, late_theirs)
    weight_outs = (
        ((12, 2304), F32),
        ((12, 768), F32),
        ((12, 3072), F32),
        ((48, 768), F32),
        ((12, 512), F32),
        ((8, 1536), F32),
        ((8, 512), F32),
        ((8, 2048), F32),
        ((32, 512), F32),
        ((8, 512), F32),
    )
    vector_outs = (((1, 12), F32),) * 6 + (((1, 8), F32),) * 6
    grads = call(unpack_kernel, "unpack", (place,), (*mine, *theirs), weight_outs + vector_outs)

    def ordered(vectors, weights):
        joint, output, widen, narrow, projection = weights
        v = [x.reshape(-1) for x in vectors]
        return [v[0], v[1], joint, output, v[2], v[3], widen, narrow, v[4], v[5], projection]

    def by_sequence(t, grad):
        return grad.reshape(t.length, BATCH, t.width).transpose(1, 0, 2)

    return (
        loss,
        units[0],
        units[1],
        by_sequence(IMAGE, backs[0][2]),
        *ordered(grads[10:16], grads[:5]),
        by_sequence(TEXT, backs[1][2]),
        *ordered(grads[16:22], grads[5:10]),
        scale_grad,
    )


def solution(mesh):
    spread = P(("tower", "dp"), None, None)
    weights = [P()] * 11
    placed = (spread, *weights, spread, spread, P(("tower", "dp")), *weights, spread, P())
    vector, matrix = P("dp"), P("dp", None)
    grads = [vector, vector, matrix, matrix, vector, vector, matrix, matrix, vector, vector, matrix]
    units = P(("tower", "dp"), None)
    return jax.shard_map(
        shards,
        mesh=mesh,
        in_specs=placed,
        out_specs=(P(), units, units, spread, *grads, spread, *grads, P()),
        check_vma=False,
    )
```

```python
import functools

import jax
import jax.numpy as jnp
from jax import lax
from jax.experimental import pallas as pl
from jax.experimental.pallas import tpu as pltpu
from jax.sharding import PartitionSpec as P

F32 = jnp.float32
BF16 = jnp.bfloat16
BATCH = 8
EMBED = 512
TILE = 256
DEVS = 64


class Tower:
    def __init__(self, width, heads, hidden, length, padded, rows, extra, causal):
        self.width = width
        self.heads = heads
        self.hidden = hidden
        self.length = length
        self.padded = padded
        self.real = BATCH * length
        self.rows = rows
        self.extra = extra
        self.spread = BATCH * padded
        self.lanes = -(-rows // 128) * 128
        self.causal = causal
        self.step = 768 if width == 768 else 512


IMAGE = Tower(768, 12, 3072, 50, 64, 416, 400, False)
TEXT = Tower(512, 8, 2048, 77, 80, 640, 624, True)

VMEM_LIMIT = 64 * 1024 * 1024


def mm(left, right):
    return lax.dot_general(left, right, (((1,), (0,)), ((), ())), preferred_element_type=F32)


def mm_nt(left, right):
    return lax.dot_general(left, right, (((1,), (1,)), ((), ())), preferred_element_type=F32)


def mm_tn(left, right):
    return lax.dot_general(left, right, (((0,), (0,)), ((), ())), preferred_element_type=F32)


def normalise(values):
    centre = jnp.mean(values, axis=-1, keepdims=True)
    offset = values - centre
    inverse = lax.rsqrt(jnp.mean(offset * offset, axis=-1, keepdims=True) + 1e-05)
    return offset * inverse, inverse


def norm_back(upstream, gain, normal, inverse):
    scaled = upstream * gain
    inner = (
        scaled
        - jnp.mean(scaled, axis=-1, keepdims=True)
        - normal * jnp.mean(scaled * normal, axis=-1, keepdims=True)
    )
    return inner * inverse


def column_sum(values):
    return jnp.sum(values, axis=0, keepdims=True)


def sigmoid(values):
    return 0.5 + 0.5 * jnp.tanh(0.5 * values)


def vec(ref):
    return ref[...].reshape(1, -1)


def chunks(count, size=128):
    return [(at, min(size, count - at)) for at in range(0, count, size)]


UNROLL_TILE, UNROLL_HEADS, UNROLL_PACK, UNROLL_TURN = 9, 8, 4, 24
UNROLL_BACK = 4


def loop(count, body, unroll=1):
    def step(i, carry):
        body(i)
        return carry

    lax.fori_loop(0, count, step, 0, unroll=min(unroll, count))


def tile_loop(width, body):
    loop(width // TILE, lambda n: body(n, pl.ds(pl.multiple_of(n * TILE, TILE), TILE)), UNROLL_TILE)


def put_tiles(ref, n, rows, values):
    for i in range(TILE // 128):
        ref[n * (TILE // 128) + i, 0:rows, :] = values[:, 128 * i : 128 * i + 128]


class Lazy:
    def __init__(self, queue, source, target, sem):
        self.copy = pltpu.make_async_copy(source, target, sem)
        self.target = target
        self.queue = queue
        self.started = self.waited = False

    def start(self):
        if not self.started:
            self.copy.start()
            self.started = True

    def get(self):
        if not self.waited:
            self.start()
            self.copy.wait()
            self.waited = True
            for item in self.queue:
                if not item.started:
                    item.start()
                    break
        return self.target


class Staged:
    def __init__(self, out, stage, sems, pending):
        self.out = out
        self.ref = stage
        self.sems = sems
        self.pending = pending

    def send(self, source, target):
        copy = pltpu.make_async_copy(source, target, self.sems.at[len(self.pending)])
        copy.start()
        self.pending.append(copy)

    def done(self):
        self.send(self.ref, self.out)

    def units_done(self, devices, units, out_units):
        self.send(self.ref.at[devices, units], self.out.at[devices, out_units])


def head_masks():
    lane = lax.broadcasted_iota(jnp.int32, (1, 128), 1)
    first = jnp.where(lane < 64, 1.0, 0.0).astype(BF16)
    second = jnp.where(lane < 64, 0.0, 1.0).astype(BF16)
    return first, second


def two_heads(values, masks):
    return jnp.concatenate([values * masks[0], values * masks[1]], axis=0)


def own_head(values, padded):
    lane = lax.broadcasted_iota(jnp.int32, (padded, 128), 1)
    return jnp.where(lane < 64, values[:padded], values[padded:])


def pooled_row(t, lengths, b):
    return b if t is IMAGE else (lengths[b] - 1) * BATCH + b


def row_parts(t):
    return {
        "raw": EMBED,
        "unit": EMBED,
        "pooled": t.width,
        "mixed": t.width,
        "grad": t.width,
        "wide": t.hidden,
    }


def row_part(t, name):
    at = 0 if t is IMAGE else sum(row_parts(IMAGE).values())
    for part, size in row_parts(t).items():
        if part == name:
            return slice(at, at + size)
        at += size


ROW_TOTAL = sum(row_parts(IMAGE).values()) + sum(row_parts(TEXT).values())


class Front:
    def __init__(self, t, lengths, ins, weights, outs, kept, scratch):
        self.t = t
        self.lengths = lengths
        (
            self.tokens,
            self.first_gain,
            self.first_shift,
            self.second_gain,
            self.second_shift,
            self.final_gain,
            self.final_shift,
            self.block_grad,
        ) = ins
        self.joint_weight, self.output_weight, self.widen, self.narrow, self.projection = weights
        self.staged = outs[:4]
        self.turned, self.joint, self.probs, self.mixed = [out.ref for out in outs[:4]]
        self.unit = outs[4]
        self.kept = kept
        self.joint_wide, self.context_wide, self.normed_one, self.context = scratch
        self.mixed_row = kept.at[:, row_part(t, "mixed")]

    def norm(self):
        t, rows = self.t, self.t.rows
        mixed, normed_one = self.mixed, self.normed_one
        grad_row = self.kept.at[:, row_part(t, "grad")]
        for at, size in chunks(t.real):
            mixed[at : at + size, :] = self.block_grad[at : at + size, :].astype(F32)
        for b in range(BATCH):
            grad_row[b : b + 1, :] = mixed[pl.ds(pooled_row(t, self.lengths, b), 1), :]
        pad = t.real - t.real % 16
        normed_one[pad:rows, :] = jnp.zeros((rows - pad, t.width), BF16)
        for at, size in chunks(t.real):
            normal, _ = normalise(self.tokens[at : at + size, :].astype(F32))
            normed_one[at : at + size, :] = (
                normal * vec(self.first_gain) + vec(self.first_shift)
            ).astype(BF16)
        if t.spread > rows:
            fill = (3 * t.width // 128, t.spread - rows, 128)
            self.joint_wide[:, rows : t.spread, :] = jnp.zeros(fill, F32)

    def joint_tile(self, n):
        cols = pl.ds(pl.multiple_of(n * TILE, TILE), TILE)
        product = mm(self.normed_one[...], self.joint_weight.get()[:, cols])
        put_tiles(self.joint_wide, n, self.t.rows, product)

    def ready(self):
        t, padded = self.t, self.t.padded
        self.masks = head_masks()
        key_at = lax.broadcasted_iota(jnp.int32, (padded, 2 * padded), 0)
        query_at = lax.broadcasted_iota(jnp.int32, (padded, 2 * padded), 1)
        query_at = jnp.where(query_at < padded, query_at, query_at - padded)
        self.valid = key_at <= query_at if t.causal else key_at < t.length

    def attend(self, b):
        t, joint, masks = self.t, self.joint, self.masks
        width, padded = t.width, t.padded
        pairs = range(t.heads // 2)
        some = pl.ds(b, padded, stride=BATCH)
        for c in range(3 * width // 128):
            joint[b, :, 128 * c : 128 * c + 128] = self.joint_wide[c, some, :].astype(BF16)
        scores = []
        for p in pairs:
            at = 128 * p
            queries = joint[b, :, at : at + 128]
            keys = joint[b, :, width + at : width + at + 128]
            scores.append(mm_nt(keys, two_heads(queries, masks)) * 0.125)
        lows = []
        for p in pairs:
            score = jnp.where(self.valid, scores[p], -1e30)
            raised = jnp.exp(score - jnp.max(score, axis=0, keepdims=True))
            low = (raised * (1.0 / column_sum(raised))).astype(BF16)
            self.probs[b, p] = low
            lows.append(low)
        for p in pairs:
            at = 2 * width + 128 * p
            both = mm_tn(lows[p], joint[b, :, at : at + 128])
            self.context_wide[p, some, :] = own_head(both, padded)

    def mix(self):
        t, rows, width = self.t, self.t.rows, self.t.width
        context, mixed = self.context, self.mixed
        self.staged[1].done()
        self.staged[2].done()
        for p in range(t.heads // 2):
            context[:, 128 * p : 128 * p + 128] = self.context_wide[p, 0:rows, :].astype(BF16)
        turn(self.normed_one, self.turned.at[0:width])
        turn(context, self.turned.at[width : 2 * width])
        self.staged[0].done()
        output_weight = self.output_weight.get()

        def mix_step(n, cols):
            mixed[:, cols] = mm(context[...], output_weight[:, cols])

        tile_loop(width, mix_step)
        for at, size in chunks(t.real):
            mixed[at : at + size, :] += self.tokens[at : at + size, :].astype(F32)
        for b in range(BATCH):
            row = mixed[pl.ds(pooled_row(t, self.lengths, b), 1), :]
            self.mixed_row[b : b + 1, :] = row
        mixed[t.real : rows, :] = jnp.zeros((rows - t.real, width), F32)
        mixed[t.extra : t.extra + BATCH, :] = self.mixed_row[...]
        self.staged[3].done()

    def embed(self):
        t, kept = self.t, self.kept
        row = self.mixed_row[...]
        normal, _ = normalise(row)
        normed = (normal * vec(self.second_gain) + vec(self.second_shift)).astype(BF16)
        wide = mm(normed, self.widen.get()[...])
        kept[:, row_part(t, "wide")] = wide
        active = (wide * sigmoid(1.702 * wide)).astype(BF16)
        last = row + mm(active, self.narrow.get()[...])
        kept[:, row_part(t, "pooled")] = last
        normal, _ = normalise(last)
        normed = (normal * vec(self.final_gain) + vec(self.final_shift)).astype(BF16)
        raw = mm(normed, self.projection.get()[...])
        kept[:, row_part(t, "raw")] = raw
        factor = lax.rsqrt(jnp.sum(raw * raw, axis=-1, keepdims=True) + 1e-06)
        unit = (raw * factor).astype(BF16)
        self.unit[...] = unit
        kept[:, row_part(t, "unit")] = unit.astype(F32)
        return unit


def fronts_kernel(scalars, held, lazies, outs, scratch):
    order = [5, 6, 0, 7, 8, 9, 1, 2, 3, 4]
    weights = [lazies[order.index(i)] for i in range(10)]
    image, text = [
        Front(
            t,
            scalars[0],
            held[8 * i : 8 * i + 8],
            weights[5 * i : 5 * i + 5],
            outs[5 * i : 5 * i + 5],
            outs[10],
            scratch[4 * i : 4 * i + 4],
        )
        for i, t in enumerate((IMAGE, TEXT))
    ]
    text.norm()
    for n in range(3 * TEXT.width // TILE):
        text.joint_tile(n)
    image.norm()
    for front in (image, text):
        front.ready()
    image.joint_weight.get()
    tiles = 3 * IMAGE.width // TILE

    def both(b):
        text.attend(b)
        image.joint_tile(b)

    loop(BATCH, both, UNROLL_HEADS)
    for n in range(BATCH, tiles):
        image.joint_tile(n)
    text.mix()
    loop(BATCH, image.attend, UNROLL_HEADS)
    image.mix()
    for i, unit in enumerate((image.embed(), text.embed())):
        outs[11][:, :, EMBED * i : EMBED * i + EMBED] = jnp.broadcast_to(unit[None], (DEVS, *unit.shape))


def middle_kernel(
    t,
    place,
    lengths,
    mixed,
    block_grad,
    second_gain,
    second_shift,
    widen_weight,
    narrow_weight,
    normed_turned,
    active_turned,
    wide_own,
    wide_send,
    narrow_own,
    narrow_send,
    mixed_grad,
    gain_grad,
    shift_grad,
    normed_two,
    narrow_in,
    wide_in,
):
    step = pl.program_id(0)
    half_steps = pl.num_programs(0) // 2

    @pl.when(step == 0)
    def _():
        wide_in[t.real : t.rows, :] = jnp.zeros((t.rows - t.real, t.width), F32)
        for at, size in chunks(t.rows):
            normal, _ = normalise(mixed[at : at + size, :])
            normed_two[at : at + size, :] = (normal * vec(second_gain) + vec(second_shift)).astype(
                BF16
            )
        turn(normed_two, normed_turned)
        for at, size in chunks(t.real):
            wide_in[at : at + size, :] = block_grad[at : at + size, :].astype(F32)
        for b in range(BATCH):
            wide_in[pl.ds(pooled_row(t, lengths, b), 1), :] = jnp.zeros((1, t.width), F32)
        narrow_in[...] = wide_in[...].astype(BF16)
        cols = t.width // 2
        own = pl.multiple_of(place[0] * cols, 128)
        narrow_own[...] = narrow_in[:, pl.ds(own, cols)]
        narrow_send[...] = narrow_in[:, pl.ds(pl.multiple_of(cols - own, 128), cols)]
        mixed_grad[...] = jnp.zeros_like(mixed_grad)

    lows = []
    for at, size in chunks(t.step, TILE):
        some = slice(at, at + size)
        wide = mm(normed_two[...], widen_weight[:, some])
        back = mm_nt(narrow_in[...], narrow_weight[some, :])
        sig = sigmoid(1.702 * wide)
        active = wide * sig
        active_turned[some, 0 : t.rows] = active.astype(BF16).T
        slope = sig + 1.702 * active * (1.0 - sig)
        lows.append((back * slope).astype(BF16))
    low = jnp.concatenate(lows, axis=1)
    mixed_grad[...] += mm_nt(low, widen_weight[...])

    @pl.when(step < half_steps)
    def _():
        wide_own[...] = low

    @pl.when(step >= half_steps)
    def _():
        wide_send[...] = low

    @pl.when(step == pl.num_programs(0) - 1)
    def _():
        gain = shift = 0.0
        for at, size in chunks(t.rows):
            some = slice(at, at + size)
            normal, inverse = normalise(mixed[some, :])
            up = mixed_grad[some, :]
            gain += column_sum(up * normal)
            shift += column_sum(up)
            mixed_grad[some, :] = wide_in[some, :] + norm_back(
                up, vec(second_gain), normal, inverse
            )
        gain_grad[...] = gain
        shift_grad[...] = shift


def split_dot(weights, right):
    high = weights.astype(BF16)
    rest = weights - high.astype(F32)
    middle = rest.astype(BF16)
    low = (rest - middle.astype(F32)).astype(BF16)
    return mm(high, right) + mm(middle, right) + mm(low, right)


def head_back(
    unit_grad,
    raw,
    pooled,
    mixed_row,
    wide_row,
    grad_row,
    final_gain,
    final_shift,
    second_gain,
    second_shift,
    projection,
    widen_weight,
    narrow_weight,
    outs,
):
    (
        final_gain_grad,
        final_shift_grad,
        second_gain_grad,
        second_shift_grad,
        factors,
        mixed_grad_row,
        narrow_in_row,
        wide_grad_row,
    ) = outs
    own = slice(0, BATCH)
    width = pooled.shape[1]
    factor = lax.rsqrt(jnp.sum(raw * raw, axis=-1, keepdims=True) + 1e-06)
    raw_grad = factor * unit_grad - raw * (factor * factor * factor) * jnp.sum(
        unit_grad * raw, axis=-1, keepdims=True
    )
    raw_grad = raw_grad.astype(BF16)
    factors[:, width:] = raw_grad.astype(F32)
    normal, inverse = normalise(pooled)
    factors[:, 0:width] = (normal * final_gain + final_shift).astype(BF16).astype(F32)
    up = mm_nt(raw_grad, projection.get()[...])
    final_gain_grad[...] = column_sum((up * normal)[own])
    final_shift_grad[...] = column_sum(up[own])
    out_grad = grad_row + norm_back(up, final_gain, normal, inverse)
    narrow_in = out_grad.astype(BF16)
    narrow_in_row[...] = narrow_in.astype(F32)
    sig = sigmoid(1.702 * wide_row)
    slope = sig + 1.702 * wide_row * sig * (1.0 - sig)
    low = (mm_nt(narrow_in, narrow_weight.get()[...]) * slope).astype(BF16)
    wide_grad_row[...] = low.astype(F32)
    up = mm_nt(low, widen_weight.get()[...])
    normal, inverse = normalise(mixed_row)
    second_gain_grad[...] = column_sum((up * normal)[own])
    second_shift_grad[...] = column_sum(up[own])
    mixed_grad_row[...] = (out_grad + norm_back(up, second_gain, normal, inverse))[own]


def kept_rows(own, other, t, name):
    some = row_part(t, name)
    return jnp.concatenate([own[:, some], other[:, some]], axis=0)


def head_of(t, unit_grad, kept, vectors, weights, outs):
    values = [kept_rows(*kept, t, name) for name in ("raw", "pooled", "mixed", "wide", "grad")]
    values += [vec(ref) for ref in vectors]
    projection, narrow, widen = weights
    head_back(unit_grad, *values, projection, widen, narrow, outs)


def pair_kernel(scalars, held, lazies, outs, scratch):
    place, log_scale = scalars
    own, other, kept_own, kept_other = held[:4]
    loss, scale_grad, text_grad = outs[:3]
    kept = (kept_own, kept_other)
    half = own.shape[0]
    pairs = 2 * half
    scale = jnp.exp(jnp.full((1, 1), log_scale[0], F32))
    blocks = (own, other)

    def totals(left_at, right_at):
        sums, moments = [], []
        for right in blocks:
            column, moment = None, None
            for left in blocks:
                for piece in range(0, half, 256):
                    sims = scale * mm_nt(
                        left[piece : piece + 256, left_at : left_at + EMBED],
                        right[:, right_at : right_at + EMBED],
                    )
                    raised = jnp.exp(sims)
                    add, more = column_sum(raised), column_sum(raised * sims)
                    column = add if column is None else column + add
                    moment = more if moment is None else moment + more
            sums.append(column)
            moments.append(moment)
        return sums, moments

    column_sums, column_moments = totals(0, EMBED)
    row_sums, row_moments = totals(EMBED, 0)
    log_total = jnp.zeros((1, 1), F32)
    weighted = jnp.zeros((1, 1), F32)
    trace = jnp.zeros((1, 1), F32)
    for i in range(2):
        for total, moment in ((column_sums[i], column_moments[i]), (row_sums[i], row_moments[i])):
            log_total += jnp.sum(jnp.log(total), axis=-1, keepdims=True)
            weighted += jnp.sum(moment / total, axis=-1, keepdims=True)
        product = blocks[i][:, :EMBED].astype(F32) * blocks[i][:, EMBED:].astype(F32)
        trace += jnp.sum(column_sum(product), axis=-1, keepdims=True)
    trace = scale * trace
    loss[...] = jnp.broadcast_to((log_total - 2.0 * trace) / (2.0 * pairs), loss.shape)
    scale_grad[...] = jnp.broadcast_to((weighted - 2.0 * trace) / (2.0 * pairs), loss.shape)

    lane = lax.broadcasted_iota(jnp.int32, (2 * BATCH, half), 1)
    sub = lax.broadcasted_iota(jnp.int32, (2 * BATCH, half), 0)
    diagonal = place[1] * BATCH
    identity = [
        jnp.where(jnp.logical_and(lane == sub + diagonal, sub < BATCH), 2.0, 0.0),
        jnp.where(jnp.logical_and(lane == sub - BATCH + diagonal, sub >= BATCH), 2.0, 0.0),
    ]

    def grads(t, at, other_sums):
        unit = kept_rows(*kept, t, "unit").astype(BF16)
        raised = [jnp.exp(scale * mm_nt(unit, block[:, at : at + EMBED])) for block in blocks]
        own_sum = sum(jnp.sum(r, axis=-1, keepdims=True) for r in raised)
        result = None
        for i in range(2):
            weight = raised[i] * (1.0 / own_sum + 1.0 / other_sums[i]) - identity[i]
            weight = weight / (2.0 * pairs)
            part = split_dot(weight, blocks[i][:, at : at + EMBED])
            result = part if result is None else result + part
        return scale * result

    image_grad = grads(IMAGE, EMBED, column_sums)
    text_grad[...] = grads(TEXT, 0, row_sums)
    head_of(IMAGE, image_grad, kept, held[4:8], lazies, outs[3:11])


class Back:
    def __init__(self, t, place, lengths, held, lazies, outs, scratch):
        self.t = t
        self.place = place
        self.lengths = lengths
        self.tokens, self.first_gain, self.row = held[:3]
        self.output_weight, self.mixed_grad, self.joint_in, self.probs_in, self.joint_weight = lazies
        self.own, self.send, self.tokens_out, self.gain_grad, self.shift_grad = outs
        self.context_grad, self.joint_grad, self.normed_grad, self.grads = scratch

    def context(self):
        t, rows, width, grads = self.t, self.t.rows, self.t.width, self.grads
        self.grad = grad = self.mixed_grad.get()
        for b in range(BATCH):
            grad[pl.ds(pooled_row(t, self.lengths, b), 1), :] = self.row[b : b + 1, :]
        mixed_low = slice(3 * width, 4 * width)
        grads[:, mixed_low] = grad[...].astype(BF16)
        if t.spread > rows:
            fill = (width // 128, t.spread - rows, 128)
            self.context_grad[:, rows : t.spread, :] = jnp.zeros(fill, F32)
        output_weight = self.output_weight.get()

        def step(n, cols):
            put_tiles(self.context_grad, n, rows, mm_nt(grads[:, mixed_low], output_weight[cols, :]))

        tile_loop(width, step)
        self.masks = head_masks()
        self.joint, self.probs = self.joint_in.get(), self.probs_in.get()

    def attend(self, b):
        t, masks, joint, joint_grad = self.t, self.masks, self.joint, self.joint_grad
        width, padded = t.width, t.padded
        pairs = range(t.heads // 2)
        some = pl.ds(b, padded, stride=BATCH)
        ups = [two_heads(self.context_grad[p, some, :].astype(BF16), masks) for p in pairs]
        backs = []
        for p in pairs:
            at = 2 * width + 128 * p
            backs.append(mm_nt(joint[b, :, at : at + 128], ups[p]))
        lows = []
        for p in pairs:
            wide = self.probs[b, p].astype(F32)
            back = wide * (backs[p] - column_sum(backs[p] * wide))
            lows.append(back.astype(BF16))
        for p in pairs:
            at = 128 * p
            queries = joint[b, :, at : at + 128]
            keys = joint[b, :, width + at : width + at + 128]
            joint_grad[2 * len(pairs) + p, some, :] = mm(self.probs[b, p], ups[p])
            joint_grad[len(pairs) + p, some, :] = mm(lows[p], two_heads(queries, masks)) * 0.125
            joint_grad[p, some, :] = own_head(mm_tn(lows[p], keys), padded) * 0.125

    def finish(self):
        t, rows, width, grads = self.t, self.t.rows, self.t.width, self.grads
        for c in range(3 * width // 128):
            grads[:, 128 * c : 128 * c + 128] = self.joint_grad[c, 0:rows, :].astype(BF16)
        start = pl.multiple_of(self.place[0] * (2 * width), 128)
        self.own.send(grads.at[:, pl.ds(start, 2 * width)], self.own.out)
        start = pl.multiple_of(2 * width - start, 128)
        self.send.send(grads.at[:, pl.ds(start, 2 * width)], self.send.out)
        joint_weight = self.joint_weight.get()

        def step(n, cols):
            self.normed_grad[:, cols] = mm_nt(grads[:, 0 : 3 * width], joint_weight[cols, :])

        tile_loop(width, step)
        gain = shift = 0.0
        for at, size in chunks(t.real):
            some = slice(at, at + size)
            normal, inverse = normalise(self.tokens[some, :].astype(F32))
            up = self.normed_grad[some, :]
            gain += column_sum(up * normal)
            shift += column_sum(up)
            self.tokens_out.ref[some, :] = self.grad[some, :] + norm_back(
                up, vec(self.first_gain), normal, inverse
            )
        self.gain_grad[...] = gain
        self.shift_grad[...] = shift
        self.tokens_out.done()


def backs_kernel(scalars, held, lazies, outs, scratch):
    head_in, held = held[:7], held[7:]
    head_weights, lazies = lazies[:3], lazies[3:]
    head_outs, outs = outs[:8], outs[8:]
    head_of(TEXT, head_in[0][...], head_in[1:3], head_in[3:7], head_weights, head_outs)
    order = [5, 6, 0, 1, 7, 8, 2, 3, 9, 4]
    lazies = [lazies[order.index(i)] for i in range(10)]
    held = [*held[:3], *held[3:5], head_outs[5]]
    image, text = [
        Back(
            t,
            *scalars,
            held[3 * i : 3 * i + 3],
            lazies[5 * i : 5 * i + 5],
            outs[5 * i : 5 * i + 5],
            scratch[4 * i : 4 * i + 4],
        )
        for i, t in enumerate((IMAGE, TEXT))
    ]
    text.context()
    image.context()

    def both(b):
        text.attend(b)
        image.attend(b)

    loop(BATCH, both, UNROLL_BACK)
    text.finish()
    image.finish()


def turn(source, target):
    def step(n):
        cols = pl.ds(pl.multiple_of(n * 128, 128), 128)
        target[cols, 0 : source.shape[0]] = source[:, cols].T

    loop(source.shape[1] // 128, step, UNROLL_TURN)


def lanes_down(values):
    return jnp.concatenate(
        [values[:, :, at : at + 128] for at in range(0, values.shape[2], 128)], axis=1
    )


def put(out, device, unit, values):
    count = values.shape[1] // 16
    size = values.shape[0]
    values = values.reshape(size, count, 16, 128).astype(BF16)
    out[pl.ds(device, size), unit : unit + count] = values


def pack_twelve(first, second, out, unit=0, each=4):
    cols = first.shape[1]
    count = cols // 128
    sub = lax.broadcasted_iota(jnp.int32, (each, 8, cols), 1) < 4

    def step(e):
        rows = pl.ds(pl.multiple_of(e * (24 * each), 8), 24 * each)
        x = first[rows, :].reshape(each, 24, cols)
        y = second[rows, :].reshape(each, 24, cols)
        left, right = x[:, 8:16], y[:, 8:16]
        even = jnp.where(sub, left, pltpu.roll(right, 4, 1))
        odd = jnp.where(sub, pltpu.roll(left, 4, 1), right)
        parts = []
        for a, b, c in ((x[:, 0:8], y[:, 0:8], even), (x[:, 16:24], y[:, 16:24], odd)):
            parts.append(jnp.concatenate([lanes_down(v) for v in (a, b, c)], axis=1))
        if parts[0].shape[1] % 16:
            fill = jnp.zeros((each, 16 - parts[0].shape[1] % 16, 128), F32)
            parts = [jnp.concatenate([part, fill], axis=1) for part in parts]
        height = parts[0].shape[1]
        values = jnp.stack(parts, axis=1).reshape(2 * each, height, 128)
        put(out, e * (2 * each), unit, values)

    loop(32 // each, step, UNROLL_PACK)


def pack_rows(result, rows, out, unit=0, each=8, device=0):
    total = result.shape[0] // rows
    cols = result.shape[1]

    def step(e):
        some = pl.ds(pl.multiple_of(e * (rows * each), 8), rows * each)
        values = lanes_down(result[some, :].reshape(each, rows, cols))
        put(out, device + e * each, unit, values)

    loop(total // each, step, UNROLL_PACK)


def put_extra(t, ref, rows):
    rows = jnp.concatenate([rows, jnp.zeros_like(rows)], axis=0)
    ref[t.extra : t.extra + 16, :] = rows.astype(BF16)


def wide_grads(t, half, product, send, at, first, second):
    if t is IMAGE:
        for i in range(3):
            first[...] = product(256 * i, 256)
            second[...] = product(768 + 256 * i, 256)
            pack_twelve(first, second, send.ref, 3 * i)
            units = slice(3 * i, 3 * i + 3)
            send.units_done(slice(None), units, slice(at + 3 * i, at + 3 * i + 3))
    else:
        for i in range(2):
            first[...] = product(512 * i, 512)
            pack_rows(first, 8, send.ref, 2 * i)
            units = slice(2 * i, 2 * i + 2)
            send.units_done(slice(None), units, slice(at + 2 * i, at + 2 * i + 2))


def feed_kernel(t, at, scalars, held, lazies, outs, scratch):
    (place,) = scalars
    wide_rows, narrow_rows = held
    normed, wides, narrows = lazies[0:2], lazies[2:4], lazies[4:6]
    actives = lazies[6:14]
    (out,) = outs
    first, second, narrow_result = scratch

    def patch(refs, rows):
        size = rows.shape[1] // 2
        some = pl.ds(pl.multiple_of(place[0] * size, 128), size)
        for side, ref in enumerate(refs):
            put_extra(t, ref.get(), rows[BATCH * side : BATCH * side + BATCH, some])

    patch(wides, wide_rows)
    lefts = [ref.get() for ref in normed]
    wides = [ref.get() for ref in wides]

    def product(tile, size):
        return sum(mm(a[:, 0 : t.rows], b[:, tile : tile + size]) for a, b in zip(lefts, wides))

    wide_grads(t, place[0], product, out, at, first, second)
    patch(narrows, narrow_rows)
    narrows = [ref.get() for ref in narrows]
    wide_units, units = (9, 9) if t is IMAGE else (4, 4)
    some = slice(wide_units, wide_units + units)
    for j in range(4):
        pair = [actives[2 * j].get(), actives[2 * j + 1].get()]
        narrow_result[...] = sum(mm(a[:, 0 : t.rows], b[...]) for a, b in zip(pair, narrows))
        pack_rows(narrow_result, t.hidden // DEVS, out.ref, wide_units, 4, 16 * j)
        out.units_done(
            slice(16 * j, 16 * j + 16), some, slice(at + wide_units, at + wide_units + units)
        )


def rest_kernel(scalars, held, lazies, outs, scratch):
    (place,) = scalars
    (out,) = outs
    first, second, third = scratch[:3]
    misc_scratch, spread = scratch[3:6], scratch[6]
    half = place[0]
    misc, text_stage, image_stage = [Staged(out.out, ref, out.sems, out.pending) for ref in scratch[7:10]]
    misc_grads(half, held[:2], held[2:], misc, misc_scratch, spread)
    for t, ins, stage, results in (
        (TEXT, lazies[0:4], text_stage, (third, None)),
        (IMAGE, lazies[4:8], image_stage, (first, second)),
    ):
        width = t.width
        lefts, rights = [ref.get() for ref in ins[0::2]], [ref.get() for ref in ins[1::2]]

        def product(tile, size):
            late = jnp.where(half * (2 * width) + tile >= 3 * width, width, 0)
            rows = pl.ds(pl.multiple_of(late, 128), width)
            return sum(
                mm(a[rows, 0 : t.rows], b[:, tile : tile + size]) for a, b in zip(lefts, rights)
            )

        wide_grads(t, half, product, stage, REST_AT["image" if t is IMAGE else "text"], *results)


IMAGE_FEED_UNITS = 18
LATE_UNITS = 24
TEXT_FEED_AT = 0
REST_AT = {"text": 8, "image": 15}
MISC_AT = 12


def misc_grads(half, factors, vectors, out, scratch, spread):
    image_factors, text_factors = factors
    first, second, third = scratch

    def product(t, ref, at, size):
        final = ref[:, 0 : t.width].astype(BF16)
        start = pl.multiple_of(t.width + half * 256 + at, 128)
        return mm_tn(final, ref[:, pl.ds(start, size)].astype(BF16))

    first[...] = product(IMAGE, image_factors, 0, 128)
    second[...] = product(IMAGE, image_factors, 128, 128)
    third[...] = product(TEXT, text_factors, 0, 256)
    pack_twelve(first, second, out.ref, 1, 8)
    pack_rows(third, 8, out.ref, 0)
    spread[...] = jnp.zeros_like(spread)
    for side, refs_of, width in ((0, vectors[:8], 768), (64, vectors[8:], 512)):
        each = width // DEVS
        device = lax.broadcasted_iota(jnp.int32, (DEVS, width), 0)
        column = lax.broadcasted_iota(jnp.int32, (DEVS, width), 1)
        mine = jnp.logical_and(column >= device * each, column < device * each + each)
        source = lax.broadcasted_iota(jnp.int32, (width, 128), 0)
        lane = lax.broadcasted_iota(jnp.int32, (width, 128), 1)
        at = lax.rem(source, each)
        high_at = jnp.where(lane == at + side, 1.0, 0.0).astype(BF16)
        low_at = jnp.where(lane == at + side + 32, 1.0, 0.0).astype(BF16)
        rows = [refs_of[0][...], refs_of[1][...], refs_of[2][...] + refs_of[3][...]]
        rows += [refs_of[4][...] + refs_of[5][...], refs_of[6][...], refs_of[7][...]]
        for k, row in enumerate(rows):
            row = jnp.where(mine, row, 0.0)
            high = row.astype(BF16)
            low = (row - high.astype(F32)).astype(BF16)
            spread[:, 8 + k, :] += mm(high, high_at) + mm(low, low_at)
    out.ref[:, 2] = (out.ref[:, 2].astype(F32) + spread[...]).astype(BF16)
    out.units_done(slice(None), slice(0, 3), slice(MISC_AT, MISC_AT + 3))


def unpack_kernel(place, feed_mine, late_mine, feed_other, late_other, *outs):
    (
        image_joint,
        image_output,
        image_widen,
        image_narrow,
        image_projection,
        text_joint,
        text_output,
        text_widen,
        text_narrow,
        text_projection,
    ) = outs[:10]
    odd = place[1] % 2

    def emit(half, feed, late):
        def into(ref, col, body, tail):
            @pl.when(odd == 0)
            def _():
                ref[0:8, col : col + 128] = body
                ref[8:12, col : col + 128] = tail

            @pl.when(odd == 1)
            def _():
                ref[0:4, col : col + 128] = tail
                ref[4:12, col : col + 128] = body

        def image_wide(source, at, store):
            for tile in range(3):
                block = source[16 * (at + 3 * tile) : 16 * (at + 3 * tile) + 48, :]
                for side in range(2):
                    for g in range(2):
                        body = block[16 * side + 8 * g : 16 * side + 8 * g + 8]
                        tail = block[32 + 8 * g + 4 * side : 36 + 8 * g + 4 * side]
                        store(half * 1536 + side * 768 + tile * 256 + g * 128, body, tail)

        def joint_store(col, body, tail):
            if col < 2304:
                into(image_joint, col, body, tail)
            else:
                into(image_output, col - 2304, body, tail)

        image_wide(feed, 0, functools.partial(into, image_widen))
        image_wide(late, REST_AT["image"], joint_store)
        at = 16 * 9
        for g in range(3):
            col = half * 384 + 128 * g
            image_narrow[:, col : col + 128] = feed[at + 48 * g : at + 48 * g + 48, :]
        at = 16 * (MISC_AT + 1)
        for side in range(2):
            col = half * 256 + 128 * side
            tail = late[at + 16 + 4 * side : at + 20 + 4 * side, :]
            into(image_projection, col, late[at + 8 * side : at + 8 * side + 8, :], tail)
        for g in range(8):
            col = half * 1024 + 128 * g
            at = 16 * TEXT_FEED_AT + 8 * g
            text_widen[:, col : col + 128] = late[at : at + 8, :]
            at = 16 * REST_AT["text"] + 8 * g
            block = late[at : at + 8, :]
            if col < 1536:
                text_joint[:, col : col + 128] = block
            else:
                text_output[:, col - 1536 : col - 1408] = block
        for g in range(2):
            col = half * 256 + 128 * g
            at = 16 * (TEXT_FEED_AT + 4) + 32 * g
            text_narrow[:, col : col + 128] = late[at : at + 32, :]
            at = 16 * MISC_AT + 8 * g
            text_projection[:, col : col + 128] = late[at : at + 8, :]

    for half in range(2):

        @pl.when(place[0] == half)
        def _():
            emit(half, feed_mine, late_mine)
            emit(1 - half, feed_other, late_other)

    at = 16 * (MISC_AT + 2) + 8
    vectors = late_mine[at : at + 8, :] + late_other[at : at + 8, :]
    for k in range(12):
        each, side = (12, 0) if k < 6 else (8, 64)
        row = vectors[k % 6 : k % 6 + 1, :]
        outs[10 + k][...] = row[:, side : side + each] + row[:, side + 32 : side + 32 + each]


SMEM = pl.BlockSpec(memory_space=pltpu.SMEM)
VMEM = pl.BlockSpec(memory_space=pltpu.VMEM)


def call(body, name, scalars, arrays, outs, scratch=(), flops=1 << 32):
    return pl.pallas_call(
        body,
        name=name,
        out_shape=tuple(jax.ShapeDtypeStruct(shape, kind) for shape, kind in outs),
        in_specs=[SMEM] * len(scalars) + [VMEM] * len(arrays),
        out_specs=tuple(VMEM for _ in outs),
        scratch_shapes=[pltpu.VMEM(shape, kind) for shape, kind in scratch],
        compiler_params=pltpu.CompilerParams(vmem_limit_bytes=VMEM_LIMIT),
        cost_estimate=pl.CostEstimate(flops=flops, bytes_accessed=20 << 20, transcendentals=0),
    )(*scalars, *arrays)


BIG = 1 << 18


def lazy_call(body, name, scalars, held, lazies, outs, scratch=(), flops=1 << 33, buffer=None, after=(), ahead=3):
    many = 24

    def kernel(*refs):
        refs = list(refs)

        def take(count):
            got = refs[:count]
            del refs[:count]
            return got

        scalar_refs, held_refs = take(len(scalars)), take(len(held))
        sources = take(len(lazies))
        take(len(after) + (buffer is not None))
        out_refs = take(len(outs))
        targets = take(len(lazies))
        stages = take(sum(1 for out in outs if out[2]))
        scratch_refs = take(len(scratch))
        in_sems, out_sems = refs
        lazy = []
        for i, (source, target, (_, index, _)) in enumerate(zip(sources, targets, lazies)):
            if index is not None:
                source = source.at[index(*scalar_refs)]
            lazy.append(Lazy(lazy, source, target, in_sems.at[i]))
        for item in lazy[:ahead]:
            item.start()
        pending = []
        results = []
        for out, ref in zip(outs, out_refs):
            if out[2] is None:
                results.append(ref)
            else:
                results.append(Staged(ref, stages.pop(0) if out[2] else None, out_sems, pending))
        body(scalar_refs, held_refs, lazy, results, scratch_refs)
        for item in lazy:
            if item.started:
                item.get()
        for copy in pending:
            copy.wait()

    any_spec = pl.BlockSpec(memory_space=pl.ANY)
    scratch_shapes = [pltpu.VMEM(shape, array.dtype) for array, _, shape in lazies]
    scratch_shapes += [pltpu.VMEM(stage, kind) for _, kind, stage in outs if stage]
    scratch_shapes += [pltpu.VMEM(shape, kind) for shape, kind in scratch]
    scratch_shapes += [pltpu.SemaphoreType.DMA((max(1, len(lazies)),)), pltpu.SemaphoreType.DMA((many,))]
    arrays = [*held, *[array for array, _, _ in lazies], *after]
    specs = [SMEM] * len(scalars) + [VMEM] * len(held) + [any_spec] * (len(lazies) + len(after))
    aliases = {}
    if buffer is not None:
        aliases = {len(scalars) + len(arrays): 0}
        arrays.append(buffer)
        specs.append(any_spec)
    return pl.pallas_call(
        kernel,
        name=name,
        out_shape=tuple(jax.ShapeDtypeStruct(shape, kind) for shape, kind, _ in outs),
        in_specs=specs,
        out_specs=tuple(VMEM if stage is None else any_spec for _, _, stage in outs),
        scratch_shapes=scratch_shapes,
        input_output_aliases=aliases,
        compiler_params=pltpu.CompilerParams(vmem_limit_bytes=VMEM_LIMIT),
        cost_estimate=pl.CostEstimate(flops=flops, bytes_accessed=20 << 20, transcendentals=0),
    )(*scalars, *arrays)


def all_of(array):
    return array, None, array.shape


def staged(shape, kind):
    return shape, kind, shape


def plain(shape, kind):
    return shape, kind, None


def fronts_call(lengths, tokens, block_grads, weights):
    held, lazies, outs, scratch = [], [], [], []
    for t, token, grad, w in zip((IMAGE, TEXT), tokens, block_grads, weights):
        rows, width, hidden = t.rows, t.width, t.hidden
        held += [token, w[0], w[1], w[4], w[5], w[8], w[9], grad]
        lazies += [all_of(w[i]) for i in (2, 3, 6, 7, 10)]
        outs += [
            staged((2 * width, t.lanes), BF16),
            staged((BATCH, t.padded, 3 * width), BF16),
            staged((BATCH, t.heads // 2, t.padded, 2 * t.padded), BF16),
            staged((rows, width), F32),
            plain((BATCH, EMBED), BF16),
        ]
        scratch += [
            ((3 * width // 128, t.spread, 128), F32),
            ((width // 128, t.spread, 128), F32),
            ((rows, width), BF16),
            ((rows, width), BF16),
        ]
    lazies = [lazies[i] for i in (5, 6, 0, 7, 8, 9, 1, 2, 3, 4)]
    outs.append(plain((BATCH, ROW_TOTAL), F32))
    outs.append(plain((DEVS, BATCH, 2 * EMBED), BF16))
    results = lazy_call(fronts_kernel, "fronts", (lengths,), held, lazies, outs, scratch, ahead=6)
    return results[:5], results[5:10], results[10], results[11]


def middle(t, name, place, lengths, mixed, block_grad, gain, shift, widen, narrow, after):
    rows, width, hidden = t.rows, t.width, t.hidden
    steps = hidden // t.step
    outs = (
        ((width, t.lanes), BF16),
        ((hidden, t.lanes), BF16),
        ((rows, hidden // 2), BF16),
        ((rows, hidden // 2), BF16),
        ((rows, width // 2), BF16),
        ((rows, width // 2), BF16),
        ((rows, width), F32),
        ((1, width), F32),
        ((1, width), F32),
    )

    def held(shape):
        return pl.BlockSpec(shape, lambda i, *_: (0,) * len(shape))

    def tile(i, place):
        return lax.rem(i + place[0] * (steps // 2), steps)

    out_specs = [held(shape) for shape, _ in outs]
    out_specs[1] = pl.BlockSpec((t.step, t.lanes), lambda i, place, lengths: (tile(i, place), 0))
    out_specs[2] = pl.BlockSpec((rows, t.step), lambda i, *_: (0, jnp.minimum(i, steps // 2 - 1)))
    out_specs[3] = pl.BlockSpec((rows, t.step), lambda i, *_: (0, jnp.maximum(i - steps // 2, 0)))
    in_specs = [held(a.shape) for a in (mixed, block_grad, gain, shift)]
    in_specs.append(pl.BlockSpec((width, t.step), lambda i, place, lengths: (0, tile(i, place))))
    in_specs.append(pl.BlockSpec((t.step, width), lambda i, place, lengths: (tile(i, place), 0)))
    in_specs += [pl.BlockSpec(memory_space=pl.ANY)] * len(after)

    def kernel(*refs):
        middle_kernel(t, *refs[:8], *refs[8 + len(after) :])

    return pl.pallas_call(
        kernel,
        name=name + "_middle",
        out_shape=tuple(jax.ShapeDtypeStruct(shape, kind) for shape, kind in outs),
        grid_spec=pltpu.PrefetchScalarGridSpec(
            num_scalar_prefetch=2,
            grid=(steps,),
            in_specs=in_specs,
            out_specs=tuple(out_specs),
            scratch_shapes=[
                pltpu.VMEM((rows, width), BF16),
                pltpu.VMEM((rows, width), BF16),
                pltpu.VMEM((rows, width), F32),
            ],
        ),
        compiler_params=pltpu.CompilerParams(vmem_limit_bytes=VMEM_LIMIT),
        cost_estimate=pl.CostEstimate(flops=1 << 35, bytes_accessed=20 << 20, transcendentals=0),
    )(place, lengths, mixed, block_grad, gain, shift, widen, narrow, *after)


def head_outs(t):
    return [plain((1, t.width), F32)] * 4 + [
        plain((2 * BATCH, t.width + EMBED), F32),
        plain((BATCH, t.width), F32),
        plain((2 * BATCH, t.width), F32),
        plain((2 * BATCH, t.hidden), F32),
    ]


def backs_call(place, lengths, head_in, head_weights, image_row, towers, after):
    held, lazies, outs, scratch = [*head_in], [], head_outs(TEXT), []
    for t, (tokens, gain, arrays) in zip((IMAGE, TEXT), towers):
        rows, width = t.rows, t.width
        held += [tokens, gain]
        if t is IMAGE:
            held.append(image_row)
        lazies += [all_of(a) for a in arrays]
        outs += [
            ((rows, 2 * width), BF16, ()),
            ((rows, 2 * width), BF16, ()),
            staged((t.real, width), F32),
            plain((1, width), F32),
            plain((1, width), F32),
        ]
        scratch += [
            ((width // 128, t.spread, 128), F32),
            ((3 * width // 128, t.spread, 128), F32),
            ((rows, width), F32),
            ((rows, 4 * width), BF16),
        ]
    lazies = [lazies[i] for i in (5, 6, 0, 1, 7, 8, 2, 3, 9, 4)]
    lazies = [all_of(w) for w in head_weights] + lazies
    results = lazy_call(
        backs_kernel, "backs", (place, lengths), held, lazies, outs, scratch, after=after, ahead=8
    )
    return results[:8], results[8:13], results[13:]


def feed(t, place, head, middle, other, buffer, after):
    rows, width = t.rows, t.width
    name = "image" if t is IMAGE else "text"
    own = (middle[0], middle[1], middle[2], middle[4])
    lazies = [all_of(own[0]), all_of(other[0]), all_of(own[2]), all_of(other[2])]
    lazies += [all_of(own[3]), all_of(other[3])]
    for j in range(4):
        some = slice(width * j, width * j + width)
        for side in (own, other):
            lazies.append((side[1], lambda *_, some=some: (some, slice(None)), (width, t.lanes)))
    cols = 256 if t is IMAGE else 512
    scratch = [
        ((width, cols), F32),
        ((width, cols) if t is IMAGE else (8, 128), F32),
        ((width, width // 2), F32),
    ]
    units = IMAGE_FEED_UNITS if t is IMAGE else 8
    total = LATE_UNITS if buffer else units
    (out,) = lazy_call(
        functools.partial(feed_kernel, t, TEXT_FEED_AT if buffer else 0),
        name + "_feed",
        (place,),
        (head[7], head[6]),
        lazies,
        [((DEVS, total, 16, 128), BF16, (DEVS, units, 16, 128))],
        scratch,
        after=after,
        ahead=10,
    )
    return out


def rest(place, factors, vectors, sides, buffer):
    lazies = []
    for own, other in (sides[1], sides[0]):
        lazies += [all_of(a) for a in (*own, *other)]
    outs = [((DEVS, LATE_UNITS, 16, 128), BF16, ())]
    scratch = [
        ((768, 256), F32),
        ((768, 256), F32),
        ((512, 512), F32),
        ((768, 128), F32),
        ((768, 128), F32),
        ((512, 256), F32),
        ((DEVS, 16, 128), F32),
        ((DEVS, 3, 16, 128), BF16),
        ((DEVS, 4, 16, 128), BF16),
        ((DEVS, 9, 16, 128), BF16),
    ]
    (out,) = lazy_call(
        rest_kernel, "rest", (place,), [*factors, *vectors], lazies, outs, scratch, buffer=buffer, ahead=4
    )
    return out


def sum_blocks(received, step):
    devices, units = received.shape[:2]

    def body(scalars, held, lazies, outs, scratch):
        for i, block in enumerate(lazies):
            total = jnp.sum(block.get()[...].astype(F32), axis=0)
            outs[0][16 * step * i : 16 * step * (i + 1), :] = total.reshape(16 * step, 128)

    lazies = []
    for at in range(0, units, step):
        some = slice(at, at + step)
        lazies.append((received, lambda *_, some=some: (slice(None), some), (devices, step, 16, 128)))
    outs = [plain((16 * units, 128), F32)]
    return lazy_call(body, "sum_blocks", (), (), lazies, outs, flops=1 << 34, ahead=len(lazies))[0]


def behind(arrays, after):
    def kernel(*refs):
        pass

    any_spec = pl.BlockSpec(memory_space=pl.ANY)
    return pl.pallas_call(
        kernel,
        name="behind",
        out_shape=[jax.ShapeDtypeStruct(array.shape, array.dtype) for array in arrays],
        in_specs=[any_spec] * (len(arrays) + len(after)),
        out_specs=[any_spec] * len(arrays),
        input_output_aliases={i: i for i in range(len(arrays))},
    )(*arrays, *after)


SWAP = [(0, 1), (1, 0)]


def by_token(tokens):
    return tokens.transpose(1, 0, 2).reshape(-1, tokens.shape[2])


def shards(*args):
    image_tokens, image_weights, image_block_grad = args[0], args[1:12], args[12]
    text_tokens, caption_lengths = args[13], args[14]
    text_weights, text_block_grad, log_scale = args[15:26], args[26], args[27]
    core = lax.axis_index("tower")
    dp = lax.axis_index("dp")
    place = jnp.stack([core, dp]).astype(jnp.int32)
    tokens = (by_token(image_tokens), by_token(text_tokens))
    block_grads = (by_token(image_block_grad), by_token(text_block_grad))
    weights = (image_weights, text_weights)
    kinds = ((0, IMAGE, "image"), (1, TEXT, "text"))
    *fronts, kept, copies = fronts_call(caption_lengths, tokens, block_grads, weights)
    units = [f[4] for f in fronts]
    own = lax.all_to_all(copies, "dp", 0, 0, tiled=True).reshape(DEVS * BATCH, 2 * EMBED)

    def swap(*arrays):
        return [lax.ppermute(array, "tower", SWAP) for array in arrays]

    def middle_of(i, after):
        _, t, name = kinds[i]
        w = weights[i]
        return middle(
            t, name, place, caption_lengths, fronts[i][3], block_grads[i], w[4], w[5], w[6], w[7], after
        )

    (kept_other,) = swap(kept)
    image_middle = list(middle_of(0, ()))
    (own,) = behind([own], (image_middle[0], kept_other))
    (other,) = swap(own)
    sent = (0, 1, 3, 5)
    for k, array in zip(sent, behind([image_middle[k] for k in sent], (other,))):
        image_middle[k] = array
    image_sent = swap(*[image_middle[k] for k in sent])

    w = image_weights
    paired = lazy_call(
        pair_kernel,
        "pairs",
        (place, log_scale),
        [own, other, kept, kept_other, w[8], w[9], w[4], w[5]],
        [all_of(w[10]), all_of(w[7]), all_of(w[6])],
        [plain((1, 128), F32), plain((1, 128), F32), plain((2 * BATCH, EMBED), F32), *head_outs(IMAGE)],
        ahead=6,
    )
    loss, scale_grad = paired[0][0, :1], paired[1][0, :1]
    image_head = paired[3:]
    image_feed = feed(IMAGE, place, image_head, image_middle, image_sent, False, ())
    feed_total = lax.all_to_all(image_feed, "dp", 0, 0, tiled=True)
    text_middle = middle_of(1, (image_feed,))
    middles = (image_middle, text_middle)

    back_in = []
    for i, _, _ in kinds:
        f, m, w = fronts[i], middles[i], weights[i]
        back_in.append((tokens[i], w[0], (w[3], m[6], f[1], f[2], w[2])))
    w = text_weights
    text_head, *backs = backs_call(
        place,
        caption_lengths,
        [paired[2], kept, kept_other, w[8], w[9], w[4], w[5]],
        [w[10], w[7], w[6]],
        image_head[5],
        back_in,
        (text_middle[0],),
    )
    heads = (image_head, text_head)
    text_sent = swap(*[text_middle[k] for k in sent])
    late = feed(TEXT, place, heads[1], text_middle, text_sent, True, (backs[1][0],))
    sides = []
    for f, k in zip(fronts, backs):
        sides.append(((f[0], k[0]), swap(f[0], k[1])))
    vectors = []
    for m, h, k in zip(middles, heads, backs):
        vectors += [k[3], k[4], m[7], h[2], m[8], h[3], h[0], h[1]]
    factors = [heads[0][4], heads[1][4]]
    (late,) = behind([rest(place, factors, vectors, sides, late)], (feed_total,))
    late_total = lax.all_to_all(late, "dp", 0, 0, tiled=True)
    feed_mine = sum_blocks(feed_total, 3)
    (feed_theirs,) = swap(feed_mine)
    (late_total,) = behind([late_total], (feed_theirs,))
    late_mine = sum_blocks(late_total, 4)
    (late_theirs,) = swap(late_mine)
    mine, theirs = (feed_mine, late_mine), (feed_theirs, late_theirs)
    weight_outs = (
        ((12, 2304), F32),
        ((12, 768), F32),
        ((12, 3072), F32),
        ((48, 768), F32),
        ((12, 512), F32),
        ((8, 1536), F32),
        ((8, 512), F32),
        ((8, 2048), F32),
        ((32, 512), F32),
        ((8, 512), F32),
    )
    vector_outs = (((1, 12), F32),) * 6 + (((1, 8), F32),) * 6
    grads = call(unpack_kernel, "unpack", (place,), (*mine, *theirs), weight_outs + vector_outs)

    def ordered(vectors, weights):
        joint, output, widen, narrow, projection = weights
        v = [x.reshape(-1) for x in vectors]
        return [v[0], v[1], joint, output, v[2], v[3], widen, narrow, v[4], v[5], projection]

    def by_sequence(t, grad):
        return grad.reshape(t.length, BATCH, t.width).transpose(1, 0, 2)

    return (
        loss,
        units[0],
        units[1],
        by_sequence(IMAGE, backs[0][2]),
        *ordered(grads[10:16], grads[:5]),
        by_sequence(TEXT, backs[1][2]),
        *ordered(grads[16:22], grads[5:10]),
        scale_grad,
    )


def solution(mesh):
    spread = P(("tower", "dp"), None, None)
    weights = [P()] * 11
    placed = (spread, *weights, spread, spread, P(("tower", "dp")), *weights, spread, P())
    vector, matrix = P("dp"), P("dp", None)
    grads = [vector, vector, matrix, matrix, vector, vector, matrix, matrix, vector, vector, matrix]
    units = P(("tower", "dp"), None)
    return jax.shard_map(
        shards,
        mesh=mesh,
        in_specs=placed,
        out_specs=(P(), units, units, spread, *grads, spread, *grads, P()),
        check_vma=False,
    )
```

```python
import functools

import jax
import jax.numpy as jnp
from jax import lax
from jax.experimental import pallas as pl
from jax.experimental.pallas import tpu as pltpu
from jax.sharding import PartitionSpec as P

F32 = jnp.float32
BF16 = jnp.bfloat16
BATCH = 8
EMBED = 512
TILE = 256
DEVS = 64


class Tower:
    def __init__(self, width, heads, hidden, length, padded, rows, extra, causal):
        self.width = width
        self.heads = heads
        self.hidden = hidden
        self.length = length
        self.padded = padded
        self.real = BATCH * length
        self.rows = rows
        self.extra = extra
        self.spread = BATCH * padded
        self.lanes = -(-rows // 128) * 128
        self.causal = causal
        self.step = 768 if width == 768 else 512


IMAGE = Tower(768, 12, 3072, 50, 64, 416, 400, False)
TEXT = Tower(512, 8, 2048, 77, 80, 640, 624, True)

VMEM_LIMIT = 64 * 1024 * 1024


def mm(left, right):
    return lax.dot_general(left, right, (((1,), (0,)), ((), ())), preferred_element_type=F32)


def mm_nt(left, right):
    return lax.dot_general(left, right, (((1,), (1,)), ((), ())), preferred_element_type=F32)


def mm_tn(left, right):
    return lax.dot_general(left, right, (((0,), (0,)), ((), ())), preferred_element_type=F32)


def normalise(values):
    centre = jnp.mean(values, axis=-1, keepdims=True)
    offset = values - centre
    inverse = lax.rsqrt(jnp.mean(offset * offset, axis=-1, keepdims=True) + 1e-05)
    return offset * inverse, inverse


def norm_back(upstream, gain, normal, inverse):
    scaled = upstream * gain
    inner = (
        scaled
        - jnp.mean(scaled, axis=-1, keepdims=True)
        - normal * jnp.mean(scaled * normal, axis=-1, keepdims=True)
    )
    return inner * inverse


def column_sum(values):
    return jnp.sum(values, axis=0, keepdims=True)


def sigmoid(values):
    return 0.5 + 0.5 * jnp.tanh(0.5 * values)


def vec(ref):
    return ref[...].reshape(1, -1)


def chunks(count, size=128):
    return [(at, min(size, count - at)) for at in range(0, count, size)]


UNROLL_TILE, UNROLL_HEADS, UNROLL_PACK, UNROLL_TURN = 9, 8, 4, 3
UNROLL_BACK = 1


def loop(count, body, unroll=1):
    def step(i, carry):
        body(i)
        return carry

    lax.fori_loop(0, count, step, 0, unroll=min(unroll, count))


def tile_loop(width, body):
    loop(width // TILE, lambda n: body(n, pl.ds(pl.multiple_of(n * TILE, TILE), TILE)), UNROLL_TILE)


def put_tiles(ref, n, rows, values):
    for i in range(TILE // 128):
        ref[n * (TILE // 128) + i, 0:rows, :] = values[:, 128 * i : 128 * i + 128]


class Lazy:
    def __init__(self, queue, source, target, sem):
        self.copy = pltpu.make_async_copy(source, target, sem)
        self.target = target
        self.queue = queue
        self.started = self.waited = False

    def start(self):
        if not self.started:
            self.copy.start()
            self.started = True

    def get(self):
        if not self.waited:
            self.start()
            self.copy.wait()
            self.waited = True
            for item in self.queue:
                if not item.started:
                    item.start()
                    break
        return self.target


class Staged:
    def __init__(self, out, stage, sems, pending):
        self.out = out
        self.ref = stage
        self.sems = sems
        self.pending = pending

    def send(self, source, target):
        copy = pltpu.make_async_copy(source, target, self.sems.at[len(self.pending)])
        copy.start()
        self.pending.append(copy)

    def done(self):
        self.send(self.ref, self.out)

    def units_done(self, devices, units, out_units):
        self.send(self.ref.at[devices, units], self.out.at[devices, out_units])


def head_masks():
    lane = lax.broadcasted_iota(jnp.int32, (1, 128), 1)
    first = jnp.where(lane < 64, 1.0, 0.0).astype(BF16)
    second = jnp.where(lane < 64, 0.0, 1.0).astype(BF16)
    return first, second


def two_heads(values, masks):
    return jnp.concatenate([values * masks[0], values * masks[1]], axis=0)


def own_head(values, padded):
    lane = lax.broadcasted_iota(jnp.int32, (padded, 128), 1)
    return jnp.where(lane < 64, values[:padded], values[padded:])


def pooled_row(t, lengths, b):
    return b if t is IMAGE else (lengths[b] - 1) * BATCH + b


def row_parts(t):
    return {
        "raw": EMBED,
        "unit": EMBED,
        "pooled": t.width,
        "mixed": t.width,
        "grad": t.width,
        "wide": t.hidden,
    }


def row_part(t, name):
    at = 0 if t is IMAGE else sum(row_parts(IMAGE).values())
    for part, size in row_parts(t).items():
        if part == name:
            return slice(at, at + size)
        at += size


ROW_TOTAL = sum(row_parts(IMAGE).values()) + sum(row_parts(TEXT).values())


class Front:
    def __init__(self, t, lengths, ins, weights, outs, kept, scratch):
        self.t = t
        self.lengths = lengths
        (
            self.tokens,
            self.first_gain,
            self.first_shift,
            self.second_gain,
            self.second_shift,
            self.final_gain,
            self.final_shift,
            self.block_grad,
        ) = ins
        self.joint_weight, self.output_weight, self.widen, self.narrow, self.projection = weights
        self.staged = outs[:4]
        self.turned, self.joint, self.probs, self.mixed = [out.ref for out in outs[:4]]
        self.unit = outs[4]
        self.kept = kept
        self.joint_wide, self.context_wide, self.normed_one, self.context = scratch
        self.mixed_row = kept.at[:, row_part(t, "mixed")]

    def norm(self):
        t, rows = self.t, self.t.rows
        mixed, normed_one = self.mixed, self.normed_one
        grad_row = self.kept.at[:, row_part(t, "grad")]
        for at, size in chunks(t.real):
            mixed[at : at + size, :] = self.block_grad[at : at + size, :].astype(F32)
        for b in range(BATCH):
            grad_row[b : b + 1, :] = mixed[pl.ds(pooled_row(t, self.lengths, b), 1), :]
        pad = t.real - t.real % 16
        normed_one[pad:rows, :] = jnp.zeros((rows - pad, t.width), BF16)
        for at, size in chunks(t.real):
            normal, _ = normalise(self.tokens[at : at + size, :].astype(F32))
            normed_one[at : at + size, :] = (
                normal * vec(self.first_gain) + vec(self.first_shift)
            ).astype(BF16)
        if t.spread > rows:
            fill = (3 * t.width // 128, t.spread - rows, 128)
            self.joint_wide[:, rows : t.spread, :] = jnp.zeros(fill, F32)

    def joint_tile(self, n):
        cols = pl.ds(pl.multiple_of(n * TILE, TILE), TILE)
        product = mm(self.normed_one[...], self.joint_weight.get()[:, cols])
        put_tiles(self.joint_wide, n, self.t.rows, product)

    def ready(self):
        t, padded = self.t, self.t.padded
        self.masks = head_masks()
        key_at = lax.broadcasted_iota(jnp.int32, (padded, 2 * padded), 0)
        query_at = lax.broadcasted_iota(jnp.int32, (padded, 2 * padded), 1)
        query_at = jnp.where(query_at < padded, query_at, query_at - padded)
        self.valid = key_at <= query_at if t.causal else key_at < t.length

    def attend(self, b):
        t, joint, masks = self.t, self.joint, self.masks
        width, padded = t.width, t.padded
        pairs = range(t.heads // 2)
        some = pl.ds(b, padded, stride=BATCH)
        for c in range(3 * width // 128):
            joint[b, :, 128 * c : 128 * c + 128] = self.joint_wide[c, some, :].astype(BF16)
        scores = []
        for p in pairs:
            at = 128 * p
            queries = joint[b, :, at : at + 128]
            keys = joint[b, :, width + at : width + at + 128]
            scores.append(mm_nt(keys, two_heads(queries, masks)) * 0.125)
        lows = []
        for p in pairs:
            score = jnp.where(self.valid, scores[p], -1e30)
            raised = jnp.exp(score - jnp.max(score, axis=0, keepdims=True))
            low = (raised * (1.0 / column_sum(raised))).astype(BF16)
            self.probs[b, p] = low
            lows.append(low)
        for p in pairs:
            at = 2 * width + 128 * p
            both = mm_tn(lows[p], joint[b, :, at : at + 128])
            self.context_wide[p, some, :] = own_head(both, padded)

    def mix(self):
        t, rows, width = self.t, self.t.rows, self.t.width
        context, mixed = self.context, self.mixed
        self.staged[1].done()
        self.staged[2].done()
        for p in range(t.heads // 2):
            context[:, 128 * p : 128 * p + 128] = self.context_wide[p, 0:rows, :].astype(BF16)
        turn(self.normed_one, self.turned.at[0:width])
        turn(context, self.turned.at[width : 2 * width])
        self.staged[0].done()
        output_weight = self.output_weight.get()

        def mix_step(n, cols):
            mixed[:, cols] = mm(context[...], output_weight[:, cols])

        tile_loop(width, mix_step)
        for at, size in chunks(t.real):
            mixed[at : at + size, :] += self.tokens[at : at + size, :].astype(F32)
        for b in range(BATCH):
            row = mixed[pl.ds(pooled_row(t, self.lengths, b), 1), :]
            self.mixed_row[b : b + 1, :] = row
        mixed[t.real : rows, :] = jnp.zeros((rows - t.real, width), F32)
        mixed[t.extra : t.extra + BATCH, :] = self.mixed_row[...]
        self.staged[3].done()

    def embed(self):
        t, kept = self.t, self.kept
        row = self.mixed_row[...]
        normal, _ = normalise(row)
        normed = (normal * vec(self.second_gain) + vec(self.second_shift)).astype(BF16)
        wide = mm(normed, self.widen.get()[...])
        kept[:, row_part(t, "wide")] = wide
        active = (wide * sigmoid(1.702 * wide)).astype(BF16)
        last = row + mm(active, self.narrow.get()[...])
        kept[:, row_part(t, "pooled")] = last
        normal, _ = normalise(last)
        normed = (normal * vec(self.final_gain) + vec(self.final_shift)).astype(BF16)
        raw = mm(normed, self.projection.get()[...])
        kept[:, row_part(t, "raw")] = raw
        factor = lax.rsqrt(jnp.sum(raw * raw, axis=-1, keepdims=True) + 1e-06)
        unit = (raw * factor).astype(BF16)
        self.unit[...] = unit
        kept[:, row_part(t, "unit")] = unit.astype(F32)
        return unit


def fronts_kernel(scalars, held, lazies, outs, scratch):
    order = [5, 6, 0, 7, 8, 9, 1, 2, 3, 4]
    weights = [lazies[order.index(i)] for i in range(10)]
    image, text = [
        Front(
            t,
            scalars[0],
            held[8 * i : 8 * i + 8],
            weights[5 * i : 5 * i + 5],
            outs[5 * i : 5 * i + 5],
            outs[10],
            scratch[4 * i : 4 * i + 4],
        )
        for i, t in enumerate((IMAGE, TEXT))
    ]
    text.norm()
    for n in range(3 * TEXT.width // TILE):
        text.joint_tile(n)
    image.norm()
    for front in (image, text):
        front.ready()
    image.joint_weight.get()
    tiles = 3 * IMAGE.width // TILE

    def both(b):
        text.attend(b)
        image.joint_tile(b)

    loop(BATCH, both, UNROLL_HEADS)
    for n in range(BATCH, tiles):
        image.joint_tile(n)
    text.mix()
    loop(BATCH, image.attend, UNROLL_HEADS)
    image.mix()
    for i, unit in enumerate((image.embed(), text.embed())):
        outs[11][:, :, EMBED * i : EMBED * i + EMBED] = jnp.broadcast_to(unit[None], (DEVS, *unit.shape))


def middle_kernel(
    t,
    place,
    lengths,
    mixed,
    block_grad,
    second_gain,
    second_shift,
    widen_weight,
    narrow_weight,
    normed_turned,
    active_turned,
    wide_own,
    wide_send,
    narrow_own,
    narrow_send,
    mixed_grad,
    gain_grad,
    shift_grad,
    normed_two,
    narrow_in,
    wide_in,
):
    step = pl.program_id(0)
    half_steps = pl.num_programs(0) // 2

    @pl.when(step == 0)
    def _():
        wide_in[t.real : t.rows, :] = jnp.zeros((t.rows - t.real, t.width), F32)
        for at, size in chunks(t.rows):
            normal, _ = normalise(mixed[at : at + size, :])
            normed_two[at : at + size, :] = (normal * vec(second_gain) + vec(second_shift)).astype(
                BF16
            )
        turn(normed_two, normed_turned)
        for at, size in chunks(t.real):
            wide_in[at : at + size, :] = block_grad[at : at + size, :].astype(F32)
        for b in range(BATCH):
            wide_in[pl.ds(pooled_row(t, lengths, b), 1), :] = jnp.zeros((1, t.width), F32)
        narrow_in[...] = wide_in[...].astype(BF16)
        cols = t.width // 2
        own = pl.multiple_of(place[0] * cols, 128)
        narrow_own[...] = narrow_in[:, pl.ds(own, cols)]
        narrow_send[...] = narrow_in[:, pl.ds(pl.multiple_of(cols - own, 128), cols)]
        mixed_grad[...] = jnp.zeros_like(mixed_grad)

    lows = []
    for at, size in chunks(t.step, TILE):
        some = slice(at, at + size)
        wide = mm(normed_two[...], widen_weight[:, some])
        back = mm_nt(narrow_in[...], narrow_weight[some, :])
        sig = sigmoid(1.702 * wide)
        active = wide * sig
        active_turned[some, 0 : t.rows] = active.astype(BF16).T
        slope = sig + 1.702 * active * (1.0 - sig)
        lows.append((back * slope).astype(BF16))
    low = jnp.concatenate(lows, axis=1)
    mixed_grad[...] += mm_nt(low, widen_weight[...])

    @pl.when(step < half_steps)
    def _():
        wide_own[...] = low

    @pl.when(step >= half_steps)
    def _():
        wide_send[...] = low

    @pl.when(step == pl.num_programs(0) - 1)
    def _():
        gain = shift = 0.0
        for at, size in chunks(t.rows):
            some = slice(at, at + size)
            normal, inverse = normalise(mixed[some, :])
            up = mixed_grad[some, :]
            gain += column_sum(up * normal)
            shift += column_sum(up)
            mixed_grad[some, :] = wide_in[some, :] + norm_back(
                up, vec(second_gain), normal, inverse
            )
        gain_grad[...] = gain
        shift_grad[...] = shift


def split_dot(weights, right):
    high = weights.astype(BF16)
    rest = weights - high.astype(F32)
    middle = rest.astype(BF16)
    low = (rest - middle.astype(F32)).astype(BF16)
    return mm(high, right) + mm(middle, right) + mm(low, right)


def head_back(
    unit_grad,
    raw,
    pooled,
    mixed_row,
    wide_row,
    grad_row,
    final_gain,
    final_shift,
    second_gain,
    second_shift,
    projection,
    widen_weight,
    narrow_weight,
    outs,
):
    (
        final_gain_grad,
        final_shift_grad,
        second_gain_grad,
        second_shift_grad,
        factors,
        mixed_grad_row,
        narrow_in_row,
        wide_grad_row,
    ) = outs
    own = slice(0, BATCH)
    width = pooled.shape[1]
    factor = lax.rsqrt(jnp.sum(raw * raw, axis=-1, keepdims=True) + 1e-06)
    raw_grad = factor * unit_grad - raw * (factor * factor * factor) * jnp.sum(
        unit_grad * raw, axis=-1, keepdims=True
    )
    raw_grad = raw_grad.astype(BF16)
    factors[:, width:] = raw_grad.astype(F32)
    normal, inverse = normalise(pooled)
    factors[:, 0:width] = (normal * final_gain + final_shift).astype(BF16).astype(F32)
    up = mm_nt(raw_grad, projection.get()[...])
    final_gain_grad[...] = column_sum((up * normal)[own])
    final_shift_grad[...] = column_sum(up[own])
    out_grad = grad_row + norm_back(up, final_gain, normal, inverse)
    narrow_in = out_grad.astype(BF16)
    narrow_in_row[...] = narrow_in.astype(F32)
    sig = sigmoid(1.702 * wide_row)
    slope = sig + 1.702 * wide_row * sig * (1.0 - sig)
    low = (mm_nt(narrow_in, narrow_weight.get()[...]) * slope).astype(BF16)
    wide_grad_row[...] = low.astype(F32)
    up = mm_nt(low, widen_weight.get()[...])
    normal, inverse = normalise(mixed_row)
    second_gain_grad[...] = column_sum((up * normal)[own])
    second_shift_grad[...] = column_sum(up[own])
    mixed_grad_row[...] = (out_grad + norm_back(up, second_gain, normal, inverse))[own]


def kept_rows(own, other, t, name):
    some = row_part(t, name)
    return jnp.concatenate([own[:, some], other[:, some]], axis=0)


def head_of(t, unit_grad, kept, vectors, weights, outs):
    values = [kept_rows(*kept, t, name) for name in ("raw", "pooled", "mixed", "wide", "grad")]
    values += [vec(ref) for ref in vectors]
    projection, narrow, widen = weights
    head_back(unit_grad, *values, projection, widen, narrow, outs)


def pair_kernel(scalars, held, lazies, outs, scratch):
    place, log_scale = scalars
    own, other, kept_own, kept_other = held[:4]
    loss, scale_grad, text_grad = outs[:3]
    kept = (kept_own, kept_other)
    half = own.shape[0]
    pairs = 2 * half
    scale = jnp.exp(jnp.full((1, 1), log_scale[0], F32))
    blocks = (own, other)

    def totals(left_at, right_at):
        sums, moments = [], []
        for right in blocks:
            column, moment = None, None
            for left in blocks:
                for piece in range(0, half, 256):
                    sims = scale * mm_nt(
                        left[piece : piece + 256, left_at : left_at + EMBED],
                        right[:, right_at : right_at + EMBED],
                    )
                    raised = jnp.exp(sims)
                    add, more = column_sum(raised), column_sum(raised * sims)
                    column = add if column is None else column + add
                    moment = more if moment is None else moment + more
            sums.append(column)
            moments.append(moment)
        return sums, moments

    column_sums, column_moments = totals(0, EMBED)
    row_sums, row_moments = totals(EMBED, 0)
    log_total = jnp.zeros((1, 1), F32)
    weighted = jnp.zeros((1, 1), F32)
    trace = jnp.zeros((1, 1), F32)
    for i in range(2):
        for total, moment in ((column_sums[i], column_moments[i]), (row_sums[i], row_moments[i])):
            log_total += jnp.sum(jnp.log(total), axis=-1, keepdims=True)
            weighted += jnp.sum(moment / total, axis=-1, keepdims=True)
        product = blocks[i][:, :EMBED].astype(F32) * blocks[i][:, EMBED:].astype(F32)
        trace += jnp.sum(column_sum(product), axis=-1, keepdims=True)
    trace = scale * trace
    loss[...] = jnp.broadcast_to((log_total - 2.0 * trace) / (2.0 * pairs), loss.shape)
    scale_grad[...] = jnp.broadcast_to((weighted - 2.0 * trace) / (2.0 * pairs), loss.shape)

    lane = lax.broadcasted_iota(jnp.int32, (2 * BATCH, half), 1)
    sub = lax.broadcasted_iota(jnp.int32, (2 * BATCH, half), 0)
    diagonal = place[1] * BATCH
    identity = [
        jnp.where(jnp.logical_and(lane == sub + diagonal, sub < BATCH), 2.0, 0.0),
        jnp.where(jnp.logical_and(lane == sub - BATCH + diagonal, sub >= BATCH), 2.0, 0.0),
    ]

    def grads(t, at, other_sums):
        unit = kept_rows(*kept, t, "unit").astype(BF16)
        raised = [jnp.exp(scale * mm_nt(unit, block[:, at : at + EMBED])) for block in blocks]
        own_sum = sum(jnp.sum(r, axis=-1, keepdims=True) for r in raised)
        result = None
        for i in range(2):
            weight = raised[i] * (1.0 / own_sum + 1.0 / other_sums[i]) - identity[i]
            weight = weight / (2.0 * pairs)
            part = split_dot(weight, blocks[i][:, at : at + EMBED])
            result = part if result is None else result + part
        return scale * result

    image_grad = grads(IMAGE, EMBED, column_sums)
    text_grad[...] = grads(TEXT, 0, row_sums)
    head_of(IMAGE, image_grad, kept, held[4:8], lazies, outs[3:11])


class Back:
    def __init__(self, t, place, lengths, held, lazies, outs, scratch):
        self.t = t
        self.place = place
        self.lengths = lengths
        self.tokens, self.first_gain, self.row = held[:3]
        self.output_weight, self.mixed_grad, self.joint_in, self.probs_in, self.joint_weight = lazies
        self.own, self.send, self.tokens_out, self.gain_grad, self.shift_grad = outs
        self.context_grad, self.joint_grad, self.normed_grad, self.grads = scratch

    def context(self):
        t, rows, width, grads = self.t, self.t.rows, self.t.width, self.grads
        self.grad = grad = self.mixed_grad.get()
        for b in range(BATCH):
            grad[pl.ds(pooled_row(t, self.lengths, b), 1), :] = self.row[b : b + 1, :]
        mixed_low = slice(3 * width, 4 * width)
        grads[:, mixed_low] = grad[...].astype(BF16)
        if t.spread > rows:
            fill = (width // 128, t.spread - rows, 128)
            self.context_grad[:, rows : t.spread, :] = jnp.zeros(fill, F32)
        output_weight = self.output_weight.get()

        def step(n, cols):
            put_tiles(self.context_grad, n, rows, mm_nt(grads[:, mixed_low], output_weight[cols, :]))

        tile_loop(width, step)
        self.masks = head_masks()
        self.joint, self.probs = self.joint_in.get(), self.probs_in.get()

    def attend(self, b):
        t, masks, joint, joint_grad = self.t, self.masks, self.joint, self.joint_grad
        width, padded = t.width, t.padded
        pairs = range(t.heads // 2)
        some = pl.ds(b, padded, stride=BATCH)
        ups = [two_heads(self.context_grad[p, some, :].astype(BF16), masks) for p in pairs]
        backs = []
        for p in pairs:
            at = 2 * width + 128 * p
            backs.append(mm_nt(joint[b, :, at : at + 128], ups[p]))
        lows = []
        for p in pairs:
            wide = self.probs[b, p].astype(F32)
            back = wide * (backs[p] - column_sum(backs[p] * wide))
            lows.append(back.astype(BF16))
        for p in pairs:
            at = 128 * p
            queries = joint[b, :, at : at + 128]
            keys = joint[b, :, width + at : width + at + 128]
            joint_grad[2 * len(pairs) + p, some, :] = mm(self.probs[b, p], ups[p])
            joint_grad[len(pairs) + p, some, :] = mm(lows[p], two_heads(queries, masks)) * 0.125
            joint_grad[p, some, :] = own_head(mm_tn(lows[p], keys), padded) * 0.125

    def finish(self):
        t, rows, width, grads = self.t, self.t.rows, self.t.width, self.grads
        for c in range(3 * width // 128):
            grads[:, 128 * c : 128 * c + 128] = self.joint_grad[c, 0:rows, :].astype(BF16)
        start = pl.multiple_of(self.place[0] * (2 * width), 128)
        self.own.send(grads.at[:, pl.ds(start, 2 * width)], self.own.out)
        start = pl.multiple_of(2 * width - start, 128)
        self.send.send(grads.at[:, pl.ds(start, 2 * width)], self.send.out)
        joint_weight = self.joint_weight.get()

        def step(n, cols):
            self.normed_grad[:, cols] = mm_nt(grads[:, 0 : 3 * width], joint_weight[cols, :])

        tile_loop(width, step)
        gain = shift = 0.0
        for at, size in chunks(t.real):
            some = slice(at, at + size)
            normal, inverse = normalise(self.tokens[some, :].astype(F32))
            up = self.normed_grad[some, :]
            gain += column_sum(up * normal)
            shift += column_sum(up)
            self.tokens_out.ref[some, :] = self.grad[some, :] + norm_back(
                up, vec(self.first_gain), normal, inverse
            )
        self.gain_grad[...] = gain
        self.shift_grad[...] = shift
        self.tokens_out.done()


def backs_kernel(scalars, held, lazies, outs, scratch):
    head_in, held = held[:7], held[7:]
    head_weights, lazies = lazies[:3], lazies[3:]
    head_outs, outs = outs[:8], outs[8:]
    head_of(TEXT, head_in[0][...], head_in[1:3], head_in[3:7], head_weights, head_outs)
    order = [5, 6, 0, 1, 7, 8, 2, 3, 9, 4]
    lazies = [lazies[order.index(i)] for i in range(10)]
    held = [*held[:3], *held[3:5], head_outs[5]]
    image, text = [
        Back(
            t,
            *scalars,
            held[3 * i : 3 * i + 3],
            lazies[5 * i : 5 * i + 5],
            outs[5 * i : 5 * i + 5],
            scratch[4 * i : 4 * i + 4],
        )
        for i, t in enumerate((IMAGE, TEXT))
    ]
    text.context()
    image.context()

    def both(b):
        text.attend(b)
        image.attend(b)

    loop(BATCH, both, UNROLL_BACK)
    text.finish()
    image.finish()


def turn(source, target):
    def step(n):
        cols = pl.ds(pl.multiple_of(n * 128, 128), 128)
        target[cols, 0 : source.shape[0]] = source[:, cols].T

    loop(source.shape[1] // 128, step, UNROLL_TURN)


def lanes_down(values):
    return jnp.concatenate(
        [values[:, :, at : at + 128] for at in range(0, values.shape[2], 128)], axis=1
    )


def put(out, device, unit, values):
    count = values.shape[1] // 16
    size = values.shape[0]
    values = values.reshape(size, count, 16, 128).astype(BF16)
    out[pl.ds(device, size), unit : unit + count] = values


def pack_twelve(first, second, out, unit=0, each=4):
    cols = first.shape[1]
    count = cols // 128
    sub = lax.broadcasted_iota(jnp.int32, (each, 8, cols), 1) < 4

    def step(e):
        rows = pl.ds(pl.multiple_of(e * (24 * each), 8), 24 * each)
        x = first[rows, :].reshape(each, 24, cols)
        y = second[rows, :].reshape(each, 24, cols)
        left, right = x[:, 8:16], y[:, 8:16]
        even = jnp.where(sub, left, pltpu.roll(right, 4, 1))
        odd = jnp.where(sub, pltpu.roll(left, 4, 1), right)
        parts = []
        for a, b, c in ((x[:, 0:8], y[:, 0:8], even), (x[:, 16:24], y[:, 16:24], odd)):
            parts.append(jnp.concatenate([lanes_down(v) for v in (a, b, c)], axis=1))
        if parts[0].shape[1] % 16:
            fill = jnp.zeros((each, 16 - parts[0].shape[1] % 16, 128), F32)
            parts = [jnp.concatenate([part, fill], axis=1) for part in parts]
        height = parts[0].shape[1]
        values = jnp.stack(parts, axis=1).reshape(2 * each, height, 128)
        put(out, e * (2 * each), unit, values)

    loop(32 // each, step, UNROLL_PACK)


def pack_rows(result, rows, out, unit=0, each=8, device=0):
    total = result.shape[0] // rows
    cols = result.shape[1]

    def step(e):
        some = pl.ds(pl.multiple_of(e * (rows * each), 8), rows * each)
        values = lanes_down(result[some, :].reshape(each, rows, cols))
        put(out, device + e * each, unit, values)

    loop(total // each, step, UNROLL_PACK)


def put_extra(t, ref, rows):
    rows = jnp.concatenate([rows, jnp.zeros_like(rows)], axis=0)
    ref[t.extra : t.extra + 16, :] = rows.astype(BF16)


def wide_grads(t, half, product, send, at, first, second):
    if t is IMAGE:
        for i in range(3):
            first[...] = product(256 * i, 256)
            second[...] = product(768 + 256 * i, 256)
            pack_twelve(first, second, send.ref, 3 * i)
            units = slice(3 * i, 3 * i + 3)
            send.units_done(slice(None), units, slice(at + 3 * i, at + 3 * i + 3))
    else:
        for i in range(2):
            first[...] = product(512 * i, 512)
            pack_rows(first, 8, send.ref, 2 * i)
            units = slice(2 * i, 2 * i + 2)
            send.units_done(slice(None), units, slice(at + 2 * i, at + 2 * i + 2))


def feed_kernel(t, at, scalars, held, lazies, outs, scratch):
    (place,) = scalars
    wide_rows, narrow_rows = held
    normed, wides, narrows = lazies[0:2], lazies[2:4], lazies[4:6]
    actives = lazies[6:14]
    (out,) = outs
    first, second, narrow_result = scratch

    def patch(refs, rows):
        size = rows.shape[1] // 2
        some = pl.ds(pl.multiple_of(place[0] * size, 128), size)
        for side, ref in enumerate(refs):
            put_extra(t, ref.get(), rows[BATCH * side : BATCH * side + BATCH, some])

    patch(wides, wide_rows)
    lefts = [ref.get() for ref in normed]
    wides = [ref.get() for ref in wides]

    def product(tile, size):
        return sum(mm(a[:, 0 : t.rows], b[:, tile : tile + size]) for a, b in zip(lefts, wides))

    wide_grads(t, place[0], product, out, at, first, second)
    patch(narrows, narrow_rows)
    narrows = [ref.get() for ref in narrows]
    wide_units, units = (9, 9) if t is IMAGE else (4, 4)
    some = slice(wide_units, wide_units + units)
    for j in range(4):
        pair = [actives[2 * j].get(), actives[2 * j + 1].get()]
        narrow_result[...] = sum(mm(a[:, 0 : t.rows], b[...]) for a, b in zip(pair, narrows))
        pack_rows(narrow_result, t.hidden // DEVS, out.ref, wide_units, 4, 16 * j)
        out.units_done(
            slice(16 * j, 16 * j + 16), some, slice(at + wide_units, at + wide_units + units)
        )


def rest_kernel(scalars, held, lazies, outs, scratch):
    (place,) = scalars
    (out,) = outs
    first, second, third = scratch[:3]
    misc_scratch, spread = scratch[3:6], scratch[6]
    half = place[0]
    misc, text_stage, image_stage = [Staged(out.out, ref, out.sems, out.pending) for ref in scratch[7:10]]
    misc_grads(half, held[:2], held[2:], misc, misc_scratch, spread)
    for t, ins, stage, results in (
        (TEXT, lazies[0:4], text_stage, (third, None)),
        (IMAGE, lazies[4:8], image_stage, (first, second)),
    ):
        width = t.width
        lefts, rights = [ref.get() for ref in ins[0::2]], [ref.get() for ref in ins[1::2]]

        def product(tile, size):
            late = jnp.where(half * (2 * width) + tile >= 3 * width, width, 0)
            rows = pl.ds(pl.multiple_of(late, 128), width)
            return sum(
                mm(a[rows, 0 : t.rows], b[:, tile : tile + size]) for a, b in zip(lefts, rights)
            )

        wide_grads(t, half, product, stage, REST_AT["image" if t is IMAGE else "text"], *results)


IMAGE_FEED_UNITS = 18
LATE_UNITS = 24
TEXT_FEED_AT = 0
REST_AT = {"text": 8, "image": 15}
MISC_AT = 12


def misc_grads(half, factors, vectors, out, scratch, spread):
    image_factors, text_factors = factors
    first, second, third = scratch

    def product(t, ref, at, size):
        final = ref[:, 0 : t.width].astype(BF16)
        start = pl.multiple_of(t.width + half * 256 + at, 128)
        return mm_tn(final, ref[:, pl.ds(start, size)].astype(BF16))

    first[...] = product(IMAGE, image_factors, 0, 128)
    second[...] = product(IMAGE, image_factors, 128, 128)
    third[...] = product(TEXT, text_factors, 0, 256)
    pack_twelve(first, second, out.ref, 1, 8)
    pack_rows(third, 8, out.ref, 0)
    spread[...] = jnp.zeros_like(spread)
    for side, refs_of, width in ((0, vectors[:8], 768), (64, vectors[8:], 512)):
        each = width // DEVS
        device = lax.broadcasted_iota(jnp.int32, (DEVS, width), 0)
        column = lax.broadcasted_iota(jnp.int32, (DEVS, width), 1)
        mine = jnp.logical_and(column >= device * each, column < device * each + each)
        source = lax.broadcasted_iota(jnp.int32, (width, 128), 0)
        lane = lax.broadcasted_iota(jnp.int32, (width, 128), 1)
        at = lax.rem(source, each)
        high_at = jnp.where(lane == at + side, 1.0, 0.0).astype(BF16)
        low_at = jnp.where(lane == at + side + 32, 1.0, 0.0).astype(BF16)
        rows = [refs_of[0][...], refs_of[1][...], refs_of[2][...] + refs_of[3][...]]
        rows += [refs_of[4][...] + refs_of[5][...], refs_of[6][...], refs_of[7][...]]
        for k, row in enumerate(rows):
            row = jnp.where(mine, row, 0.0)
            high = row.astype(BF16)
            low = (row - high.astype(F32)).astype(BF16)
            spread[:, 8 + k, :] += mm(high, high_at) + mm(low, low_at)
    out.ref[:, 2] = (out.ref[:, 2].astype(F32) + spread[...]).astype(BF16)
    out.units_done(slice(None), slice(0, 3), slice(MISC_AT, MISC_AT + 3))


def unpack_kernel(place, feed_mine, late_mine, feed_other, late_other, *outs):
    (
        image_joint,
        image_output,
        image_widen,
        image_narrow,
        image_projection,
        text_joint,
        text_output,
        text_widen,
        text_narrow,
        text_projection,
    ) = outs[:10]
    odd = place[1] % 2

    def emit(half, feed, late):
        def into(ref, col, body, tail):
            @pl.when(odd == 0)
            def _():
                ref[0:8, col : col + 128] = body
                ref[8:12, col : col + 128] = tail

            @pl.when(odd == 1)
            def _():
                ref[0:4, col : col + 128] = tail
                ref[4:12, col : col + 128] = body

        def image_wide(source, at, store):
            for tile in range(3):
                block = source[16 * (at + 3 * tile) : 16 * (at + 3 * tile) + 48, :]
                for side in range(2):
                    for g in range(2):
                        body = block[16 * side + 8 * g : 16 * side + 8 * g + 8]
                        tail = block[32 + 8 * g + 4 * side : 36 + 8 * g + 4 * side]
                        store(half * 1536 + side * 768 + tile * 256 + g * 128, body, tail)

        def joint_store(col, body, tail):
            if col < 2304:
                into(image_joint, col, body, tail)
            else:
                into(image_output, col - 2304, body, tail)

        image_wide(feed, 0, functools.partial(into, image_widen))
        image_wide(late, REST_AT["image"], joint_store)
        at = 16 * 9
        for g in range(3):
            col = half * 384 + 128 * g
            image_narrow[:, col : col + 128] = feed[at + 48 * g : at + 48 * g + 48, :]
        at = 16 * (MISC_AT + 1)
        for side in range(2):
            col = half * 256 + 128 * side
            tail = late[at + 16 + 4 * side : at + 20 + 4 * side, :]
            into(image_projection, col, late[at + 8 * side : at + 8 * side + 8, :], tail)
        for g in range(8):
            col = half * 1024 + 128 * g
            at = 16 * TEXT_FEED_AT + 8 * g
            text_widen[:, col : col + 128] = late[at : at + 8, :]
            at = 16 * REST_AT["text"] + 8 * g
            block = late[at : at + 8, :]
            if col < 1536:
                text_joint[:, col : col + 128] = block
            else:
                text_output[:, col - 1536 : col - 1408] = block
        for g in range(2):
            col = half * 256 + 128 * g
            at = 16 * (TEXT_FEED_AT + 4) + 32 * g
            text_narrow[:, col : col + 128] = late[at : at + 32, :]
            at = 16 * MISC_AT + 8 * g
            text_projection[:, col : col + 128] = late[at : at + 8, :]

    for half in range(2):

        @pl.when(place[0] == half)
        def _():
            emit(half, feed_mine, late_mine)
            emit(1 - half, feed_other, late_other)

    at = 16 * (MISC_AT + 2) + 8
    vectors = late_mine[at : at + 8, :] + late_other[at : at + 8, :]
    for k in range(12):
        each, side = (12, 0) if k < 6 else (8, 64)
        row = vectors[k % 6 : k % 6 + 1, :]
        outs[10 + k][...] = row[:, side : side + each] + row[:, side + 32 : side + 32 + each]


SMEM = pl.BlockSpec(memory_space=pltpu.SMEM)
VMEM = pl.BlockSpec(memory_space=pltpu.VMEM)


def call(body, name, scalars, arrays, outs, scratch=(), flops=1 << 32):
    return pl.pallas_call(
        body,
        name=name,
        out_shape=tuple(jax.ShapeDtypeStruct(shape, kind) for shape, kind in outs),
        in_specs=[SMEM] * len(scalars) + [VMEM] * len(arrays),
        out_specs=tuple(VMEM for _ in outs),
        scratch_shapes=[pltpu.VMEM(shape, kind) for shape, kind in scratch],
        compiler_params=pltpu.CompilerParams(vmem_limit_bytes=VMEM_LIMIT),
        cost_estimate=pl.CostEstimate(flops=flops, bytes_accessed=20 << 20, transcendentals=0),
    )(*scalars, *arrays)


BIG = 1 << 18


def lazy_call(body, name, scalars, held, lazies, outs, scratch=(), flops=1 << 33, buffer=None, after=(), ahead=3):
    many = 24

    def kernel(*refs):
        refs = list(refs)

        def take(count):
            got = refs[:count]
            del refs[:count]
            return got

        scalar_refs, held_refs = take(len(scalars)), take(len(held))
        sources = take(len(lazies))
        take(len(after) + (buffer is not None))
        out_refs = take(len(outs))
        targets = take(len(lazies))
        stages = take(sum(1 for out in outs if out[2]))
        scratch_refs = take(len(scratch))
        in_sems, out_sems = refs
        lazy = []
        for i, (source, target, (_, index, _)) in enumerate(zip(sources, targets, lazies)):
            if index is not None:
                source = source.at[index(*scalar_refs)]
            lazy.append(Lazy(lazy, source, target, in_sems.at[i]))
        for item in lazy[:ahead]:
            item.start()
        pending = []
        results = []
        for out, ref in zip(outs, out_refs):
            if out[2] is None:
                results.append(ref)
            else:
                results.append(Staged(ref, stages.pop(0) if out[2] else None, out_sems, pending))
        body(scalar_refs, held_refs, lazy, results, scratch_refs)
        for item in lazy:
            if item.started:
                item.get()
        for copy in pending:
            copy.wait()

    any_spec = pl.BlockSpec(memory_space=pl.ANY)
    scratch_shapes = [pltpu.VMEM(shape, array.dtype) for array, _, shape in lazies]
    scratch_shapes += [pltpu.VMEM(stage, kind) for _, kind, stage in outs if stage]
    scratch_shapes += [pltpu.VMEM(shape, kind) for shape, kind in scratch]
    scratch_shapes += [pltpu.SemaphoreType.DMA((max(1, len(lazies)),)), pltpu.SemaphoreType.DMA((many,))]
    arrays = [*held, *[array for array, _, _ in lazies], *after]
    specs = [SMEM] * len(scalars) + [VMEM] * len(held) + [any_spec] * (len(lazies) + len(after))
    aliases = {}
    if buffer is not None:
        aliases = {len(scalars) + len(arrays): 0}
        arrays.append(buffer)
        specs.append(any_spec)
    return pl.pallas_call(
        kernel,
        name=name,
        out_shape=tuple(jax.ShapeDtypeStruct(shape, kind) for shape, kind, _ in outs),
        in_specs=specs,
        out_specs=tuple(VMEM if stage is None else any_spec for _, _, stage in outs),
        scratch_shapes=scratch_shapes,
        input_output_aliases=aliases,
        compiler_params=pltpu.CompilerParams(vmem_limit_bytes=VMEM_LIMIT),
        cost_estimate=pl.CostEstimate(flops=flops, bytes_accessed=20 << 20, transcendentals=0),
    )(*scalars, *arrays)


def all_of(array):
    return array, None, array.shape


def staged(shape, kind):
    return shape, kind, shape


def plain(shape, kind):
    return shape, kind, None


def fronts_call(lengths, tokens, block_grads, weights):
    held, lazies, outs, scratch = [], [], [], []
    for t, token, grad, w in zip((IMAGE, TEXT), tokens, block_grads, weights):
        rows, width, hidden = t.rows, t.width, t.hidden
        held += [token, w[0], w[1], w[4], w[5], w[8], w[9], grad]
        lazies += [all_of(w[i]) for i in (2, 3, 6, 7, 10)]
        outs += [
            staged((2 * width, t.lanes), BF16),
            staged((BATCH, t.padded, 3 * width), BF16),
            staged((BATCH, t.heads // 2, t.padded, 2 * t.padded), BF16),
            staged((rows, width), F32),
            plain((BATCH, EMBED), BF16),
        ]
        scratch += [
            ((3 * width // 128, t.spread, 128), F32),
            ((width // 128, t.spread, 128), F32),
            ((rows, width), BF16),
            ((rows, width), BF16),
        ]
    lazies = [lazies[i] for i in (5, 6, 0, 7, 8, 9, 1, 2, 3, 4)]
    outs.append(plain((BATCH, ROW_TOTAL), F32))
    outs.append(plain((DEVS, BATCH, 2 * EMBED), BF16))
    results = lazy_call(fronts_kernel, "fronts", (lengths,), held, lazies, outs, scratch, ahead=6)
    return results[:5], results[5:10], results[10], results[11]


def middle(t, name, place, lengths, mixed, block_grad, gain, shift, widen, narrow, after):
    rows, width, hidden = t.rows, t.width, t.hidden
    steps = hidden // t.step
    outs = (
        ((width, t.lanes), BF16),
        ((hidden, t.lanes), BF16),
        ((rows, hidden // 2), BF16),
        ((rows, hidden // 2), BF16),
        ((rows, width // 2), BF16),
        ((rows, width // 2), BF16),
        ((rows, width), F32),
        ((1, width), F32),
        ((1, width), F32),
    )

    def held(shape):
        return pl.BlockSpec(shape, lambda i, *_: (0,) * len(shape))

    def tile(i, place):
        return lax.rem(i + place[0] * (steps // 2), steps)

    out_specs = [held(shape) for shape, _ in outs]
    out_specs[1] = pl.BlockSpec((t.step, t.lanes), lambda i, place, lengths: (tile(i, place), 0))
    out_specs[2] = pl.BlockSpec((rows, t.step), lambda i, *_: (0, jnp.minimum(i, steps // 2 - 1)))
    out_specs[3] = pl.BlockSpec((rows, t.step), lambda i, *_: (0, jnp.maximum(i - steps // 2, 0)))
    in_specs = [held(a.shape) for a in (mixed, block_grad, gain, shift)]
    in_specs.append(pl.BlockSpec((width, t.step), lambda i, place, lengths: (0, tile(i, place))))
    in_specs.append(pl.BlockSpec((t.step, width), lambda i, place, lengths: (tile(i, place), 0)))
    in_specs += [pl.BlockSpec(memory_space=pl.ANY)] * len(after)

    def kernel(*refs):
        middle_kernel(t, *refs[:8], *refs[8 + len(after) :])

    return pl.pallas_call(
        kernel,
        name=name + "_middle",
        out_shape=tuple(jax.ShapeDtypeStruct(shape, kind) for shape, kind in outs),
        grid_spec=pltpu.PrefetchScalarGridSpec(
            num_scalar_prefetch=2,
            grid=(steps,),
            in_specs=in_specs,
            out_specs=tuple(out_specs),
            scratch_shapes=[
                pltpu.VMEM((rows, width), BF16),
                pltpu.VMEM((rows, width), BF16),
                pltpu.VMEM((rows, width), F32),
            ],
        ),
        compiler_params=pltpu.CompilerParams(vmem_limit_bytes=VMEM_LIMIT),
        cost_estimate=pl.CostEstimate(flops=1 << 35, bytes_accessed=20 << 20, transcendentals=0),
    )(place, lengths, mixed, block_grad, gain, shift, widen, narrow, *after)


def head_outs(t):
    return [plain((1, t.width), F32)] * 4 + [
        plain((2 * BATCH, t.width + EMBED), F32),
        plain((BATCH, t.width), F32),
        plain((2 * BATCH, t.width), F32),
        plain((2 * BATCH, t.hidden), F32),
    ]


def backs_call(place, lengths, head_in, head_weights, image_row, towers, after):
    held, lazies, outs, scratch = [*head_in], [], head_outs(TEXT), []
    for t, (tokens, gain, arrays) in zip((IMAGE, TEXT), towers):
        rows, width = t.rows, t.width
        held += [tokens, gain]
        if t is IMAGE:
            held.append(image_row)
        lazies += [all_of(a) for a in arrays]
        outs += [
            ((rows, 2 * width), BF16, ()),
            ((rows, 2 * width), BF16, ()),
            staged((t.real, width), F32),
            plain((1, width), F32),
            plain((1, width), F32),
        ]
        scratch += [
            ((width // 128, t.spread, 128), F32),
            ((3 * width // 128, t.spread, 128), F32),
            ((rows, width), F32),
            ((rows, 4 * width), BF16),
        ]
    lazies = [lazies[i] for i in (5, 6, 0, 1, 7, 8, 2, 3, 9, 4)]
    lazies = [all_of(w) for w in head_weights] + lazies
    results = lazy_call(
        backs_kernel, "backs", (place, lengths), held, lazies, outs, scratch, after=after, ahead=8
    )
    return results[:8], results[8:13], results[13:]


def feed(t, place, head, middle, other, buffer, after):
    rows, width = t.rows, t.width
    name = "image" if t is IMAGE else "text"
    own = (middle[0], middle[1], middle[2], middle[4])
    lazies = [all_of(own[0]), all_of(other[0]), all_of(own[2]), all_of(other[2])]
    lazies += [all_of(own[3]), all_of(other[3])]
    for j in range(4):
        some = slice(width * j, width * j + width)
        for side in (own, other):
            lazies.append((side[1], lambda *_, some=some: (some, slice(None)), (width, t.lanes)))
    cols = 256 if t is IMAGE else 512
    scratch = [
        ((width, cols), F32),
        ((width, cols) if t is IMAGE else (8, 128), F32),
        ((width, width // 2), F32),
    ]
    units = IMAGE_FEED_UNITS if t is IMAGE else 8
    total = LATE_UNITS if buffer else units
    (out,) = lazy_call(
        functools.partial(feed_kernel, t, TEXT_FEED_AT if buffer else 0),
        name + "_feed",
        (place,),
        (head[7], head[6]),
        lazies,
        [((DEVS, total, 16, 128), BF16, (DEVS, units, 16, 128))],
        scratch,
        after=after,
        ahead=10,
    )
    return out


def rest(place, factors, vectors, sides, buffer):
    lazies = []
    for own, other in (sides[1], sides[0]):
        lazies += [all_of(a) for a in (*own, *other)]
    outs = [((DEVS, LATE_UNITS, 16, 128), BF16, ())]
    scratch = [
        ((768, 256), F32),
        ((768, 256), F32),
        ((512, 512), F32),
        ((768, 128), F32),
        ((768, 128), F32),
        ((512, 256), F32),
        ((DEVS, 16, 128), F32),
        ((DEVS, 3, 16, 128), BF16),
        ((DEVS, 4, 16, 128), BF16),
        ((DEVS, 9, 16, 128), BF16),
    ]
    (out,) = lazy_call(
        rest_kernel, "rest", (place,), [*factors, *vectors], lazies, outs, scratch, buffer=buffer, ahead=4
    )
    return out


def sum_blocks(received, step):
    devices, units = received.shape[:2]

    def body(scalars, held, lazies, outs, scratch):
        for i, block in enumerate(lazies):
            total = jnp.sum(block.get()[...].astype(F32), axis=0)
            outs[0][16 * step * i : 16 * step * (i + 1), :] = total.reshape(16 * step, 128)

    lazies = []
    for at in range(0, units, step):
        some = slice(at, at + step)
        lazies.append((received, lambda *_, some=some: (slice(None), some), (devices, step, 16, 128)))
    outs = [plain((16 * units, 128), F32)]
    return lazy_call(body, "sum_blocks", (), (), lazies, outs, flops=1 << 34, ahead=len(lazies))[0]


def behind(arrays, after):
    def kernel(*refs):
        pass

    any_spec = pl.BlockSpec(memory_space=pl.ANY)
    return pl.pallas_call(
        kernel,
        name="behind",
        out_shape=[jax.ShapeDtypeStruct(array.shape, array.dtype) for array in arrays],
        in_specs=[any_spec] * (len(arrays) + len(after)),
        out_specs=[any_spec] * len(arrays),
        input_output_aliases={i: i for i in range(len(arrays))},
    )(*arrays, *after)


SWAP = [(0, 1), (1, 0)]


def by_token(tokens):
    return tokens.transpose(1, 0, 2).reshape(-1, tokens.shape[2])


def shards(*args):
    image_tokens, image_weights, image_block_grad = args[0], args[1:12], args[12]
    text_tokens, caption_lengths = args[13], args[14]
    text_weights, text_block_grad, log_scale = args[15:26], args[26], args[27]
    core = lax.axis_index("tower")
    dp = lax.axis_index("dp")
    place = jnp.stack([core, dp]).astype(jnp.int32)
    tokens = (by_token(image_tokens), by_token(text_tokens))
    block_grads = (by_token(image_block_grad), by_token(text_block_grad))
    weights = (image_weights, text_weights)
    kinds = ((0, IMAGE, "image"), (1, TEXT, "text"))
    *fronts, kept, copies = fronts_call(caption_lengths, tokens, block_grads, weights)
    units = [f[4] for f in fronts]
    own = lax.all_to_all(copies, "dp", 0, 0, tiled=True).reshape(DEVS * BATCH, 2 * EMBED)

    def swap(*arrays):
        return [lax.ppermute(array, "tower", SWAP) for array in arrays]

    def middle_of(i, after):
        _, t, name = kinds[i]
        w = weights[i]
        return middle(
            t, name, place, caption_lengths, fronts[i][3], block_grads[i], w[4], w[5], w[6], w[7], after
        )

    (kept_other,) = swap(kept)
    image_middle = list(middle_of(0, ()))
    (own,) = behind([own], (image_middle[0], kept_other))
    (other,) = swap(own)
    sent = (0, 1, 3, 5)
    for k, array in zip(sent, behind([image_middle[k] for k in sent], (other,))):
        image_middle[k] = array
    image_sent = swap(*[image_middle[k] for k in sent])

    w = image_weights
    paired = lazy_call(
        pair_kernel,
        "pairs",
        (place, log_scale),
        [own, other, kept, kept_other, w[8], w[9], w[4], w[5]],
        [all_of(w[10]), all_of(w[7]), all_of(w[6])],
        [plain((1, 128), F32), plain((1, 128), F32), plain((2 * BATCH, EMBED), F32), *head_outs(IMAGE)],
        ahead=6,
    )
    loss, scale_grad = paired[0][0, :1], paired[1][0, :1]
    image_head = paired[3:]
    image_feed = feed(IMAGE, place, image_head, image_middle, image_sent, False, ())
    feed_total = lax.all_to_all(image_feed, "dp", 0, 0, tiled=True)
    text_middle = middle_of(1, (image_feed,))
    middles = (image_middle, text_middle)

    back_in = []
    for i, _, _ in kinds:
        f, m, w = fronts[i], middles[i], weights[i]
        back_in.append((tokens[i], w[0], (w[3], m[6], f[1], f[2], w[2])))
    w = text_weights
    text_head, *backs = backs_call(
        place,
        caption_lengths,
        [paired[2], kept, kept_other, w[8], w[9], w[4], w[5]],
        [w[10], w[7], w[6]],
        image_head[5],
        back_in,
        (text_middle[0],),
    )
    heads = (image_head, text_head)
    text_sent = swap(*[text_middle[k] for k in sent])
    late = feed(TEXT, place, heads[1], text_middle, text_sent, True, (backs[1][0],))
    sides = []
    for f, k in zip(fronts, backs):
        sides.append(((f[0], k[0]), swap(f[0], k[1])))
    vectors = []
    for m, h, k in zip(middles, heads, backs):
        vectors += [k[3], k[4], m[7], h[2], m[8], h[3], h[0], h[1]]
    factors = [heads[0][4], heads[1][4]]
    (late,) = behind([rest(place, factors, vectors, sides, late)], (feed_total,))
    late_total = lax.all_to_all(late, "dp", 0, 0, tiled=True)
    feed_mine = sum_blocks(feed_total, 3)
    (feed_theirs,) = swap(feed_mine)
    (late_total,) = behind([late_total], (feed_theirs,))
    late_mine = sum_blocks(late_total, 4)
    (late_theirs,) = swap(late_mine)
    mine, theirs = (feed_mine, late_mine), (feed_theirs, late_theirs)
    weight_outs = (
        ((12, 2304), F32),
        ((12, 768), F32),
        ((12, 3072), F32),
        ((48, 768), F32),
        ((12, 512), F32),
        ((8, 1536), F32),
        ((8, 512), F32),
        ((8, 2048), F32),
        ((32, 512), F32),
        ((8, 512), F32),
    )
    vector_outs = (((1, 12), F32),) * 6 + (((1, 8), F32),) * 6
    grads = call(unpack_kernel, "unpack", (place,), (*mine, *theirs), weight_outs + vector_outs)

    def ordered(vectors, weights):
        joint, output, widen, narrow, projection = weights
        v = [x.reshape(-1) for x in vectors]
        return [v[0], v[1], joint, output, v[2], v[3], widen, narrow, v[4], v[5], projection]

    def by_sequence(t, grad):
        return grad.reshape(t.length, BATCH, t.width).transpose(1, 0, 2)

    return (
        loss,
        units[0],
        units[1],
        by_sequence(IMAGE, backs[0][2]),
        *ordered(grads[10:16], grads[:5]),
        by_sequence(TEXT, backs[1][2]),
        *ordered(grads[16:22], grads[5:10]),
        scale_grad,
    )


def solution(mesh):
    spread = P(("tower", "dp"), None, None)
    weights = [P()] * 11
    placed = (spread, *weights, spread, spread, P(("tower", "dp")), *weights, spread, P())
    vector, matrix = P("dp"), P("dp", None)
    grads = [vector, vector, matrix, matrix, vector, vector, matrix, matrix, vector, vector, matrix]
    units = P(("tower", "dp"), None)
    return jax.shard_map(
        shards,
        mesh=mesh,
        in_specs=placed,
        out_specs=(P(), units, units, spread, *grads, spread, *grads, P()),
        check_vma=False,
    )
```

```python
import functools

import jax
import jax.numpy as jnp
from jax import lax
from jax.experimental import pallas as pl
from jax.experimental.pallas import tpu as pltpu
from jax.sharding import PartitionSpec as P

F32 = jnp.float32
BF16 = jnp.bfloat16
BATCH = 8
EMBED = 512
TILE = 256
DEVS = 64


class Tower:
    def __init__(self, width, heads, hidden, length, padded, rows, extra, causal):
        self.width = width
        self.heads = heads
        self.hidden = hidden
        self.length = length
        self.padded = padded
        self.real = BATCH * length
        self.rows = rows
        self.extra = extra
        self.spread = BATCH * padded
        self.lanes = -(-rows // 128) * 128
        self.causal = causal
        self.step = 768 if width == 768 else 512


IMAGE = Tower(768, 12, 3072, 50, 64, 416, 400, False)
TEXT = Tower(512, 8, 2048, 77, 80, 640, 624, True)

VMEM_LIMIT = 64 * 1024 * 1024


def mm(left, right):
    return lax.dot_general(left, right, (((1,), (0,)), ((), ())), preferred_element_type=F32)


def mm_nt(left, right):
    return lax.dot_general(left, right, (((1,), (1,)), ((), ())), preferred_element_type=F32)


def mm_tn(left, right):
    return lax.dot_general(left, right, (((0,), (0,)), ((), ())), preferred_element_type=F32)


def normalise(values):
    centre = jnp.mean(values, axis=-1, keepdims=True)
    offset = values - centre
    inverse = lax.rsqrt(jnp.mean(offset * offset, axis=-1, keepdims=True) + 1e-05)
    return offset * inverse, inverse


def norm_back(upstream, gain, normal, inverse):
    scaled = upstream * gain
    inner = (
        scaled
        - jnp.mean(scaled, axis=-1, keepdims=True)
        - normal * jnp.mean(scaled * normal, axis=-1, keepdims=True)
    )
    return inner * inverse


def column_sum(values):
    return jnp.sum(values, axis=0, keepdims=True)


def sigmoid(values):
    return 0.5 + 0.5 * jnp.tanh(0.5 * values)


def vec(ref):
    return ref[...].reshape(1, -1)


def chunks(count, size=128):
    return [(at, min(size, count - at)) for at in range(0, count, size)]


UNROLL_TILE, UNROLL_HEADS, UNROLL_PACK = 9, 8, 4
UNROLL_BACK = 1


def loop(count, body, unroll=1):
    def step(i, carry):
        body(i)
        return carry

    lax.fori_loop(0, count, step, 0, unroll=min(unroll, count))


def tile_loop(width, body):
    loop(width // TILE, lambda n: body(n, pl.ds(pl.multiple_of(n * TILE, TILE), TILE)), UNROLL_TILE)


def put_tiles(ref, n, rows, values):
    for i in range(TILE // 128):
        ref[n * (TILE // 128) + i, 0:rows, :] = values[:, 128 * i : 128 * i + 128]


class Lazy:
    def __init__(self, queue, source, target, sem):
        self.copy = pltpu.make_async_copy(source, target, sem)
        self.target = target
        self.queue = queue
        self.started = self.waited = False

    def start(self):
        if not self.started:
            self.copy.start()
            self.started = True

    def get(self):
        if not self.waited:
            self.start()
            self.copy.wait()
            self.waited = True
            for item in self.queue:
                if not item.started:
                    item.start()
                    break
        return self.target


class Staged:
    def __init__(self, out, stage, sems, pending):
        self.out = out
        self.ref = stage
        self.sems = sems
        self.pending = pending

    def send(self, source, target):
        copy = pltpu.make_async_copy(source, target, self.sems.at[len(self.pending)])
        copy.start()
        self.pending.append(copy)

    def done(self):
        self.send(self.ref, self.out)

    def units_done(self, devices, units, out_units):
        self.send(self.ref.at[devices, units], self.out.at[devices, out_units])


def head_masks():
    lane = lax.broadcasted_iota(jnp.int32, (1, 128), 1)
    first = jnp.where(lane < 64, 1.0, 0.0).astype(BF16)
    second = jnp.where(lane < 64, 0.0, 1.0).astype(BF16)
    return first, second


def two_heads(values, masks):
    return jnp.concatenate([values * masks[0], values * masks[1]], axis=0)


def own_head(values, padded):
    lane = lax.broadcasted_iota(jnp.int32, (padded, 128), 1)
    return jnp.where(lane < 64, values[:padded], values[padded:])


def pooled_row(t, lengths, b):
    return b if t is IMAGE else (lengths[b] - 1) * BATCH + b


def row_parts(t):
    return {
        "raw": EMBED,
        "unit": EMBED,
        "pooled": t.width,
        "mixed": t.width,
        "grad": t.width,
        "wide": t.hidden,
    }


def row_part(t, name):
    at = 0 if t is IMAGE else sum(row_parts(IMAGE).values())
    for part, size in row_parts(t).items():
        if part == name:
            return slice(at, at + size)
        at += size


ROW_TOTAL = sum(row_parts(IMAGE).values()) + sum(row_parts(TEXT).values())


class Front:
    def __init__(self, t, lengths, ins, weights, outs, kept, scratch):
        self.t = t
        self.lengths = lengths
        (
            self.tokens,
            self.first_gain,
            self.first_shift,
            self.second_gain,
            self.second_shift,
            self.final_gain,
            self.final_shift,
            self.block_grad,
        ) = ins
        self.joint_weight, self.output_weight, self.widen, self.narrow, self.projection = weights
        self.staged = outs[:4]
        self.turned, self.joint, self.probs, self.mixed = [out.ref for out in outs[:4]]
        self.unit = outs[4]
        self.kept = kept
        self.joint_wide, self.context_wide, self.normed_one, self.context = scratch
        self.mixed_row = kept.at[:, row_part(t, "mixed")]

    def norm(self):
        t, rows = self.t, self.t.rows
        mixed, normed_one = self.mixed, self.normed_one
        grad_row = self.kept.at[:, row_part(t, "grad")]
        for at, size in chunks(t.real):
            mixed[at : at + size, :] = self.block_grad[at : at + size, :].astype(F32)
        for b in range(BATCH):
            grad_row[b : b + 1, :] = mixed[pl.ds(pooled_row(t, self.lengths, b), 1), :]
        pad = t.real - t.real % 16
        normed_one[pad:rows, :] = jnp.zeros((rows - pad, t.width), BF16)
        for at, size in chunks(t.real):
            normal, _ = normalise(self.tokens[at : at + size, :].astype(F32))
            normed_one[at : at + size, :] = (
                normal * vec(self.first_gain) + vec(self.first_shift)
            ).astype(BF16)
        if t.spread > rows:
            fill = (3 * t.width // 128, t.spread - rows, 128)
            self.joint_wide[:, rows : t.spread, :] = jnp.zeros(fill, F32)

    def joint_tile(self, n):
        cols = pl.ds(pl.multiple_of(n * TILE, TILE), TILE)
        product = mm(self.normed_one[...], self.joint_weight.get()[:, cols])
        put_tiles(self.joint_wide, n, self.t.rows, product)

    def ready(self):
        t, padded = self.t, self.t.padded
        self.masks = head_masks()
        key_at = lax.broadcasted_iota(jnp.int32, (padded, 2 * padded), 0)
        query_at = lax.broadcasted_iota(jnp.int32, (padded, 2 * padded), 1)
        query_at = jnp.where(query_at < padded, query_at, query_at - padded)
        self.valid = key_at <= query_at if t.causal else key_at < t.length

    def attend(self, b):
        t, joint, masks = self.t, self.joint, self.masks
        width, padded = t.width, t.padded
        pairs = range(t.heads // 2)
        some = pl.ds(b, padded, stride=BATCH)
        for c in range(3 * width // 128):
            joint[b, :, 128 * c : 128 * c + 128] = self.joint_wide[c, some, :].astype(BF16)
        scores = []
        for p in pairs:
            at = 128 * p
            queries = joint[b, :, at : at + 128]
            keys = joint[b, :, width + at : width + at + 128]
            scores.append(mm_nt(keys, two_heads(queries, masks)) * 0.125)
        lows = []
        for p in pairs:
            score = jnp.where(self.valid, scores[p], -1e30)
            raised = jnp.exp(score - jnp.max(score, axis=0, keepdims=True))
            low = (raised * (1.0 / column_sum(raised))).astype(BF16)
            self.probs[b, p] = low
            lows.append(low)
        for p in pairs:
            at = 2 * width + 128 * p
            both = mm_tn(lows[p], joint[b, :, at : at + 128])
            self.context_wide[p, some, :] = own_head(both, padded)

    def mix(self):
        t, rows, width = self.t, self.t.rows, self.t.width
        context, mixed = self.context, self.mixed
        self.staged[1].done()
        self.staged[2].done()
        for p in range(t.heads // 2):
            context[:, 128 * p : 128 * p + 128] = self.context_wide[p, 0:rows, :].astype(BF16)
        turn(self.normed_one, self.turned.at[0:width], 6)
        turn(context, self.turned.at[width : 2 * width], 6)
        self.staged[0].done()
        output_weight = self.output_weight.get()

        def mix_step(n, cols):
            mixed[:, cols] = mm(context[...], output_weight[:, cols])

        tile_loop(width, mix_step)
        for at, size in chunks(t.real):
            mixed[at : at + size, :] += self.tokens[at : at + size, :].astype(F32)
        for b in range(BATCH):
            row = mixed[pl.ds(pooled_row(t, self.lengths, b), 1), :]
            self.mixed_row[b : b + 1, :] = row
        mixed[t.real : rows, :] = jnp.zeros((rows - t.real, width), F32)
        mixed[t.extra : t.extra + BATCH, :] = self.mixed_row[...]
        self.staged[3].done()

    def embed(self):
        t, kept = self.t, self.kept
        row = self.mixed_row[...]
        normal, _ = normalise(row)
        normed = (normal * vec(self.second_gain) + vec(self.second_shift)).astype(BF16)
        wide = mm(normed, self.widen.get()[...])
        kept[:, row_part(t, "wide")] = wide
        active = (wide * sigmoid(1.702 * wide)).astype(BF16)
        last = row + mm(active, self.narrow.get()[...])
        kept[:, row_part(t, "pooled")] = last
        normal, _ = normalise(last)
        normed = (normal * vec(self.final_gain) + vec(self.final_shift)).astype(BF16)
        raw = mm(normed, self.projection.get()[...])
        kept[:, row_part(t, "raw")] = raw
        factor = lax.rsqrt(jnp.sum(raw * raw, axis=-1, keepdims=True) + 1e-06)
        unit = (raw * factor).astype(BF16)
        self.unit[...] = unit
        kept[:, row_part(t, "unit")] = unit.astype(F32)
        return unit


def fronts_kernel(scalars, held, lazies, outs, scratch):
    order = [5, 6, 0, 7, 8, 9, 1, 2, 3, 4]
    weights = [lazies[order.index(i)] for i in range(10)]
    image, text = [
        Front(
            t,
            scalars[0],
            held[8 * i : 8 * i + 8],
            weights[5 * i : 5 * i + 5],
            outs[5 * i : 5 * i + 5],
            outs[10],
            scratch[4 * i : 4 * i + 4],
        )
        for i, t in enumerate((IMAGE, TEXT))
    ]
    text.norm()
    for n in range(3 * TEXT.width // TILE):
        text.joint_tile(n)
    image.norm()
    for front in (image, text):
        front.ready()
    image.joint_weight.get()
    tiles = 3 * IMAGE.width // TILE

    def both(b):
        text.attend(b)
        image.joint_tile(b)

    loop(BATCH, both, UNROLL_HEADS)
    for n in range(BATCH, tiles):
        image.joint_tile(n)
    text.mix()
    loop(BATCH, image.attend, UNROLL_HEADS)
    image.mix()
    for i, unit in enumerate((image.embed(), text.embed())):
        outs[11][:, :, EMBED * i : EMBED * i + EMBED] = jnp.broadcast_to(unit[None], (DEVS, *unit.shape))


def middle_kernel(
    t,
    place,
    lengths,
    mixed,
    block_grad,
    second_gain,
    second_shift,
    widen_weight,
    narrow_weight,
    normed_turned,
    active_turned,
    wide_own,
    wide_send,
    narrow_own,
    narrow_send,
    mixed_grad,
    gain_grad,
    shift_grad,
    normed_two,
    narrow_in,
    wide_in,
):
    step = pl.program_id(0)
    half_steps = pl.num_programs(0) // 2

    @pl.when(step == 0)
    def _():
        wide_in[t.real : t.rows, :] = jnp.zeros((t.rows - t.real, t.width), F32)
        for at, size in chunks(t.rows):
            normal, _ = normalise(mixed[at : at + size, :])
            normed_two[at : at + size, :] = (normal * vec(second_gain) + vec(second_shift)).astype(
                BF16
            )
        turn(normed_two, normed_turned)
        for at, size in chunks(t.real):
            wide_in[at : at + size, :] = block_grad[at : at + size, :].astype(F32)
        for b in range(BATCH):
            wide_in[pl.ds(pooled_row(t, lengths, b), 1), :] = jnp.zeros((1, t.width), F32)
        narrow_in[...] = wide_in[...].astype(BF16)
        cols = t.width // 2
        own = pl.multiple_of(place[0] * cols, 128)
        narrow_own[...] = narrow_in[:, pl.ds(own, cols)]
        narrow_send[...] = narrow_in[:, pl.ds(pl.multiple_of(cols - own, 128), cols)]
        mixed_grad[...] = jnp.zeros_like(mixed_grad)

    lows = []
    for at, size in chunks(t.step, TILE):
        some = slice(at, at + size)
        wide = mm(normed_two[...], widen_weight[:, some])
        back = mm_nt(narrow_in[...], narrow_weight[some, :])
        sig = sigmoid(1.702 * wide)
        active = wide * sig
        active_turned[some, 0 : t.rows] = active.astype(BF16).T
        slope = sig + 1.702 * active * (1.0 - sig)
        lows.append((back * slope).astype(BF16))
    low = jnp.concatenate(lows, axis=1)
    mixed_grad[...] += mm_nt(low, widen_weight[...])

    @pl.when(step < half_steps)
    def _():
        wide_own[...] = low

    @pl.when(step >= half_steps)
    def _():
        wide_send[...] = low

    @pl.when(step == pl.num_programs(0) - 1)
    def _():
        gain = shift = 0.0
        for at, size in chunks(t.rows):
            some = slice(at, at + size)
            normal, inverse = normalise(mixed[some, :])
            up = mixed_grad[some, :]
            gain += column_sum(up * normal)
            shift += column_sum(up)
            mixed_grad[some, :] = wide_in[some, :] + norm_back(
                up, vec(second_gain), normal, inverse
            )
        gain_grad[...] = gain
        shift_grad[...] = shift


def split_dot(weights, right):
    high = weights.astype(BF16)
    rest = weights - high.astype(F32)
    middle = rest.astype(BF16)
    low = (rest - middle.astype(F32)).astype(BF16)
    return mm(high, right) + mm(middle, right) + mm(low, right)


def head_back(
    unit_grad,
    raw,
    pooled,
    mixed_row,
    wide_row,
    grad_row,
    final_gain,
    final_shift,
    second_gain,
    second_shift,
    projection,
    widen_weight,
    narrow_weight,
    outs,
):
    (
        final_gain_grad,
        final_shift_grad,
        second_gain_grad,
        second_shift_grad,
        factors,
        mixed_grad_row,
        narrow_in_row,
        wide_grad_row,
    ) = outs
    own = slice(0, BATCH)
    width = pooled.shape[1]
    factor = lax.rsqrt(jnp.sum(raw * raw, axis=-1, keepdims=True) + 1e-06)
    raw_grad = factor * unit_grad - raw * (factor * factor * factor) * jnp.sum(
        unit_grad * raw, axis=-1, keepdims=True
    )
    raw_grad = raw_grad.astype(BF16)
    factors[:, width:] = raw_grad.astype(F32)
    normal, inverse = normalise(pooled)
    factors[:, 0:width] = (normal * final_gain + final_shift).astype(BF16).astype(F32)
    up = mm_nt(raw_grad, projection.get()[...])
    final_gain_grad[...] = column_sum((up * normal)[own])
    final_shift_grad[...] = column_sum(up[own])
    out_grad = grad_row + norm_back(up, final_gain, normal, inverse)
    narrow_in = out_grad.astype(BF16)
    narrow_in_row[...] = narrow_in.astype(F32)
    sig = sigmoid(1.702 * wide_row)
    slope = sig + 1.702 * wide_row * sig * (1.0 - sig)
    low = (mm_nt(narrow_in, narrow_weight.get()[...]) * slope).astype(BF16)
    wide_grad_row[...] = low.astype(F32)
    up = mm_nt(low, widen_weight.get()[...])
    normal, inverse = normalise(mixed_row)
    second_gain_grad[...] = column_sum((up * normal)[own])
    second_shift_grad[...] = column_sum(up[own])
    mixed_grad_row[...] = (out_grad + norm_back(up, second_gain, normal, inverse))[own]


def kept_rows(own, other, t, name):
    some = row_part(t, name)
    return jnp.concatenate([own[:, some], other[:, some]], axis=0)


def head_of(t, unit_grad, kept, vectors, weights, outs):
    values = [kept_rows(*kept, t, name) for name in ("raw", "pooled", "mixed", "wide", "grad")]
    values += [vec(ref) for ref in vectors]
    projection, narrow, widen = weights
    head_back(unit_grad, *values, projection, widen, narrow, outs)


def pair_kernel(scalars, held, lazies, outs, scratch):
    place, log_scale = scalars
    own, other, kept_own, kept_other = held[:4]
    loss, scale_grad, text_grad = outs[:3]
    kept = (kept_own, kept_other)
    half = own.shape[0]
    pairs = 2 * half
    scale = jnp.exp(jnp.full((1, 1), log_scale[0], F32))
    blocks = (own, other)

    def totals(left_at, right_at):
        sums, moments = [], []
        for right in blocks:
            column, moment = None, None
            for left in blocks:
                for piece in range(0, half, 256):
                    sims = scale * mm_nt(
                        left[piece : piece + 256, left_at : left_at + EMBED],
                        right[:, right_at : right_at + EMBED],
                    )
                    raised = jnp.exp(sims)
                    add, more = column_sum(raised), column_sum(raised * sims)
                    column = add if column is None else column + add
                    moment = more if moment is None else moment + more
            sums.append(column)
            moments.append(moment)
        return sums, moments

    column_sums, column_moments = totals(0, EMBED)
    row_sums, row_moments = totals(EMBED, 0)
    log_total = jnp.zeros((1, 1), F32)
    weighted = jnp.zeros((1, 1), F32)
    trace = jnp.zeros((1, 1), F32)
    for i in range(2):
        for total, moment in ((column_sums[i], column_moments[i]), (row_sums[i], row_moments[i])):
            log_total += jnp.sum(jnp.log(total), axis=-1, keepdims=True)
            weighted += jnp.sum(moment / total, axis=-1, keepdims=True)
        product = blocks[i][:, :EMBED].astype(F32) * blocks[i][:, EMBED:].astype(F32)
        trace += jnp.sum(column_sum(product), axis=-1, keepdims=True)
    trace = scale * trace
    loss[...] = jnp.broadcast_to((log_total - 2.0 * trace) / (2.0 * pairs), loss.shape)
    scale_grad[...] = jnp.broadcast_to((weighted - 2.0 * trace) / (2.0 * pairs), loss.shape)

    lane = lax.broadcasted_iota(jnp.int32, (2 * BATCH, half), 1)
    sub = lax.broadcasted_iota(jnp.int32, (2 * BATCH, half), 0)
    diagonal = place[1] * BATCH
    identity = [
        jnp.where(jnp.logical_and(lane == sub + diagonal, sub < BATCH), 2.0, 0.0),
        jnp.where(jnp.logical_and(lane == sub - BATCH + diagonal, sub >= BATCH), 2.0, 0.0),
    ]

    def grads(t, at, other_sums):
        unit = kept_rows(*kept, t, "unit").astype(BF16)
        raised = [jnp.exp(scale * mm_nt(unit, block[:, at : at + EMBED])) for block in blocks]
        own_sum = sum(jnp.sum(r, axis=-1, keepdims=True) for r in raised)
        result = None
        for i in range(2):
            weight = raised[i] * (1.0 / own_sum + 1.0 / other_sums[i]) - identity[i]
            weight = weight / (2.0 * pairs)
            part = split_dot(weight, blocks[i][:, at : at + EMBED])
            result = part if result is None else result + part
        return scale * result

    image_grad = grads(IMAGE, EMBED, column_sums)
    text_grad[...] = grads(TEXT, 0, row_sums)
    head_of(IMAGE, image_grad, kept, held[4:8], lazies, outs[3:11])


class Back:
    def __init__(self, t, place, lengths, held, lazies, outs, scratch):
        self.t = t
        self.place = place
        self.lengths = lengths
        self.tokens, self.first_gain, self.row = held[:3]
        self.output_weight, self.mixed_grad, self.joint_in, self.probs_in, self.joint_weight = lazies
        self.own, self.send, self.tokens_out, self.gain_grad, self.shift_grad = outs
        self.context_grad, self.joint_grad, self.normed_grad, self.grads = scratch

    def context(self):
        t, rows, width, grads = self.t, self.t.rows, self.t.width, self.grads
        self.grad = grad = self.mixed_grad.get()
        for b in range(BATCH):
            grad[pl.ds(pooled_row(t, self.lengths, b), 1), :] = self.row[b : b + 1, :]
        mixed_low = slice(3 * width, 4 * width)
        grads[:, mixed_low] = grad[...].astype(BF16)
        if t.spread > rows:
            fill = (width // 128, t.spread - rows, 128)
            self.context_grad[:, rows : t.spread, :] = jnp.zeros(fill, F32)
        output_weight = self.output_weight.get()

        def step(n, cols):
            put_tiles(self.context_grad, n, rows, mm_nt(grads[:, mixed_low], output_weight[cols, :]))

        tile_loop(width, step)
        self.masks = head_masks()
        self.joint, self.probs = self.joint_in.get(), self.probs_in.get()

    def attend(self, b):
        t, masks, joint, joint_grad = self.t, self.masks, self.joint, self.joint_grad
        width, padded = t.width, t.padded
        pairs = range(t.heads // 2)
        some = pl.ds(b, padded, stride=BATCH)
        ups = [two_heads(self.context_grad[p, some, :].astype(BF16), masks) for p in pairs]
        backs = []
        for p in pairs:
            at = 2 * width + 128 * p
            backs.append(mm_nt(joint[b, :, at : at + 128], ups[p]))
        lows = []
        for p in pairs:
            wide = self.probs[b, p].astype(F32)
            back = wide * (backs[p] - column_sum(backs[p] * wide))
            lows.append(back.astype(BF16))
        for p in pairs:
            at = 128 * p
            queries = joint[b, :, at : at + 128]
            keys = joint[b, :, width + at : width + at + 128]
            joint_grad[2 * len(pairs) + p, some, :] = mm(self.probs[b, p], ups[p])
            joint_grad[len(pairs) + p, some, :] = mm(lows[p], two_heads(queries, masks)) * 0.125
            joint_grad[p, some, :] = own_head(mm_tn(lows[p], keys), padded) * 0.125

    def finish(self):
        t, rows, width, grads = self.t, self.t.rows, self.t.width, self.grads
        for c in range(3 * width // 128):
            grads[:, 128 * c : 128 * c + 128] = self.joint_grad[c, 0:rows, :].astype(BF16)
        start = pl.multiple_of(self.place[0] * (2 * width), 128)
        self.own.send(grads.at[:, pl.ds(start, 2 * width)], self.own.out)
        start = pl.multiple_of(2 * width - start, 128)
        self.send.send(grads.at[:, pl.ds(start, 2 * width)], self.send.out)
        joint_weight = self.joint_weight.get()

        def step(n, cols):
            self.normed_grad[:, cols] = mm_nt(grads[:, 0 : 3 * width], joint_weight[cols, :])

        tile_loop(width, step)
        gain = shift = 0.0
        for at, size in chunks(t.real):
            some = slice(at, at + size)
            normal, inverse = normalise(self.tokens[some, :].astype(F32))
            up = self.normed_grad[some, :]
            gain += column_sum(up * normal)
            shift += column_sum(up)
            self.tokens_out.ref[some, :] = self.grad[some, :] + norm_back(
                up, vec(self.first_gain), normal, inverse
            )
        self.gain_grad[...] = gain
        self.shift_grad[...] = shift
        self.tokens_out.done()


def backs_kernel(scalars, held, lazies, outs, scratch):
    head_in, held = held[:7], held[7:]
    head_weights, lazies = lazies[:3], lazies[3:]
    head_outs, outs = outs[:8], outs[8:]
    head_of(TEXT, head_in[0][...], head_in[1:3], head_in[3:7], head_weights, head_outs)
    order = [5, 6, 0, 1, 7, 8, 2, 3, 9, 4]
    lazies = [lazies[order.index(i)] for i in range(10)]
    held = [*held[:3], *held[3:5], head_outs[5]]
    image, text = [
        Back(
            t,
            *scalars,
            held[3 * i : 3 * i + 3],
            lazies[5 * i : 5 * i + 5],
            outs[5 * i : 5 * i + 5],
            scratch[4 * i : 4 * i + 4],
        )
        for i, t in enumerate((IMAGE, TEXT))
    ]
    text.context()
    image.context()

    def both(b):
        text.attend(b)
        image.attend(b)

    loop(BATCH, both, UNROLL_BACK)
    text.finish()
    image.finish()


def turn(source, target, unroll=3):
    def step(n):
        cols = pl.ds(pl.multiple_of(n * 128, 128), 128)
        target[cols, 0 : source.shape[0]] = source[:, cols].T

    loop(source.shape[1] // 128, step, unroll)


def lanes_down(values):
    return jnp.concatenate(
        [values[:, :, at : at + 128] for at in range(0, values.shape[2], 128)], axis=1
    )


def put(out, device, unit, values):
    count = values.shape[1] // 16
    size = values.shape[0]
    values = values.reshape(size, count, 16, 128).astype(BF16)
    out[pl.ds(device, size), unit : unit + count] = values


def pack_twelve(first, second, out, unit=0, each=4):
    cols = first.shape[1]
    count = cols // 128
    sub = lax.broadcasted_iota(jnp.int32, (each, 8, cols), 1) < 4

    def step(e):
        rows = pl.ds(pl.multiple_of(e * (24 * each), 8), 24 * each)
        x = first[rows, :].reshape(each, 24, cols)
        y = second[rows, :].reshape(each, 24, cols)
        left, right = x[:, 8:16], y[:, 8:16]
        even = jnp.where(sub, left, pltpu.roll(right, 4, 1))
        odd = jnp.where(sub, pltpu.roll(left, 4, 1), right)
        parts = []
        for a, b, c in ((x[:, 0:8], y[:, 0:8], even), (x[:, 16:24], y[:, 16:24], odd)):
            parts.append(jnp.concatenate([lanes_down(v) for v in (a, b, c)], axis=1))
        if parts[0].shape[1] % 16:
            fill = jnp.zeros((each, 16 - parts[0].shape[1] % 16, 128), F32)
            parts = [jnp.concatenate([part, fill], axis=1) for part in parts]
        height = parts[0].shape[1]
        values = jnp.stack(parts, axis=1).reshape(2 * each, height, 128)
        put(out, e * (2 * each), unit, values)

    loop(32 // each, step, UNROLL_PACK)


def pack_rows(result, rows, out, unit=0, each=8, device=0):
    total = result.shape[0] // rows
    cols = result.shape[1]

    def step(e):
        some = pl.ds(pl.multiple_of(e * (rows * each), 8), rows * each)
        values = lanes_down(result[some, :].reshape(each, rows, cols))
        put(out, device + e * each, unit, values)

    loop(total // each, step, UNROLL_PACK)


def put_extra(t, ref, rows):
    rows = jnp.concatenate([rows, jnp.zeros_like(rows)], axis=0)
    ref[t.extra : t.extra + 16, :] = rows.astype(BF16)


def wide_grads(t, half, product, send, at, first, second):
    if t is IMAGE:
        for i in range(3):
            first[...] = product(256 * i, 256)
            second[...] = product(768 + 256 * i, 256)
            pack_twelve(first, second, send.ref, 3 * i)
            units = slice(3 * i, 3 * i + 3)
            send.units_done(slice(None), units, slice(at + 3 * i, at + 3 * i + 3))
    else:
        for i in range(2):
            first[...] = product(512 * i, 512)
            pack_rows(first, 8, send.ref, 2 * i)
            units = slice(2 * i, 2 * i + 2)
            send.units_done(slice(None), units, slice(at + 2 * i, at + 2 * i + 2))


def feed_kernel(t, at, scalars, held, lazies, outs, scratch):
    (place,) = scalars
    wide_rows, narrow_rows = held
    normed, wides, narrows = lazies[0:2], lazies[2:4], lazies[4:6]
    actives = lazies[6:14]
    (out,) = outs
    first, second, narrow_result = scratch

    def patch(refs, rows):
        size = rows.shape[1] // 2
        some = pl.ds(pl.multiple_of(place[0] * size, 128), size)
        for side, ref in enumerate(refs):
            put_extra(t, ref.get(), rows[BATCH * side : BATCH * side + BATCH, some])

    patch(wides, wide_rows)
    lefts = [ref.get() for ref in normed]
    wides = [ref.get() for ref in wides]

    def product(tile, size):
        return sum(mm(a[:, 0 : t.rows], b[:, tile : tile + size]) for a, b in zip(lefts, wides))

    wide_grads(t, place[0], product, out, at, first, second)
    patch(narrows, narrow_rows)
    narrows = [ref.get() for ref in narrows]
    wide_units, units = (9, 9) if t is IMAGE else (4, 4)
    some = slice(wide_units, wide_units + units)
    for j in range(4):
        pair = [actives[2 * j].get(), actives[2 * j + 1].get()]
        narrow_result[...] = sum(mm(a[:, 0 : t.rows], b[...]) for a, b in zip(pair, narrows))
        pack_rows(narrow_result, t.hidden // DEVS, out.ref, wide_units, 4, 16 * j)
        out.units_done(
            slice(16 * j, 16 * j + 16), some, slice(at + wide_units, at + wide_units + units)
        )


def rest_kernel(scalars, held, lazies, outs, scratch):
    (place,) = scalars
    (out,) = outs
    first, second, third = scratch[:3]
    misc_scratch, spread = scratch[3:6], scratch[6]
    half = place[0]
    misc, text_stage, image_stage = [Staged(out.out, ref, out.sems, out.pending) for ref in scratch[7:10]]
    misc_grads(half, held[:2], held[2:], misc, misc_scratch, spread)
    for t, ins, stage, results in (
        (TEXT, lazies[0:4], text_stage, (third, None)),
        (IMAGE, lazies[4:8], image_stage, (first, second)),
    ):
        width = t.width
        lefts, rights = [ref.get() for ref in ins[0::2]], [ref.get() for ref in ins[1::2]]

        def product(tile, size):
            late = jnp.where(half * (2 * width) + tile >= 3 * width, width, 0)
            rows = pl.ds(pl.multiple_of(late, 128), width)
            return sum(
                mm(a[rows, 0 : t.rows], b[:, tile : tile + size]) for a, b in zip(lefts, rights)
            )

        wide_grads(t, half, product, stage, REST_AT["image" if t is IMAGE else "text"], *results)


IMAGE_FEED_UNITS = 18
LATE_UNITS = 24
TEXT_FEED_AT = 0
REST_AT = {"text": 8, "image": 15}
MISC_AT = 12


def misc_grads(half, factors, vectors, out, scratch, spread):
    image_factors, text_factors = factors
    first, second, third = scratch

    def product(t, ref, at, size):
        final = ref[:, 0 : t.width].astype(BF16)
        start = pl.multiple_of(t.width + half * 256 + at, 128)
        return mm_tn(final, ref[:, pl.ds(start, size)].astype(BF16))

    first[...] = product(IMAGE, image_factors, 0, 128)
    second[...] = product(IMAGE, image_factors, 128, 128)
    third[...] = product(TEXT, text_factors, 0, 256)
    pack_twelve(first, second, out.ref, 1, 8)
    pack_rows(third, 8, out.ref, 0)
    spread[...] = jnp.zeros_like(spread)
    for side, refs_of, width in ((0, vectors[:8], 768), (64, vectors[8:], 512)):
        each = width // DEVS
        device = lax.broadcasted_iota(jnp.int32, (DEVS, width), 0)
        column = lax.broadcasted_iota(jnp.int32, (DEVS, width), 1)
        mine = jnp.logical_and(column >= device * each, column < device * each + each)
        source = lax.broadcasted_iota(jnp.int32, (width, 128), 0)
        lane = lax.broadcasted_iota(jnp.int32, (width, 128), 1)
        at = lax.rem(source, each)
        high_at = jnp.where(lane == at + side, 1.0, 0.0).astype(BF16)
        low_at = jnp.where(lane == at + side + 32, 1.0, 0.0).astype(BF16)
        rows = [refs_of[0][...], refs_of[1][...], refs_of[2][...] + refs_of[3][...]]
        rows += [refs_of[4][...] + refs_of[5][...], refs_of[6][...], refs_of[7][...]]
        for k, row in enumerate(rows):
            row = jnp.where(mine, row, 0.0)
            high = row.astype(BF16)
            low = (row - high.astype(F32)).astype(BF16)
            spread[:, 8 + k, :] += mm(high, high_at) + mm(low, low_at)
    out.ref[:, 2] = (out.ref[:, 2].astype(F32) + spread[...]).astype(BF16)
    out.units_done(slice(None), slice(0, 3), slice(MISC_AT, MISC_AT + 3))


def unpack_kernel(place, mine, other, *outs):
    split = 16 * IMAGE_FEED_UNITS
    feed_mine, feed_other = mine.at[0:split], other.at[0:split]
    late_mine, late_other = mine.at[split:], other.at[split:]
    (
        image_joint,
        image_output,
        image_widen,
        image_narrow,
        image_projection,
        text_joint,
        text_output,
        text_widen,
        text_narrow,
        text_projection,
    ) = outs[:10]
    odd = place[1] % 2

    def emit(half, feed, late):
        def into(ref, col, body, tail):
            @pl.when(odd == 0)
            def _():
                ref[0:8, col : col + 128] = body
                ref[8:12, col : col + 128] = tail

            @pl.when(odd == 1)
            def _():
                ref[0:4, col : col + 128] = tail
                ref[4:12, col : col + 128] = body

        def image_wide(source, at, store):
            for tile in range(3):
                block = source[16 * (at + 3 * tile) : 16 * (at + 3 * tile) + 48, :]
                for side in range(2):
                    for g in range(2):
                        body = block[16 * side + 8 * g : 16 * side + 8 * g + 8]
                        tail = block[32 + 8 * g + 4 * side : 36 + 8 * g + 4 * side]
                        store(half * 1536 + side * 768 + tile * 256 + g * 128, body, tail)

        def joint_store(col, body, tail):
            if col < 2304:
                into(image_joint, col, body, tail)
            else:
                into(image_output, col - 2304, body, tail)

        image_wide(feed, 0, functools.partial(into, image_widen))
        image_wide(late, REST_AT["image"], joint_store)
        at = 16 * 9
        for g in range(3):
            col = half * 384 + 128 * g
            image_narrow[:, col : col + 128] = feed[at + 48 * g : at + 48 * g + 48, :]
        at = 16 * (MISC_AT + 1)
        for side in range(2):
            col = half * 256 + 128 * side
            tail = late[at + 16 + 4 * side : at + 20 + 4 * side, :]
            into(image_projection, col, late[at + 8 * side : at + 8 * side + 8, :], tail)
        for g in range(8):
            col = half * 1024 + 128 * g
            at = 16 * TEXT_FEED_AT + 8 * g
            text_widen[:, col : col + 128] = late[at : at + 8, :]
            at = 16 * REST_AT["text"] + 8 * g
            block = late[at : at + 8, :]
            if col < 1536:
                text_joint[:, col : col + 128] = block
            else:
                text_output[:, col - 1536 : col - 1408] = block
        for g in range(2):
            col = half * 256 + 128 * g
            at = 16 * (TEXT_FEED_AT + 4) + 32 * g
            text_narrow[:, col : col + 128] = late[at : at + 32, :]
            at = 16 * MISC_AT + 8 * g
            text_projection[:, col : col + 128] = late[at : at + 8, :]

    for half in range(2):

        @pl.when(place[0] == half)
        def _():
            emit(half, feed_mine, late_mine)
            emit(1 - half, feed_other, late_other)

    at = 16 * (MISC_AT + 2) + 8
    vectors = late_mine[at : at + 8, :] + late_other[at : at + 8, :]
    for k in range(12):
        each, side = (12, 0) if k < 6 else (8, 64)
        row = vectors[k % 6 : k % 6 + 1, :]
        outs[10 + k][...] = row[:, side : side + each] + row[:, side + 32 : side + 32 + each]


SMEM = pl.BlockSpec(memory_space=pltpu.SMEM)
VMEM = pl.BlockSpec(memory_space=pltpu.VMEM)


def call(body, name, scalars, arrays, outs, scratch=(), flops=1 << 32):
    return pl.pallas_call(
        body,
        name=name,
        out_shape=tuple(jax.ShapeDtypeStruct(shape, kind) for shape, kind in outs),
        in_specs=[SMEM] * len(scalars) + [VMEM] * len(arrays),
        out_specs=tuple(VMEM for _ in outs),
        scratch_shapes=[pltpu.VMEM(shape, kind) for shape, kind in scratch],
        compiler_params=pltpu.CompilerParams(vmem_limit_bytes=VMEM_LIMIT),
        cost_estimate=pl.CostEstimate(flops=flops, bytes_accessed=20 << 20, transcendentals=0),
    )(*scalars, *arrays)


BIG = 1 << 18


def lazy_call(body, name, scalars, held, lazies, outs, scratch=(), flops=1 << 33, buffer=None, after=(), ahead=3):
    many = 24

    def kernel(*refs):
        refs = list(refs)

        def take(count):
            got = refs[:count]
            del refs[:count]
            return got

        scalar_refs, held_refs = take(len(scalars)), take(len(held))
        sources = take(len(lazies))
        take(len(after) + (buffer is not None))
        out_refs = take(len(outs))
        targets = take(len(lazies))
        stages = take(sum(1 for out in outs if out[2]))
        scratch_refs = take(len(scratch))
        in_sems, out_sems = refs
        lazy = []
        for i, (source, target, (_, index, _)) in enumerate(zip(sources, targets, lazies)):
            if index is not None:
                source = source.at[index(*scalar_refs)]
            lazy.append(Lazy(lazy, source, target, in_sems.at[i]))
        for item in lazy[:ahead]:
            item.start()
        pending = []
        results = []
        for out, ref in zip(outs, out_refs):
            if out[2] is None:
                results.append(ref)
            else:
                results.append(Staged(ref, stages.pop(0) if out[2] else None, out_sems, pending))
        body(scalar_refs, held_refs, lazy, results, scratch_refs)
        for item in lazy:
            if item.started:
                item.get()
        for copy in pending:
            copy.wait()

    any_spec = pl.BlockSpec(memory_space=pl.ANY)
    scratch_shapes = [pltpu.VMEM(shape, array.dtype) for array, _, shape in lazies]
    scratch_shapes += [pltpu.VMEM(stage, kind) for _, kind, stage in outs if stage]
    scratch_shapes += [pltpu.VMEM(shape, kind) for shape, kind in scratch]
    scratch_shapes += [pltpu.SemaphoreType.DMA((max(1, len(lazies)),)), pltpu.SemaphoreType.DMA((many,))]
    arrays = [*held, *[array for array, _, _ in lazies], *after]
    specs = [SMEM] * len(scalars) + [VMEM] * len(held) + [any_spec] * (len(lazies) + len(after))
    aliases = {}
    if buffer is not None:
        aliases = {len(scalars) + len(arrays): 0}
        arrays.append(buffer)
        specs.append(any_spec)
    return pl.pallas_call(
        kernel,
        name=name,
        out_shape=tuple(jax.ShapeDtypeStruct(shape, kind) for shape, kind, _ in outs),
        in_specs=specs,
        out_specs=tuple(VMEM if stage is None else any_spec for _, _, stage in outs),
        scratch_shapes=scratch_shapes,
        input_output_aliases=aliases,
        compiler_params=pltpu.CompilerParams(vmem_limit_bytes=VMEM_LIMIT),
        cost_estimate=pl.CostEstimate(flops=flops, bytes_accessed=20 << 20, transcendentals=0),
    )(*scalars, *arrays)


def all_of(array):
    return array, None, array.shape


def staged(shape, kind):
    return shape, kind, shape


def plain(shape, kind):
    return shape, kind, None


def fronts_call(lengths, tokens, block_grads, weights):
    held, lazies, outs, scratch = [], [], [], []
    for t, token, grad, w in zip((IMAGE, TEXT), tokens, block_grads, weights):
        rows, width, hidden = t.rows, t.width, t.hidden
        held += [token, w[0], w[1], w[4], w[5], w[8], w[9], grad]
        lazies += [all_of(w[i]) for i in (2, 3, 6, 7, 10)]
        outs += [
            staged((2 * width, t.lanes), BF16),
            staged((BATCH, t.padded, 3 * width), BF16),
            staged((BATCH, t.heads // 2, t.padded, 2 * t.padded), BF16),
            staged((rows, width), F32),
            plain((BATCH, EMBED), BF16),
        ]
        scratch += [
            ((3 * width // 128, t.spread, 128), F32),
            ((width // 128, t.spread, 128), F32),
            ((rows, width), BF16),
            ((rows, width), BF16),
        ]
    lazies = [lazies[i] for i in (5, 6, 0, 7, 8, 9, 1, 2, 3, 4)]
    outs.append(plain((BATCH, ROW_TOTAL), F32))
    outs.append(plain((DEVS, BATCH, 2 * EMBED), BF16))
    results = lazy_call(fronts_kernel, "fronts", (lengths,), held, lazies, outs, scratch, ahead=6)
    return results[:5], results[5:10], results[10], results[11]


def middle(t, name, place, lengths, mixed, block_grad, gain, shift, widen, narrow, after):
    rows, width, hidden = t.rows, t.width, t.hidden
    steps = hidden // t.step
    outs = (
        ((width, t.lanes), BF16),
        ((hidden, t.lanes), BF16),
        ((rows, hidden // 2), BF16),
        ((rows, hidden // 2), BF16),
        ((rows, width // 2), BF16),
        ((rows, width // 2), BF16),
        ((rows, width), F32),
        ((1, width), F32),
        ((1, width), F32),
    )

    def held(shape):
        return pl.BlockSpec(shape, lambda i, *_: (0,) * len(shape))

    def tile(i, place):
        return lax.rem(i + place[0] * (steps // 2), steps)

    out_specs = [held(shape) for shape, _ in outs]
    out_specs[1] = pl.BlockSpec((t.step, t.lanes), lambda i, place, lengths: (tile(i, place), 0))
    out_specs[2] = pl.BlockSpec((rows, t.step), lambda i, *_: (0, jnp.minimum(i, steps // 2 - 1)))
    out_specs[3] = pl.BlockSpec((rows, t.step), lambda i, *_: (0, jnp.maximum(i - steps // 2, 0)))
    in_specs = [held(a.shape) for a in (mixed, block_grad, gain, shift)]
    in_specs.append(pl.BlockSpec((width, t.step), lambda i, place, lengths: (0, tile(i, place))))
    in_specs.append(pl.BlockSpec((t.step, width), lambda i, place, lengths: (tile(i, place), 0)))
    in_specs += [pl.BlockSpec(memory_space=pl.ANY)] * len(after)

    def kernel(*refs):
        middle_kernel(t, *refs[:8], *refs[8 + len(after) :])

    return pl.pallas_call(
        kernel,
        name=name + "_middle",
        out_shape=tuple(jax.ShapeDtypeStruct(shape, kind) for shape, kind in outs),
        grid_spec=pltpu.PrefetchScalarGridSpec(
            num_scalar_prefetch=2,
            grid=(steps,),
            in_specs=in_specs,
            out_specs=tuple(out_specs),
            scratch_shapes=[
                pltpu.VMEM((rows, width), BF16),
                pltpu.VMEM((rows, width), BF16),
                pltpu.VMEM((rows, width), F32),
            ],
        ),
        compiler_params=pltpu.CompilerParams(vmem_limit_bytes=VMEM_LIMIT),
        cost_estimate=pl.CostEstimate(flops=1 << 35, bytes_accessed=20 << 20, transcendentals=0),
    )(place, lengths, mixed, block_grad, gain, shift, widen, narrow, *after)


def head_outs(t):
    return [plain((1, t.width), F32)] * 4 + [
        plain((2 * BATCH, t.width + EMBED), F32),
        plain((BATCH, t.width), F32),
        plain((2 * BATCH, t.width), F32),
        plain((2 * BATCH, t.hidden), F32),
    ]


def backs_call(place, lengths, head_in, head_weights, image_row, towers, after):
    held, lazies, outs, scratch = [*head_in], [], head_outs(TEXT), []
    for t, (tokens, gain, arrays) in zip((IMAGE, TEXT), towers):
        rows, width = t.rows, t.width
        held += [tokens, gain]
        if t is IMAGE:
            held.append(image_row)
        lazies += [all_of(a) for a in arrays]
        outs += [
            ((rows, 2 * width), BF16, ()),
            ((rows, 2 * width), BF16, ()),
            staged((t.real, width), F32),
            plain((1, width), F32),
            plain((1, width), F32),
        ]
        scratch += [
            ((width // 128, t.spread, 128), F32),
            ((3 * width // 128, t.spread, 128), F32),
            ((rows, width), F32),
            ((rows, 4 * width), BF16),
        ]
    lazies = [lazies[i] for i in (5, 6, 0, 1, 7, 8, 2, 3, 9, 4)]
    lazies = [all_of(w) for w in head_weights] + lazies
    results = lazy_call(
        backs_kernel, "backs", (place, lengths), held, lazies, outs, scratch, after=after, ahead=8
    )
    return results[:8], results[8:13], results[13:]


def feed(t, place, head, middle, other, buffer, after):
    rows, width = t.rows, t.width
    name = "image" if t is IMAGE else "text"
    own = (middle[0], middle[1], middle[2], middle[4])
    lazies = [all_of(own[0]), all_of(other[0]), all_of(own[2]), all_of(other[2])]
    lazies += [all_of(own[3]), all_of(other[3])]
    for j in range(4):
        some = slice(width * j, width * j + width)
        for side in (own, other):
            lazies.append((side[1], lambda *_, some=some: (some, slice(None)), (width, t.lanes)))
    cols = 256 if t is IMAGE else 512
    scratch = [
        ((width, cols), F32),
        ((width, cols) if t is IMAGE else (8, 128), F32),
        ((width, width // 2), F32),
    ]
    units = IMAGE_FEED_UNITS if t is IMAGE else 8
    total = LATE_UNITS if buffer else units
    (out,) = lazy_call(
        functools.partial(feed_kernel, t, TEXT_FEED_AT if buffer else 0),
        name + "_feed",
        (place,),
        (head[7], head[6]),
        lazies,
        [((DEVS, total, 16, 128), BF16, (DEVS, units, 16, 128))],
        scratch,
        after=after,
        ahead=10,
    )
    return out


def rest(place, factors, vectors, sides, buffer):
    lazies = []
    for own, other in (sides[1], sides[0]):
        lazies += [all_of(a) for a in (*own, *other)]
    outs = [((DEVS, LATE_UNITS, 16, 128), BF16, ())]
    scratch = [
        ((768, 256), F32),
        ((768, 256), F32),
        ((512, 512), F32),
        ((768, 128), F32),
        ((768, 128), F32),
        ((512, 256), F32),
        ((DEVS, 16, 128), F32),
        ((DEVS, 3, 16, 128), BF16),
        ((DEVS, 4, 16, 128), BF16),
        ((DEVS, 9, 16, 128), BF16),
    ]
    (out,) = lazy_call(
        rest_kernel, "rest", (place,), [*factors, *vectors], lazies, outs, scratch, buffer=buffer, ahead=4
    )
    return out


def sum_blocks(pieces):
    lazies, steps = [], []
    for received, step in pieces:
        devices, units = received.shape[:2]
        for at in range(0, units, step):
            some = slice(at, at + step)
            lazies.append(
                (received, lambda *_, some=some: (slice(None), some), (devices, step, 16, 128))
            )
            steps.append(step)

    def body(scalars, held, blocks, outs, scratch):
        at = 0
        for step, block in zip(steps, blocks):
            total = jnp.sum(block.get()[...].astype(F32), axis=0)
            outs[0][at : at + 16 * step, :] = total.reshape(16 * step, 128)
            at += 16 * step

    outs = [plain((16 * sum(steps), 128), F32)]
    return lazy_call(body, "sum_blocks", (), (), lazies, outs, flops=1 << 34, ahead=len(lazies))[0]


def behind(arrays, after):
    def kernel(*refs):
        pass

    any_spec = pl.BlockSpec(memory_space=pl.ANY)
    return pl.pallas_call(
        kernel,
        name="behind",
        out_shape=[jax.ShapeDtypeStruct(array.shape, array.dtype) for array in arrays],
        in_specs=[any_spec] * (len(arrays) + len(after)),
        out_specs=[any_spec] * len(arrays),
        input_output_aliases={i: i for i in range(len(arrays))},
    )(*arrays, *after)


SWAP = [(0, 1), (1, 0)]


def by_token(tokens):
    return tokens.transpose(1, 0, 2).reshape(-1, tokens.shape[2])


def shards(*args):
    image_tokens, image_weights, image_block_grad = args[0], args[1:12], args[12]
    text_tokens, caption_lengths = args[13], args[14]
    text_weights, text_block_grad, log_scale = args[15:26], args[26], args[27]
    core = lax.axis_index("tower")
    dp = lax.axis_index("dp")
    place = jnp.stack([core, dp]).astype(jnp.int32)
    tokens = (by_token(image_tokens), by_token(text_tokens))
    block_grads = (by_token(image_block_grad), by_token(text_block_grad))
    weights = (image_weights, text_weights)
    kinds = ((0, IMAGE, "image"), (1, TEXT, "text"))
    *fronts, kept, copies = fronts_call(caption_lengths, tokens, block_grads, weights)
    units = [f[4] for f in fronts]
    own = lax.all_to_all(copies, "dp", 0, 0, tiled=True).reshape(DEVS * BATCH, 2 * EMBED)

    def swap(*arrays):
        return [lax.ppermute(array, "tower", SWAP) for array in arrays]

    def middle_of(i, after):
        _, t, name = kinds[i]
        w = weights[i]
        return middle(
            t, name, place, caption_lengths, fronts[i][3], block_grads[i], w[4], w[5], w[6], w[7], after
        )

    (kept_other,) = swap(kept)
    image_middle = list(middle_of(0, ()))
    (own,) = behind([own], (image_middle[0], kept_other))
    (other,) = swap(own)
    sent = (0, 1, 3, 5)
    for k, array in zip(sent, behind([image_middle[k] for k in sent], (other,))):
        image_middle[k] = array
    image_sent = swap(*[image_middle[k] for k in sent])

    w = image_weights
    paired = lazy_call(
        pair_kernel,
        "pairs",
        (place, log_scale),
        [own, other, kept, kept_other, w[8], w[9], w[4], w[5]],
        [all_of(w[10]), all_of(w[7]), all_of(w[6])],
        [plain((1, 128), F32), plain((1, 128), F32), plain((2 * BATCH, EMBED), F32), *head_outs(IMAGE)],
        ahead=6,
    )
    loss, scale_grad = paired[0][0, :1], paired[1][0, :1]
    image_head = paired[3:]
    image_feed = feed(IMAGE, place, image_head, image_middle, image_sent, False, ())
    feed_total = lax.all_to_all(image_feed, "dp", 0, 0, tiled=True)
    text_middle = middle_of(1, (image_feed,))
    middles = (image_middle, text_middle)

    back_in = []
    for i, _, _ in kinds:
        f, m, w = fronts[i], middles[i], weights[i]
        back_in.append((tokens[i], w[0], (w[3], m[6], f[1], f[2], w[2])))
    w = text_weights
    text_head, *backs = backs_call(
        place,
        caption_lengths,
        [paired[2], kept, kept_other, w[8], w[9], w[4], w[5]],
        [w[10], w[7], w[6]],
        image_head[5],
        back_in,
        (text_middle[0],),
    )
    heads = (image_head, text_head)
    text_sent = swap(*[text_middle[k] for k in sent])
    late = feed(TEXT, place, heads[1], text_middle, text_sent, True, (backs[1][0],))
    sides = []
    for f, k in zip(fronts, backs):
        sides.append(((f[0], k[0]), swap(f[0], k[1])))
    vectors = []
    for m, h, k in zip(middles, heads, backs):
        vectors += [k[3], k[4], m[7], h[2], m[8], h[3], h[0], h[1]]
    factors = [heads[0][4], heads[1][4]]
    (late,) = behind([rest(place, factors, vectors, sides, late)], (feed_total,))
    late_total = lax.all_to_all(late, "dp", 0, 0, tiled=True)
    mine = sum_blocks(((feed_total, 6), (late_total, 4)))
    (theirs,) = swap(mine)
    weight_outs = (
        ((12, 2304), F32),
        ((12, 768), F32),
        ((12, 3072), F32),
        ((48, 768), F32),
        ((12, 512), F32),
        ((8, 1536), F32),
        ((8, 512), F32),
        ((8, 2048), F32),
        ((32, 512), F32),
        ((8, 512), F32),
    )
    vector_outs = (((1, 12), F32),) * 6 + (((1, 8), F32),) * 6
    grads = call(unpack_kernel, "unpack", (place,), (mine, theirs), weight_outs + vector_outs)

    def ordered(vectors, weights):
        joint, output, widen, narrow, projection = weights
        v = [x.reshape(-1) for x in vectors]
        return [v[0], v[1], joint, output, v[2], v[3], widen, narrow, v[4], v[5], projection]

    def by_sequence(t, grad):
        return grad.reshape(t.length, BATCH, t.width).transpose(1, 0, 2)

    return (
        loss,
        units[0],
        units[1],
        by_sequence(IMAGE, backs[0][2]),
        *ordered(grads[10:16], grads[:5]),
        by_sequence(TEXT, backs[1][2]),
        *ordered(grads[16:22], grads[5:10]),
        scale_grad,
    )


def solution(mesh):
    spread = P(("tower", "dp"), None, None)
    weights = [P()] * 11
    placed = (spread, *weights, spread, spread, P(("tower", "dp")), *weights, spread, P())
    vector, matrix = P("dp"), P("dp", None)
    grads = [vector, vector, matrix, matrix, vector, vector, matrix, matrix, vector, vector, matrix]
    units = P(("tower", "dp"), None)
    return jax.shard_map(
        shards,
        mesh=mesh,
        in_specs=placed,
        out_specs=(P(), units, units, spread, *grads, spread, *grads, P()),
        check_vma=False,
    )
```

```python
import functools

import jax
import jax.numpy as jnp
from jax import lax
from jax.experimental import pallas as pl
from jax.experimental.pallas import tpu as pltpu
from jax.sharding import PartitionSpec as P

F32 = jnp.float32
BF16 = jnp.bfloat16
BATCH = 8
EMBED = 512
TILE = 256
DEVS = 64


class Tower:
    def __init__(self, width, heads, hidden, length, padded, rows, extra, causal):
        self.width = width
        self.heads = heads
        self.hidden = hidden
        self.length = length
        self.padded = padded
        self.real = BATCH * length
        self.rows = rows
        self.extra = extra
        self.spread = BATCH * padded
        self.lanes = -(-rows // 128) * 128
        self.causal = causal
        self.step = 768 if width == 768 else 512


IMAGE = Tower(768, 12, 3072, 50, 64, 416, 400, False)
TEXT = Tower(512, 8, 2048, 77, 80, 640, 624, True)

VMEM_LIMIT = 64 * 1024 * 1024


def mm(left, right):
    return lax.dot_general(left, right, (((1,), (0,)), ((), ())), preferred_element_type=F32)


def mm_nt(left, right):
    return lax.dot_general(left, right, (((1,), (1,)), ((), ())), preferred_element_type=F32)


def mm_tn(left, right):
    return lax.dot_general(left, right, (((0,), (0,)), ((), ())), preferred_element_type=F32)


def normalise(values):
    centre = jnp.mean(values, axis=-1, keepdims=True)
    offset = values - centre
    inverse = lax.rsqrt(jnp.mean(offset * offset, axis=-1, keepdims=True) + 1e-05)
    return offset * inverse, inverse


def norm_back(upstream, gain, normal, inverse):
    scaled = upstream * gain
    inner = (
        scaled
        - jnp.mean(scaled, axis=-1, keepdims=True)
        - normal * jnp.mean(scaled * normal, axis=-1, keepdims=True)
    )
    return inner * inverse


def column_sum(values):
    return jnp.sum(values, axis=0, keepdims=True)


def sigmoid(values):
    return 0.5 + 0.5 * jnp.tanh(0.5 * values)


def vec(ref):
    return ref[...].reshape(1, -1)


def chunks(count, size=128):
    return [(at, min(size, count - at)) for at in range(0, count, size)]


UNROLL_TILE, UNROLL_HEADS, UNROLL_PACK = 9, 8, 4
UNROLL_BACK = 1


def loop(count, body, unroll=1):
    def step(i, carry):
        body(i)
        return carry

    lax.fori_loop(0, count, step, 0, unroll=min(unroll, count))


def tile_loop(width, body):
    loop(width // TILE, lambda n: body(n, pl.ds(pl.multiple_of(n * TILE, TILE), TILE)), UNROLL_TILE)


def put_tiles(ref, n, rows, values):
    for i in range(TILE // 128):
        ref[n * (TILE // 128) + i, 0:rows, :] = values[:, 128 * i : 128 * i + 128]


class Lazy:
    def __init__(self, queue, source, target, sem):
        self.copy = pltpu.make_async_copy(source, target, sem)
        self.target = target
        self.queue = queue
        self.started = self.waited = False

    def start(self):
        if not self.started:
            self.copy.start()
            self.started = True

    def get(self):
        if not self.waited:
            self.start()
            self.copy.wait()
            self.waited = True
            for item in self.queue:
                if not item.started:
                    item.start()
                    break
        return self.target


class Staged:
    def __init__(self, out, stage, sems, pending):
        self.out = out
        self.ref = stage
        self.sems = sems
        self.pending = pending

    def send(self, source, target):
        copy = pltpu.make_async_copy(source, target, self.sems.at[len(self.pending)])
        copy.start()
        self.pending.append(copy)

    def done(self):
        self.send(self.ref, self.out)

    def units_done(self, devices, units, out_units):
        self.send(self.ref.at[devices, units], self.out.at[devices, out_units])


def head_masks():
    lane = lax.broadcasted_iota(jnp.int32, (1, 128), 1)
    first = jnp.where(lane < 64, 1.0, 0.0).astype(BF16)
    second = jnp.where(lane < 64, 0.0, 1.0).astype(BF16)
    return first, second


def two_heads(values, masks):
    return jnp.concatenate([values * masks[0], values * masks[1]], axis=0)


def own_head(values, padded):
    lane = lax.broadcasted_iota(jnp.int32, (padded, 128), 1)
    return jnp.where(lane < 64, values[:padded], values[padded:])


def pooled_row(t, lengths, b):
    return b if t is IMAGE else (lengths[b] - 1) * BATCH + b


def row_parts(t):
    return {
        "raw": EMBED,
        "unit": EMBED,
        "pooled": t.width,
        "mixed": t.width,
        "grad": t.width,
        "wide": t.hidden,
    }


def row_part(t, name):
    at = 0 if t is IMAGE else sum(row_parts(IMAGE).values())
    for part, size in row_parts(t).items():
        if part == name:
            return slice(at, at + size)
        at += size


ROW_TOTAL = sum(row_parts(IMAGE).values()) + sum(row_parts(TEXT).values())


class Front:
    def __init__(self, t, lengths, ins, weights, outs, kept, scratch):
        self.t = t
        self.lengths = lengths
        (
            self.tokens,
            self.first_gain,
            self.first_shift,
            self.second_gain,
            self.second_shift,
            self.final_gain,
            self.final_shift,
            self.block_grad,
        ) = ins
        self.joint_weight, self.output_weight, self.widen, self.narrow, self.projection = weights
        self.staged = outs[:4]
        self.turned, self.joint, self.probs, self.mixed = [out.ref for out in outs[:4]]
        self.unit = outs[4]
        self.kept = kept
        self.joint_wide, self.context_wide, self.normed_one, self.context = scratch
        self.mixed_row = kept.at[:, row_part(t, "mixed")]

    def norm(self):
        t, rows = self.t, self.t.rows
        mixed, normed_one = self.mixed, self.normed_one
        grad_row = self.kept.at[:, row_part(t, "grad")]
        for at, size in chunks(t.real):
            mixed[at : at + size, :] = self.block_grad[at : at + size, :].astype(F32)
        for b in range(BATCH):
            grad_row[b : b + 1, :] = mixed[pl.ds(pooled_row(t, self.lengths, b), 1), :]
        pad = t.real - t.real % 16
        normed_one[pad:rows, :] = jnp.zeros((rows - pad, t.width), BF16)
        for at, size in chunks(t.real):
            normal, _ = normalise(self.tokens[at : at + size, :].astype(F32))
            normed_one[at : at + size, :] = (
                normal * vec(self.first_gain) + vec(self.first_shift)
            ).astype(BF16)
        if t.spread > rows:
            fill = (3 * t.width // 128, t.spread - rows, 128)
            self.joint_wide[:, rows : t.spread, :] = jnp.zeros(fill, F32)

    def joint_tile(self, n):
        cols = pl.ds(pl.multiple_of(n * TILE, TILE), TILE)
        product = mm(self.normed_one[...], self.joint_weight.get()[:, cols])
        put_tiles(self.joint_wide, n, self.t.rows, product)

    def ready(self):
        t, padded = self.t, self.t.padded
        self.masks = head_masks()
        key_at = lax.broadcasted_iota(jnp.int32, (padded, 2 * padded), 0)
        query_at = lax.broadcasted_iota(jnp.int32, (padded, 2 * padded), 1)
        query_at = jnp.where(query_at < padded, query_at, query_at - padded)
        self.valid = key_at <= query_at if t.causal else key_at < t.length

    def attend(self, b):
        t, joint, masks = self.t, self.joint, self.masks
        width, padded = t.width, t.padded
        pairs = range(t.heads // 2)
        some = pl.ds(b, padded, stride=BATCH)
        for c in range(3 * width // 128):
            joint[b, :, 128 * c : 128 * c + 128] = self.joint_wide[c, some, :].astype(BF16)
        scores = []
        for p in pairs:
            at = 128 * p
            queries = joint[b, :, at : at + 128]
            keys = joint[b, :, width + at : width + at + 128]
            scores.append(mm_nt(keys, two_heads(queries, masks)) * 0.125)
        lows = []
        for p in pairs:
            score = jnp.where(self.valid, scores[p], -1e30)
            raised = jnp.exp(score - jnp.max(score, axis=0, keepdims=True))
            low = (raised * (1.0 / column_sum(raised))).astype(BF16)
            self.probs[b, p] = low
            lows.append(low)
        for p in pairs:
            at = 2 * width + 128 * p
            both = mm_tn(lows[p], joint[b, :, at : at + 128])
            self.context_wide[p, some, :] = own_head(both, padded)

    def mix(self):
        t, rows, width = self.t, self.t.rows, self.t.width
        context, mixed = self.context, self.mixed
        self.staged[1].done()
        self.staged[2].done()
        for p in range(t.heads // 2):
            context[:, 128 * p : 128 * p + 128] = self.context_wide[p, 0:rows, :].astype(BF16)
        turn(self.normed_one, self.turned.at[0:width], 6)
        turn(context, self.turned.at[width : 2 * width], 6)
        self.staged[0].done()
        output_weight = self.output_weight.get()

        def mix_step(n, cols):
            mixed[:, cols] = mm(context[...], output_weight[:, cols])

        tile_loop(width, mix_step)
        for at, size in chunks(t.real):
            mixed[at : at + size, :] += self.tokens[at : at + size, :].astype(F32)
        for b in range(BATCH):
            row = mixed[pl.ds(pooled_row(t, self.lengths, b), 1), :]
            self.mixed_row[b : b + 1, :] = row
        mixed[t.real : rows, :] = jnp.zeros((rows - t.real, width), F32)
        mixed[t.extra : t.extra + BATCH, :] = self.mixed_row[...]
        self.staged[3].done()

    def embed(self):
        t, kept = self.t, self.kept
        row = self.mixed_row[...]
        normal, _ = normalise(row)
        normed = (normal * vec(self.second_gain) + vec(self.second_shift)).astype(BF16)
        wide = mm(normed, self.widen.get()[...])
        kept[:, row_part(t, "wide")] = wide
        active = (wide * sigmoid(1.702 * wide)).astype(BF16)
        last = row + mm(active, self.narrow.get()[...])
        kept[:, row_part(t, "pooled")] = last
        normal, _ = normalise(last)
        normed = (normal * vec(self.final_gain) + vec(self.final_shift)).astype(BF16)
        raw = mm(normed, self.projection.get()[...])
        kept[:, row_part(t, "raw")] = raw
        factor = lax.rsqrt(jnp.sum(raw * raw, axis=-1, keepdims=True) + 1e-06)
        unit = (raw * factor).astype(BF16)
        self.unit[...] = unit
        kept[:, row_part(t, "unit")] = unit.astype(F32)
        return unit


def fronts_kernel(scalars, held, lazies, outs, scratch):
    order = [5, 6, 0, 7, 8, 9, 1, 2, 3, 4]
    weights = [lazies[order.index(i)] for i in range(10)]
    image, text = [
        Front(
            t,
            scalars[0],
            held[8 * i : 8 * i + 8],
            weights[5 * i : 5 * i + 5],
            outs[5 * i : 5 * i + 5],
            outs[10],
            scratch[4 * i : 4 * i + 4],
        )
        for i, t in enumerate((IMAGE, TEXT))
    ]
    text.norm()
    for n in range(3 * TEXT.width // TILE):
        text.joint_tile(n)
    image.norm()
    for front in (image, text):
        front.ready()
    image.joint_weight.get()
    tiles = 3 * IMAGE.width // TILE

    def both(b):
        text.attend(b)
        image.joint_tile(b)

    loop(BATCH, both, UNROLL_HEADS)
    for n in range(BATCH, tiles):
        image.joint_tile(n)
    text.mix()
    loop(BATCH, image.attend, UNROLL_HEADS)
    image.mix()
    for i, unit in enumerate((image.embed(), text.embed())):
        outs[11][:, :, EMBED * i : EMBED * i + EMBED] = jnp.broadcast_to(unit[None], (DEVS, *unit.shape))


def middle_kernel(
    t,
    place,
    lengths,
    mixed,
    block_grad,
    second_gain,
    second_shift,
    widen_weight,
    narrow_weight,
    normed_turned,
    active_turned,
    wide_own,
    wide_send,
    narrow_own,
    narrow_send,
    mixed_grad,
    gain_grad,
    shift_grad,
    normed_two,
    narrow_in,
    wide_in,
):
    step = pl.program_id(0)
    half_steps = pl.num_programs(0) // 2

    @pl.when(step == 0)
    def _():
        wide_in[t.real : t.rows, :] = jnp.zeros((t.rows - t.real, t.width), F32)
        for at, size in chunks(t.rows):
            normal, _ = normalise(mixed[at : at + size, :])
            normed_two[at : at + size, :] = (normal * vec(second_gain) + vec(second_shift)).astype(
                BF16
            )
        turn(normed_two, normed_turned)
        for at, size in chunks(t.real):
            wide_in[at : at + size, :] = block_grad[at : at + size, :].astype(F32)
        for b in range(BATCH):
            wide_in[pl.ds(pooled_row(t, lengths, b), 1), :] = jnp.zeros((1, t.width), F32)
        narrow_in[...] = wide_in[...].astype(BF16)
        cols = t.width // 2
        own = pl.multiple_of(place[0] * cols, 128)
        narrow_own[...] = narrow_in[:, pl.ds(own, cols)]
        narrow_send[...] = narrow_in[:, pl.ds(pl.multiple_of(cols - own, 128), cols)]
        mixed_grad[...] = jnp.zeros_like(mixed_grad)

    lows = []
    for at, size in chunks(t.step, TILE):
        some = slice(at, at + size)
        wide = mm(normed_two[...], widen_weight[:, some])
        back = mm_nt(narrow_in[...], narrow_weight[some, :])
        sig = sigmoid(1.702 * wide)
        active = wide * sig
        active_turned[some, 0 : t.rows] = active.astype(BF16).T
        slope = sig + 1.702 * active * (1.0 - sig)
        lows.append((back * slope).astype(BF16))
    low = jnp.concatenate(lows, axis=1)
    mixed_grad[...] += mm_nt(low, widen_weight[...])

    @pl.when(step < half_steps)
    def _():
        wide_own[...] = low

    @pl.when(step >= half_steps)
    def _():
        wide_send[...] = low

    @pl.when(step == pl.num_programs(0) - 1)
    def _():
        gain = shift = 0.0
        for at, size in chunks(t.rows):
            some = slice(at, at + size)
            normal, inverse = normalise(mixed[some, :])
            up = mixed_grad[some, :]
            gain += column_sum(up * normal)
            shift += column_sum(up)
            mixed_grad[some, :] = wide_in[some, :] + norm_back(
                up, vec(second_gain), normal, inverse
            )
        gain_grad[...] = gain
        shift_grad[...] = shift


def split_dot(weights, right):
    high = weights.astype(BF16)
    rest = weights - high.astype(F32)
    middle = rest.astype(BF16)
    low = (rest - middle.astype(F32)).astype(BF16)
    return mm(high, right) + mm(middle, right) + mm(low, right)


def head_back(
    unit_grad,
    raw,
    pooled,
    mixed_row,
    wide_row,
    grad_row,
    final_gain,
    final_shift,
    second_gain,
    second_shift,
    projection,
    widen_weight,
    narrow_weight,
    outs,
):
    (
        final_gain_grad,
        final_shift_grad,
        second_gain_grad,
        second_shift_grad,
        factors,
        mixed_grad_row,
        narrow_in_row,
        wide_grad_row,
    ) = outs
    own = slice(0, BATCH)
    width = pooled.shape[1]
    factor = lax.rsqrt(jnp.sum(raw * raw, axis=-1, keepdims=True) + 1e-06)
    raw_grad = factor * unit_grad - raw * (factor * factor * factor) * jnp.sum(
        unit_grad * raw, axis=-1, keepdims=True
    )
    raw_grad = raw_grad.astype(BF16)
    factors[:, width:] = raw_grad.astype(F32)
    normal, inverse = normalise(pooled)
    factors[:, 0:width] = (normal * final_gain + final_shift).astype(BF16).astype(F32)
    up = mm_nt(raw_grad, projection.get()[...])
    final_gain_grad[...] = column_sum((up * normal)[own])
    final_shift_grad[...] = column_sum(up[own])
    out_grad = grad_row + norm_back(up, final_gain, normal, inverse)
    narrow_in = out_grad.astype(BF16)
    narrow_in_row[...] = narrow_in.astype(F32)
    sig = sigmoid(1.702 * wide_row)
    slope = sig + 1.702 * wide_row * sig * (1.0 - sig)
    low = (mm_nt(narrow_in, narrow_weight.get()[...]) * slope).astype(BF16)
    wide_grad_row[...] = low.astype(F32)
    up = mm_nt(low, widen_weight.get()[...])
    normal, inverse = normalise(mixed_row)
    second_gain_grad[...] = column_sum((up * normal)[own])
    second_shift_grad[...] = column_sum(up[own])
    mixed_grad_row[...] = (out_grad + norm_back(up, second_gain, normal, inverse))[own]


def kept_rows(own, other, t, name):
    some = row_part(t, name)
    return jnp.concatenate([own[:, some], other[:, some]], axis=0)


def head_of(t, unit_grad, kept, vectors, weights, outs):
    values = [kept_rows(*kept, t, name) for name in ("raw", "pooled", "mixed", "wide", "grad")]
    values += [vec(ref) for ref in vectors]
    projection, narrow, widen = weights
    head_back(unit_grad, *values, projection, widen, narrow, outs)


def pair_kernel(scalars, held, lazies, outs, scratch):
    place, log_scale = scalars
    own, other, kept_own, kept_other = held[:4]
    loss, scale_grad, text_grad = outs[:3]
    kept = (kept_own, kept_other)
    half = own.shape[0]
    pairs = 2 * half
    scale = jnp.exp(jnp.full((1, 1), log_scale[0], F32))
    blocks = (own, other)

    def totals(left_at, right_at):
        sums, moments = [], []
        for right in blocks:
            column, moment = None, None
            for left in blocks:
                for piece in range(0, half, 256):
                    sims = scale * mm_nt(
                        left[piece : piece + 256, left_at : left_at + EMBED],
                        right[:, right_at : right_at + EMBED],
                    )
                    raised = jnp.exp(sims)
                    add, more = column_sum(raised), column_sum(raised * sims)
                    column = add if column is None else column + add
                    moment = more if moment is None else moment + more
            sums.append(column)
            moments.append(moment)
        return sums, moments

    column_sums, column_moments = totals(0, EMBED)
    row_sums, row_moments = totals(EMBED, 0)
    log_total = jnp.zeros((1, 1), F32)
    weighted = jnp.zeros((1, 1), F32)
    trace = jnp.zeros((1, 1), F32)
    for i in range(2):
        for total, moment in ((column_sums[i], column_moments[i]), (row_sums[i], row_moments[i])):
            log_total += jnp.sum(jnp.log(total), axis=-1, keepdims=True)
            weighted += jnp.sum(moment / total, axis=-1, keepdims=True)
        product = blocks[i][:, :EMBED].astype(F32) * blocks[i][:, EMBED:].astype(F32)
        trace += jnp.sum(column_sum(product), axis=-1, keepdims=True)
    trace = scale * trace
    loss[...] = jnp.broadcast_to((log_total - 2.0 * trace) / (2.0 * pairs), loss.shape)
    scale_grad[...] = jnp.broadcast_to((weighted - 2.0 * trace) / (2.0 * pairs), loss.shape)

    lane = lax.broadcasted_iota(jnp.int32, (2 * BATCH, half), 1)
    sub = lax.broadcasted_iota(jnp.int32, (2 * BATCH, half), 0)
    diagonal = place[1] * BATCH
    identity = [
        jnp.where(jnp.logical_and(lane == sub + diagonal, sub < BATCH), 2.0, 0.0),
        jnp.where(jnp.logical_and(lane == sub - BATCH + diagonal, sub >= BATCH), 2.0, 0.0),
    ]

    def grads(t, at, other_sums):
        unit = kept_rows(*kept, t, "unit").astype(BF16)
        raised = [jnp.exp(scale * mm_nt(unit, block[:, at : at + EMBED])) for block in blocks]
        own_sum = sum(jnp.sum(r, axis=-1, keepdims=True) for r in raised)
        result = None
        for i in range(2):
            weight = raised[i] * (1.0 / own_sum + 1.0 / other_sums[i]) - identity[i]
            weight = weight / (2.0 * pairs)
            part = split_dot(weight, blocks[i][:, at : at + EMBED])
            result = part if result is None else result + part
        return scale * result

    image_grad = grads(IMAGE, EMBED, column_sums)
    text_grad[...] = grads(TEXT, 0, row_sums)
    head_of(IMAGE, image_grad, kept, held[4:8], lazies, outs[3:11])


class Back:
    def __init__(self, t, place, lengths, held, lazies, outs, scratch):
        self.t = t
        self.place = place
        self.lengths = lengths
        self.tokens, self.first_gain, self.row = held[:3]
        self.output_weight, self.mixed_grad, self.joint_in, self.probs_in, self.joint_weight = lazies
        self.own, self.send, self.tokens_out, self.gain_grad, self.shift_grad = outs
        self.context_grad, self.joint_grad, self.normed_grad, self.grads = scratch

    def context(self):
        t, rows, width, grads = self.t, self.t.rows, self.t.width, self.grads
        self.grad = grad = self.mixed_grad.get()
        for b in range(BATCH):
            grad[pl.ds(pooled_row(t, self.lengths, b), 1), :] = self.row[b : b + 1, :]
        mixed_low = slice(3 * width, 4 * width)
        grads[:, mixed_low] = grad[...].astype(BF16)
        if t.spread > rows:
            fill = (width // 128, t.spread - rows, 128)
            self.context_grad[:, rows : t.spread, :] = jnp.zeros(fill, F32)
        output_weight = self.output_weight.get()

        def step(n, cols):
            put_tiles(self.context_grad, n, rows, mm_nt(grads[:, mixed_low], output_weight[cols, :]))

        tile_loop(width, step)
        self.masks = head_masks()
        self.joint, self.probs = self.joint_in.get(), self.probs_in.get()

    def attend(self, b):
        t, masks, joint, joint_grad = self.t, self.masks, self.joint, self.joint_grad
        width, padded = t.width, t.padded
        pairs = range(t.heads // 2)
        some = pl.ds(b, padded, stride=BATCH)
        ups = [two_heads(self.context_grad[p, some, :].astype(BF16), masks) for p in pairs]
        backs = []
        for p in pairs:
            at = 2 * width + 128 * p
            backs.append(mm_nt(joint[b, :, at : at + 128], ups[p]))
        lows = []
        for p in pairs:
            wide = self.probs[b, p].astype(F32)
            back = wide * (backs[p] - column_sum(backs[p] * wide))
            lows.append(back.astype(BF16))
        for p in pairs:
            at = 128 * p
            queries = joint[b, :, at : at + 128]
            keys = joint[b, :, width + at : width + at + 128]
            joint_grad[2 * len(pairs) + p, some, :] = mm(self.probs[b, p], ups[p])
            joint_grad[len(pairs) + p, some, :] = mm(lows[p], two_heads(queries, masks)) * 0.125
            joint_grad[p, some, :] = own_head(mm_tn(lows[p], keys), padded) * 0.125

    def finish(self):
        t, rows, width, grads = self.t, self.t.rows, self.t.width, self.grads
        for c in range(3 * width // 128):
            grads[:, 128 * c : 128 * c + 128] = self.joint_grad[c, 0:rows, :].astype(BF16)
        start = pl.multiple_of(self.place[0] * (2 * width), 128)
        self.own.send(grads.at[:, pl.ds(start, 2 * width)], self.own.out)
        start = pl.multiple_of(2 * width - start, 128)
        self.send.send(grads.at[:, pl.ds(start, 2 * width)], self.send.out)
        joint_weight = self.joint_weight.get()

        def step(n, cols):
            self.normed_grad[:, cols] = mm_nt(grads[:, 0 : 3 * width], joint_weight[cols, :])

        tile_loop(width, step)
        gain = shift = 0.0
        for at, size in chunks(t.real):
            some = slice(at, at + size)
            normal, inverse = normalise(self.tokens[some, :].astype(F32))
            up = self.normed_grad[some, :]
            gain += column_sum(up * normal)
            shift += column_sum(up)
            self.tokens_out.ref[some, :] = self.grad[some, :] + norm_back(
                up, vec(self.first_gain), normal, inverse
            )
        self.gain_grad[...] = gain
        self.shift_grad[...] = shift
        self.tokens_out.done()


def backs_kernel(scalars, held, lazies, outs, scratch):
    head_in, held = held[:7], held[7:]
    head_weights, lazies = lazies[:3], lazies[3:]
    head_outs, outs = outs[:8], outs[8:]
    head_of(TEXT, head_in[0][...], head_in[1:3], head_in[3:7], head_weights, head_outs)
    order = [5, 6, 0, 1, 7, 8, 2, 3, 9, 4]
    lazies = [lazies[order.index(i)] for i in range(10)]
    held = [*held[:3], *held[3:5], head_outs[5]]
    image, text = [
        Back(
            t,
            *scalars,
            held[3 * i : 3 * i + 3],
            lazies[5 * i : 5 * i + 5],
            outs[5 * i : 5 * i + 5],
            scratch[4 * i : 4 * i + 4],
        )
        for i, t in enumerate((IMAGE, TEXT))
    ]
    text.context()
    image.context()

    def both(b):
        text.attend(b)
        image.attend(b)

    loop(BATCH, both, UNROLL_BACK)
    text.finish()
    image.finish()


def turn(source, target, unroll=3):
    def step(n):
        cols = pl.ds(pl.multiple_of(n * 128, 128), 128)
        target[cols, 0 : source.shape[0]] = source[:, cols].T

    loop(source.shape[1] // 128, step, unroll)


def lanes_down(values):
    return jnp.concatenate(
        [values[:, :, at : at + 128] for at in range(0, values.shape[2], 128)], axis=1
    )


def put(out, device, unit, values):
    count = values.shape[1] // 16
    size = values.shape[0]
    values = values.reshape(size, count, 16, 128).astype(BF16)
    out[pl.ds(device, size), unit : unit + count] = values


def pack_twelve(first, second, out, unit=0, each=4):
    cols = first.shape[1]
    count = cols // 128
    sub = lax.broadcasted_iota(jnp.int32, (each, 8, cols), 1) < 4

    def step(e):
        rows = pl.ds(pl.multiple_of(e * (24 * each), 8), 24 * each)
        x = first[rows, :].reshape(each, 24, cols)
        y = second[rows, :].reshape(each, 24, cols)
        left, right = x[:, 8:16], y[:, 8:16]
        even = jnp.where(sub, left, pltpu.roll(right, 4, 1))
        odd = jnp.where(sub, pltpu.roll(left, 4, 1), right)
        parts = []
        for a, b, c in ((x[:, 0:8], y[:, 0:8], even), (x[:, 16:24], y[:, 16:24], odd)):
            parts.append(jnp.concatenate([lanes_down(v) for v in (a, b, c)], axis=1))
        if parts[0].shape[1] % 16:
            fill = jnp.zeros((each, 16 - parts[0].shape[1] % 16, 128), F32)
            parts = [jnp.concatenate([part, fill], axis=1) for part in parts]
        height = parts[0].shape[1]
        values = jnp.stack(parts, axis=1).reshape(2 * each, height, 128)
        put(out, e * (2 * each), unit, values)

    loop(32 // each, step, UNROLL_PACK)


def pack_rows(result, rows, out, unit=0, each=8, device=0):
    total = result.shape[0] // rows
    cols = result.shape[1]

    def step(e):
        some = pl.ds(pl.multiple_of(e * (rows * each), 8), rows * each)
        values = lanes_down(result[some, :].reshape(each, rows, cols))
        put(out, device + e * each, unit, values)

    loop(total // each, step, UNROLL_PACK)


def put_extra(t, ref, rows):
    rows = jnp.concatenate([rows, jnp.zeros_like(rows)], axis=0)
    ref[t.extra : t.extra + 16, :] = rows.astype(BF16)


def wide_grads(t, half, product, send, at, first, second):
    if t is IMAGE:
        for i in range(3):
            first[...] = product(256 * i, 256)
            second[...] = product(768 + 256 * i, 256)
            pack_twelve(first, second, send.ref, 3 * i)
            units = slice(3 * i, 3 * i + 3)
            send.units_done(slice(None), units, slice(at + 3 * i, at + 3 * i + 3))
    else:
        for i in range(2):
            first[...] = product(512 * i, 512)
            pack_rows(first, 8, send.ref, 2 * i)
            units = slice(2 * i, 2 * i + 2)
            send.units_done(slice(None), units, slice(at + 2 * i, at + 2 * i + 2))


def feed_kernel(t, at, scalars, held, lazies, outs, scratch):
    (place,) = scalars
    wide_rows, narrow_rows = held
    normed, wides, narrows = lazies[0:2], lazies[2:4], lazies[4:6]
    actives = lazies[6:14]
    (out,) = outs
    first, second, narrow_result = scratch

    def patch(refs, rows):
        size = rows.shape[1] // 2
        some = pl.ds(pl.multiple_of(place[0] * size, 128), size)
        for side, ref in enumerate(refs):
            put_extra(t, ref.get(), rows[BATCH * side : BATCH * side + BATCH, some])

    patch(wides, wide_rows)
    lefts = [ref.get() for ref in normed]
    wides = [ref.get() for ref in wides]

    def product(tile, size):
        return sum(mm(a[:, 0 : t.rows], b[:, tile : tile + size]) for a, b in zip(lefts, wides))

    wide_grads(t, place[0], product, out, at, first, second)
    patch(narrows, narrow_rows)
    narrows = [ref.get() for ref in narrows]
    wide_units, units = (9, 9) if t is IMAGE else (4, 4)
    some = slice(wide_units, wide_units + units)
    for j in range(4):
        pair = [actives[2 * j].get(), actives[2 * j + 1].get()]
        narrow_result[...] = sum(mm(a[:, 0 : t.rows], b[...]) for a, b in zip(pair, narrows))
        pack_rows(narrow_result, t.hidden // DEVS, out.ref, wide_units, 4, 16 * j)
        out.units_done(
            slice(16 * j, 16 * j + 16), some, slice(at + wide_units, at + wide_units + units)
        )


def rest_kernel(scalars, held, lazies, outs, scratch):
    (place,) = scalars
    (out,) = outs
    first, second, third = scratch[:3]
    misc_scratch, spread = scratch[3:6], scratch[6]
    half = place[0]
    misc, text_stage, image_stage = [Staged(out.out, ref, out.sems, out.pending) for ref in scratch[7:10]]
    misc_grads(half, held[:2], held[2:], misc, misc_scratch, spread)
    for t, ins, stage, results in (
        (TEXT, lazies[0:4], text_stage, (third, None)),
        (IMAGE, lazies[4:8], image_stage, (first, second)),
    ):
        width = t.width
        lefts, rights = [ref.get() for ref in ins[0::2]], [ref.get() for ref in ins[1::2]]

        def product(tile, size):
            late = jnp.where(half * (2 * width) + tile >= 3 * width, width, 0)
            rows = pl.ds(pl.multiple_of(late, 128), width)
            return sum(
                mm(a[rows, 0 : t.rows], b[:, tile : tile + size]) for a, b in zip(lefts, rights)
            )

        wide_grads(t, half, product, stage, REST_AT["image" if t is IMAGE else "text"], *results)


IMAGE_FEED_UNITS = 18
LATE_UNITS = 24
TEXT_FEED_AT = 0
REST_AT = {"text": 8, "image": 15}
MISC_AT = 12


def misc_grads(half, factors, vectors, out, scratch, spread):
    image_factors, text_factors = factors
    first, second, third = scratch

    def product(t, ref, at, size):
        final = ref[:, 0 : t.width].astype(BF16)
        start = pl.multiple_of(t.width + half * 256 + at, 128)
        return mm_tn(final, ref[:, pl.ds(start, size)].astype(BF16))

    first[...] = product(IMAGE, image_factors, 0, 128)
    second[...] = product(IMAGE, image_factors, 128, 128)
    third[...] = product(TEXT, text_factors, 0, 256)
    pack_twelve(first, second, out.ref, 1, 8)
    pack_rows(third, 8, out.ref, 0)
    spread[...] = jnp.zeros_like(spread)
    for side, refs_of, width in ((0, vectors[:8], 768), (64, vectors[8:], 512)):
        each = width // DEVS
        device = lax.broadcasted_iota(jnp.int32, (DEVS, width), 0)
        column = lax.broadcasted_iota(jnp.int32, (DEVS, width), 1)
        mine = jnp.logical_and(column >= device * each, column < device * each + each)
        source = lax.broadcasted_iota(jnp.int32, (width, 128), 0)
        lane = lax.broadcasted_iota(jnp.int32, (width, 128), 1)
        at = lax.rem(source, each)
        high_at = jnp.where(lane == at + side, 1.0, 0.0).astype(BF16)
        low_at = jnp.where(lane == at + side + 32, 1.0, 0.0).astype(BF16)
        rows = [refs_of[0][...], refs_of[1][...], refs_of[2][...] + refs_of[3][...]]
        rows += [refs_of[4][...] + refs_of[5][...], refs_of[6][...], refs_of[7][...]]
        for k, row in enumerate(rows):
            row = jnp.where(mine, row, 0.0)
            high = row.astype(BF16)
            low = (row - high.astype(F32)).astype(BF16)
            spread[:, 8 + k, :] += mm(high, high_at) + mm(low, low_at)
    out.ref[:, 2] = (out.ref[:, 2].astype(F32) + spread[...]).astype(BF16)
    out.units_done(slice(None), slice(0, 3), slice(MISC_AT, MISC_AT + 3))


def unpack_kernel(place, mine, other, *outs):
    split = 16 * IMAGE_FEED_UNITS
    feed_mine, feed_other = mine.at[0:split], other.at[0:split]
    late_mine, late_other = mine.at[split:], other.at[split:]
    (
        image_joint,
        image_output,
        image_widen,
        image_narrow,
        image_projection,
        text_joint,
        text_output,
        text_widen,
        text_narrow,
        text_projection,
    ) = outs[:10]
    odd = place[1] % 2

    def emit(half, feed, late):
        def into(ref, col, body, tail):
            @pl.when(odd == 0)
            def _():
                ref[0:8, col : col + 128] = body
                ref[8:12, col : col + 128] = tail

            @pl.when(odd == 1)
            def _():
                ref[0:4, col : col + 128] = tail
                ref[4:12, col : col + 128] = body

        def image_wide(source, at, store):
            for tile in range(3):
                block = source[16 * (at + 3 * tile) : 16 * (at + 3 * tile) + 48, :]
                for side in range(2):
                    for g in range(2):
                        body = block[16 * side + 8 * g : 16 * side + 8 * g + 8]
                        tail = block[32 + 8 * g + 4 * side : 36 + 8 * g + 4 * side]
                        store(half * 1536 + side * 768 + tile * 256 + g * 128, body, tail)

        def joint_store(col, body, tail):
            if col < 2304:
                into(image_joint, col, body, tail)
            else:
                into(image_output, col - 2304, body, tail)

        image_wide(feed, 0, functools.partial(into, image_widen))
        image_wide(late, REST_AT["image"], joint_store)
        at = 16 * 9
        for g in range(3):
            col = half * 384 + 128 * g
            image_narrow[:, col : col + 128] = feed[at + 48 * g : at + 48 * g + 48, :]
        at = 16 * (MISC_AT + 1)
        for side in range(2):
            col = half * 256 + 128 * side
            tail = late[at + 16 + 4 * side : at + 20 + 4 * side, :]
            into(image_projection, col, late[at + 8 * side : at + 8 * side + 8, :], tail)
        for g in range(8):
            col = half * 1024 + 128 * g
            at = 16 * TEXT_FEED_AT + 8 * g
            text_widen[:, col : col + 128] = late[at : at + 8, :]
            at = 16 * REST_AT["text"] + 8 * g
            block = late[at : at + 8, :]
            if col < 1536:
                text_joint[:, col : col + 128] = block
            else:
                text_output[:, col - 1536 : col - 1408] = block
        for g in range(2):
            col = half * 256 + 128 * g
            at = 16 * (TEXT_FEED_AT + 4) + 32 * g
            text_narrow[:, col : col + 128] = late[at : at + 32, :]
            at = 16 * MISC_AT + 8 * g
            text_projection[:, col : col + 128] = late[at : at + 8, :]

    for half in range(2):

        @pl.when(place[0] == half)
        def _():
            emit(half, feed_mine, late_mine)
            emit(1 - half, feed_other, late_other)

    at = 16 * (MISC_AT + 2) + 8
    vectors = late_mine[at : at + 8, :] + late_other[at : at + 8, :]
    for k in range(12):
        each, side = (12, 0) if k < 6 else (8, 64)
        row = vectors[k % 6 : k % 6 + 1, :]
        outs[10 + k][...] = row[:, side : side + each] + row[:, side + 32 : side + 32 + each]


SMEM = pl.BlockSpec(memory_space=pltpu.SMEM)
VMEM = pl.BlockSpec(memory_space=pltpu.VMEM)


def call(body, name, scalars, arrays, outs, scratch=(), flops=1 << 32):
    return pl.pallas_call(
        body,
        name=name,
        out_shape=tuple(jax.ShapeDtypeStruct(shape, kind) for shape, kind in outs),
        in_specs=[SMEM] * len(scalars) + [VMEM] * len(arrays),
        out_specs=tuple(VMEM for _ in outs),
        scratch_shapes=[pltpu.VMEM(shape, kind) for shape, kind in scratch],
        compiler_params=pltpu.CompilerParams(vmem_limit_bytes=VMEM_LIMIT),
        cost_estimate=pl.CostEstimate(flops=flops, bytes_accessed=20 << 20, transcendentals=0),
    )(*scalars, *arrays)


BIG = 1 << 18


def lazy_call(body, name, scalars, held, lazies, outs, scratch=(), flops=1 << 33, buffer=None, after=(), ahead=3):
    many = 24

    def kernel(*refs):
        refs = list(refs)

        def take(count):
            got = refs[:count]
            del refs[:count]
            return got

        scalar_refs, held_refs = take(len(scalars)), take(len(held))
        sources = take(len(lazies))
        take(len(after) + (buffer is not None))
        out_refs = take(len(outs))
        targets = take(len(lazies))
        stages = take(sum(1 for out in outs if out[2]))
        scratch_refs = take(len(scratch))
        in_sems, out_sems = refs
        lazy = []
        for i, (source, target, (_, index, _)) in enumerate(zip(sources, targets, lazies)):
            if index is not None:
                source = source.at[index(*scalar_refs)]
            lazy.append(Lazy(lazy, source, target, in_sems.at[i]))
        for item in lazy[:ahead]:
            item.start()
        pending = []
        results = []
        for out, ref in zip(outs, out_refs):
            if out[2] is None:
                results.append(ref)
            else:
                results.append(Staged(ref, stages.pop(0) if out[2] else None, out_sems, pending))
        body(scalar_refs, held_refs, lazy, results, scratch_refs)
        for item in lazy:
            if item.started:
                item.get()
        for copy in pending:
            copy.wait()

    any_spec = pl.BlockSpec(memory_space=pl.ANY)
    scratch_shapes = [pltpu.VMEM(shape, array.dtype) for array, _, shape in lazies]
    scratch_shapes += [pltpu.VMEM(stage, kind) for _, kind, stage in outs if stage]
    scratch_shapes += [pltpu.VMEM(shape, kind) for shape, kind in scratch]
    scratch_shapes += [pltpu.SemaphoreType.DMA((max(1, len(lazies)),)), pltpu.SemaphoreType.DMA((many,))]
    arrays = [*held, *[array for array, _, _ in lazies], *after]
    specs = [SMEM] * len(scalars) + [VMEM] * len(held) + [any_spec] * (len(lazies) + len(after))
    aliases = {}
    if buffer is not None:
        aliases = {len(scalars) + len(arrays): 0}
        arrays.append(buffer)
        specs.append(any_spec)
    return pl.pallas_call(
        kernel,
        name=name,
        out_shape=tuple(jax.ShapeDtypeStruct(shape, kind) for shape, kind, _ in outs),
        in_specs=specs,
        out_specs=tuple(VMEM if stage is None else any_spec for _, _, stage in outs),
        scratch_shapes=scratch_shapes,
        input_output_aliases=aliases,
        compiler_params=pltpu.CompilerParams(vmem_limit_bytes=VMEM_LIMIT),
        cost_estimate=pl.CostEstimate(flops=flops, bytes_accessed=20 << 20, transcendentals=0),
    )(*scalars, *arrays)


def all_of(array):
    return array, None, array.shape


def staged(shape, kind):
    return shape, kind, shape


def plain(shape, kind):
    return shape, kind, None


def fronts_call(lengths, tokens, block_grads, weights):
    held, lazies, outs, scratch = [], [], [], []
    for t, token, grad, w in zip((IMAGE, TEXT), tokens, block_grads, weights):
        rows, width, hidden = t.rows, t.width, t.hidden
        held += [token, w[0], w[1], w[4], w[5], w[8], w[9], grad]
        lazies += [all_of(w[i]) for i in (2, 3, 6, 7, 10)]
        outs += [
            staged((2 * width, t.lanes), BF16),
            staged((BATCH, t.padded, 3 * width), BF16),
            staged((BATCH, t.heads // 2, t.padded, 2 * t.padded), BF16),
            staged((rows, width), F32),
            plain((BATCH, EMBED), BF16),
        ]
        scratch += [
            ((3 * width // 128, t.spread, 128), F32),
            ((width // 128, t.spread, 128), F32),
            ((rows, width), BF16),
            ((rows, width), BF16),
        ]
    lazies = [lazies[i] for i in (5, 6, 0, 7, 8, 9, 1, 2, 3, 4)]
    outs.append(plain((BATCH, ROW_TOTAL), F32))
    outs.append(plain((DEVS, BATCH, 2 * EMBED), BF16))
    results = lazy_call(fronts_kernel, "fronts", (lengths,), held, lazies, outs, scratch, ahead=6)
    return results[:5], results[5:10], results[10], results[11]


def middle(t, name, place, lengths, mixed, block_grad, gain, shift, widen, narrow, after):
    rows, width, hidden = t.rows, t.width, t.hidden
    steps = hidden // t.step
    outs = (
        ((width, t.lanes), BF16),
        ((hidden, t.lanes), BF16),
        ((rows, hidden // 2), BF16),
        ((rows, hidden // 2), BF16),
        ((rows, width // 2), BF16),
        ((rows, width // 2), BF16),
        ((rows, width), F32),
        ((1, width), F32),
        ((1, width), F32),
    )

    def held(shape):
        return pl.BlockSpec(shape, lambda i, *_: (0,) * len(shape))

    def tile(i, place):
        return lax.rem(i + place[0] * (steps // 2), steps)

    out_specs = [held(shape) for shape, _ in outs]
    out_specs[1] = pl.BlockSpec((t.step, t.lanes), lambda i, place, lengths: (tile(i, place), 0))
    out_specs[2] = pl.BlockSpec((rows, t.step), lambda i, *_: (0, jnp.minimum(i, steps // 2 - 1)))
    out_specs[3] = pl.BlockSpec((rows, t.step), lambda i, *_: (0, jnp.maximum(i - steps // 2, 0)))
    in_specs = [held(a.shape) for a in (mixed, block_grad, gain, shift)]
    in_specs.append(pl.BlockSpec((width, t.step), lambda i, place, lengths: (0, tile(i, place))))
    in_specs.append(pl.BlockSpec((t.step, width), lambda i, place, lengths: (tile(i, place), 0)))
    in_specs += [pl.BlockSpec(memory_space=pl.ANY)] * len(after)

    def kernel(*refs):
        middle_kernel(t, *refs[:8], *refs[8 + len(after) :])

    return pl.pallas_call(
        kernel,
        name=name + "_middle",
        out_shape=tuple(jax.ShapeDtypeStruct(shape, kind) for shape, kind in outs),
        grid_spec=pltpu.PrefetchScalarGridSpec(
            num_scalar_prefetch=2,
            grid=(steps,),
            in_specs=in_specs,
            out_specs=tuple(out_specs),
            scratch_shapes=[
                pltpu.VMEM((rows, width), BF16),
                pltpu.VMEM((rows, width), BF16),
                pltpu.VMEM((rows, width), F32),
            ],
        ),
        compiler_params=pltpu.CompilerParams(vmem_limit_bytes=VMEM_LIMIT),
        cost_estimate=pl.CostEstimate(flops=1 << 35, bytes_accessed=20 << 20, transcendentals=0),
    )(place, lengths, mixed, block_grad, gain, shift, widen, narrow, *after)


def head_outs(t):
    return [plain((1, t.width), F32)] * 4 + [
        plain((2 * BATCH, t.width + EMBED), F32),
        plain((BATCH, t.width), F32),
        plain((2 * BATCH, t.width), F32),
        plain((2 * BATCH, t.hidden), F32),
    ]


def backs_call(place, lengths, head_in, head_weights, image_row, towers, after):
    held, lazies, outs, scratch = [*head_in], [], head_outs(TEXT), []
    for t, (tokens, gain, arrays) in zip((IMAGE, TEXT), towers):
        rows, width = t.rows, t.width
        held += [tokens, gain]
        if t is IMAGE:
            held.append(image_row)
        lazies += [all_of(a) for a in arrays]
        outs += [
            ((rows, 2 * width), BF16, ()),
            ((rows, 2 * width), BF16, ()),
            staged((t.real, width), F32),
            plain((1, width), F32),
            plain((1, width), F32),
        ]
        scratch += [
            ((width // 128, t.spread, 128), F32),
            ((3 * width // 128, t.spread, 128), F32),
            ((rows, width), F32),
            ((rows, 4 * width), BF16),
        ]
    lazies = [lazies[i] for i in (5, 6, 0, 1, 7, 8, 2, 3, 9, 4)]
    lazies = [all_of(w) for w in head_weights] + lazies
    results = lazy_call(
        backs_kernel, "backs", (place, lengths), held, lazies, outs, scratch, after=after, ahead=8
    )
    return results[:8], results[8:13], results[13:]


def feed(t, place, head, middle, other, buffer, after):
    rows, width = t.rows, t.width
    name = "image" if t is IMAGE else "text"
    own = (middle[0], middle[1], middle[2], middle[4])
    lazies = [all_of(own[0]), all_of(other[0]), all_of(own[2]), all_of(other[2])]
    lazies += [all_of(own[3]), all_of(other[3])]
    for j in range(4):
        some = slice(width * j, width * j + width)
        for side in (own, other):
            lazies.append((side[1], lambda *_, some=some: (some, slice(None)), (width, t.lanes)))
    cols = 256 if t is IMAGE else 512
    scratch = [
        ((width, cols), F32),
        ((width, cols) if t is IMAGE else (8, 128), F32),
        ((width, width // 2), F32),
    ]
    units = IMAGE_FEED_UNITS if t is IMAGE else 8
    total = LATE_UNITS if buffer else units
    (out,) = lazy_call(
        functools.partial(feed_kernel, t, TEXT_FEED_AT if buffer else 0),
        name + "_feed",
        (place,),
        (head[7], head[6]),
        lazies,
        [((DEVS, total, 16, 128), BF16, (DEVS, units, 16, 128))],
        scratch,
        after=after,
        ahead=10,
    )
    return out


def rest(place, factors, vectors, sides, buffer):
    lazies = []
    for own, other in (sides[1], sides[0]):
        lazies += [all_of(a) for a in (*own, *other)]
    outs = [((DEVS, LATE_UNITS, 16, 128), BF16, ())]
    scratch = [
        ((768, 256), F32),
        ((768, 256), F32),
        ((512, 512), F32),
        ((768, 128), F32),
        ((768, 128), F32),
        ((512, 256), F32),
        ((DEVS, 16, 128), F32),
        ((DEVS, 3, 16, 128), BF16),
        ((DEVS, 4, 16, 128), BF16),
        ((DEVS, 9, 16, 128), BF16),
    ]
    (out,) = lazy_call(
        rest_kernel, "rest", (place,), [*factors, *vectors], lazies, outs, scratch, buffer=buffer, ahead=4
    )
    return out


def sum_blocks(pieces):
    lazies, steps = [], []
    for received, step in pieces:
        devices, units = received.shape[:2]
        for at in range(0, units, step):
            some = slice(at, at + step)
            lazies.append(
                (received, lambda *_, some=some: (slice(None), some), (devices, step, 16, 128))
            )
            steps.append(step)

    def body(scalars, held, blocks, outs, scratch):
        at = 0
        for step, block in zip(steps, blocks):
            total = jnp.sum(block.get()[...].astype(F32), axis=0)
            outs[0][at : at + 16 * step, :] = total.reshape(16 * step, 128)
            at += 16 * step

    outs = [plain((16 * sum(steps), 128), F32)]
    return lazy_call(body, "sum_blocks", (), (), lazies, outs, flops=1 << 34, ahead=len(lazies))[0]


def behind(arrays, after):
    def kernel(*refs):
        pass

    any_spec = pl.BlockSpec(memory_space=pltpu.HBM)
    return pl.pallas_call(
        kernel,
        name="behind",
        out_shape=[jax.ShapeDtypeStruct(array.shape, array.dtype) for array in arrays],
        in_specs=[any_spec] * (len(arrays) + len(after)),
        out_specs=[any_spec] * len(arrays),
        input_output_aliases={i: i for i in range(len(arrays))},
    )(*arrays, *after)


SWAP = [(0, 1), (1, 0)]


def by_token(tokens):
    return tokens.transpose(1, 0, 2).reshape(-1, tokens.shape[2])


def shards(*args):
    image_tokens, image_weights, image_block_grad = args[0], args[1:12], args[12]
    text_tokens, caption_lengths = args[13], args[14]
    text_weights, text_block_grad, log_scale = args[15:26], args[26], args[27]
    core = lax.axis_index("tower")
    dp = lax.axis_index("dp")
    place = jnp.stack([core, dp]).astype(jnp.int32)
    tokens = (by_token(image_tokens), by_token(text_tokens))
    block_grads = (by_token(image_block_grad), by_token(text_block_grad))
    weights = (image_weights, text_weights)
    kinds = ((0, IMAGE, "image"), (1, TEXT, "text"))
    *fronts, kept, copies = fronts_call(caption_lengths, tokens, block_grads, weights)
    units = [f[4] for f in fronts]
    own = lax.all_to_all(copies, "dp", 0, 0, tiled=True).reshape(DEVS * BATCH, 2 * EMBED)

    def swap(*arrays):
        return [lax.ppermute(array, "tower", SWAP) for array in arrays]

    def middle_of(i, after):
        _, t, name = kinds[i]
        w = weights[i]
        return middle(
            t, name, place, caption_lengths, fronts[i][3], block_grads[i], w[4], w[5], w[6], w[7], after
        )

    (kept_other,) = swap(kept)
    image_middle = list(middle_of(0, ()))
    (own,) = behind([own], (image_middle[0], kept_other))
    (other,) = swap(own)
    sent = (0, 1, 3, 5)
    for k, array in zip(sent, behind([image_middle[k] for k in sent], (other,))):
        image_middle[k] = array
    image_sent = swap(*[image_middle[k] for k in sent])

    w = image_weights
    paired = lazy_call(
        pair_kernel,
        "pairs",
        (place, log_scale),
        [own, other, kept, kept_other, w[8], w[9], w[4], w[5]],
        [all_of(w[10]), all_of(w[7]), all_of(w[6])],
        [plain((1, 128), F32), plain((1, 128), F32), plain((2 * BATCH, EMBED), F32), *head_outs(IMAGE)],
        ahead=6,
    )
    loss, scale_grad = paired[0][0, :1], paired[1][0, :1]
    image_head = paired[3:]
    image_feed = feed(IMAGE, place, image_head, image_middle, image_sent, False, ())
    feed_total = lax.all_to_all(image_feed, "dp", 0, 0, tiled=True)
    text_middle = middle_of(1, (image_feed,))
    middles = (image_middle, text_middle)

    back_in = []
    for i, _, _ in kinds:
        f, m, w = fronts[i], middles[i], weights[i]
        back_in.append((tokens[i], w[0], (w[3], m[6], f[1], f[2], w[2])))
    w = text_weights
    text_head, *backs = backs_call(
        place,
        caption_lengths,
        [paired[2], kept, kept_other, w[8], w[9], w[4], w[5]],
        [w[10], w[7], w[6]],
        image_head[5],
        back_in,
        (text_middle[0],),
    )
    heads = (image_head, text_head)
    text_sent = swap(*[text_middle[k] for k in sent])
    late = feed(TEXT, place, heads[1], text_middle, text_sent, True, (backs[1][0],))
    sides = []
    for f, k in zip(fronts, backs):
        sides.append(((f[0], k[0]), swap(f[0], k[1])))
    vectors = []
    for m, h, k in zip(middles, heads, backs):
        vectors += [k[3], k[4], m[7], h[2], m[8], h[3], h[0], h[1]]
    factors = [heads[0][4], heads[1][4]]
    (late,) = behind([rest(place, factors, vectors, sides, late)], (feed_total,))
    late_total = lax.all_to_all(late, "dp", 0, 0, tiled=True)
    mine = sum_blocks(((feed_total, 3), (late_total, 3)))
    (theirs,) = swap(mine)
    weight_outs = (
        ((12, 2304), F32),
        ((12, 768), F32),
        ((12, 3072), F32),
        ((48, 768), F32),
        ((12, 512), F32),
        ((8, 1536), F32),
        ((8, 512), F32),
        ((8, 2048), F32),
        ((32, 512), F32),
        ((8, 512), F32),
    )
    vector_outs = (((1, 12), F32),) * 6 + (((1, 8), F32),) * 6
    grads = call(unpack_kernel, "unpack", (place,), (mine, theirs), weight_outs + vector_outs)

    def ordered(vectors, weights):
        joint, output, widen, narrow, projection = weights
        v = [x.reshape(-1) for x in vectors]
        return [v[0], v[1], joint, output, v[2], v[3], widen, narrow, v[4], v[5], projection]

    def by_sequence(t, grad):
        return grad.reshape(t.length, BATCH, t.width).transpose(1, 0, 2)

    return (
        loss,
        units[0],
        units[1],
        by_sequence(IMAGE, backs[0][2]),
        *ordered(grads[10:16], grads[:5]),
        by_sequence(TEXT, backs[1][2]),
        *ordered(grads[16:22], grads[5:10]),
        scale_grad,
    )


def solution(mesh):
    spread = P(("tower", "dp"), None, None)
    weights = [P()] * 11
    placed = (spread, *weights, spread, spread, P(("tower", "dp")), *weights, spread, P())
    vector, matrix = P("dp"), P("dp", None)
    grads = [vector, vector, matrix, matrix, vector, vector, matrix, matrix, vector, vector, matrix]
    units = P(("tower", "dp"), None)
    return jax.shard_map(
        shards,
        mesh=mesh,
        in_specs=placed,
        out_specs=(P(), units, units, spread, *grads, spread, *grads, P()),
        check_vma=False,
    )
```
